32 devices in a mesh: ctx: 16 (over z, y, x), ch: 2 (over core).
Axes of the slice: x: 2, y: 2, z: 4, core: 2. Of those that a mesh axis runs over, the one named last changes fastest.
Arguments:
- q_proj: bfloat16 [4096, 4096], P('ctx', 'ch'), may hold values from -6 to 6
- k_proj: bfloat16 [4096, 4096], P('ctx', 'ch'), may hold values from -6 to 6
- v_proj: bfloat16 [4096, 4096], P('ctx', 'ch'), may hold values from -6 to 6
- residue: float32 [16, 4096], P(None, 'ch'), may hold values from -4 to 4
- rate: float32 [16, 4096], P(None, 'ch'), may hold values from 4.8828125e-05 to 0.1
- skip: float32 [4096], P('ch'), may hold values from -4 to 4
- w_out: bfloat16 [4096, 6144], P('ctx', 'ch'), may hold values from -0.09375 to 0.09375
Outputs:
- mixed: bfloat16 [4096, 6144], P('ctx', 'ch')
The draws below stay inside these ranges and needn't reach their ends.
All inputs are finite; a program needn't handle non-finite values.
Results may differ from the reference program's by a relative error of at most 0.0049.
Values may be sent and summed in bfloat16 or wider, within the bound.
No kernel may reach another device: no remote copies, remote signals or barrier semaphores. Data moves between devices by JAX's collectives and lax.ppermute only.
A program may use at most 192 MiB of HBM per device.

```python
import math
import jax
import jax.numpy as jnp
from jax import lax

D = 6144
SLAB = 4096
MODES = 16
SEQ = 4096


def draw_rate(key, part):
    key_pick, key_fast, key_middle, key_slow = jax.random.split(jax.random.fold_in(key, 7), 4)
    shape = (MODES, SLAB)
    picks = jax.random.randint(key_pick, shape, 0, 8)
    fast_pick = picks < 3
    middle_pick = jnp.logical_and(picks >= 3, picks < 6)
    fast_rate = jnp.exp(jax.random.uniform(key_fast, shape, jnp.float32, jnp.log(0.02), jnp.log(0.1)))
    middle_rate = jnp.exp(jax.random.uniform(key_middle, shape, jnp.float32, jnp.log(2.0 / SEQ), jnp.log(0.02)))
    slow_rate = jnp.exp(jax.random.uniform(key_slow, shape, jnp.float32, jnp.log(0.2 / SEQ), jnp.log(2.0 / SEQ)))
    chosen = jnp.where(fast_pick, fast_rate, jnp.where(middle_pick, middle_rate, slow_rate))
    return chosen.astype(jnp.float32)


def shard_levels(own_key, dims, shards, least, high):
    loudness = 1.0
    for dim, shards_of in shards:
        steps = jax.random.uniform(jax.random.fold_in(jax.random.fold_in(own_key, 6), dim), (shards_of,), jnp.float32, least / len(shards), high / len(shards))
        loudness = loudness * jnp.repeat(jnp.exp(steps), dims[dim] // shards_of).reshape((-1,) + (1,) * (len(dims) - 1 - dim))
    return loudness


def bell_draw(stream_key, shape, scale, most, pieces=(), kind=jnp.bfloat16):
    factor_of = shard_levels(stream_key, shape, pieces, -0.22, 0.18) if pieces else 1.0
    values = jax.random.normal(stream_key, shape, jnp.float32) * scale * factor_of
    return jnp.minimum(jnp.maximum(values, -most), most).astype(kind)


def setup_inputs(seed: int = 0) -> dict:
    keys = jax.random.split(jax.random.key(seed), 8)
    return {
        "q_proj": bell_draw(keys[0], (SEQ, SLAB), 1.0, 6.0, ((0, 16), (1, 2))),
        "k_proj": bell_draw(keys[1], (SEQ, SLAB), 1.0, 6.0, ((0, 16), (1, 2))),
        "v_proj": bell_draw(keys[2], (SEQ, SLAB), 1.0, 6.0, ((0, 16), (1, 2))),
        "residue": bell_draw(keys[3], (MODES, SLAB), 1.0, 4.0, ((1, 2),), jnp.float32),
        "rate": draw_rate(jax.random.fold_in(keys[7], 71), 0),
        "skip": bell_draw(keys[5], (SLAB,), 1.0, 4.0, ((0, 2),), jnp.float32),
        "w_out": bell_draw(keys[6], (SLAB, D), SLAB ** -0.5, 0.09375, ((0, 16), (1, 2))),
    }


def filter_block(operands):
    signal_block, coefficient_block, rate_block = operands
    position = jnp.arange(SEQ).astype(jnp.float32)
    filt = jnp.zeros(signal_block.shape, jnp.float32)
    for mode_index in range(MODES):
        filt = filt + coefficient_block[mode_index][None, :] * jnp.exp(-rate_block[mode_index][None, :] * position[:, None])
    length = 2 * SEQ
    spectrum = jnp.fft.rfft(signal_block, n=length, axis=0) * jnp.fft.rfft(filt, n=length, axis=0)
    return jnp.fft.irfft(spectrum, n=length, axis=0)[:SEQ]

def reference(q_proj, k_proj, v_proj, residue, rate, skip, w_out):
    signal = k_proj.astype(jnp.float32) * v_proj.astype(jnp.float32)
    coefficient = residue * jnp.sqrt(2.0 * rate)
    width = math.gcd(SLAB, 128)
    blocks = SLAB // width
    signal_blocks = signal.reshape(SEQ, blocks, width).transpose(1, 0, 2)
    coefficient_blocks = coefficient.reshape(MODES, blocks, width).transpose(1, 0, 2)
    rate_blocks = rate.reshape(MODES, blocks, width).transpose(1, 0, 2)
    conv = lax.map(filter_block, (signal_blocks, coefficient_blocks, rate_blocks))
    conv = conv.transpose(1, 0, 2).reshape(SEQ, SLAB)
    conv = conv + skip[None, :] * signal
    gated = (q_proj.astype(jnp.float32) * conv).astype(jnp.bfloat16)
    row_block = math.gcd(SEQ, 4096)

    def project(rows_in):
        return jnp.dot(rows_in, w_out, preferred_element_type=jnp.float32).astype(jnp.bfloat16)
    mixed = lax.map(project, gated.reshape(SEQ // row_block, row_block, SLAB))
    return mixed.reshape(SEQ, D)
```

```python
import jax
import jax.numpy as jnp
from jax import lax
from jax.experimental import pallas as pl
from jax.experimental.pallas import tpu as pltpu
from jax.sharding import PartitionSpec as P

LANES = 128
RADIX = 4


def spread_signal(k_ref, v_ref, sig_ref):
    rows, width = k_ref.shape
    groups = width // LANES
    for g in range(groups):
        cols = pl.ds(g * LANES, LANES)
        product = k_ref[:, cols].astype(jnp.float32) * v_ref[:, cols].astype(jnp.float32)
        sig_ref[pl.ds(g, rows, stride=groups), :] = product


def ends_kernel(k_ref, v_ref, rate_ref, end_ref, sig_ref):
    rows, width = k_ref.shape
    modes, groups, _ = rate_ref.shape
    spread_signal(k_ref, v_ref, sig_ref)
    decay = [jnp.exp(-rate_ref[m]) for m in range(modes)]

    def step(t, state):
        s = sig_ref[pl.ds(pl.multiple_of(t * groups, groups), groups), :]
        return tuple(d * h + s for d, h in zip(decay, state))

    zero = jnp.zeros((groups, LANES), jnp.float32)
    state = lax.fori_loop(0, rows, step, (zero,) * modes, unroll=8)
    for m in range(modes):
        end_ref[m] = state[m]


def conv_kernel(q_ref, k_ref, v_ref, rate_ref, residue_ref, skip_ref, enter_ref, out_ref, sig_ref, conv_ref):
    rows, width = k_ref.shape
    modes, groups, _ = rate_ref.shape
    spread_signal(k_ref, v_ref, sig_ref)
    decay = [jnp.exp(-rate_ref[m]) for m in range(modes)]
    weight = [residue_ref[m] * jnp.sqrt(2.0 * rate_ref[m]) for m in range(modes)]
    skip = skip_ref[...]

    def step(t, state):
        at = pl.ds(pl.multiple_of(t * groups, groups), groups)
        s = sig_ref[at, :]
        state = tuple(d * h + s for d, h in zip(decay, state))
        terms = [c * h for c, h in zip(weight, state)] + [skip * s]
        while len(terms) > 1:
            terms = [sum(terms[i : i + 2]) for i in range(0, len(terms), 2)]
        conv_ref[at, :] = terms[0]
        return state

    lax.fori_loop(0, rows, step, tuple(enter_ref[m] for m in range(modes)), unroll=4)
    for g in range(groups):
        cols = pl.ds(g * LANES, LANES)
        conv = conv_ref[pl.ds(g, rows, stride=groups), :]
        out_ref[:, cols] = (q_ref[:, cols].astype(jnp.float32) * conv).astype(out_ref.dtype)


def block_specs(rows, modes, width):
    groups = width // LANES
    return (
        pl.BlockSpec((rows, width), lambda i: (0, i)),
        pl.BlockSpec((modes, groups, LANES), lambda i: (0, i, 0)),
        pl.BlockSpec((groups, LANES), lambda i: (i, 0)),
    )


def end_states(k, v, rate):
    rows, chan = k.shape
    modes = rate.shape[0]
    width = min(chan, 8 * LANES)
    wide, moded, _ = block_specs(rows, modes, width)
    return pl.pallas_call(
        ends_kernel,
        grid=(chan // width,),
        in_specs=[wide, wide, moded],
        out_specs=moded,
        out_shape=jax.ShapeDtypeStruct(rate.shape, jnp.float32),
        scratch_shapes=[pltpu.VMEM((rows * width // LANES, LANES), jnp.float32)],
        compiler_params=pltpu.CompilerParams(vmem_limit_bytes=32 << 20),
        cost_estimate=pl.CostEstimate(
            flops=2 * modes * rows * chan, bytes_accessed=4 * rows * chan, transcendentals=modes * chan
        ),
        name="end_states",
    )(k, v, rate)


def gated_conv(q, k, v, rate, residue, skip, enter):
    rows, chan = k.shape
    modes = rate.shape[0]
    width = min(chan, 8 * LANES)
    wide, moded, single = block_specs(rows, modes, width)
    spread = pltpu.VMEM((rows * width // LANES, LANES), jnp.float32)
    return pl.pallas_call(
        conv_kernel,
        grid=(chan // width,),
        in_specs=[wide, wide, wide, moded, moded, single, moded],
        out_specs=wide,
        out_shape=jax.ShapeDtypeStruct((rows, chan), jnp.bfloat16),
        scratch_shapes=[spread, spread],
        compiler_params=pltpu.CompilerParams(vmem_limit_bytes=32 << 20),
        cost_estimate=pl.CostEstimate(
            flops=4 * modes * rows * chan, bytes_accessed=8 * rows * chan, transcendentals=2 * modes * chan
        ),
        name="gated_conv",
    )(q, k, v, rate, residue, skip, enter)


def shift_ctx(x, by, count):
    return lax.ppermute(x, "ctx", [(i, i + by) for i in range(count - by)])


def entering_states(ends, rate, rows):
    count = lax.axis_size("ctx")
    total = jnp.zeros_like(ends)
    for k in range(1, min(RADIX, count - 1) + 1):
        total = total + jnp.exp(-rate * float(rows * (k - 1))) * shift_ctx(ends, k, count)
    stride = RADIX
    while stride < count:
        base = total
        for k in range(1, RADIX):
            if stride * k < count:
                total = total + jnp.exp(-rate * float(rows * stride * k)) * shift_ctx(base, stride * k, count)
        stride *= RADIX
    return total


def body(q, k, v, residue, rate, skip, w_out):
    rows, chan = q.shape
    modes = rate.shape[0]
    groups = chan // LANES
    w_full = lax.all_gather(w_out, "ctx", axis=0, tiled=True)
    rate = rate.reshape(modes, groups, LANES)
    residue = residue.reshape(modes, groups, LANES)
    skip = skip.reshape(groups, LANES)
    ends = end_states(k, v, rate)
    enter = entering_states(ends, rate, rows)
    gated = gated_conv(q, k, v, rate, residue, skip, enter)
    full_gated = lax.all_gather(gated, "ch", axis=1, tiled=True)
    mixed = jnp.dot(full_gated, w_full, preferred_element_type=jnp.float32)
    return mixed.astype(jnp.bfloat16)


def solution(mesh):
    placed = (
        P("ctx", "ch"),
        P("ctx", "ch"),
        P("ctx", "ch"),
        P(None, "ch"),
        P(None, "ch"),
        P("ch"),
        P("ctx", "ch"),
    )
    return jax.shard_map(
        body, mesh=mesh, in_specs=placed, out_specs=P("ctx", "ch"), check_vma=False
    )
```

```python
import jax
import jax.numpy as jnp
from jax import lax
from jax.experimental import pallas as pl
from jax.experimental.pallas import tpu as pltpu
from jax.sharding import PartitionSpec as P

LANES = 128
RADIX = 4
PLANE = 4


def spread_signal(k_ref, v_ref, sig_ref):
    rows, width = k_ref.shape
    groups = width // LANES
    for g in range(groups):
        cols = pl.ds(g * LANES, LANES)
        product = k_ref[:, cols].astype(jnp.float32) * v_ref[:, cols].astype(jnp.float32)
        sig_ref[pl.ds(g, rows, stride=groups), :] = product


def ends_kernel(k_ref, v_ref, rate_ref, end_ref, sig_ref):
    rows, width = k_ref.shape
    modes, groups, _ = rate_ref.shape
    spread_signal(k_ref, v_ref, sig_ref)
    decay = [jnp.exp(-rate_ref[m]) for m in range(modes)]

    def step(t, state):
        s = sig_ref[pl.ds(pl.multiple_of(t * groups, groups), groups), :]
        return tuple(d * h + s for d, h in zip(decay, state))

    zero = jnp.zeros((groups, LANES), jnp.float32)
    state = lax.fori_loop(0, rows, step, (zero,) * modes, unroll=8)
    for m in range(modes):
        end_ref[m] = state[m]


def conv_kernel(q_ref, k_ref, v_ref, rate_ref, residue_ref, skip_ref, enter_ref, out_ref, sig_ref, conv_ref):
    rows, width = k_ref.shape
    modes, groups, _ = rate_ref.shape
    spread_signal(k_ref, v_ref, sig_ref)
    decay = [jnp.exp(-rate_ref[m]) for m in range(modes)]
    weight = [residue_ref[m] * jnp.sqrt(2.0 * rate_ref[m]) for m in range(modes)]
    skip = skip_ref[...]

    def step(t, state):
        at = pl.ds(pl.multiple_of(t * groups, groups), groups)
        s = sig_ref[at, :]
        state = tuple(d * h + s for d, h in zip(decay, state))
        terms = [c * h for c, h in zip(weight, state)] + [skip * s]
        while len(terms) > 1:
            terms = [sum(terms[i : i + 2]) for i in range(0, len(terms), 2)]
        conv_ref[at, :] = terms[0]
        return state

    lax.fori_loop(0, rows, step, tuple(enter_ref[m] for m in range(modes)), unroll=4)
    for g in range(groups):
        cols = pl.ds(g * LANES, LANES)
        conv = conv_ref[pl.ds(g, rows, stride=groups), :]
        out_ref[:, cols] = (q_ref[:, cols].astype(jnp.float32) * conv).astype(out_ref.dtype)


def block_specs(rows, modes, width):
    groups = width // LANES
    return (
        pl.BlockSpec((rows, width), lambda i: (0, i)),
        pl.BlockSpec((modes, groups, LANES), lambda i: (0, i, 0)),
        pl.BlockSpec((groups, LANES), lambda i: (i, 0)),
    )


def end_states(k, v, rate):
    rows, chan = k.shape
    modes = rate.shape[0]
    width = min(chan, 8 * LANES)
    wide, moded, _ = block_specs(rows, modes, width)
    return pl.pallas_call(
        ends_kernel,
        grid=(chan // width,),
        in_specs=[wide, wide, moded],
        out_specs=moded,
        out_shape=jax.ShapeDtypeStruct(rate.shape, jnp.float32),
        scratch_shapes=[pltpu.VMEM((rows * width // LANES, LANES), jnp.float32)],
        compiler_params=pltpu.CompilerParams(vmem_limit_bytes=32 << 20),
        cost_estimate=pl.CostEstimate(
            flops=2 * modes * rows * chan, bytes_accessed=4 * rows * chan, transcendentals=modes * chan
        ),
        name="end_states",
    )(k, v, rate)


def gated_conv(q, k, v, rate, residue, skip, enter):
    rows, chan = k.shape
    modes = rate.shape[0]
    width = min(chan, 8 * LANES)
    wide, moded, single = block_specs(rows, modes, width)
    spread = pltpu.VMEM((rows * width // LANES, LANES), jnp.float32)
    return pl.pallas_call(
        conv_kernel,
        grid=(chan // width,),
        in_specs=[wide, wide, wide, moded, moded, single, moded],
        out_specs=pl.BlockSpec((None, rows, width), lambda i: (i, 0, 0)),
        out_shape=jax.ShapeDtypeStruct((chan // width, rows, width), jnp.bfloat16),
        scratch_shapes=[spread, spread],
        compiler_params=pltpu.CompilerParams(vmem_limit_bytes=32 << 20),
        cost_estimate=pl.CostEstimate(
            flops=4 * modes * rows * chan, bytes_accessed=8 * rows * chan, transcendentals=2 * modes * chan
        ),
        name="gated_conv",
    )(q, k, v, rate, residue, skip, enter)


def shift_ctx(x, by, count):
    return lax.ppermute(x, "ctx", [(i, i + by) for i in range(count - by)])


def entering_states(ends, rate, rows):
    count = lax.axis_size("ctx")
    total = jnp.zeros_like(ends)
    for k in range(1, min(RADIX, count - 1) + 1):
        total = total + jnp.exp(-rate * float(rows * (k - 1))) * shift_ctx(ends, k, count)
    stride = RADIX
    while stride < count:
        base = total
        for k in range(1, RADIX):
            if stride * k < count:
                total = total + jnp.exp(-rate * float(rows * stride * k)) * shift_ctx(base, stride * k, count)
        stride *= RADIX
    return total


def exchange(x, axis, flip):
    count = lax.axis_size(axis)
    return lax.ppermute(x, axis, [(i, i ^ flip) for i in range(count)])


def project(pick, gated, weights, acc, out_dtype):
    _, _, rows, depth = gated.shape
    chunk = depth // PLANE
    cols = weights[0][0].shape[1]
    blocks = len(weights)
    flat = [piece for block in weights for piece in block]
    sizes = [[piece.shape[0] // chunk for piece in block] for block in weights]

    def kernel(pick_ref, *refs):
        gated_refs, refs = refs[:blocks], refs[blocks:]
        piece_refs, refs = refs[: len(flat)], refs[len(flat) :]
        out_ref = refs[-1]
        total = refs[0][...] if acc is not None else jnp.zeros((rows, cols), jnp.float32)
        at = 0
        for b in range(blocks):
            r = 0
            for size in sizes[b]:
                for part in range(size):
                    start = pl.multiple_of(pick_ref[blocks + r] * chunk, chunk)
                    total = total + jnp.dot(
                        gated_refs[b][:, pl.ds(start, chunk)],
                        piece_refs[at][pl.ds(part * chunk, chunk), :],
                        preferred_element_type=jnp.float32,
                    )
                    r += 1
                at += 1
        out_ref[...] = total.astype(out_ref.dtype)

    def gated_spec(b):
        return pl.BlockSpec((None, None, rows, depth), lambda i, pick_ref: (pick_ref[b], i, 0, 0))

    row_spec = pl.BlockSpec((None, rows, cols), lambda i, pick_ref: (i, 0, 0))
    whole = [pl.BlockSpec(piece.shape, lambda i, pick_ref: (0, 0)) for piece in flat]
    args = [gated] * blocks + flat + ([] if acc is None else [acc])
    return pl.pallas_call(
        kernel,
        grid_spec=pltpu.PrefetchScalarGridSpec(
            num_scalar_prefetch=1,
            grid=(PLANE,),
            in_specs=[gated_spec(b) for b in range(blocks)] + whole + ([] if acc is None else [row_spec]),
            out_specs=row_spec,
        ),
        out_shape=jax.ShapeDtypeStruct((PLANE, rows, cols), out_dtype),
        compiler_params=pltpu.CompilerParams(vmem_limit_bytes=48 << 20),
        cost_estimate=pl.CostEstimate(
            flops=2 * PLANE * rows * depth * blocks * cols,
            bytes_accessed=2 * blocks * depth * (PLANE * rows + cols) + 4 * PLANE * rows * cols,
            transcendentals=0,
        ),
        name="project",
    )(pick, *args)


def assemble(place, pieces):
    rows, cols = pieces[0].shape

    def kernel(place_ref, *refs):
        *piece_refs, out_ref, sems = refs
        copies = []
        for r, piece_ref in enumerate(piece_refs):
            start = pl.multiple_of(place_ref[r] * cols, cols)
            copies.append(pltpu.make_async_copy(piece_ref, out_ref.at[:, pl.ds(start, cols)], sems.at[r]))
            copies[-1].start()
        for copy in copies:
            copy.wait()

    return pl.pallas_call(
        kernel,
        in_specs=[pl.BlockSpec(memory_space=pltpu.SMEM)] + [pl.BlockSpec(memory_space=pl.ANY)] * len(pieces),
        out_specs=pl.BlockSpec(memory_space=pl.ANY),
        out_shape=jax.ShapeDtypeStruct((rows, cols * len(pieces)), pieces[0].dtype),
        scratch_shapes=[pltpu.SemaphoreType.DMA((len(pieces),))],
        name="assemble",
    )(place, *pieces)


def split_projection(gated_halves, w_out):
    me = lax.axis_index("ctx")
    core = lax.axis_index("ch")
    spot, plane = me % PLANE, me // PLANE
    count = lax.axis_size("ctx")
    chunk, feats = w_out.shape
    cols = feats // PLANE
    rows = gated_halves.shape[1]

    def group(r):
        return lax.dynamic_slice_in_dim(w_out, (spot ^ r) * cols, cols, axis=1)

    first = group(0)
    first_far = exchange(first, "ctx", 2 * PLANE)
    first_near = exchange(first, "ctx", PLANE)
    rest = jnp.concatenate([exchange(group(r), "ctx", r) for r in range(1, PLANE)], axis=0)
    rest_far = exchange(rest, "ctx", 2 * PLANE)
    rest_near = exchange(rest, "ctx", PLANE)
    middle = [i for i in range(count) if PLANE <= i < 3 * PLANE]
    across_pairs = [(i, i ^ (3 * PLANE)) for i in middle]
    end_pairs = [(i, i ^ PLANE) for i in middle]
    own_block = jnp.concatenate([first, rest], axis=0)
    far_block = jnp.concatenate([first_far, rest_far], axis=0)
    across = lax.ppermute(own_block, "ctx", across_pairs)
    ends = lax.ppermute(far_block, "ctx", end_pairs)

    one, two = gated_halves[0], gated_halves[1]
    one_x, two_y = exchange(one, "ctx", 1), exchange(two, "ctx", 2)
    one_pair = jnp.stack([one, one_x])
    two_pair = jnp.stack([two, two_y])
    one_far, two_far = exchange(one_pair, "ctx", 2), exchange(two_pair, "ctx", 1)
    ours = jnp.stack(
        [
            jnp.concatenate([one_pair, one_far]),
            jnp.stack([two, two_far[0], two_y, two_far[1]]),
        ]
    )
    theirs = exchange(ours, "ch", 1)
    everything = jnp.concatenate([ours, theirs])

    def block_at(b):
        return jnp.where(b // 2 == core, b % 2, 2 + b % 2)

    chunks = [spot ^ r for r in range(PLANE)]
    most = jnp.stack([block_at(plane), block_at(plane ^ 1), block_at(plane ^ 2)] + chunks).astype(jnp.int32)
    last = jnp.stack([block_at(plane ^ 3)] + chunks).astype(jnp.int32)
    acc = project(most, everything, [[own_block], [first_near, rest_near], [far_block]], None, jnp.float32)
    made = project(last, everything, [[across + ends]], acc, jnp.bfloat16)
    back = [made[0]] + [exchange(made[r], "ctx", r) for r in range(1, PLANE)]
    return assemble(jnp.stack(chunks).astype(jnp.int32), back)


def body(q, k, v, residue, rate, skip, w_out):
    rows, chan = q.shape
    modes = rate.shape[0]
    groups = chan // LANES
    count, cores = lax.axis_size("ctx"), lax.axis_size("ch")
    chunk, feats = w_out.shape
    split = (
        count == 4 * PLANE
        and cores == 2
        and chan == 8 * chunk
        and chunk % LANES == 0
        and feats % (PLANE * LANES) == 0
    )
    rate = rate.reshape(modes, groups, LANES)
    residue = residue.reshape(modes, groups, LANES)
    skip = skip.reshape(groups, LANES)
    ends = end_states(k, v, rate)
    enter = entering_states(ends, rate, rows)
    gated = gated_conv(q, k, v, rate, residue, skip, enter)
    if split:
        return split_projection(gated, w_out)
    gated = gated.transpose(1, 0, 2).reshape(rows, chan)
    full_gated = lax.all_gather(gated, "ch", axis=1, tiled=True)
    w_full = lax.all_gather(w_out, "ctx", axis=0, tiled=True)
    mixed = jnp.dot(full_gated, w_full, preferred_element_type=jnp.float32)
    return mixed.astype(jnp.bfloat16)


def solution(mesh):
    placed = (
        P("ctx", "ch"),
        P("ctx", "ch"),
        P("ctx", "ch"),
        P(None, "ch"),
        P(None, "ch"),
        P("ch"),
        P("ctx", "ch"),
    )
    return jax.shard_map(
        body, mesh=mesh, in_specs=placed, out_specs=P("ctx", "ch"), check_vma=False
    )
```

```python
import jax
import jax.numpy as jnp
from jax import lax
from jax.experimental import pallas as pl
from jax.experimental.pallas import tpu as pltpu
from jax.sharding import PartitionSpec as P

LANES = 128
RADIX = 4
PLANE = 4


def spread_signal(k_ref, v_ref, sig_ref):
    rows, width = k_ref.shape
    groups = width // LANES
    for g in range(groups):
        cols = pl.ds(g * LANES, LANES)
        product = k_ref[:, cols].astype(jnp.float32) * v_ref[:, cols].astype(jnp.float32)
        sig_ref[pl.ds(g, rows, stride=groups), :] = product


def ends_kernel(k_ref, v_ref, rate_ref, end_ref, sig_ref):
    rows, width = k_ref.shape
    modes, groups, _ = rate_ref.shape
    spread_signal(k_ref, v_ref, sig_ref)
    decay = [jnp.exp(-rate_ref[m]) for m in range(modes)]

    def step(t, state):
        s = sig_ref[pl.ds(pl.multiple_of(t * groups, groups), groups), :]
        return tuple(d * h + s for d, h in zip(decay, state))

    zero = jnp.zeros((groups, LANES), jnp.float32)
    state = lax.fori_loop(0, rows, step, (zero,) * modes, unroll=8)
    for m in range(modes):
        end_ref[m] = state[m]


def conv_kernel(q_ref, k_ref, v_ref, rate_ref, residue_ref, skip_ref, enter_ref, out_ref, sig_ref, conv_ref):
    rows, width = k_ref.shape
    modes, groups, _ = rate_ref.shape
    spread_signal(k_ref, v_ref, sig_ref)
    decay = [jnp.exp(-rate_ref[m]) for m in range(modes)]
    weight = [residue_ref[m] * jnp.sqrt(2.0 * rate_ref[m]) for m in range(modes)]
    skip = skip_ref[...]

    def step(t, state):
        at = pl.ds(pl.multiple_of(t * groups, groups), groups)
        s = sig_ref[at, :]
        state = tuple(d * h + s for d, h in zip(decay, state))
        terms = [c * h for c, h in zip(weight, state)] + [skip * s]
        while len(terms) > 1:
            terms = [sum(terms[i : i + 2]) for i in range(0, len(terms), 2)]
        conv_ref[at, :] = terms[0]
        return state

    lax.fori_loop(0, rows, step, tuple(enter_ref[m] for m in range(modes)), unroll=4)
    for g in range(groups):
        cols = pl.ds(g * LANES, LANES)
        conv = conv_ref[pl.ds(g, rows, stride=groups), :]
        out_ref[:, cols] = (q_ref[:, cols].astype(jnp.float32) * conv).astype(out_ref.dtype)


def block_specs(rows, modes, width):
    groups = width // LANES
    return (
        pl.BlockSpec((rows, width), lambda i: (0, i)),
        pl.BlockSpec((modes, groups, LANES), lambda i: (0, i, 0)),
        pl.BlockSpec((groups, LANES), lambda i: (i, 0)),
    )


def end_states(k, v, rate):
    rows, chan = k.shape
    modes = rate.shape[0]
    width = min(chan, 8 * LANES)
    wide, moded, _ = block_specs(rows, modes, width)
    return pl.pallas_call(
        ends_kernel,
        grid=(chan // width,),
        in_specs=[wide, wide, moded],
        out_specs=moded,
        out_shape=jax.ShapeDtypeStruct(rate.shape, jnp.float32),
        scratch_shapes=[pltpu.VMEM((rows * width // LANES, LANES), jnp.float32)],
        compiler_params=pltpu.CompilerParams(vmem_limit_bytes=32 << 20),
        cost_estimate=pl.CostEstimate(
            flops=2 * modes * rows * chan, bytes_accessed=4 * rows * chan, transcendentals=modes * chan
        ),
        name="end_states",
    )(k, v, rate)


def gated_conv(q, k, v, rate, residue, skip, enter):
    rows, chan = k.shape
    modes = rate.shape[0]
    width = min(chan, 8 * LANES)
    wide, moded, single = block_specs(rows, modes, width)
    spread = pltpu.VMEM((rows * width // LANES, LANES), jnp.float32)
    return pl.pallas_call(
        conv_kernel,
        grid=(chan // width,),
        in_specs=[wide, wide, wide, moded, moded, single, moded],
        out_specs=pl.BlockSpec((None, rows, width), lambda i: (i, 0, 0)),
        out_shape=jax.ShapeDtypeStruct((chan // width, rows, width), jnp.bfloat16),
        scratch_shapes=[spread, spread],
        compiler_params=pltpu.CompilerParams(vmem_limit_bytes=32 << 20),
        cost_estimate=pl.CostEstimate(
            flops=4 * modes * rows * chan, bytes_accessed=8 * rows * chan, transcendentals=2 * modes * chan
        ),
        name="gated_conv",
    )(q, k, v, rate, residue, skip, enter)


def shift_ctx(x, by):
    count = lax.axis_size("ctx")
    return lax.ppermute(x, "ctx", [(i, i + by) for i in range(count - by)])


def exchange(x, axis, flip):
    count = lax.axis_size(axis)
    return lax.ppermute(x, axis, [(i, i ^ flip) for i in range(count)])


def tie(*values):
    return lax.optimization_barrier(values)


def entering_states(ends, rate, rows):
    count = lax.axis_size("ctx")
    total = jnp.zeros_like(ends)
    for k in range(1, min(RADIX, count - 1) + 1):
        total = total + jnp.exp(-rate * float(rows * (k - 1))) * shift_ctx(ends, k)
    stride = RADIX
    while stride < count:
        base = total
        for k in range(1, RADIX):
            if stride * k < count:
                total = total + jnp.exp(-rate * float(rows * stride * k)) * shift_ctx(base, stride * k)
        stride *= RADIX
    return total


def fold_pair(ends, before, rate, flip, span):
    other = exchange(ends, "ctx", flip)
    later = (lax.axis_index("ctx") & flip) != 0
    decay = jnp.exp(-rate * float(span))
    both = jnp.where(later, decay * other + ends, decay * ends + other)
    return both, other, later


def take_copies(copies):
    for copy in copies:
        copy.start()
    return copies


def project(flags, places, gated, weights, accs, out_widths, out_dtype):
    rows, depth = gated[0][0][0].shape[1:]
    chunk = depth // PLANE
    cols = sum(out_widths)
    blocks = len(weights)
    arrays = []

    def index_of(array):
        for at, known in enumerate(arrays):
            if known is array:
                return at
        arrays.append(array)
        return len(arrays) - 1

    gated_at = [[(index_of(a), at) for a, at in rows_of] for rows_of in gated]
    plan = []
    for b, (flag, pieces) in enumerate(weights):
        for choices, choice_flag, place, offset, first_col in pieces:
            plan.append((b, [index_of(a) for a in choices], choice_flag, place, offset, first_col, choices[0].shape))
    count_in = len(arrays)
    parts = len(out_widths)
    count_acc = 0 if accs is None else len(accs)

    def kernel(flag_ref, place_ref, *refs):
        ins, refs = refs[:count_in], refs[count_in:]
        acc_refs, refs = refs[:count_acc], refs[count_acc:]
        out_refs, (gated_buf, weight_buf, gated_sems, weight_sems) = refs[: PLANE * parts], refs[PLANE * parts :]

        for n, (b, choices, choice_flag, place, offset, first_col, shape) in enumerate(plan):
            start = pl.multiple_of(b * depth + place_ref[place] * chunk + offset, 64)
            target = weight_buf.at[pl.ds(start, shape[0]), pl.ds(first_col, shape[1])]
            for c, choice in enumerate(choices):
                copy = pltpu.make_async_copy(ins[choice], target, weight_sems.at[n])
                if choice_flag is None:
                    copy.start()
                else:
                    pl.when(flag_ref[choice_flag] == c)(copy.start)
        for r in range(PLANE):
            for b, (flag, _) in enumerate(weights):
                for source in range(len(gated_at)):
                    at, index = gated_at[source][r]
                    copy = pltpu.make_async_copy(ins[at].at[index], gated_buf.at[r, b], gated_sems.at[r, b])
                    pl.when(flag_ref[flag] == source)(copy.start)
        for n, (b, choices, choice_flag, place, offset, first_col, shape) in enumerate(plan):
            start = pl.multiple_of(b * depth + place_ref[place] * chunk + offset, 64)
            target = weight_buf.at[pl.ds(start, shape[0]), pl.ds(first_col, shape[1])]
            pltpu.make_async_copy(ins[choices[0]], target, weight_sems.at[n]).wait()
        for r in range(PLANE):
            for b in range(blocks):
                at, index = gated_at[0][r]
                pltpu.make_async_copy(ins[at].at[index], gated_buf.at[r, b], gated_sems.at[r, b]).wait()
            first_col = 0
            for part, width in enumerate(out_widths):
                total = None
                for b in range(blocks):
                    product = jnp.dot(
                        gated_buf[r, b],
                        weight_buf[pl.ds(b * depth, depth), pl.ds(first_col, width)],
                        preferred_element_type=jnp.float32,
                    )
                    total = product if total is None else total + product
                if accs is not None:
                    total = total + acc_refs[part * PLANE + r][...]
                out_refs[part * PLANE + r][...] = total.astype(out_dtype)
                first_col += width

    smem = pl.BlockSpec(memory_space=pltpu.SMEM)
    vmem = pl.BlockSpec(memory_space=pltpu.VMEM)
    anywhere = pl.BlockSpec(memory_space=pl.ANY)
    made = pl.pallas_call(
        kernel,
        in_specs=[smem, smem] + [anywhere] * count_in + [vmem] * count_acc,
        out_specs=[vmem] * (PLANE * parts),
        out_shape=[jax.ShapeDtypeStruct((rows, width), out_dtype) for width in out_widths for _ in range(PLANE)],
        scratch_shapes=[
            pltpu.VMEM((PLANE, blocks, rows, depth), jnp.bfloat16),
            pltpu.VMEM((blocks * depth, cols), jnp.bfloat16),
            pltpu.SemaphoreType.DMA((PLANE, blocks)),
            pltpu.SemaphoreType.DMA((len(plan),)),
        ],
        compiler_params=pltpu.CompilerParams(vmem_limit_bytes=32 << 20),
        cost_estimate=pl.CostEstimate(
            flops=2 * PLANE * rows * depth * blocks * cols,
            bytes_accessed=2 * blocks * depth * (PLANE * rows + cols),
            transcendentals=0,
        ),
        name="project",
    )(flags, places, *arrays, *([] if accs is None else accs))
    return [made[part * PLANE : (part + 1) * PLANE] for part in range(parts)]


def assemble(spot, parts):
    rows = parts[0][0].shape[0]
    widths = [part[0].shape[1] for part in parts]
    cols = sum(widths)

    def kernel(spot_ref, *refs):
        out_ref = refs[-1]
        group = pl.program_id(0)
        for r in range(PLANE):

            @pl.when((spot_ref[0] ^ r) == group)
            def _():
                first = 0
                for part, width in enumerate(widths):
                    out_ref[:, pl.ds(first, width)] = refs[part * PLANE + r][...]
                    first += width

    flat = [piece for part in parts for piece in part]
    return pl.pallas_call(
        kernel,
        grid=(PLANE,),
        in_specs=[pl.BlockSpec(memory_space=pltpu.SMEM)] + [pl.BlockSpec(p.shape, lambda i: (0, 0)) for p in flat],
        out_specs=pl.BlockSpec((rows, cols), lambda i: (0, i)),
        out_shape=jax.ShapeDtypeStruct((rows, cols * PLANE), flat[0].dtype),
        name="assemble",
    )(spot.reshape(1), *flat)


def split_block(q, k, v, residue, rate, skip, w_out):
    rows, chan = q.shape
    me = lax.axis_index("ctx")
    core = lax.axis_index("ch")
    spot, plane = me & (PLANE - 1), me // PLANE
    count = lax.axis_size("ctx")
    chunk, feats = w_out.shape
    cols = feats // PLANE
    far_flip, near_flip = 2 * PLANE, PLANE

    def far(x):
        return exchange(x, "ctx", far_flip)

    def near(x):
        return exchange(x, "ctx", near_flip)

    middle = [i for i in range(count) if PLANE <= i < 3 * PLANE]

    def across(x):
        return lax.ppermute(x, "ctx", [(i, i ^ (3 * PLANE)) for i in middle])

    def outward(x):
        return lax.ppermute(x, "ctx", [(i, i ^ PLANE) for i in middle])

    own = [lax.dynamic_slice_in_dim(w_out, (spot ^ r) * cols, cols, axis=1) for r in range(PLANE)]
    w0 = own[0]
    f0, n0 = far(w0), near(w0)
    w1, w2, w3 = [exchange(own[r], "ctx", r) for r in range(1, PLANE)]
    ends = end_states(k, v, rate)
    both, other, later = fold_pair(ends, None, rate, 1, rows)
    before = jnp.where(later, other, 0.0)
    f0, n0, w0, w1, w2, w3, both, before, rate = tie(f0, n0, w0, w1, w2, w3, both, before, rate)

    f1, n1 = far(w1), near(w1)
    half = chunk // 2
    both, other, later = fold_pair(both, before, rate, 2, 2 * rows)
    odd = (me & 1).astype(jnp.float32)
    before = before + jnp.where(later, jnp.exp(-rate * (odd * rows)) * other, 0.0)
    last = shift_ctx(both, PLANE)
    decay = jnp.exp(-rate * float(PLANE * rows))
    carried = last + decay * shift_ctx(both + decay * last, 2 * PLANE)
    enter = before + jnp.exp(-rate * (spot * rows).astype(jnp.float32)) * carried
    f1, n1, w2, w3, enter, q = tie(f1, n1, w2, w3, enter, q)

    f2a, n2a = far(w2[:half]), near(w2[:half])
    gated = gated_conv(q, k, v, rate, residue, skip, enter)
    one, two = gated
    f2a, n2a, w2, w3, one, two = tie(f2a, n2a, w2, w3, one, two)

    f2b, n2b = far(w2[half:]), near(w2[half:])
    one_x, two_y = exchange(one, "ctx", 1), exchange(two, "ctx", 2)
    f2b, n2b, w3, f0, w0, one_x, two_y = tie(f2b, n2b, w3, f0, w0, one_x, two_y)

    f3, n3 = far(w3), near(w3)
    out0, mid0 = outward(f0), across(w0)
    one_pair = jnp.stack([one, one_x])
    two_pair = jnp.stack([two, two_y])
    one_far, two_far = exchange(one_pair, "ctx", 2), exchange(two_pair, "ctx", 1)
    one_pair_t, two_pair_t = exchange(one_pair, "ch", 1), exchange(two_pair, "ch", 1)
    f3, n3, out0, mid0, one_far, two_far, one_pair_t, two_pair_t = tie(
        f3, n3, out0, mid0, one_far, two_far, one_pair_t, two_pair_t
    )

    wide = 2 * cols // 3
    rest_out = jnp.concatenate([f1, f2a, f2b, f3])
    rest_mid = jnp.concatenate([w1, w2, w3])
    outA, midA = outward(rest_out[:, :wide]), across(rest_mid[:, :wide])
    one_far_t, two_far_t = exchange(one_far, "ch", 1), exchange(two_far, "ch", 1)

    def row_blocks(pair_one, far_one, pair_two, far_two):
        return [
            [(pair_one, 0), (pair_one, 1), (far_one, 0), (far_one, 1)],
            [(pair_two, 0), (far_two, 0), (pair_two, 1), (far_two, 1)],
        ]

    sources = row_blocks(one_pair, one_far, two_pair, two_far) + row_blocks(one_pair_t, one_far_t, two_pair_t, two_far_t)

    def source_of(b):
        return jnp.where(b // 2 == core, b & 1, 2 + (b & 1))

    ends_plane = jnp.where((plane == 0) | (plane == 3), 0, 1)
    flags = jnp.stack([source_of(plane), source_of(plane ^ 1), source_of(plane ^ 2), source_of(plane ^ 3), ends_plane])
    flags = flags.astype(jnp.int32)
    places = jnp.stack([spot ^ r for r in range(PLANE)]).astype(jnp.int32)

    def pieces(p0, p1, p2a, p2b, p3):
        return [((p0,), None, 0, 0, 0), ((p1,), None, 1, 0, 0), ((p2a,), None, 2, 0, 0), ((p2b,), None, 2, half, 0), ((p3,), None, 3, 0, 0)]

    weights = [
        (0, [((w,), None, r, 0, 0) for r, w in enumerate((w0, w1, w2, w3))]),
        (1, pieces(n0, n1, n2a, n2b, n3)),
        (2, pieces(f0, f1, f2a, f2b, f3)),
    ]
    accs = project(flags, places, sources, weights, None, [wide, cols - wide], jnp.float32)
    tied = tie(outA, midA, rest_out, rest_mid, *accs[0], *accs[1])
    outA, midA, rest_out, rest_mid = tied[:4]
    accs = [tied[4 : 4 + PLANE], tied[4 + PLANE :]]

    outB, midB = outward(rest_out[:, wide:]), across(rest_mid[:, wide:])

    def last_block(out_first, mid_first, out_rest, mid_rest):
        found = [((out_first, mid_first), 4, 0, 0, 0)]
        for r in range(1, PLANE):
            at = (r - 1) * chunk
            found.append(((out_rest[at : at + chunk], mid_rest[at : at + chunk]), 4, r, 0, 0))
        return [(3, found)]

    (madeA,) = project(
        flags, places, sources, last_block(out0[:, :wide], mid0[:, :wide], outA, midA), accs[0], [wide], jnp.bfloat16
    )
    backA = [madeA[0]] + [exchange(madeA[r], "ctx", r) for r in range(1, PLANE)]
    (madeB,) = project(
        flags, places, sources, last_block(out0[:, wide:], mid0[:, wide:], outB, midB), accs[1], [cols - wide], jnp.bfloat16
    )
    backB = [madeB[0]] + [exchange(madeB[r], "ctx", r) for r in range(1, PLANE)]
    return assemble(spot.astype(jnp.int32), [backA, backB])


def body(q, k, v, residue, rate, skip, w_out):
    rows, chan = q.shape
    modes = rate.shape[0]
    groups = chan // LANES
    count, cores = lax.axis_size("ctx"), lax.axis_size("ch")
    chunk, feats = w_out.shape
    split = (
        count == 4 * PLANE
        and cores == 2
        and chan == 8 * chunk
        and chunk % LANES == 0
        and feats % (PLANE * LANES) == 0
    )
    rate = rate.reshape(modes, groups, LANES)
    residue = residue.reshape(modes, groups, LANES)
    skip = skip.reshape(groups, LANES)
    if split:
        return split_block(q, k, v, residue, rate, skip, w_out)
    ends = end_states(k, v, rate)
    enter = entering_states(ends, rate, rows)
    gated = gated_conv(q, k, v, rate, residue, skip, enter)
    gated = gated.transpose(1, 0, 2).reshape(rows, chan)
    full_gated = lax.all_gather(gated, "ch", axis=1, tiled=True)
    w_full = lax.all_gather(w_out, "ctx", axis=0, tiled=True)
    mixed = jnp.dot(full_gated, w_full, preferred_element_type=jnp.float32)
    return mixed.astype(jnp.bfloat16)


def solution(mesh):
    placed = (
        P("ctx", "ch"),
        P("ctx", "ch"),
        P("ctx", "ch"),
        P(None, "ch"),
        P(None, "ch"),
        P("ch"),
        P("ctx", "ch"),
    )
    return jax.shard_map(
        body, mesh=mesh, in_specs=placed, out_specs=P("ctx", "ch"), check_vma=False
    )
```

```python
import jax
import jax.numpy as jnp
from jax import lax
from jax.experimental import pallas as pl
from jax.experimental.pallas import tpu as pltpu
from jax.sharding import PartitionSpec as P

LANES = 128
RADIX = 4
PLANE = 4


def spread_signal(k_ref, v_ref, sig_ref):
    rows, width = k_ref.shape
    groups = width // LANES
    for g in range(groups):
        cols = pl.ds(g * LANES, LANES)
        product = k_ref[:, cols].astype(jnp.float32) * v_ref[:, cols].astype(jnp.float32)
        sig_ref[pl.ds(g, rows, stride=groups), :] = product


def ends_kernel(k_ref, v_ref, rate_ref, end_ref, sig_ref):
    rows, width = k_ref.shape
    modes, groups, _ = rate_ref.shape
    spread_signal(k_ref, v_ref, sig_ref)
    decay = [jnp.exp(-rate_ref[m]) for m in range(modes)]

    def step(t, state):
        s = sig_ref[pl.ds(pl.multiple_of(t * groups, groups), groups), :]
        return tuple(d * h + s for d, h in zip(decay, state))

    zero = jnp.zeros((groups, LANES), jnp.float32)
    state = lax.fori_loop(0, rows, step, (zero,) * modes, unroll=8)
    for m in range(modes):
        end_ref[m] = state[m]


def conv_kernel(q_ref, k_ref, v_ref, rate_ref, residue_ref, skip_ref, enter_ref, out_ref, sig_ref, conv_ref):
    rows, width = k_ref.shape
    modes, groups, _ = rate_ref.shape
    spread_signal(k_ref, v_ref, sig_ref)
    decay = [jnp.exp(-rate_ref[m]) for m in range(modes)]
    weight = [residue_ref[m] * jnp.sqrt(2.0 * rate_ref[m]) for m in range(modes)]
    skip = skip_ref[...]

    def step(t, state):
        at = pl.ds(pl.multiple_of(t * groups, groups), groups)
        s = sig_ref[at, :]
        state = tuple(d * h + s for d, h in zip(decay, state))
        terms = [c * h for c, h in zip(weight, state)] + [skip * s]
        while len(terms) > 1:
            terms = [sum(terms[i : i + 2]) for i in range(0, len(terms), 2)]
        conv_ref[at, :] = terms[0]
        return state

    lax.fori_loop(0, rows, step, tuple(enter_ref[m] for m in range(modes)), unroll=4)
    for g in range(groups):
        cols = pl.ds(g * LANES, LANES)
        conv = conv_ref[pl.ds(g, rows, stride=groups), :]
        out_ref[:, cols] = (q_ref[:, cols].astype(jnp.float32) * conv).astype(out_ref.dtype)


def block_specs(rows, modes, width):
    groups = width // LANES
    return (
        pl.BlockSpec((rows, width), lambda i: (0, i)),
        pl.BlockSpec((modes, groups, LANES), lambda i: (0, i, 0)),
        pl.BlockSpec((groups, LANES), lambda i: (i, 0)),
    )


def end_states(k, v, rate):
    rows, chan = k.shape
    modes = rate.shape[0]
    width = min(chan, 8 * LANES)
    wide, moded, _ = block_specs(rows, modes, width)
    return pl.pallas_call(
        ends_kernel,
        grid=(chan // width,),
        in_specs=[wide, wide, moded],
        out_specs=moded,
        out_shape=jax.ShapeDtypeStruct(rate.shape, jnp.float32),
        scratch_shapes=[pltpu.VMEM((rows * width // LANES, LANES), jnp.float32)],
        compiler_params=pltpu.CompilerParams(vmem_limit_bytes=32 << 20),
        cost_estimate=pl.CostEstimate(
            flops=2 * modes * rows * chan, bytes_accessed=4 * rows * chan, transcendentals=modes * chan
        ),
        name="end_states",
    )(k, v, rate)


def gated_conv(q, k, v, rate, residue, skip, enter):
    rows, chan = k.shape
    modes = rate.shape[0]
    width = min(chan, 8 * LANES)
    wide, moded, single = block_specs(rows, modes, width)
    spread = pltpu.VMEM((rows * width // LANES, LANES), jnp.float32)
    return pl.pallas_call(
        conv_kernel,
        grid=(chan // width,),
        in_specs=[wide, wide, wide, moded, moded, single, moded],
        out_specs=pl.BlockSpec((None, rows, width), lambda i: (i, 0, 0)),
        out_shape=jax.ShapeDtypeStruct((chan // width, rows, width), jnp.bfloat16),
        scratch_shapes=[spread, spread],
        compiler_params=pltpu.CompilerParams(vmem_limit_bytes=32 << 20),
        cost_estimate=pl.CostEstimate(
            flops=4 * modes * rows * chan, bytes_accessed=8 * rows * chan, transcendentals=2 * modes * chan
        ),
        name="gated_conv",
    )(q, k, v, rate, residue, skip, enter)


def shift_ctx(x, by):
    count = lax.axis_size("ctx")
    return lax.ppermute(x, "ctx", [(i, i + by) for i in range(count - by)])


def exchange(x, axis, flip):
    count = lax.axis_size(axis)
    return lax.ppermute(x, axis, [(i, i ^ flip) for i in range(count)])


def tie(*values):
    return lax.optimization_barrier(values)


def entering_states(ends, rate, rows):
    count = lax.axis_size("ctx")
    total = jnp.zeros_like(ends)
    for k in range(1, min(RADIX, count - 1) + 1):
        total = total + jnp.exp(-rate * float(rows * (k - 1))) * shift_ctx(ends, k)
    stride = RADIX
    while stride < count:
        base = total
        for k in range(1, RADIX):
            if stride * k < count:
                total = total + jnp.exp(-rate * float(rows * stride * k)) * shift_ctx(base, stride * k)
        stride *= RADIX
    return total


def box(fn, *args):
    once = (lax.axis_index("ctx") >= 0).astype(jnp.int32)
    shapes = jax.eval_shape(fn, *args)
    empty = jax.tree.map(lambda a: jnp.zeros(a.shape, a.dtype), shapes)

    def run(step, _):
        return fn(*tie(step, *args)[1:])

    return lax.fori_loop(0, once, run, empty)


def fold_pair(ends, rate, flip, span):
    other = exchange(ends, "ctx", flip)
    later = (lax.axis_index("ctx") & flip) != 0
    decay = jnp.exp(-rate * float(span))
    both = jnp.where(later, decay * other + ends, decay * ends + other)
    return both, other, later


def in_order(gated_ref, index, place_ref, chunk):
    found = []
    for r in range(PLANE):
        start = pl.multiple_of(place_ref[r] * chunk, chunk)
        found.append(gated_ref[index, :, pl.ds(start, chunk)])
    return jnp.concatenate(found, axis=1)


def project(flags, places, sources, blocks, widths):
    rows, depth = sources[0][0][0].shape[1:]
    chunk = depth // PLANE
    arrays = []
    for source in sources:
        for array, _ in source:
            if not any(array is known for known in arrays):
                arrays.append(array)
    where = [[([a is known for known in arrays].index(True), at) for a, at in source] for source in sources]
    count = len(arrays)

    def kernel(flag_ref, place_ref, *refs):
        gated_refs, refs = refs[:count], refs[count:]
        weight_refs, out_refs = refs[: len(weights)], refs[len(weights) :]
        pieces = len(weights) // len(blocks)
        for b in range(len(blocks)):
            piece_refs = weight_refs[pieces * b : pieces * (b + 1)]
            for n, source in enumerate(where):

                @pl.when(flag_ref[b] == n)
                def _():
                    for r, (at, index) in enumerate(source):
                        lhs = in_order(gated_refs[at], index, place_ref, chunk)
                        first = 0
                        for part, width in enumerate(widths):
                            cols = pl.ds(first, width)
                            out_ref = out_refs[part * PLANE + r]
                            total = out_ref[...] if b else jnp.zeros(out_ref.shape, jnp.float32)
                            at_row = 0
                            for piece_ref in piece_refs:
                                depth_here = piece_ref.shape[0]
                                total += jnp.dot(
                                    lhs[:, at_row : at_row + depth_here],
                                    piece_ref[:, cols],
                                    preferred_element_type=jnp.float32,
                                )
                                at_row += depth_here
                            out_ref[...] = total
                            first += width

    smem = pl.BlockSpec(memory_space=pltpu.SMEM)
    vmem = pl.BlockSpec(memory_space=pltpu.VMEM)
    weights = [piece for block in blocks for piece in block]
    cols = sum(widths)
    made = pl.pallas_call(
        kernel,
        in_specs=[smem, smem] + [vmem] * (count + len(weights)),
        out_specs=[vmem] * (PLANE * len(widths)),
        out_shape=[jax.ShapeDtypeStruct((rows, width), jnp.float32) for width in widths for _ in range(PLANE)],
        compiler_params=pltpu.CompilerParams(vmem_limit_bytes=16 << 20),
        cost_estimate=pl.CostEstimate(
            flops=2 * PLANE * rows * depth * len(blocks) * cols,
            bytes_accessed=2 * len(blocks) * depth * (PLANE * rows + cols),
            transcendentals=0,
        ),
        name="project",
    )(flags, places, *arrays, *weights)
    return [made[part * PLANE : (part + 1) * PLANE] for part in range(len(widths))]


def finish(flags, places, sources, heads, rests, accs, first_col):
    rows, depth = sources[0][0][0].shape[1:]
    chunk = depth // PLANE
    width = accs[0].shape[1]
    arrays = []
    for source in sources:
        for array, _ in source:
            if not any(array is known for known in arrays):
                arrays.append(array)
    where = [[([a is known for known in arrays].index(True), at) for a, at in source] for source in sources]
    count = len(arrays)

    def kernel(flag_ref, place_ref, *refs):
        gated_refs, refs = refs[:count], refs[count:]
        head_a, head_b, rest_a, rest_b = refs[:4]
        acc_refs, out_refs, weight_ref = refs[4 : 4 + PLANE], refs[4 + PLANE : 4 + 2 * PLANE], refs[-1]
        cols = pl.ds(first_col, width)
        weight_ref[pl.ds(0, chunk), :] = head_a[:, cols] + head_b[:, cols]
        weight_ref[pl.ds(chunk, depth - chunk), :] = rest_a[...] + rest_b[...]
        for n, source in enumerate(where):

            @pl.when(flag_ref[3] == n)
            def _():
                for r, (at, index) in enumerate(source):
                    lhs = in_order(gated_refs[at], index, place_ref, chunk)
                    total = acc_refs[r][...] + jnp.dot(lhs, weight_ref[...], preferred_element_type=jnp.float32)
                    out_refs[r][...] = total.astype(jnp.bfloat16)

    smem = pl.BlockSpec(memory_space=pltpu.SMEM)
    vmem = pl.BlockSpec(memory_space=pltpu.VMEM)
    return pl.pallas_call(
        kernel,
        in_specs=[smem, smem] + [vmem] * (count + 4 + PLANE),
        out_specs=[vmem] * PLANE,
        out_shape=[jax.ShapeDtypeStruct((rows, width), jnp.bfloat16)] * PLANE,
        scratch_shapes=[pltpu.VMEM((depth, width), jnp.bfloat16)],
        compiler_params=pltpu.CompilerParams(vmem_limit_bytes=16 << 20),
        cost_estimate=pl.CostEstimate(
            flops=2 * PLANE * rows * depth * width, bytes_accessed=2 * depth * (PLANE * rows + width), transcendentals=0
        ),
        name="finish",
    )(flags, places, *arrays, *heads, *rests, *accs)


def assemble(spot, parts):
    rows = parts[0][0].shape[0]
    widths = [part[0].shape[1] for part in parts]
    cols = sum(widths)

    def kernel(spot_ref, *refs):
        out_ref = refs[-1]
        group = pl.program_id(0)
        for r in range(PLANE):

            @pl.when((spot_ref[0] ^ r) == group)
            def _():
                first = 0
                for part, width in enumerate(widths):
                    out_ref[:, pl.ds(first, width)] = refs[part * PLANE + r][...]
                    first += width

    flat = [piece for part in parts for piece in part]
    return pl.pallas_call(
        kernel,
        grid=(PLANE,),
        in_specs=[pl.BlockSpec(memory_space=pltpu.SMEM)] + [pl.BlockSpec(p.shape, lambda i: (0, 0)) for p in flat],
        out_specs=pl.BlockSpec((rows, cols), lambda i: (0, i)),
        out_shape=jax.ShapeDtypeStruct((rows, cols * PLANE), flat[0].dtype),
        name="assemble",
    )(spot.reshape(1), *flat)


def split_block(q, k, v, residue, rate, skip, w_out):
    rows, chan = q.shape
    me = lax.axis_index("ctx")
    core = lax.axis_index("ch")
    spot, plane = me & (PLANE - 1), me // PLANE
    count = lax.axis_size("ctx")
    chunk, feats = w_out.shape
    cols = feats // PLANE
    wide = 2 * cols // 3
    widths = [wide, cols - wide]

    def far(x):
        return exchange(x, "ctx", 2 * PLANE)

    def near(x):
        return exchange(x, "ctx", PLANE)

    middle = [i for i in range(count) if PLANE <= i < 3 * PLANE]

    def across(x):
        return lax.ppermute(x, "ctx", [(i, i ^ (3 * PLANE)) for i in middle])

    def outward(x):
        return lax.ppermute(x, "ctx", [(i, i ^ PLANE) for i in middle])

    def plane_scan(k, v, rate):
        ends = end_states(k, v, rate)
        both, other, later = fold_pair(ends, rate, 1, rows)
        before = jnp.where(later, other, 0.0)
        both, other, later = fold_pair(both, rate, 2, 2 * rows)
        odd = (me & 1).astype(jnp.float32)
        return both, before + jnp.where(later, jnp.exp(-rate * (odd * rows)) * other, 0.0)

    own = [lax.dynamic_slice_in_dim(w_out, (spot ^ r) * cols, cols, axis=1) for r in range(PLANE)]
    w0, w1, w2, w3 = tie(*own)
    f0, n0 = far(w0), near(w0)
    w1, w2 = exchange(w1, "ctx", 1), exchange(w2, "ctx", 2)
    both, before = box(plane_scan, k, v, rate)
    f0, n0, w0, w1, w2, w3, both, before = tie(f0, n0, w0, w1, w2, w3, both, before)

    w3 = exchange(w3, "ctx", 3)
    out0, mid0 = outward(f0), across(w0)
    last = shift_ctx(both, PLANE)
    decay = jnp.exp(-rate * float(PLANE * rows))
    carried = last + decay * shift_ctx(both + decay * last, 2 * PLANE)
    enter = before + jnp.exp(-rate * (spot * rows).astype(jnp.float32)) * carried
    out0, mid0, w1, w2, w3, enter = tie(out0, mid0, w1, w2, w3, enter)

    def convolve(q, k, v, enter):
        one, two = gated_conv(q, k, v, rate, residue, skip, enter)
        one_x, two_y = exchange(one, "ctx", 1), exchange(two, "ctx", 2)
        return jnp.stack([one, one_x]), jnp.stack([two, two_y]), jnp.stack([one, one_x, two, two_y])

    f1, n1 = far(w1), near(w1)
    one_pair, two_pair, pairs = box(convolve, q, k, v, enter)
    early = 3 * chunk // 2
    w23 = jnp.concatenate([w2, w3])
    w23, w4 = w23[:early], w23[early:]
    f1, n1, w1, w23, w4, one_pair, two_pair, pairs = tie(f1, n1, w1, w23, w4, one_pair, two_pair, pairs)

    f23, n23 = far(w23), near(w23)
    one_far, two_far = exchange(one_pair, "ctx", 2), exchange(two_pair, "ctx", 1)
    pairs_t = exchange(pairs, "ch", 1)
    f23, n23, w4, one_far, two_far, pairs_t = tie(f23, n23, w4, one_far, two_far, pairs_t)

    f4, n4 = far(w4), near(w4)
    one_far_t, two_far_t = exchange(one_far, "ch", 1), exchange(two_far, "ch", 1)
    f4, n4, one_far_t, two_far_t = tie(f4, n4, one_far_t, two_far_t)

    def row_blocks(nearest, far_one, far_two):
        return [
            [(nearest, 0), (nearest, 1), (far_one, 0), (far_one, 1)],
            [(nearest, 2), (far_two, 0), (nearest, 3), (far_two, 1)],
        ]

    def source_of(b):
        return jnp.where(b // 2 == core, b & 1, 2 + (b & 1))

    flags = jnp.stack([source_of(plane ^ r) for r in range(4)]).astype(jnp.int32)
    places = jnp.stack([spot ^ r for r in range(PLANE)]).astype(jnp.int32)

    def side(part, *blocks):
        span = slice(wide, None) if part else slice(0, wide)
        return jnp.concatenate([block[:, span] for block in blocks])

    outA, midA = outward(side(0, f1, f23, f4)), across(side(0, w1, w23, w4))
    sources = row_blocks(pairs, one_far, two_far) + row_blocks(pairs_t, one_far_t, two_far_t)
    accA, accB = project(flags, places, sources, [(w0, w1, w23, w4), (n0, n1, n23, n4), (f0, f1, f23, f4)], widths)
    outA, midA, f1, f23, f4, w1, w23, w4, *accs = tie(outA, midA, f1, f23, f4, w1, w23, w4, *accA, *accB)
    accA, accB = accs[:PLANE], accs[PLANE:]

    outB, midB = outward(side(1, f1, f23, f4)), across(side(1, w1, w23, w4))
    madeA = finish(flags, places, sources, (out0, mid0), (outA, midA), accA, 0)
    backA = [madeA[0]] + [exchange(madeA[r], "ctx", r) for r in range(1, PLANE)]
    madeB = finish(flags, places, sources, (out0, mid0), (outB, midB), accB, wide)
    backB = [madeB[0]] + [exchange(madeB[r], "ctx", r) for r in range(1, PLANE)]
    return assemble(spot.astype(jnp.int32), [backA, backB])


def body(q, k, v, residue, rate, skip, w_out):
    rows, chan = q.shape
    modes = rate.shape[0]
    groups = chan // LANES
    count, cores = lax.axis_size("ctx"), lax.axis_size("ch")
    chunk, feats = w_out.shape
    split = (
        count == 4 * PLANE
        and cores == 2
        and chan == 8 * chunk
        and chunk % LANES == 0
        and feats % (PLANE * LANES) == 0
    )
    rate = rate.reshape(modes, groups, LANES)
    residue = residue.reshape(modes, groups, LANES)
    skip = skip.reshape(groups, LANES)
    if split:
        return split_block(q, k, v, residue, rate, skip, w_out)
    ends = end_states(k, v, rate)
    enter = entering_states(ends, rate, rows)
    gated = gated_conv(q, k, v, rate, residue, skip, enter)
    gated = gated.transpose(1, 0, 2).reshape(rows, chan)
    full_gated = lax.all_gather(gated, "ch", axis=1, tiled=True)
    w_full = lax.all_gather(w_out, "ctx", axis=0, tiled=True)
    mixed = jnp.dot(full_gated, w_full, preferred_element_type=jnp.float32)
    return mixed.astype(jnp.bfloat16)


def solution(mesh):
    placed = (
        P("ctx", "ch"),
        P("ctx", "ch"),
        P("ctx", "ch"),
        P(None, "ch"),
        P(None, "ch"),
        P("ch"),
        P("ctx", "ch"),
    )
    return jax.shard_map(
        body, mesh=mesh, in_specs=placed, out_specs=P("ctx", "ch"), check_vma=False
    )
```

```python
import jax
import jax.numpy as jnp
from jax import lax
from jax.experimental import pallas as pl
from jax.experimental.pallas import tpu as pltpu
from jax.sharding import PartitionSpec as P

LANES = 128
RADIX = 4
PLANE = 4
VMEM_BYTES = 60 << 20


def spread_signal(k_ref, v_ref, sig_ref):
    rows, width = k_ref.shape
    groups = width // LANES
    for g in range(groups):
        cols = pl.ds(g * LANES, LANES)
        product = k_ref[:, cols].astype(jnp.float32) * v_ref[:, cols].astype(jnp.float32)
        sig_ref[pl.ds(g, rows, stride=groups), :] = product


def ends_kernel(k_ref, v_ref, rate_ref, end_ref, sig_ref):
    rows, width = k_ref.shape
    modes, groups, _ = rate_ref.shape
    spread_signal(k_ref, v_ref, sig_ref)
    decay = [jnp.exp(-rate_ref[m]) for m in range(modes)]

    def step(t, state):
        s = sig_ref[pl.ds(pl.multiple_of(t * groups, groups), groups), :]
        return tuple(d * h + s for d, h in zip(decay, state))

    zero = jnp.zeros((groups, LANES), jnp.float32)
    state = lax.fori_loop(0, rows, step, (zero,) * modes, unroll=8)
    for m in range(modes):
        end_ref[m] = state[m]


def conv_kernel(q_ref, k_ref, v_ref, rate_ref, residue_ref, skip_ref, enter_ref, out_ref, sig_ref, conv_ref):
    rows, width = k_ref.shape
    modes, groups, _ = rate_ref.shape
    spread_signal(k_ref, v_ref, sig_ref)
    decay = [jnp.exp(-rate_ref[m]) for m in range(modes)]
    weight = [residue_ref[m] * jnp.sqrt(2.0 * rate_ref[m]) for m in range(modes)]
    skip = skip_ref[...]

    def step(t, state):
        at = pl.ds(pl.multiple_of(t * groups, groups), groups)
        s = sig_ref[at, :]
        state = tuple(d * h + s for d, h in zip(decay, state))
        terms = [c * h for c, h in zip(weight, state)] + [skip * s]
        while len(terms) > 1:
            terms = [sum(terms[i : i + 2]) for i in range(0, len(terms), 2)]
        conv_ref[at, :] = terms[0]
        return state

    lax.fori_loop(0, rows, step, tuple(enter_ref[m] for m in range(modes)), unroll=4)
    for g in range(groups):
        cols = pl.ds(g * LANES, LANES)
        conv = conv_ref[pl.ds(g, rows, stride=groups), :]
        out_ref[:, cols] = (q_ref[:, cols].astype(jnp.float32) * conv).astype(out_ref.dtype)


def block_specs(rows, modes, width):
    groups = width // LANES
    return (
        pl.BlockSpec((rows, width), lambda i: (0, i)),
        pl.BlockSpec((modes, groups, LANES), lambda i: (0, i, 0)),
        pl.BlockSpec((groups, LANES), lambda i: (i, 0)),
    )


def end_states(k, v, rate):
    rows, chan = k.shape
    modes = rate.shape[0]
    width = min(chan, 8 * LANES)
    wide, moded, _ = block_specs(rows, modes, width)
    return pl.pallas_call(
        ends_kernel,
        grid=(chan // width,),
        in_specs=[wide, wide, moded],
        out_specs=moded,
        out_shape=jax.ShapeDtypeStruct(rate.shape, jnp.float32),
        scratch_shapes=[pltpu.VMEM((rows * width // LANES, LANES), jnp.float32)],
        compiler_params=pltpu.CompilerParams(vmem_limit_bytes=VMEM_BYTES),
        cost_estimate=pl.CostEstimate(
            flops=2 * modes * rows * chan, bytes_accessed=4 * rows * chan, transcendentals=modes * chan
        ),
        name="end_states",
    )(k, v, rate)


def gated_conv(q, k, v, rate, residue, skip, enter):
    rows, chan = k.shape
    modes = rate.shape[0]
    width = min(chan, 8 * LANES)
    wide, moded, single = block_specs(rows, modes, width)
    spread = pltpu.VMEM((rows * width // LANES, LANES), jnp.float32)
    return pl.pallas_call(
        conv_kernel,
        grid=(chan // width,),
        in_specs=[wide, wide, wide, moded, moded, single, moded],
        out_specs=pl.BlockSpec((None, rows, width), lambda i: (i, 0, 0)),
        out_shape=jax.ShapeDtypeStruct((chan // width, rows, width), jnp.bfloat16),
        scratch_shapes=[spread, spread],
        compiler_params=pltpu.CompilerParams(vmem_limit_bytes=VMEM_BYTES),
        cost_estimate=pl.CostEstimate(
            flops=4 * modes * rows * chan, bytes_accessed=8 * rows * chan, transcendentals=2 * modes * chan
        ),
        name="gated_conv",
    )(q, k, v, rate, residue, skip, enter)


def shift_ctx(x, by):
    count = lax.axis_size("ctx")
    return lax.ppermute(x, "ctx", [(i, i + by) for i in range(count - by)])


def exchange(x, axis, flip):
    count = lax.axis_size(axis)
    return lax.ppermute(x, axis, [(i, i ^ flip) for i in range(count)])


def tie(*values):
    return lax.optimization_barrier(values)


def entering_states(ends, rate, rows):
    count = lax.axis_size("ctx")
    total = jnp.zeros_like(ends)
    for k in range(1, min(RADIX, count - 1) + 1):
        total = total + jnp.exp(-rate * float(rows * (k - 1))) * shift_ctx(ends, k)
    stride = RADIX
    while stride < count:
        base = total
        for k in range(1, RADIX):
            if stride * k < count:
                total = total + jnp.exp(-rate * float(rows * stride * k)) * shift_ctx(base, stride * k)
        stride *= RADIX
    return total


def fold_pair(ends, rate, flip, span):
    other = exchange(ends, "ctx", flip)
    later = (lax.axis_index("ctx") & flip) != 0
    decay = jnp.exp(-rate * float(span))
    both = jnp.where(later, decay * other + ends, decay * ends + other)
    return both, other, later


def in_order(gated_ref, index, place_ref, chunk):
    found = []
    for r in range(PLANE):
        start = pl.multiple_of(place_ref[r] * chunk, chunk)
        found.append(gated_ref[index, :, pl.ds(start, chunk)])
    return jnp.concatenate(found, axis=1)


def project(flags, places, sources, blocks, widths):
    rows, depth = sources[0][0][0].shape[1:]
    chunk = depth // PLANE
    arrays = []
    for source in sources:
        for array, _ in source:
            if not any(array is known for known in arrays):
                arrays.append(array)
    where = [[([a is known for known in arrays].index(True), at) for a, at in source] for source in sources]
    count = len(arrays)

    def kernel(flag_ref, place_ref, *refs):
        gated_refs, refs = refs[:count], refs[count:]
        weight_refs, out_refs = refs[: len(weights)], refs[len(weights) :]
        pieces = len(weights) // len(blocks)
        for b in range(len(blocks)):
            piece_refs = weight_refs[pieces * b : pieces * (b + 1)]
            for n, source in enumerate(where):

                @pl.when(flag_ref[b] == n)
                def _():
                    for r, (at, index) in enumerate(source):
                        lhs = in_order(gated_refs[at], index, place_ref, chunk)
                        first = 0
                        for part, width in enumerate(widths):
                            cols = pl.ds(first, width)
                            out_ref = out_refs[part * PLANE + r]
                            total = out_ref[...] if b else jnp.zeros(out_ref.shape, jnp.float32)
                            at_row = 0
                            for piece_ref in piece_refs:
                                depth_here = piece_ref.shape[0]
                                total += jnp.dot(
                                    lhs[:, at_row : at_row + depth_here],
                                    piece_ref[:, cols],
                                    preferred_element_type=jnp.float32,
                                )
                                at_row += depth_here
                            out_ref[...] = total
                            first += width

    smem = pl.BlockSpec(memory_space=pltpu.SMEM)
    vmem = pl.BlockSpec(memory_space=pltpu.VMEM)
    weights = [piece for block in blocks for piece in block]
    cols = sum(widths)
    made = pl.pallas_call(
        kernel,
        in_specs=[smem, smem] + [vmem] * (count + len(weights)),
        out_specs=[vmem] * (PLANE * len(widths)),
        out_shape=[jax.ShapeDtypeStruct((rows, width), jnp.float32) for width in widths for _ in range(PLANE)],
        compiler_params=pltpu.CompilerParams(vmem_limit_bytes=VMEM_BYTES),
        cost_estimate=pl.CostEstimate(
            flops=2 * PLANE * rows * depth * len(blocks) * cols,
            bytes_accessed=2 * len(blocks) * depth * (PLANE * rows + cols),
            transcendentals=0,
        ),
        name="project",
    )(flags, places, *arrays, *weights)
    return [made[part * PLANE : (part + 1) * PLANE] for part in range(len(widths))]


def finish(flags, places, sources, heads, rests, accs, first_col):
    rows, depth = sources[0][0][0].shape[1:]
    chunk = depth // PLANE
    width = accs[0].shape[1]
    arrays = []
    for source in sources:
        for array, _ in source:
            if not any(array is known for known in arrays):
                arrays.append(array)
    where = [[([a is known for known in arrays].index(True), at) for a, at in source] for source in sources]
    count = len(arrays)

    def kernel(flag_ref, place_ref, *refs):
        gated_refs, refs = refs[:count], refs[count:]
        head_a, head_b, rest_a, rest_b = refs[:4]
        acc_refs, out_refs, weight_ref = refs[4 : 4 + PLANE], refs[4 + PLANE : 4 + 2 * PLANE], refs[-1]
        cols = pl.ds(first_col, width)
        weight_ref[pl.ds(0, chunk), :] = head_a[:, cols] + head_b[:, cols]
        weight_ref[pl.ds(chunk, depth - chunk), :] = rest_a[...] + rest_b[...]
        for n, source in enumerate(where):

            @pl.when(flag_ref[3] == n)
            def _():
                for r, (at, index) in enumerate(source):
                    lhs = in_order(gated_refs[at], index, place_ref, chunk)
                    total = acc_refs[r][...] + jnp.dot(lhs, weight_ref[...], preferred_element_type=jnp.float32)
                    out_refs[r][...] = total.astype(jnp.bfloat16)

    smem = pl.BlockSpec(memory_space=pltpu.SMEM)
    vmem = pl.BlockSpec(memory_space=pltpu.VMEM)
    return pl.pallas_call(
        kernel,
        in_specs=[smem, smem] + [vmem] * (count + 4 + PLANE),
        out_specs=[vmem] * PLANE,
        out_shape=[jax.ShapeDtypeStruct((rows, width), jnp.bfloat16)] * PLANE,
        scratch_shapes=[pltpu.VMEM((depth, width), jnp.bfloat16)],
        compiler_params=pltpu.CompilerParams(vmem_limit_bytes=16 << 20),
        cost_estimate=pl.CostEstimate(
            flops=2 * PLANE * rows * depth * width, bytes_accessed=2 * depth * (PLANE * rows + width), transcendentals=0
        ),
        name="finish",
    )(flags, places, *arrays, *heads, *rests, *accs)


def assemble(spot, parts):
    rows = parts[0][0].shape[0]
    widths = [part[0].shape[1] for part in parts]
    cols = sum(widths)

    def kernel(spot_ref, *refs):
        out_ref = refs[-1]
        group = pl.program_id(0)
        for r in range(PLANE):

            @pl.when((spot_ref[0] ^ r) == group)
            def _():
                first = 0
                for part, width in enumerate(widths):
                    out_ref[:, pl.ds(first, width)] = refs[part * PLANE + r][...]
                    first += width

    flat = [piece for part in parts for piece in part]
    return pl.pallas_call(
        kernel,
        grid=(PLANE,),
        in_specs=[pl.BlockSpec(memory_space=pltpu.SMEM)] + [pl.BlockSpec(p.shape, lambda i: (0, 0)) for p in flat],
        out_specs=pl.BlockSpec((rows, cols), lambda i: (0, i)),
        out_shape=jax.ShapeDtypeStruct((rows, cols * PLANE), flat[0].dtype),
        name="assemble",
    )(spot.reshape(1), *flat)


def split_block(q, k, v, residue, rate, skip, w_out):
    rows, chan = q.shape
    me = lax.axis_index("ctx")
    core = lax.axis_index("ch")
    spot, plane = me & (PLANE - 1), me // PLANE
    count = lax.axis_size("ctx")
    chunk, feats = w_out.shape
    cols = feats // PLANE
    wide = 2 * cols // 3
    widths = [wide, cols - wide]

    def far(x):
        return exchange(x, "ctx", 2 * PLANE)

    def near(x):
        return exchange(x, "ctx", PLANE)

    middle = [i for i in range(count) if PLANE <= i < 3 * PLANE]

    def across(x):
        return lax.ppermute(x, "ctx", [(i, i ^ (3 * PLANE)) for i in middle])

    def outward(x):
        return lax.ppermute(x, "ctx", [(i, i ^ PLANE) for i in middle])

    own = [lax.dynamic_slice_in_dim(w_out, (spot ^ r) * cols, cols, axis=1) for r in range(PLANE)]
    w0, w1, w2, w3 = tie(*own)
    f0, n0 = far(w0), near(w0)
    ends = end_states(k, v, rate)
    both, other, later = fold_pair(ends, rate, 1, rows)
    before = jnp.where(later, other, 0.0)
    both, other, later = fold_pair(both, rate, 2, 2 * rows)
    odd = (me & 1).astype(jnp.float32)
    before = before + jnp.where(later, jnp.exp(-rate * (odd * rows)) * other, 0.0)
    f0, n0, w1, w2, w3, both, before = tie(f0, n0, w1, w2, w3, both, before)

    arrived = [exchange(w, "ctx", r + 1) for r, w in enumerate((w1, w2, w3))]
    last = shift_ctx(both, PLANE)
    decay = jnp.exp(-rate * float(PLANE * rows))
    carried = last + decay * shift_ctx(both + decay * last, 2 * PLANE)
    enter = before + jnp.exp(-rate * (spot * rows).astype(jnp.float32)) * carried
    gated = gated_conv(q, k, v, rate, residue, skip, enter)
    rest = jnp.concatenate(arrived)
    gated, rest = tie(gated, rest)

    fr, nr = far(rest), near(rest)
    held = [gated] + [exchange(gated, "ctx", r) for r in range(1, PLANE)]
    mid_first, mid_second = rest[:, :wide], rest[:, wide:]
    fr, nr, mid_first, mid_second, *held = tie(fr, nr, mid_first, mid_second, *held)

    out0 = outward(f0)
    outA = outward(fr[:, :wide])
    theirs = [exchange(x, "ch", 1) for x in held]
    out0, outA, *held = tie(out0, outA, *held, *theirs)

    def row_blocks(found):
        return [[(x, half) for x in found] for half in range(2)]

    def source_of(b):
        return jnp.where(b // 2 == core, b & 1, 2 + (b & 1))

    flags = jnp.stack([source_of(plane ^ r) for r in range(4)]).astype(jnp.int32)
    places = jnp.stack([spot ^ r for r in range(PLANE)]).astype(jnp.int32)

    def side(part, *blocks):
        span = slice(wide, None) if part else slice(0, wide)
        return jnp.concatenate([block[:, span] for block in blocks])

    mid0, midA = across(w0), across(mid_first)
    sources = row_blocks(held[:PLANE]) + row_blocks(held[PLANE:])
    accA, accB = project(flags, places, sources, [(w0, rest), (n0, nr), (f0, fr)], widths)
    mid0, midA, fr, mid_second, *accs = tie(mid0, midA, fr, mid_second, *accA, *accB)
    accA, accB = accs[:PLANE], accs[PLANE:]

    outB, midB = outward(fr[:, wide:]), across(mid_second)
    madeA = finish(flags, places, sources, (out0, mid0), (outA, midA), accA, 0)
    backA = [madeA[0]] + [exchange(madeA[r], "ctx", r) for r in range(1, PLANE)]
    madeB = finish(flags, places, sources, (out0, mid0), (outB, midB), accB, wide)
    backB = [madeB[0]] + [exchange(madeB[r], "ctx", r) for r in range(1, PLANE)]
    return assemble(spot.astype(jnp.int32), [backA, backB])


def body(q, k, v, residue, rate, skip, w_out):
    rows, chan = q.shape
    modes = rate.shape[0]
    groups = chan // LANES
    count, cores = lax.axis_size("ctx"), lax.axis_size("ch")
    chunk, feats = w_out.shape
    split = (
        count == 4 * PLANE
        and cores == 2
        and chan == 8 * chunk
        and chunk % LANES == 0
        and feats % (PLANE * LANES) == 0
    )
    rate = rate.reshape(modes, groups, LANES)
    residue = residue.reshape(modes, groups, LANES)
    skip = skip.reshape(groups, LANES)
    if split:
        return split_block(q, k, v, residue, rate, skip, w_out)
    ends = end_states(k, v, rate)
    enter = entering_states(ends, rate, rows)
    gated = gated_conv(q, k, v, rate, residue, skip, enter)
    gated = gated.transpose(1, 0, 2).reshape(rows, chan)
    full_gated = lax.all_gather(gated, "ch", axis=1, tiled=True)
    w_full = lax.all_gather(w_out, "ctx", axis=0, tiled=True)
    mixed = jnp.dot(full_gated, w_full, preferred_element_type=jnp.float32)
    return mixed.astype(jnp.bfloat16)


def solution(mesh):
    placed = (
        P("ctx", "ch"),
        P("ctx", "ch"),
        P("ctx", "ch"),
        P(None, "ch"),
        P(None, "ch"),
        P("ch"),
        P("ctx", "ch"),
    )
    return jax.shard_map(
        body, mesh=mesh, in_specs=placed, out_specs=P("ctx", "ch"), check_vma=False
    )
```

```python
import jax
import jax.numpy as jnp
from jax import lax
from jax.experimental import pallas as pl
from jax.experimental.pallas import tpu as pltpu
from jax.sharding import PartitionSpec as P

LANES = 128
RADIX = 4
PLANE = 4
VMEM_BYTES = 60 << 20


def spread_signal(k_ref, v_ref, sig_ref):
    rows, width = k_ref.shape
    groups = width // LANES
    for g in range(groups):
        cols = pl.ds(g * LANES, LANES)
        product = k_ref[:, cols].astype(jnp.float32) * v_ref[:, cols].astype(jnp.float32)
        sig_ref[pl.ds(g, rows, stride=groups), :] = product


def spread_modes(ref, out_ref):
    modes, width = ref.shape
    groups = width // LANES
    for g in range(groups):
        out_ref[pl.ds(g, modes, stride=groups), :] = ref[:, pl.ds(g * LANES, LANES)]


def ends_kernel(k_ref, v_ref, rate_ref, end_ref, sig_ref, mode_ref):
    rows, width = k_ref.shape
    modes, groups, _ = end_ref.shape
    spread_signal(k_ref, v_ref, sig_ref)
    spread_modes(rate_ref, mode_ref)
    decay = [jnp.exp(-mode_ref[pl.ds(m * groups, groups), :]) for m in range(modes)]

    def step(t, state):
        s = sig_ref[pl.ds(pl.multiple_of(t * groups, groups), groups), :]
        return tuple(d * h + s for d, h in zip(decay, state))

    zero = jnp.zeros((groups, LANES), jnp.float32)
    state = lax.fori_loop(0, rows, step, (zero,) * modes, unroll=8)
    for m in range(modes):
        end_ref[m] = state[m]


def conv_kernel(q_ref, k_ref, v_ref, rate_ref, residue_ref, skip_ref, enter_ref, out_ref, sig_ref, conv_ref, mode_ref, weight_ref):
    rows, width = k_ref.shape
    modes, groups, _ = enter_ref.shape
    spread_signal(k_ref, v_ref, sig_ref)
    spread_modes(rate_ref, mode_ref)
    spread_modes(residue_ref, weight_ref)
    rates = [mode_ref[pl.ds(m * groups, groups), :] for m in range(modes)]
    decay = [jnp.exp(-rate) for rate in rates]
    weight = [weight_ref[pl.ds(m * groups, groups), :] * jnp.sqrt(2.0 * rate) for m, rate in enumerate(rates)]
    skip = skip_ref[...]

    def step(t, state):
        at = pl.ds(pl.multiple_of(t * groups, groups), groups)
        s = sig_ref[at, :]
        state = tuple(d * h + s for d, h in zip(decay, state))
        terms = [c * h for c, h in zip(weight, state)] + [skip * s]
        while len(terms) > 1:
            terms = [sum(terms[i : i + 2]) for i in range(0, len(terms), 2)]
        conv_ref[at, :] = terms[0]
        return state

    lax.fori_loop(0, rows, step, tuple(enter_ref[m] for m in range(modes)), unroll=4)
    for g in range(groups):
        cols = pl.ds(g * LANES, LANES)
        conv = conv_ref[pl.ds(g, rows, stride=groups), :]
        out_ref[:, cols] = (q_ref[:, cols].astype(jnp.float32) * conv).astype(out_ref.dtype)


def block_specs(rows, modes, width):
    groups = width // LANES
    return (
        pl.BlockSpec((rows, width), lambda i: (0, i)),
        pl.BlockSpec((modes, width), lambda i: (0, i)),
        pl.BlockSpec((modes, groups, LANES), lambda i: (0, i, 0)),
        pl.BlockSpec((groups, LANES), lambda i: (i, 0)),
    )


def end_states(k, v, rate):
    rows, chan = k.shape
    modes = rate.shape[0]
    width = min(chan, 8 * LANES)
    wide, moded, state, _ = block_specs(rows, modes, width)
    return pl.pallas_call(
        ends_kernel,
        grid=(chan // width,),
        in_specs=[wide, wide, moded],
        out_specs=state,
        out_shape=jax.ShapeDtypeStruct((modes, chan // LANES, LANES), jnp.float32),
        scratch_shapes=[
            pltpu.VMEM((rows * width // LANES, LANES), jnp.float32),
            pltpu.VMEM((modes * width // LANES, LANES), jnp.float32),
        ],
        compiler_params=pltpu.CompilerParams(vmem_limit_bytes=VMEM_BYTES),
        cost_estimate=pl.CostEstimate(
            flops=2 * modes * rows * chan, bytes_accessed=4 * rows * chan, transcendentals=modes * chan
        ),
        name="end_states",
    )(k, v, rate)


def gated_conv(q, k, v, rate, residue, skip, enter):
    rows, chan = k.shape
    modes = rate.shape[0]
    width = min(chan, 8 * LANES)
    wide, moded, state, single = block_specs(rows, modes, width)
    spread = pltpu.VMEM((rows * width // LANES, LANES), jnp.float32)
    moded_spread = pltpu.VMEM((modes * width // LANES, LANES), jnp.float32)
    return pl.pallas_call(
        conv_kernel,
        grid=(chan // width,),
        in_specs=[wide, wide, wide, moded, moded, single, state],
        out_specs=pl.BlockSpec((None, rows, width), lambda i: (i, 0, 0)),
        out_shape=jax.ShapeDtypeStruct((chan // width, rows, width), jnp.bfloat16),
        scratch_shapes=[spread, spread, moded_spread, moded_spread],
        compiler_params=pltpu.CompilerParams(vmem_limit_bytes=VMEM_BYTES),
        cost_estimate=pl.CostEstimate(
            flops=4 * modes * rows * chan, bytes_accessed=8 * rows * chan, transcendentals=2 * modes * chan
        ),
        name="gated_conv",
    )(q, k, v, rate, residue, skip, enter)


def shift_ctx(x, by):
    count = lax.axis_size("ctx")
    return lax.ppermute(x, "ctx", [(i, i + by) for i in range(count - by)])


def exchange(x, axis, flip):
    count = lax.axis_size(axis)
    return lax.ppermute(x, axis, [(i, i ^ flip) for i in range(count)])


def tie(*values):
    return lax.optimization_barrier(values)


def entering_states(ends, rate, rows):
    count = lax.axis_size("ctx")
    total = jnp.zeros_like(ends)
    for k in range(1, min(RADIX, count - 1) + 1):
        total = total + jnp.exp(-rate * float(rows * (k - 1))) * shift_ctx(ends, k)
    stride = RADIX
    while stride < count:
        base = total
        for k in range(1, RADIX):
            if stride * k < count:
                total = total + jnp.exp(-rate * float(rows * stride * k)) * shift_ctx(base, stride * k)
        stride *= RADIX
    return total


def box(fn, *args):
    once = (lax.axis_index("ctx") >= 0).astype(jnp.int32)
    shapes = jax.eval_shape(fn, *args)
    empty = jax.tree.map(lambda a: jnp.zeros(a.shape, a.dtype), shapes)

    def run(step, _):
        return fn(*tie(step, *args)[1:])

    return lax.fori_loop(0, once, run, empty)


def product(flags, places, ours, theirs, blocks, accs, widths, out_dtype):
    _, rows, depth = ours[0].shape
    chunk = depth // PLANE
    cols = sum(widths)
    count = len(blocks)
    weights = [array for _, _, pieces in blocks for choices, *_ in pieces for array in choices]
    accs = accs or []

    def kernel(flag_ref, place_ref, *refs):
        our_refs, their_refs, refs = refs[:PLANE], refs[PLANE : 2 * PLANE], refs[2 * PLANE :]
        weight_refs, refs = list(refs[: len(weights)]), refs[len(weights) :]
        acc_refs, out_refs = refs[: len(accs)], refs[len(accs) : len(accs) + PLANE * len(widths)]
        gated_buf, weight_buf, gated_sems, weight_sems = refs[-4:]

        def target(b, r):
            start = pl.multiple_of(b * depth + place_ref[r] * chunk, chunk)
            return weight_buf.at[pl.ds(start, chunk), :]

        for b, (flag, pick, pieces) in enumerate(blocks):
            for choices, first, chunks, col in pieces:
                for c in range(len(choices)):
                    ref = weight_refs.pop(0)
                    for r in range(first, first + chunks):
                        source = ref.at[pl.ds((r - first) * chunk, chunk), pl.ds(col, cols)]
                        copy = pltpu.make_async_copy(source, target(b, r), weight_sems.at[b])
                        if pick is None:
                            copy.start()
                        else:
                            pl.when(flag_ref[pick] == c)(copy.start)
            half = flag_ref[flag] & 1
            for r in range(PLANE):
                for c, refs_of in enumerate((our_refs, their_refs)):
                    copy = pltpu.make_async_copy(refs_of[r].at[half], gated_buf.at[b, r], gated_sems.at[b, r])
                    pl.when(flag_ref[flag] // 2 == c)(copy.start)
        for b in range(count):
            block = weight_buf.at[pl.ds(b * depth, depth), :]
            pltpu.make_async_copy(block, block, weight_sems.at[b]).wait()
            for r in range(PLANE):
                pltpu.make_async_copy(our_refs[r].at[0], gated_buf.at[b, r], gated_sems.at[b, r]).wait()
                first = 0
                for part, width in enumerate(widths):
                    at = part * PLANE + r
                    total = jnp.dot(
                        gated_buf[b, r],
                        weight_buf[pl.ds(b * depth, depth), pl.ds(first, width)],
                        preferred_element_type=jnp.float32,
                    )
                    if b:
                        total = total + out_refs[at][...]
                    elif accs:
                        total = total + acc_refs[at][...]
                    out_refs[at][...] = total.astype(out_dtype)
                    first += width

    smem = pl.BlockSpec(memory_space=pltpu.SMEM)
    vmem = pl.BlockSpec(memory_space=pltpu.VMEM)
    anywhere = pl.BlockSpec(memory_space=pl.ANY)
    made = pl.pallas_call(
        kernel,
        in_specs=[smem, smem] + [anywhere] * (2 * PLANE + len(weights)) + [vmem] * len(accs),
        out_specs=[vmem] * (PLANE * len(widths)),
        out_shape=[jax.ShapeDtypeStruct((rows, width), out_dtype) for width in widths for _ in range(PLANE)],
        scratch_shapes=[
            pltpu.VMEM((count, PLANE, rows, depth), jnp.bfloat16),
            pltpu.VMEM((count * depth, cols), jnp.bfloat16),
            pltpu.SemaphoreType.DMA((count, PLANE)),
            pltpu.SemaphoreType.DMA((count,)),
        ],
        compiler_params=pltpu.CompilerParams(vmem_limit_bytes=VMEM_BYTES),
        cost_estimate=pl.CostEstimate(
            flops=2 * PLANE * rows * depth * count * cols,
            bytes_accessed=2 * count * depth * (PLANE * rows + cols),
            transcendentals=0,
        ),
        name="product",
    )(flags, places, *ours, *theirs, *weights, *accs)
    return [list(made[part * PLANE : (part + 1) * PLANE]) for part in range(len(widths))]


def assemble(places, parts):
    rows = parts[0][0].shape[0]
    widths = [part[0].shape[1] for part in parts]
    cols = sum(widths)
    flat = [piece for part in parts for piece in part]

    def kernel(place_ref, *refs):
        *piece_refs, out_ref, sems = refs
        copies = []
        first = 0
        for part, width in enumerate(widths):
            for r in range(PLANE):
                at = part * PLANE + r
                start = pl.multiple_of(place_ref[r] * cols + first, LANES)
                target = out_ref.at[:, pl.ds(start, width)]
                copies.append(pltpu.make_async_copy(piece_refs[at], target, sems.at[at]))
                copies[-1].start()
            first += width
        for copy in copies:
            copy.wait()

    return pl.pallas_call(
        kernel,
        in_specs=[pl.BlockSpec(memory_space=pltpu.SMEM)] + [pl.BlockSpec(memory_space=pltpu.VMEM)] * len(flat),
        out_specs=pl.BlockSpec(memory_space=pl.ANY),
        out_shape=jax.ShapeDtypeStruct((rows, cols * PLANE), flat[0].dtype),
        scratch_shapes=[pltpu.SemaphoreType.DMA((len(flat),))],
        compiler_params=pltpu.CompilerParams(vmem_limit_bytes=16 << 20),
        name="assemble",
    )(places, *flat)


def split_block(q, k, v, residue, rate, skip, w_out):
    rows, chan = q.shape
    modes = rate.shape[0]
    me = lax.axis_index("ctx")
    core = lax.axis_index("ch")
    spot, plane = me & (PLANE - 1), me // PLANE
    count = lax.axis_size("ctx")
    chunk, feats = w_out.shape
    cols = feats // PLANE
    wide = 2 * cols // 3
    widths = [wide, cols - wide]
    speed = rate.reshape(modes, chan // LANES, LANES)

    def far(x):
        return exchange(x, "ctx", 2 * PLANE)

    def near(x):
        return exchange(x, "ctx", PLANE)

    middle = [i for i in range(count) if PLANE <= i < 3 * PLANE]

    def across(x):
        return lax.ppermute(x, "ctx", [(i, i ^ (3 * PLANE)) for i in middle])

    def outward(x):
        return lax.ppermute(x, "ctx", [(i, i ^ PLANE) for i in middle])

    def fade(span):
        return jnp.exp(-speed * span)

    def line_scan(k, v, rate, speed):
        ends = end_states(k, v, rate)
        decay = jnp.exp(-speed * float(PLANE * rows))
        last = shift_ctx(ends, PLANE)
        line = last + decay * shift_ctx(ends + decay * last, 2 * PLANE)
        return jnp.stack([ends, line])

    own = [lax.dynamic_slice_in_dim(w_out, (spot ^ r) * cols, cols, axis=1) for r in range(PLANE)]
    w0, w1, w2, w3 = tie(*own)
    f0 = far(w0)
    w1, w2, w3 = [exchange(w, "ctx", r + 1) for r, w in enumerate((w1, w2, w3))]
    pair = box(line_scan, k, v, rate, speed)
    f0, w0, w1, w2, w3, pair = tie(f0, w0, w1, w2, w3, pair)

    f1, n0 = far(w1), near(w0)
    out0, mid0 = outward(f0), across(w0)
    x_later, y_later = (spot & 1) != 0, (spot & 2) != 0
    other = exchange(pair, "ctx", 1)
    both = jnp.where(x_later, fade(float(rows)) * other + pair, fade(float(rows)) * pair + other)
    before = jnp.where(x_later, other[0], 0.0)
    other = exchange(both, "ctx", 2)
    before = before + jnp.where(y_later, fade((spot & 1).astype(jnp.float32) * rows) * other[0], 0.0)
    line = jnp.where(y_later, fade(2.0 * rows) * other[1] + both[1], fade(2.0 * rows) * both[1] + other[1])
    enter = before + fade((spot * rows).astype(jnp.float32)) * line
    gated = gated_conv(q, k, v, rate, residue, skip, enter)
    rest, last_two = jnp.concatenate([w1, w2, w3]), jnp.concatenate([w2, w3])
    f1, n0, out0, mid0, gated, rest, last_two = tie(f1, n0, out0, mid0, gated, rest, last_two)

    f23, nr = far(last_two), near(rest)
    ours = [gated] + [exchange(gated, "ctx", r) for r in range(1, PLANE)]
    theirs = [exchange(x, "ch", 1) for x in ours]
    midA, midB = rest[:, :wide], rest[:, wide:]
    f23, nr, midA, midB, *held = tie(f23, nr, midA, midB, *ours, *theirs)
    ours, theirs = held[:PLANE], held[PLANE:]

    def source_of(b):
        return jnp.where(b // 2 == core, b & 1, 2 + (b & 1))

    is_middle = jnp.where((plane == 0) | (plane == 3), 0, 1)
    flags = jnp.stack([source_of(plane ^ r) for r in range(4)] + [is_middle]).astype(jnp.int32)
    places = jnp.stack([spot ^ r for r in range(PLANE)]).astype(jnp.int32)

    outA, midA = outward(jnp.concatenate([f1[:, :wide], f23[:, :wide]])), across(midA)
    blocks = [
        (0, None, [((w0,), 0, 1, 0), ((rest,), 1, 3, 0)]),
        (1, None, [((n0,), 0, 1, 0), ((nr,), 1, 3, 0)]),
        (2, None, [((f0,), 0, 1, 0), ((f1,), 1, 1, 0), ((f23,), 2, 2, 0)]),
    ]
    accA, accB = product(flags, places, ours, theirs, blocks, None, widths, jnp.float32)
    outA, midA, f1, f23, midB, *accs = tie(outA, midA, f1, f23, midB, *accA, *accB)
    accA, accB = accs[:PLANE], accs[PLANE:]

    outB, midB = outward(jnp.concatenate([f1[:, wide:], f23[:, wide:]])), across(midB)
    blocks = [(3, 4, [((out0, mid0), 0, 1, 0), ((outA, midA), 1, 3, 0)])]
    (madeA,) = product(flags, places, ours, theirs, blocks, accA, widths[:1], jnp.bfloat16)
    backA = [madeA[0]] + [exchange(madeA[r], "ctx", r) for r in range(1, PLANE)]
    blocks = [(3, 4, [((out0, mid0), 0, 1, wide), ((outB, midB), 1, 3, 0)])]
    (madeB,) = product(flags, places, ours, theirs, blocks, accB, widths[1:], jnp.bfloat16)
    backB = [madeB[0]] + [exchange(madeB[r], "ctx", r) for r in range(1, PLANE)]
    return assemble(places, [backA, backB])


def body(q, k, v, residue, rate, skip, w_out):
    rows, chan = q.shape
    modes = rate.shape[0]
    groups = chan // LANES
    count, cores = lax.axis_size("ctx"), lax.axis_size("ch")
    chunk, feats = w_out.shape
    split = (
        count == 4 * PLANE
        and cores == 2
        and chan == 8 * chunk
        and chunk % LANES == 0
        and feats % (PLANE * LANES) == 0
    )
    skip = skip.reshape(groups, LANES)
    if split:
        return split_block(q, k, v, residue, rate, skip, w_out)
    ends = end_states(k, v, rate)
    enter = entering_states(ends, rate.reshape(modes, groups, LANES), rows)
    gated = gated_conv(q, k, v, rate, residue, skip, enter)
    gated = gated.transpose(1, 0, 2).reshape(rows, chan)
    full_gated = lax.all_gather(gated, "ch", axis=1, tiled=True)
    w_full = lax.all_gather(w_out, "ctx", axis=0, tiled=True)
    mixed = jnp.dot(full_gated, w_full, preferred_element_type=jnp.float32)
    return mixed.astype(jnp.bfloat16)


def solution(mesh):
    placed = (
        P("ctx", "ch"),
        P("ctx", "ch"),
        P("ctx", "ch"),
        P(None, "ch"),
        P(None, "ch"),
        P("ch"),
        P("ctx", "ch"),
    )
    return jax.shard_map(
        body, mesh=mesh, in_specs=placed, out_specs=P("ctx", "ch"), check_vma=False
    )
```

```python
import jax
import jax.numpy as jnp
from jax import lax
from jax.experimental import pallas as pl
from jax.experimental.pallas import tpu as pltpu
from jax.sharding import PartitionSpec as P

LANES = 128
RADIX = 4
PLANE = 4
VMEM_BYTES = 60 << 20


def spread_signal(k_ref, v_ref, sig_ref):
    rows, width = k_ref.shape
    groups = width // LANES
    for g in range(groups):
        cols = pl.ds(g * LANES, LANES)
        product = k_ref[:, cols].astype(jnp.float32) * v_ref[:, cols].astype(jnp.float32)
        sig_ref[pl.ds(g, rows, stride=groups), :] = product


def spread_modes(ref, out_ref):
    modes, width = ref.shape
    groups = width // LANES
    for g in range(groups):
        out_ref[pl.ds(g, modes, stride=groups), :] = ref[:, pl.ds(g * LANES, LANES)]


def ends_kernel(k_ref, v_ref, rate_ref, end_ref, sig_ref, mode_ref):
    rows, width = k_ref.shape
    modes, groups, _ = end_ref.shape
    spread_signal(k_ref, v_ref, sig_ref)
    spread_modes(rate_ref, mode_ref)
    decay = [jnp.exp(-mode_ref[pl.ds(m * groups, groups), :]) for m in range(modes)]

    def step(t, state):
        s = sig_ref[pl.ds(pl.multiple_of(t * groups, groups), groups), :]
        return tuple(d * h + s for d, h in zip(decay, state))

    zero = jnp.zeros((groups, LANES), jnp.float32)
    state = lax.fori_loop(0, rows, step, (zero,) * modes, unroll=8)
    for m in range(modes):
        end_ref[m] = state[m]


def conv_kernel(q_ref, k_ref, v_ref, rate_ref, residue_ref, skip_ref, enter_ref, out_ref, sig_ref, conv_ref, mode_ref, weight_ref):
    rows, width = k_ref.shape
    modes, groups, _ = enter_ref.shape
    spread_signal(k_ref, v_ref, sig_ref)
    spread_modes(rate_ref, mode_ref)
    spread_modes(residue_ref, weight_ref)
    rates = [mode_ref[pl.ds(m * groups, groups), :] for m in range(modes)]
    decay = [jnp.exp(-rate) for rate in rates]
    weight = [weight_ref[pl.ds(m * groups, groups), :] * jnp.sqrt(2.0 * rate) for m, rate in enumerate(rates)]
    skip = skip_ref[...]

    def step(t, state):
        at = pl.ds(pl.multiple_of(t * groups, groups), groups)
        s = sig_ref[at, :]
        state = tuple(d * h + s for d, h in zip(decay, state))
        terms = [c * h for c, h in zip(weight, state)] + [skip * s]
        while len(terms) > 1:
            terms = [sum(terms[i : i + 2]) for i in range(0, len(terms), 2)]
        conv_ref[at, :] = terms[0]
        return state

    lax.fori_loop(0, rows, step, tuple(enter_ref[m] for m in range(modes)), unroll=4)
    for g in range(groups):
        cols = pl.ds(g * LANES, LANES)
        conv = conv_ref[pl.ds(g, rows, stride=groups), :]
        out_ref[:, cols] = (q_ref[:, cols].astype(jnp.float32) * conv).astype(out_ref.dtype)


def block_specs(rows, modes, width):
    groups = width // LANES
    return (
        pl.BlockSpec((rows, width), lambda i: (0, i)),
        pl.BlockSpec((modes, width), lambda i: (0, i)),
        pl.BlockSpec((modes, groups, LANES), lambda i: (0, i, 0)),
        pl.BlockSpec((groups, LANES), lambda i: (i, 0)),
    )


def end_states(k, v, rate):
    rows, chan = k.shape
    modes = rate.shape[0]
    width = min(chan, 8 * LANES)
    wide, moded, state, _ = block_specs(rows, modes, width)
    return pl.pallas_call(
        ends_kernel,
        grid=(chan // width,),
        in_specs=[wide, wide, moded],
        out_specs=state,
        out_shape=jax.ShapeDtypeStruct((modes, chan // LANES, LANES), jnp.float32),
        scratch_shapes=[
            pltpu.VMEM((rows * width // LANES, LANES), jnp.float32),
            pltpu.VMEM((modes * width // LANES, LANES), jnp.float32),
        ],
        compiler_params=pltpu.CompilerParams(vmem_limit_bytes=VMEM_BYTES),
        cost_estimate=pl.CostEstimate(
            flops=2 * modes * rows * chan, bytes_accessed=4 * rows * chan, transcendentals=modes * chan
        ),
        name="end_states",
    )(k, v, rate)


def gated_conv(q, k, v, rate, residue, skip, enter):
    rows, chan = k.shape
    modes = rate.shape[0]
    width = min(chan, 8 * LANES)
    wide, moded, state, single = block_specs(rows, modes, width)
    spread = pltpu.VMEM((rows * width // LANES, LANES), jnp.float32)
    moded_spread = pltpu.VMEM((modes * width // LANES, LANES), jnp.float32)
    return pl.pallas_call(
        conv_kernel,
        grid=(chan // width,),
        in_specs=[wide, wide, wide, moded, moded, single, state],
        out_specs=pl.BlockSpec((None, rows, width), lambda i: (i, 0, 0)),
        out_shape=jax.ShapeDtypeStruct((chan // width, rows, width), jnp.bfloat16),
        scratch_shapes=[spread, spread, moded_spread, moded_spread],
        compiler_params=pltpu.CompilerParams(vmem_limit_bytes=VMEM_BYTES),
        cost_estimate=pl.CostEstimate(
            flops=4 * modes * rows * chan, bytes_accessed=8 * rows * chan, transcendentals=2 * modes * chan
        ),
        name="gated_conv",
    )(q, k, v, rate, residue, skip, enter)


def shift_ctx(x, by):
    count = lax.axis_size("ctx")
    return lax.ppermute(x, "ctx", [(i, i + by) for i in range(count - by)])


def exchange(x, axis, flip):
    count = lax.axis_size(axis)
    return lax.ppermute(x, axis, [(i, i ^ flip) for i in range(count)])


def tie(*values):
    return lax.optimization_barrier(values)


def entering_states(ends, rate, rows):
    count = lax.axis_size("ctx")
    total = jnp.zeros_like(ends)
    for k in range(1, min(RADIX, count - 1) + 1):
        total = total + jnp.exp(-rate * float(rows * (k - 1))) * shift_ctx(ends, k)
    stride = RADIX
    while stride < count:
        base = total
        for k in range(1, RADIX):
            if stride * k < count:
                total = total + jnp.exp(-rate * float(rows * stride * k)) * shift_ctx(base, stride * k)
        stride *= RADIX
    return total


def box(fn, *args):
    once = (lax.axis_index("ctx") >= 0).astype(jnp.int32)
    shapes = jax.eval_shape(fn, *args)
    empty = jax.tree.map(lambda a: jnp.zeros(a.shape, a.dtype), shapes)

    def run(step, _):
        return fn(*tie(step, *args)[1:])

    return lax.fori_loop(0, once, run, empty)


def pack(sources, recipes):
    shapes = [(sum(part[1].stop - part[1].start for part in recipe), recipe[0][3]) for recipe in recipes]
    moves = []
    for out, recipe in enumerate(recipes):
        row = 0
        for source, span, col, cols in recipe:
            moves.append((source, span.start, span.stop - span.start, col, cols, out, row))
            row += span.stop - span.start

    def kernel(*refs):
        in_refs, out_refs, sems = refs[: len(sources)], refs[len(sources) : -1], refs[-1]
        copies = []
        for n, (source, first, count, col, cols, out, row) in enumerate(moves):
            block = in_refs[source].at[pl.ds(first, count), pl.ds(col, cols)]
            copies.append(pltpu.make_async_copy(block, out_refs[out].at[pl.ds(row, count), :], sems.at[n]))
            copies[-1].start()
        for copy in copies:
            copy.wait()

    return pl.pallas_call(
        kernel,
        in_specs=[pl.BlockSpec(memory_space=pl.ANY)] * len(sources),
        out_specs=[pl.BlockSpec(memory_space=pltpu.VMEM)] * len(recipes),
        out_shape=[jax.ShapeDtypeStruct(shape, sources[0].dtype) for shape in shapes],
        scratch_shapes=[pltpu.SemaphoreType.DMA((len(moves),))],
        compiler_params=pltpu.CompilerParams(vmem_limit_bytes=VMEM_BYTES),
        name="pack",
    )(*sources)


def product(flags, places, ours, theirs, blocks, accs, widths, out_dtype):
    _, rows, depth = ours[0].shape
    chunk = depth // PLANE
    cols = sum(widths)
    count = len(blocks)
    weights = [array for _, _, pieces in blocks for choices, *_ in pieces for array in choices]
    accs = accs or []

    def kernel(flag_ref, place_ref, *refs):
        our_refs, their_refs, refs = refs[:PLANE], refs[PLANE : 2 * PLANE], refs[2 * PLANE :]
        weight_refs, refs = list(refs[: len(weights)]), refs[len(weights) :]
        acc_refs, out_refs = refs[: len(accs)], refs[len(accs) : len(accs) + PLANE * len(widths)]
        gated_buf, weight_buf, gated_sems, weight_sems = refs[-4:]

        step = chunk // 2

        def target(b, at):
            start = pl.multiple_of(b * depth + place_ref[at // chunk] * chunk + at % chunk, step)
            return weight_buf.at[pl.ds(start, step), :]

        for b, (flag, pick, pieces) in enumerate(blocks):
            row = 0
            for choices, col in pieces:
                for c in range(len(choices)):
                    ref = weight_refs.pop(0)
                    for at in range(0, ref.shape[0], step):
                        source = ref.at[pl.ds(at, step), pl.ds(col, cols)]
                        copy = pltpu.make_async_copy(source, target(b, row + at), weight_sems.at[b])
                        if pick is None:
                            copy.start()
                        else:
                            pl.when(flag_ref[pick] == c)(copy.start)
                row += choices[0].shape[0]
            half = flag_ref[flag] & 1
            for r in range(PLANE):
                for c, refs_of in enumerate((our_refs, their_refs)):
                    target_rows = gated_buf.at[b, pl.ds(r * rows, rows), :]
                    copy = pltpu.make_async_copy(refs_of[r].at[half], target_rows, gated_sems.at[b])
                    pl.when(flag_ref[flag] // 2 == c)(copy.start)
        for b in range(count):
            block = weight_buf.at[pl.ds(b * depth, depth), :]
            pltpu.make_async_copy(block, block, weight_sems.at[b]).wait()
            pltpu.make_async_copy(gated_buf.at[b], gated_buf.at[b], gated_sems.at[b]).wait()
            first = 0
            for part, width in enumerate(widths):
                for col in range(0, width, 2 * LANES):
                    here = pl.ds(col, 2 * LANES)
                    made = jnp.dot(
                        gated_buf[b],
                        weight_buf[pl.ds(b * depth, depth), pl.ds(first + col, 2 * LANES)],
                        preferred_element_type=jnp.float32,
                    )
                    for r in range(PLANE):
                        at = part * PLANE + r
                        total = made[r * rows : (r + 1) * rows]
                        if b:
                            total = total + out_refs[at][:, here]
                        elif accs:
                            total = total + acc_refs[at][:, here]
                        out_refs[at][:, here] = total.astype(out_dtype)
                first += width

    smem = pl.BlockSpec(memory_space=pltpu.SMEM)
    vmem = pl.BlockSpec(memory_space=pltpu.VMEM)
    anywhere = pl.BlockSpec(memory_space=pl.ANY)
    made = pl.pallas_call(
        kernel,
        in_specs=[smem, smem] + [anywhere] * (2 * PLANE + len(weights)) + [vmem] * len(accs),
        out_specs=[vmem] * (PLANE * len(widths)),
        out_shape=[jax.ShapeDtypeStruct((rows, width), out_dtype) for width in widths for _ in range(PLANE)],
        scratch_shapes=[
            pltpu.VMEM((count, PLANE * rows, depth), jnp.bfloat16),
            pltpu.VMEM((count * depth, cols), jnp.bfloat16),
            pltpu.SemaphoreType.DMA((count,)),
            pltpu.SemaphoreType.DMA((count,)),
        ],
        compiler_params=pltpu.CompilerParams(vmem_limit_bytes=VMEM_BYTES),
        cost_estimate=pl.CostEstimate(
            flops=2 * PLANE * rows * depth * count * cols,
            bytes_accessed=2 * count * depth * (PLANE * rows + cols),
            transcendentals=0,
        ),
        name="product",
    )(flags, places, *ours, *theirs, *weights, *accs)
    return [list(made[part * PLANE : (part + 1) * PLANE]) for part in range(len(widths))]


def assemble(places, parts):
    rows = parts[0][0].shape[0]
    widths = [part[0].shape[1] for part in parts]
    cols = sum(widths)
    flat = [piece for part in parts for piece in part]

    def kernel(place_ref, *refs):
        *piece_refs, out_ref, sems = refs
        copies = []
        first = 0
        for part, width in enumerate(widths):
            for r in range(PLANE):
                at = part * PLANE + r
                start = pl.multiple_of(place_ref[r] * cols + first, LANES)
                target = out_ref.at[:, pl.ds(start, width)]
                copies.append(pltpu.make_async_copy(piece_refs[at], target, sems.at[at]))
                copies[-1].start()
            first += width
        for copy in copies:
            copy.wait()

    return pl.pallas_call(
        kernel,
        in_specs=[pl.BlockSpec(memory_space=pltpu.SMEM)] + [pl.BlockSpec(memory_space=pltpu.VMEM)] * len(flat),
        out_specs=pl.BlockSpec(memory_space=pl.ANY),
        out_shape=jax.ShapeDtypeStruct((rows, cols * PLANE), flat[0].dtype),
        scratch_shapes=[pltpu.SemaphoreType.DMA((len(flat),))],
        compiler_params=pltpu.CompilerParams(vmem_limit_bytes=16 << 20),
        name="assemble",
    )(places, *flat)


def split_block(q, k, v, residue, rate, skip, w_out):
    rows, chan = q.shape
    modes = rate.shape[0]
    me = lax.axis_index("ctx")
    core = lax.axis_index("ch")
    spot, plane = me & (PLANE - 1), me // PLANE
    count = lax.axis_size("ctx")
    chunk, feats = w_out.shape
    cols = feats // PLANE
    wide = 2 * cols // 3
    widths = [wide, cols - wide]
    speed = rate.reshape(modes, chan // LANES, LANES)

    def far(x):
        return exchange(x, "ctx", 2 * PLANE)

    def near(x):
        return exchange(x, "ctx", PLANE)

    middle = [i for i in range(count) if PLANE <= i < 3 * PLANE]

    def across(x):
        return lax.ppermute(x, "ctx", [(i, i ^ (3 * PLANE)) for i in middle])

    def outward(x):
        return lax.ppermute(x, "ctx", [(i, i ^ PLANE) for i in middle])

    def fade(span):
        return jnp.exp(-speed * span)

    def line_scan(k, v, rate, speed):
        ends = end_states(k, v, rate)
        decay = jnp.exp(-speed * float(PLANE * rows))
        last = shift_ctx(ends, PLANE)
        line = last + decay * shift_ctx(ends + decay * last, 2 * PLANE)
        return jnp.stack([ends, line])

    own = [lax.dynamic_slice_in_dim(w_out, (spot ^ r) * cols, cols, axis=1) for r in range(PLANE)]
    w0, w1, w2, w3 = tie(*own)
    w1, w2, w3 = [exchange(w, "ctx", r + 1) for r, w in enumerate((w1, w2, w3))]
    pair = box(line_scan, k, v, rate, speed)
    w0, w1, w2, w3, pair = tie(w0, w1, w2, w3, pair)

    half = chunk // 2
    every, upper, lower = slice(0, chunk), slice(0, half), slice(half, chunk)
    head, tail, tail1, tail2, midA, midB = pack(
        [w0, w1, w2, w3],
        [
            [(0, every, 0, cols), (1, upper, 0, cols)],
            [(1, lower, 0, cols), (2, every, 0, cols), (3, every, 0, cols)],
            [(1, lower, 0, cols), (2, every, 0, cols), (3, upper, 0, cols)],
            [(3, lower, 0, cols)],
            [(r, every, 0, wide) for r in range(PLANE)],
            [(r, every, wide, cols - wide) for r in range(PLANE)],
        ],
    )
    f0, n0 = far(head), near(head)
    x_later, y_later = (spot & 1) != 0, (spot & 2) != 0
    other = exchange(pair, "ctx", 1)
    both = jnp.where(x_later, fade(float(rows)) * other + pair, fade(float(rows)) * pair + other)
    before = jnp.where(x_later, other[0], 0.0)
    other = exchange(both, "ctx", 2)
    before = before + jnp.where(y_later, fade((spot & 1).astype(jnp.float32) * rows) * other[0], 0.0)
    line = jnp.where(y_later, fade(2.0 * rows) * other[1] + both[1], fade(2.0 * rows) * both[1] + other[1])
    enter = before + fade((spot * rows).astype(jnp.float32)) * line
    gated = gated_conv(q, k, v, rate, residue, skip, enter)
    f0, n0, tail, tail1, tail2, midA, midB, gated = tie(f0, n0, tail, tail1, tail2, midA, midB, gated)

    f1, n1 = far(tail1), near(tail)
    ours = [gated] + [exchange(gated, "ctx", r) for r in range(1, PLANE)]
    f1, n1, tail2, midA, midB, *ours = tie(f1, n1, tail2, midA, midB, *ours)

    f2 = far(tail2)
    theirs = [exchange(x, "ch", 1) for x in ours]
    f0, f1, f2, midA, midB, *held = tie(f0, f1, f2, midA, midB, *ours, *theirs)
    ours, theirs = held[:PLANE], held[PLANE:]

    def source_of(b):
        return jnp.where(b // 2 == core, b & 1, 2 + (b & 1))

    is_middle = jnp.where((plane == 0) | (plane == 3), 0, 1)
    flags = jnp.stack([source_of(plane ^ r) for r in range(4)] + [is_middle]).astype(jnp.int32)
    places = jnp.stack([spot ^ r for r in range(PLANE)]).astype(jnp.int32)

    full = [slice(0, x.shape[0]) for x in (f0, f1, f2)]
    outA, outB = pack(
        [f0, f1, f2],
        [
            [(n, span, 0, wide) for n, span in enumerate(full)],
            [(n, span, wide, cols - wide) for n, span in enumerate(full)],
        ],
    )
    outA, midA = outward(outA), across(midA)
    blocks = [
        (0, None, [((w,), 0) for w in (w0, w1, w2, w3)]),
        (1, None, [((n0,), 0), ((n1,), 0)]),
        (2, None, [((f0,), 0), ((f1,), 0), ((f2,), 0)]),
    ]
    accA, accB = product(flags, places, ours, theirs, blocks, None, widths, jnp.float32)
    outA, midA, outB, midB, *accs = tie(outA, midA, outB, midB, *accA, *accB)
    accA, accB = accs[:PLANE], accs[PLANE:]

    outB, midB = outward(outB), across(midB)
    blocks = [(3, 4, [((outA, midA), 0)])]
    (madeA,) = product(flags, places, ours, theirs, blocks, accA, widths[:1], jnp.bfloat16)
    backA = [madeA[0]] + [exchange(madeA[r], "ctx", r) for r in range(1, PLANE)]
    blocks = [(3, 4, [((outB, midB), 0)])]
    (madeB,) = product(flags, places, ours, theirs, blocks, accB, widths[1:], jnp.bfloat16)
    backB = [madeB[0]] + [exchange(madeB[r], "ctx", r) for r in range(1, PLANE)]
    return assemble(places, [backA, backB])


def body(q, k, v, residue, rate, skip, w_out):
    rows, chan = q.shape
    modes = rate.shape[0]
    groups = chan // LANES
    count, cores = lax.axis_size("ctx"), lax.axis_size("ch")
    chunk, feats = w_out.shape
    split = (
        count == 4 * PLANE
        and cores == 2
        and chan == 8 * chunk
        and chunk % LANES == 0
        and feats % (6 * PLANE * LANES) == 0
    )
    skip = skip.reshape(groups, LANES)
    if split:
        return split_block(q, k, v, residue, rate, skip, w_out)
    ends = end_states(k, v, rate)
    enter = entering_states(ends, rate.reshape(modes, groups, LANES), rows)
    gated = gated_conv(q, k, v, rate, residue, skip, enter)
    gated = gated.transpose(1, 0, 2).reshape(rows, chan)
    full_gated = lax.all_gather(gated, "ch", axis=1, tiled=True)
    w_full = lax.all_gather(w_out, "ctx", axis=0, tiled=True)
    mixed = jnp.dot(full_gated, w_full, preferred_element_type=jnp.float32)
    return mixed.astype(jnp.bfloat16)


def solution(mesh):
    placed = (
        P("ctx", "ch"),
        P("ctx", "ch"),
        P("ctx", "ch"),
        P(None, "ch"),
        P(None, "ch"),
        P("ch"),
        P("ctx", "ch"),
    )
    return jax.shard_map(
        body, mesh=mesh, in_specs=placed, out_specs=P("ctx", "ch"), check_vma=False
    )
```

```python
import jax
import jax.numpy as jnp
from jax import lax
from jax.experimental import pallas as pl
from jax.experimental.pallas import tpu as pltpu
from jax.sharding import PartitionSpec as P

LANES = 128
RADIX = 4
PLANE = 4
VMEM_BYTES = 60 << 20


def spread_signal(k_ref, v_ref, sig_ref):
    rows, width = k_ref.shape
    groups = width // LANES
    for g in range(groups):
        cols = pl.ds(g * LANES, LANES)
        product = k_ref[:, cols].astype(jnp.float32) * v_ref[:, cols].astype(jnp.float32)
        sig_ref[pl.ds(g, rows, stride=groups), :] = product


def spread_modes(ref, out_ref):
    modes, width = ref.shape
    groups = width // LANES
    for g in range(groups):
        out_ref[pl.ds(g, modes, stride=groups), :] = ref[:, pl.ds(g * LANES, LANES)]


def ends_kernel(k_ref, v_ref, rate_ref, end_ref, sig_ref, mode_ref):
    rows, width = k_ref.shape
    modes, groups, _ = end_ref.shape
    spread_signal(k_ref, v_ref, sig_ref)
    spread_modes(rate_ref, mode_ref)
    decay = [jnp.exp(-mode_ref[pl.ds(m * groups, groups), :]) for m in range(modes)]

    def step(t, state):
        s = sig_ref[pl.ds(pl.multiple_of(t * groups, groups), groups), :]
        return tuple(d * h + s for d, h in zip(decay, state))

    zero = jnp.zeros((groups, LANES), jnp.float32)
    state = lax.fori_loop(0, rows, step, (zero,) * modes, unroll=8)
    for m in range(modes):
        end_ref[m] = state[m]


def conv_kernel(q_ref, k_ref, v_ref, rate_ref, residue_ref, skip_ref, enter_ref, out_ref, sig_ref, conv_ref, mode_ref, weight_ref):
    rows, width = k_ref.shape
    modes, groups, _ = enter_ref.shape
    spread_signal(k_ref, v_ref, sig_ref)
    spread_modes(rate_ref, mode_ref)
    spread_modes(residue_ref, weight_ref)
    rates = [mode_ref[pl.ds(m * groups, groups), :] for m in range(modes)]
    decay = [jnp.exp(-rate) for rate in rates]
    weight = [weight_ref[pl.ds(m * groups, groups), :] * jnp.sqrt(2.0 * rate) for m, rate in enumerate(rates)]
    skip = skip_ref[...]

    def step(t, state):
        at = pl.ds(pl.multiple_of(t * groups, groups), groups)
        s = sig_ref[at, :]
        state = tuple(d * h + s for d, h in zip(decay, state))
        terms = [c * h for c, h in zip(weight, state)] + [skip * s]
        while len(terms) > 1:
            terms = [sum(terms[i : i + 2]) for i in range(0, len(terms), 2)]
        conv_ref[at, :] = terms[0]
        return state

    lax.fori_loop(0, rows, step, tuple(enter_ref[m] for m in range(modes)), unroll=4)
    for g in range(groups):
        cols = pl.ds(g * LANES, LANES)
        conv = conv_ref[pl.ds(g, rows, stride=groups), :]
        out_ref[:, cols] = (q_ref[:, cols].astype(jnp.float32) * conv).astype(out_ref.dtype)


def block_specs(rows, modes, width):
    groups = width // LANES
    return (
        pl.BlockSpec((rows, width), lambda i: (0, i)),
        pl.BlockSpec((modes, width), lambda i: (0, i)),
        pl.BlockSpec((modes, groups, LANES), lambda i: (0, i, 0)),
        pl.BlockSpec((groups, LANES), lambda i: (i, 0)),
    )


def end_states(k, v, rate):
    rows, chan = k.shape
    modes = rate.shape[0]
    width = min(chan, 8 * LANES)
    wide, moded, state, _ = block_specs(rows, modes, width)
    return pl.pallas_call(
        ends_kernel,
        grid=(chan // width,),
        in_specs=[wide, wide, moded],
        out_specs=state,
        out_shape=jax.ShapeDtypeStruct((modes, chan // LANES, LANES), jnp.float32),
        scratch_shapes=[
            pltpu.VMEM((rows * width // LANES, LANES), jnp.float32),
            pltpu.VMEM((modes * width // LANES, LANES), jnp.float32),
        ],
        compiler_params=pltpu.CompilerParams(vmem_limit_bytes=VMEM_BYTES),
        cost_estimate=pl.CostEstimate(
            flops=2 * modes * rows * chan, bytes_accessed=4 * rows * chan, transcendentals=modes * chan
        ),
        name="end_states",
    )(k, v, rate)


def gated_conv(q, k, v, rate, residue, skip, enter):
    rows, chan = k.shape
    modes = rate.shape[0]
    width = min(chan, 8 * LANES)
    wide, moded, state, single = block_specs(rows, modes, width)
    spread = pltpu.VMEM((rows * width // LANES, LANES), jnp.float32)
    moded_spread = pltpu.VMEM((modes * width // LANES, LANES), jnp.float32)
    return pl.pallas_call(
        conv_kernel,
        grid=(chan // width,),
        in_specs=[wide, wide, wide, moded, moded, single, state],
        out_specs=pl.BlockSpec((None, rows, width), lambda i: (i, 0, 0)),
        out_shape=jax.ShapeDtypeStruct((chan // width, rows, width), jnp.bfloat16),
        scratch_shapes=[spread, spread, moded_spread, moded_spread],
        compiler_params=pltpu.CompilerParams(vmem_limit_bytes=VMEM_BYTES),
        cost_estimate=pl.CostEstimate(
            flops=4 * modes * rows * chan, bytes_accessed=8 * rows * chan, transcendentals=2 * modes * chan
        ),
        name="gated_conv",
    )(q, k, v, rate, residue, skip, enter)


def shift_ctx(x, by):
    count = lax.axis_size("ctx")
    return lax.ppermute(x, "ctx", [(i, i + by) for i in range(count - by)])


def exchange(x, axis, flip):
    count = lax.axis_size(axis)
    return lax.ppermute(x, axis, [(i, i ^ flip) for i in range(count)])


def tie(*values):
    return lax.optimization_barrier(values)


def entering_states(ends, rate, rows):
    count = lax.axis_size("ctx")
    total = jnp.zeros_like(ends)
    for k in range(1, min(RADIX, count - 1) + 1):
        total = total + jnp.exp(-rate * float(rows * (k - 1))) * shift_ctx(ends, k)
    stride = RADIX
    while stride < count:
        base = total
        for k in range(1, RADIX):
            if stride * k < count:
                total = total + jnp.exp(-rate * float(rows * stride * k)) * shift_ctx(base, stride * k)
        stride *= RADIX
    return total


def box(fn, *args):
    once = (lax.axis_index("ctx") >= 0).astype(jnp.int32)
    shapes = jax.eval_shape(fn, *args)
    empty = jax.tree.map(lambda a: jnp.zeros(a.shape, a.dtype), shapes)

    def run(step, _):
        return fn(*tie(step, *args)[1:])

    return lax.fori_loop(0, once, run, empty)


def product(flags, places, ours, theirs, blocks, accs, widths, out_dtype):
    _, rows, depth = ours[0].shape
    chunk = depth // PLANE
    cols = sum(widths)
    count = len(blocks)
    weights = [array for _, _, pieces in blocks for choices, *_ in pieces for array in choices]
    accs = accs or []

    def kernel(flag_ref, place_ref, *refs):
        our_refs, their_refs, refs = refs[:PLANE], refs[PLANE : 2 * PLANE], refs[2 * PLANE :]
        weight_refs, refs = list(refs[: len(weights)]), refs[len(weights) :]
        acc_refs, out_refs = refs[: len(accs)], refs[len(accs) : len(accs) + PLANE * len(widths)]
        gated_buf, weight_buf, acc_buf, gated_sems, weight_sems, acc_sem = refs[-6:]

        step = chunk // 2

        def target(b, at):
            start = pl.multiple_of(b * depth + place_ref[at // chunk] * chunk + at % chunk, step)
            return weight_buf.at[pl.ds(start, step), :]

        for b, (flag, pick, pieces) in enumerate(blocks):
            row = 0
            for choices, col in pieces:
                for c in range(len(choices)):
                    ref = weight_refs.pop(0)
                    for at in range(0, ref.shape[0], step):
                        source = ref.at[pl.ds(at, step), pl.ds(col, cols)]
                        copy = pltpu.make_async_copy(source, target(b, row + at), weight_sems.at[b])
                        if pick is None:
                            copy.start()
                        else:
                            pl.when(flag_ref[pick] == c)(copy.start)
                row += choices[0].shape[0]
            half = flag_ref[flag] & 1
            for r in range(PLANE):
                for c, refs_of in enumerate((our_refs, their_refs)):
                    target_rows = gated_buf.at[b, pl.ds(r * rows, rows), :]
                    copy = pltpu.make_async_copy(refs_of[r].at[half], target_rows, gated_sems.at[b])
                    pl.when(flag_ref[flag] // 2 == c)(copy.start)
        for at, acc_ref in enumerate(acc_refs):
            pltpu.make_async_copy(acc_ref, acc_buf.at[at], acc_sem).start()
        for b in range(count):
            block = weight_buf.at[pl.ds(b * depth, depth), :]
            pltpu.make_async_copy(block, block, weight_sems.at[b]).wait()
            pltpu.make_async_copy(gated_buf.at[b], gated_buf.at[b], gated_sems.at[b]).wait()
            if accs and not b:
                pltpu.make_async_copy(acc_buf, acc_buf, acc_sem).wait()
            first = 0
            for part, width in enumerate(widths):
                for col in range(0, width, 2 * LANES):
                    here = pl.ds(col, 2 * LANES)
                    made = jnp.dot(
                        gated_buf[b],
                        weight_buf[pl.ds(b * depth, depth), pl.ds(first + col, 2 * LANES)],
                        preferred_element_type=jnp.float32,
                    )
                    for r in range(PLANE):
                        at = part * PLANE + r
                        total = made[r * rows : (r + 1) * rows]
                        if b:
                            total = total + out_refs[at][:, here]
                        elif accs:
                            total = total + acc_buf[at, :, here]
                        out_refs[at][:, here] = total.astype(out_dtype)
                first += width

    smem = pl.BlockSpec(memory_space=pltpu.SMEM)
    vmem = pl.BlockSpec(memory_space=pltpu.VMEM)
    anywhere = pl.BlockSpec(memory_space=pl.ANY)
    made = pl.pallas_call(
        kernel,
        in_specs=[smem, smem] + [anywhere] * (2 * PLANE + len(weights) + len(accs)),
        out_specs=[vmem] * (PLANE * len(widths)),
        out_shape=[jax.ShapeDtypeStruct((rows, width), out_dtype) for width in widths for _ in range(PLANE)],
        scratch_shapes=[
            pltpu.VMEM((count, PLANE * rows, depth), jnp.bfloat16),
            pltpu.VMEM((count * depth, cols), jnp.bfloat16),
            pltpu.VMEM((len(accs), *accs[0].shape) if accs else (8, LANES), jnp.float32),
            pltpu.SemaphoreType.DMA((count,)),
            pltpu.SemaphoreType.DMA((count,)),
            pltpu.SemaphoreType.DMA,
        ],
        compiler_params=pltpu.CompilerParams(vmem_limit_bytes=VMEM_BYTES),
        cost_estimate=pl.CostEstimate(
            flops=2 * PLANE * rows * depth * count * cols,
            bytes_accessed=2 * count * depth * (PLANE * rows + cols),
            transcendentals=0,
        ),
        name="product",
    )(flags, places, *ours, *theirs, *weights, *accs)
    return [list(made[part * PLANE : (part + 1) * PLANE]) for part in range(len(widths))]


def assemble(places, parts):
    rows = parts[0][0].shape[0]
    widths = [part[0].shape[1] for part in parts]
    cols = sum(widths)
    flat = [piece for part in parts for piece in part]

    def kernel(place_ref, *refs):
        *piece_refs, out_ref, sems = refs
        copies = []
        first = 0
        for part, width in enumerate(widths):
            for r in range(PLANE):
                at = part * PLANE + r
                start = pl.multiple_of(place_ref[r] * cols + first, LANES)
                target = out_ref.at[:, pl.ds(start, width)]
                copies.append(pltpu.make_async_copy(piece_refs[at], target, sems.at[at]))
                copies[-1].start()
            first += width
        for copy in copies:
            copy.wait()

    return pl.pallas_call(
        kernel,
        in_specs=[pl.BlockSpec(memory_space=pltpu.SMEM)] + [pl.BlockSpec(memory_space=pltpu.VMEM)] * len(flat),
        out_specs=pl.BlockSpec(memory_space=pl.ANY),
        out_shape=jax.ShapeDtypeStruct((rows, cols * PLANE), flat[0].dtype),
        scratch_shapes=[pltpu.SemaphoreType.DMA((len(flat),))],
        compiler_params=pltpu.CompilerParams(vmem_limit_bytes=16 << 20),
        name="assemble",
    )(places, *flat)


def split_block(q, k, v, residue, rate, skip, w_out):
    rows, chan = q.shape
    modes = rate.shape[0]
    me = lax.axis_index("ctx")
    core = lax.axis_index("ch")
    spot, plane = me & (PLANE - 1), me // PLANE
    count = lax.axis_size("ctx")
    chunk, feats = w_out.shape
    cols = feats // PLANE
    speed = rate.reshape(modes, chan // LANES, LANES)

    def far(x):
        return exchange(x, "ctx", 2 * PLANE)

    def near(x):
        return exchange(x, "ctx", PLANE)

    middle = [i for i in range(count) if PLANE <= i < 3 * PLANE]

    def across(x):
        return lax.ppermute(x, "ctx", [(i, i ^ (3 * PLANE)) for i in middle])

    def outward(x):
        return lax.ppermute(x, "ctx", [(i, i ^ PLANE) for i in middle])

    def group(x, r):
        return lax.dynamic_slice_in_dim(x, (spot ^ r) * cols, cols, axis=1)

    def plane_scan(k, v, rate, speed):
        def fade(span):
            return jnp.exp(-speed * span)

        ends = end_states(k, v, rate)
        other = exchange(ends, "ctx", 1)
        both = jnp.where(x_later, fade(float(rows)) * other + ends, fade(float(rows)) * ends + other)
        before = jnp.where(x_later, other, 0.0)
        other = exchange(both, "ctx", 2)
        before = before + jnp.where(y_later, fade((spot & 1).astype(jnp.float32) * rows) * other, 0.0)
        both = jnp.where(y_later, fade(2.0 * rows) * other + both, fade(2.0 * rows) * both + other)
        return jnp.stack([both, before])

    x_later, y_later = (spot & 1) != 0, (spot & 2) != 0
    w0, w_out = tie(group(w_out, 0), w_out)
    f0, n0 = far(w0), near(w0)
    scanned = box(plane_scan, k, v, rate, speed)
    f0, n0, w0, scanned, w_out = tie(f0, n0, w0, scanned, w_out)

    arrived = [exchange(group(w_out, r), "ctx", r) for r in range(1, PLANE)]
    both, before = scanned[0], scanned[1]
    decay = jnp.exp(-speed * float(PLANE * rows))
    last = shift_ctx(both, PLANE)
    line = last + decay * shift_ctx(both + decay * last, 2 * PLANE)
    enter = before + jnp.exp(-speed * (spot * rows).astype(jnp.float32)) * line
    gated = gated_conv(q, k, v, rate, residue, skip, enter)
    rest = jnp.concatenate(arrived)
    gated, rest = tie(gated, rest)

    fr, nr = far(rest), near(rest)
    ours = [gated] + [exchange(gated, "ctx", r) for r in range(1, PLANE)]
    fr, nr, f0, w0, rest, *ours = tie(fr, nr, f0, w0, rest, *ours)

    out0, mid0 = outward(f0), across(w0)
    theirs = [exchange(x, "ch", 1) for x in ours[1:]]
    out0, mid0, fr, rest, *held = tie(out0, mid0, fr, rest, *ours, *theirs)
    ours, theirs = held[:PLANE], held[PLANE:]

    def source_of(b):
        return jnp.where(b // 2 == core, b & 1, 2 + (b & 1))

    is_middle = jnp.where((plane == 0) | (plane == 3), 0, 1)
    flags = jnp.stack([source_of(plane ^ r) for r in range(4)] + [is_middle]).astype(jnp.int32)
    places = jnp.stack([spot ^ r for r in range(PLANE)]).astype(jnp.int32)

    out1, mid1 = outward(fr), across(rest)
    theirs = [exchange(ours[0], "ch", 1)] + theirs
    blocks = [
        (0, None, [((w0,), 0), ((rest,), 0)]),
        (1, None, [((n0,), 0), ((nr,), 0)]),
        (2, None, [((f0,), 0), ((fr,), 0)]),
    ]
    (accs,) = product(flags, places, ours, theirs, blocks, None, [cols], jnp.float32)
    out1, mid1, *accs = tie(out1, mid1, *accs)

    blocks = [(3, 4, [((out0, mid0), 0), ((out1, mid1), 0)])]
    (made,) = product(flags, places, ours, theirs, blocks, accs, [cols], jnp.bfloat16)
    back = [made[0]] + [exchange(made[r], "ctx", r) for r in range(1, PLANE)]
    return assemble(places, [back])


def body(q, k, v, residue, rate, skip, w_out):
    rows, chan = q.shape
    modes = rate.shape[0]
    groups = chan // LANES
    count, cores = lax.axis_size("ctx"), lax.axis_size("ch")
    chunk, feats = w_out.shape
    split = (
        count == 4 * PLANE
        and cores == 2
        and chan == 8 * chunk
        and chunk % LANES == 0
        and feats % (2 * PLANE * LANES) == 0
    )
    skip = skip.reshape(groups, LANES)
    if split:
        return split_block(q, k, v, residue, rate, skip, w_out)
    ends = end_states(k, v, rate)
    enter = entering_states(ends, rate.reshape(modes, groups, LANES), rows)
    gated = gated_conv(q, k, v, rate, residue, skip, enter)
    gated = gated.transpose(1, 0, 2).reshape(rows, chan)
    full_gated = lax.all_gather(gated, "ch", axis=1, tiled=True)
    w_full = lax.all_gather(w_out, "ctx", axis=0, tiled=True)
    mixed = jnp.dot(full_gated, w_full, preferred_element_type=jnp.float32)
    return mixed.astype(jnp.bfloat16)


def solution(mesh):
    placed = (
        P("ctx", "ch"),
        P("ctx", "ch"),
        P("ctx", "ch"),
        P(None, "ch"),
        P(None, "ch"),
        P("ch"),
        P("ctx", "ch"),
    )
    return jax.shard_map(
        body, mesh=mesh, in_specs=placed, out_specs=P("ctx", "ch"), check_vma=False
    )
```

```python
import jax
import jax.numpy as jnp
from jax import lax
from jax.experimental import pallas as pl
from jax.experimental.pallas import tpu as pltpu
from jax.sharding import PartitionSpec as P

LANES = 128
RADIX = 4
PLANE = 4
VMEM_BYTES = 60 << 20


def spread_signal(k_ref, v_ref, sig_ref):
    rows, width = k_ref.shape
    groups = width // LANES
    for g in range(groups):
        cols = pl.ds(g * LANES, LANES)
        product = k_ref[:, cols].astype(jnp.float32) * v_ref[:, cols].astype(jnp.float32)
        sig_ref[pl.ds(g, rows, stride=groups), :] = product


def spread_modes(ref, out_ref):
    modes, width = ref.shape
    groups = width // LANES
    for g in range(groups):
        out_ref[pl.ds(g, modes, stride=groups), :] = ref[:, pl.ds(g * LANES, LANES)]


def ends_kernel(k_ref, v_ref, rate_ref, end_ref, sig_ref, mode_ref):
    rows, width = k_ref.shape
    modes, groups, _ = end_ref.shape
    spread_signal(k_ref, v_ref, sig_ref)
    spread_modes(rate_ref, mode_ref)
    decay = [jnp.exp(-mode_ref[pl.ds(m * groups, groups), :]) for m in range(modes)]

    def step(t, state):
        s = sig_ref[pl.ds(pl.multiple_of(t * groups, groups), groups), :]
        return tuple(d * h + s for d, h in zip(decay, state))

    zero = jnp.zeros((groups, LANES), jnp.float32)
    state = lax.fori_loop(0, rows, step, (zero,) * modes, unroll=8)
    for m in range(modes):
        end_ref[m] = state[m]


def conv_kernel(q_ref, k_ref, v_ref, rate_ref, residue_ref, skip_ref, enter_ref, out_ref, sig_ref, conv_ref, mode_ref, weight_ref):
    rows, width = k_ref.shape
    modes, groups, _ = enter_ref.shape
    spread_signal(k_ref, v_ref, sig_ref)
    spread_modes(rate_ref, mode_ref)
    spread_modes(residue_ref, weight_ref)
    rates = [mode_ref[pl.ds(m * groups, groups), :] for m in range(modes)]
    decay = [jnp.exp(-rate) for rate in rates]
    weight = [weight_ref[pl.ds(m * groups, groups), :] * jnp.sqrt(2.0 * rate) for m, rate in enumerate(rates)]
    skip = skip_ref[...]

    def step(t, state):
        at = pl.ds(pl.multiple_of(t * groups, groups), groups)
        s = sig_ref[at, :]
        state = tuple(d * h + s for d, h in zip(decay, state))
        terms = [c * h for c, h in zip(weight, state)] + [skip * s]
        while len(terms) > 1:
            terms = [sum(terms[i : i + 2]) for i in range(0, len(terms), 2)]
        conv_ref[at, :] = terms[0]
        return state

    lax.fori_loop(0, rows, step, tuple(enter_ref[m] for m in range(modes)), unroll=4)
    for g in range(groups):
        cols = pl.ds(g * LANES, LANES)
        conv = conv_ref[pl.ds(g, rows, stride=groups), :]
        out_ref[:, cols] = (q_ref[:, cols].astype(jnp.float32) * conv).astype(out_ref.dtype)


def block_specs(rows, modes, width):
    groups = width // LANES
    return (
        pl.BlockSpec((rows, width), lambda i: (0, i)),
        pl.BlockSpec((modes, width), lambda i: (0, i)),
        pl.BlockSpec((modes, groups, LANES), lambda i: (0, i, 0)),
        pl.BlockSpec((groups, LANES), lambda i: (i, 0)),
    )


def end_states(k, v, rate):
    rows, chan = k.shape
    modes = rate.shape[0]
    width = min(chan, 8 * LANES)
    wide, moded, state, _ = block_specs(rows, modes, width)
    return pl.pallas_call(
        ends_kernel,
        grid=(chan // width,),
        in_specs=[wide, wide, moded],
        out_specs=state,
        out_shape=jax.ShapeDtypeStruct((modes, chan // LANES, LANES), jnp.float32),
        scratch_shapes=[
            pltpu.VMEM((rows * width // LANES, LANES), jnp.float32),
            pltpu.VMEM((modes * width // LANES, LANES), jnp.float32),
        ],
        compiler_params=pltpu.CompilerParams(vmem_limit_bytes=VMEM_BYTES),
        cost_estimate=pl.CostEstimate(
            flops=2 * modes * rows * chan, bytes_accessed=4 * rows * chan, transcendentals=modes * chan
        ),
        name="end_states",
    )(k, v, rate)


def gated_conv(q, k, v, rate, residue, skip, enter):
    rows, chan = k.shape
    modes = rate.shape[0]
    width = min(chan, 8 * LANES)
    wide, moded, state, single = block_specs(rows, modes, width)
    spread = pltpu.VMEM((rows * width // LANES, LANES), jnp.float32)
    moded_spread = pltpu.VMEM((modes * width // LANES, LANES), jnp.float32)
    return pl.pallas_call(
        conv_kernel,
        grid=(chan // width,),
        in_specs=[wide, wide, wide, moded, moded, single, state],
        out_specs=pl.BlockSpec((None, rows, width), lambda i: (i, 0, 0)),
        out_shape=jax.ShapeDtypeStruct((chan // width, rows, width), jnp.bfloat16),
        scratch_shapes=[spread, spread, moded_spread, moded_spread],
        compiler_params=pltpu.CompilerParams(vmem_limit_bytes=VMEM_BYTES),
        cost_estimate=pl.CostEstimate(
            flops=4 * modes * rows * chan, bytes_accessed=8 * rows * chan, transcendentals=2 * modes * chan
        ),
        name="gated_conv",
    )(q, k, v, rate, residue, skip, enter)


def shift_ctx(x, by):
    count = lax.axis_size("ctx")
    return lax.ppermute(x, "ctx", [(i, i + by) for i in range(count - by)])


def exchange(x, axis, flip):
    count = lax.axis_size(axis)
    return lax.ppermute(x, axis, [(i, i ^ flip) for i in range(count)])


def tie(*values):
    return lax.optimization_barrier(values)


def entering_states(ends, rate, rows):
    count = lax.axis_size("ctx")
    total = jnp.zeros_like(ends)
    for k in range(1, min(RADIX, count - 1) + 1):
        total = total + jnp.exp(-rate * float(rows * (k - 1))) * shift_ctx(ends, k)
    stride = RADIX
    while stride < count:
        base = total
        for k in range(1, RADIX):
            if stride * k < count:
                total = total + jnp.exp(-rate * float(rows * stride * k)) * shift_ctx(base, stride * k)
        stride *= RADIX
    return total


def box(fn, *args):
    once = (lax.axis_index("ctx") >= 0).astype(jnp.int32)
    shapes = jax.eval_shape(fn, *args)
    empty = jax.tree.map(lambda a: jnp.zeros(a.shape, a.dtype), shapes)

    def run(step, _):
        return fn(*tie(step, *args)[1:])

    return lax.fori_loop(0, once, run, empty)


def product(flags, places, ours, theirs, blocks, accs, out_dtype):
    _, rows, depth = ours[0].shape
    chunk = depth // PLANE
    cols = blocks[0][2][0][0][0].shape[1]
    count, parts = len(blocks), len(ours)
    weights = [array for _, _, pieces in blocks for choices, _ in pieces for array in choices]
    accs = accs or []

    def kernel(flag_ref, place_ref, *refs):
        our_refs, their_refs, refs = refs[:parts], refs[parts : 2 * parts], refs[2 * parts :]
        weight_refs, refs = list(refs[: len(weights)]), refs[len(weights) :]
        acc_refs, out_refs = refs[: len(accs)], refs[len(accs) : len(accs) + parts]
        gated_buf, weight_buf, acc_buf, gated_sems, weight_sems, acc_sem = refs[-6:]

        def target(b, at):
            start = pl.multiple_of(b * depth + place_ref[at // chunk] * chunk, chunk)
            return weight_buf.at[pl.ds(start, chunk), :]

        for b, (flag, pick, pieces) in enumerate(blocks):
            row = 0
            for choices, col in pieces:
                for c in range(len(choices)):
                    ref = weight_refs.pop(0)
                    for at in range(0, ref.shape[0], chunk):
                        source = ref.at[pl.ds(at, chunk), pl.ds(col, cols)]
                        copy = pltpu.make_async_copy(source, target(b, row + at), weight_sems.at[b])
                        if pick is None:
                            copy.start()
                        else:
                            pl.when(flag_ref[pick] == c)(copy.start)
                row += choices[0].shape[0]
            half = flag_ref[flag] & 1
            for r in range(parts):
                for c, refs_of in enumerate((our_refs, their_refs)):
                    target_rows = gated_buf.at[b, pl.ds(r * rows, rows), :]
                    copy = pltpu.make_async_copy(refs_of[r].at[half], target_rows, gated_sems.at[b])
                    pl.when(flag_ref[flag] // 2 == c)(copy.start)
        for r, acc_ref in enumerate(acc_refs):
            pltpu.make_async_copy(acc_ref, acc_buf.at[r], acc_sem).start()
        for b in range(count):
            block = weight_buf.at[pl.ds(b * depth, depth), :]
            pltpu.make_async_copy(block, block, weight_sems.at[b]).wait()
            pltpu.make_async_copy(gated_buf.at[b], gated_buf.at[b], gated_sems.at[b]).wait()
            if accs and not b:
                pltpu.make_async_copy(acc_buf, acc_buf, acc_sem).wait()
            for col in range(0, cols, 2 * LANES):
                here = pl.ds(col, 2 * LANES)
                made = jnp.dot(
                    gated_buf[b], weight_buf[pl.ds(b * depth, depth), here], preferred_element_type=jnp.float32
                )
                for r in range(parts):
                    total = made[r * rows : (r + 1) * rows]
                    if b:
                        total = total + out_refs[r][:, here]
                    elif accs:
                        total = total + acc_buf[r, :, here]
                    out_refs[r][:, here] = total.astype(out_dtype)

    smem = pl.BlockSpec(memory_space=pltpu.SMEM)
    anywhere = pl.BlockSpec(memory_space=pl.ANY)
    return pl.pallas_call(
        kernel,
        in_specs=[smem, smem] + [anywhere] * (2 * parts + len(weights) + len(accs)),
        out_specs=[pl.BlockSpec(memory_space=pltpu.VMEM)] * parts,
        out_shape=[jax.ShapeDtypeStruct((rows, cols), out_dtype)] * parts,
        scratch_shapes=[
            pltpu.VMEM((count, parts * rows, depth), jnp.bfloat16),
            pltpu.VMEM((count * depth, cols), jnp.bfloat16),
            pltpu.VMEM((len(accs), *accs[0].shape) if accs else (8, LANES), jnp.float32),
            pltpu.SemaphoreType.DMA((count,)),
            pltpu.SemaphoreType.DMA((count,)),
            pltpu.SemaphoreType.DMA,
        ],
        compiler_params=pltpu.CompilerParams(vmem_limit_bytes=VMEM_BYTES),
        cost_estimate=pl.CostEstimate(
            flops=2 * parts * rows * depth * count * cols,
            bytes_accessed=2 * count * depth * (parts * rows + cols),
            transcendentals=0,
        ),
        name="product",
    )(flags, places, *ours, *theirs, *weights, *accs)


def assemble(places, pieces):
    rows, cols = pieces[0].shape

    def kernel(place_ref, *refs):
        *piece_refs, out_ref, sems = refs
        copies = []
        for r, piece_ref in enumerate(piece_refs):
            target = out_ref.at[:, pl.ds(pl.multiple_of(place_ref[r] * cols, cols), cols)]
            copies.append(pltpu.make_async_copy(piece_ref, target, sems.at[r]))
            copies[-1].start()
        for copy in copies:
            copy.wait()

    return pl.pallas_call(
        kernel,
        in_specs=[pl.BlockSpec(memory_space=pltpu.SMEM)] + [pl.BlockSpec(memory_space=pltpu.VMEM)] * len(pieces),
        out_specs=pl.BlockSpec(memory_space=pl.ANY),
        out_shape=jax.ShapeDtypeStruct((rows, cols * PLANE), pieces[0].dtype),
        scratch_shapes=[pltpu.SemaphoreType.DMA((len(pieces),))],
        compiler_params=pltpu.CompilerParams(vmem_limit_bytes=16 << 20),
        name="assemble",
    )(places, *pieces)


def split_block(q, k, v, residue, rate, skip, w_out):
    rows, chan = q.shape
    modes = rate.shape[0]
    me = lax.axis_index("ctx")
    core = lax.axis_index("ch")
    spot, plane = me & (PLANE - 1), me // PLANE
    count = lax.axis_size("ctx")
    chunk, feats = w_out.shape
    cols = feats // PLANE
    speed = rate.reshape(modes, chan // LANES, LANES)

    def far(x):
        return exchange(x, "ctx", 2 * PLANE)

    def near(x):
        return exchange(x, "ctx", PLANE)

    middle = [i for i in range(count) if PLANE <= i < 3 * PLANE]

    def across(x):
        return lax.ppermute(x, "ctx", [(i, i ^ (3 * PLANE)) for i in middle])

    def outward(x):
        return lax.ppermute(x, "ctx", [(i, i ^ PLANE) for i in middle])

    def group(x, r):
        return lax.dynamic_slice_in_dim(x, (spot ^ r) * cols, cols, axis=1)

    def plane_scan(k, v, rate, speed):
        def fade(span):
            return jnp.exp(-speed * span)

        ends = end_states(k, v, rate)
        other = exchange(ends, "ctx", 1)
        both = jnp.where(x_later, fade(float(rows)) * other + ends, fade(float(rows)) * ends + other)
        before = jnp.where(x_later, other, 0.0)
        other = exchange(both, "ctx", 2)
        before = before + jnp.where(y_later, fade((spot & 1).astype(jnp.float32) * rows) * other, 0.0)
        both = jnp.where(y_later, fade(2.0 * rows) * other + both, fade(2.0 * rows) * both + other)
        return jnp.stack([both, before])

    x_later, y_later = (spot & 1) != 0, (spot & 2) != 0
    w0, w_out = tie(group(w_out, 0), w_out)
    f0, n0 = far(w0), near(w0)
    scanned = box(plane_scan, k, v, rate, speed)
    f0, n0, w0, scanned, w_out = tie(f0, n0, w0, scanned, w_out)

    arrived = [exchange(group(w_out, r), "ctx", r) for r in range(1, PLANE)]
    both, before = scanned[0], scanned[1]
    decay = jnp.exp(-speed * float(PLANE * rows))
    last = shift_ctx(both, PLANE)
    line = last + decay * shift_ctx(both + decay * last, 2 * PLANE)
    enter = before + jnp.exp(-speed * (spot * rows).astype(jnp.float32)) * line
    f0, w0, enter = tie(f0, w0, enter)
    out0, mid0 = outward(f0), across(w0)
    gated = gated_conv(q, k, v, rate, residue, skip, enter)
    rest = jnp.concatenate(arrived)
    gated, rest, out0, mid0 = tie(gated, rest, out0, mid0)

    fr, nr = far(rest), near(rest)
    ours = [gated] + [exchange(gated, "ctx", r) for r in range(1, PLANE)]
    fr, nr, rest, *ours = tie(fr, nr, rest, *ours)

    def source_of(b):
        return jnp.where(b // 2 == core, b & 1, 2 + (b & 1))

    is_middle = jnp.where((plane == 0) | (plane == 3), 0, 1)
    flags = jnp.stack([source_of(plane ^ r) for r in range(4)] + [is_middle]).astype(jnp.int32)
    places = jnp.stack([spot ^ r for r in range(PLANE)]).astype(jnp.int32)

    out1, mid1 = outward(fr), across(rest)
    theirs = [exchange(x, "ch", 1) for x in ours]
    blocks = [
        (0, None, [((w0,), 0), ((rest,), 0)]),
        (1, None, [((n0,), 0), ((nr,), 0)]),
        (2, None, [((f0,), 0), ((fr,), 0)]),
    ]
    accs = product(flags, places, ours, theirs, blocks, None, jnp.float32)
    out1, mid1, *accs = tie(out1, mid1, *accs)

    blocks = [(3, 4, [((out0, mid0), 0), ((out1, mid1), 0)])]

    def finish(*spots):
        chosen = [ours[r] for r in spots], [theirs[r] for r in spots]
        return product(flags, places, *chosen, blocks, [accs[r] for r in spots], jnp.bfloat16)

    (made3,) = finish(3)
    back3 = exchange(made3, "ctx", 3)
    back3, made0, made1, made2 = tie(back3, *finish(0, 1, 2))
    return assemble(places, [made0, exchange(made1, "ctx", 1), exchange(made2, "ctx", 2), back3])


def body(q, k, v, residue, rate, skip, w_out):
    rows, chan = q.shape
    modes = rate.shape[0]
    groups = chan // LANES
    count, cores = lax.axis_size("ctx"), lax.axis_size("ch")
    chunk, feats = w_out.shape
    split = (
        count == 4 * PLANE
        and cores == 2
        and chan == 8 * chunk
        and chunk % LANES == 0
        and feats % (2 * PLANE * LANES) == 0
    )
    skip = skip.reshape(groups, LANES)
    if split:
        return split_block(q, k, v, residue, rate, skip, w_out)
    ends = end_states(k, v, rate)
    enter = entering_states(ends, rate.reshape(modes, groups, LANES), rows)
    gated = gated_conv(q, k, v, rate, residue, skip, enter)
    gated = gated.transpose(1, 0, 2).reshape(rows, chan)
    full_gated = lax.all_gather(gated, "ch", axis=1, tiled=True)
    w_full = lax.all_gather(w_out, "ctx", axis=0, tiled=True)
    mixed = jnp.dot(full_gated, w_full, preferred_element_type=jnp.float32)
    return mixed.astype(jnp.bfloat16)


def solution(mesh):
    placed = (
        P("ctx", "ch"),
        P("ctx", "ch"),
        P("ctx", "ch"),
        P(None, "ch"),
        P(None, "ch"),
        P("ch"),
        P("ctx", "ch"),
    )
    return jax.shard_map(
        body, mesh=mesh, in_specs=placed, out_specs=P("ctx", "ch"), check_vma=False
    )
```

```python
import jax
import jax.numpy as jnp
from jax import lax
from jax.experimental import pallas as pl
from jax.experimental.pallas import tpu as pltpu
from jax.sharding import PartitionSpec as P

LANES = 128
RADIX = 4
PLANE = 4
VMEM_BYTES = 60 << 20


def spread_signal(k_ref, v_ref, sig_ref):
    rows, width = k_ref.shape
    groups = width // LANES
    for g in range(groups):
        cols = pl.ds(g * LANES, LANES)
        product = k_ref[:, cols].astype(jnp.float32) * v_ref[:, cols].astype(jnp.float32)
        sig_ref[pl.ds(g, rows, stride=groups), :] = product


def spread_modes(ref, out_ref):
    modes, width = ref.shape
    groups = width // LANES
    for g in range(groups):
        out_ref[pl.ds(g, modes, stride=groups), :] = ref[:, pl.ds(g * LANES, LANES)]


def ends_kernel(k_ref, v_ref, rate_ref, end_ref, sig_ref, mode_ref):
    rows, width = k_ref.shape
    modes, groups, _ = end_ref.shape
    spread_signal(k_ref, v_ref, sig_ref)
    spread_modes(rate_ref, mode_ref)
    decay = [jnp.exp(-mode_ref[pl.ds(m * groups, groups), :]) for m in range(modes)]

    def step(t, state):
        s = sig_ref[pl.ds(pl.multiple_of(t * groups, groups), groups), :]
        return tuple(d * h + s for d, h in zip(decay, state))

    zero = jnp.zeros((groups, LANES), jnp.float32)
    state = lax.fori_loop(0, rows, step, (zero,) * modes, unroll=8)
    for m in range(modes):
        end_ref[m] = state[m]


def conv_kernel(q_ref, k_ref, v_ref, rate_ref, residue_ref, skip_ref, enter_ref, out_ref, sig_ref, conv_ref, mode_ref, weight_ref):
    rows, width = k_ref.shape
    modes, groups, _ = enter_ref.shape
    spread_signal(k_ref, v_ref, sig_ref)
    spread_modes(rate_ref, mode_ref)
    spread_modes(residue_ref, weight_ref)
    rates = [mode_ref[pl.ds(m * groups, groups), :] for m in range(modes)]
    decay = [jnp.exp(-rate) for rate in rates]
    weight = [weight_ref[pl.ds(m * groups, groups), :] * jnp.sqrt(2.0 * rate) for m, rate in enumerate(rates)]
    skip = skip_ref[...]

    def step(t, state):
        at = pl.ds(pl.multiple_of(t * groups, groups), groups)
        s = sig_ref[at, :]
        state = tuple(d * h + s for d, h in zip(decay, state))
        terms = [c * h for c, h in zip(weight, state)] + [skip * s]
        while len(terms) > 1:
            terms = [sum(terms[i : i + 2]) for i in range(0, len(terms), 2)]
        conv_ref[at, :] = terms[0]
        return state

    lax.fori_loop(0, rows, step, tuple(enter_ref[m] for m in range(modes)), unroll=4)
    for g in range(groups):
        cols = pl.ds(g * LANES, LANES)
        conv = conv_ref[pl.ds(g, rows, stride=groups), :]
        out_ref[:, cols] = (q_ref[:, cols].astype(jnp.float32) * conv).astype(out_ref.dtype)


def block_specs(rows, modes, width):
    groups = width // LANES
    return (
        pl.BlockSpec((rows, width), lambda i: (0, i)),
        pl.BlockSpec((modes, width), lambda i: (0, i)),
        pl.BlockSpec((modes, groups, LANES), lambda i: (0, i, 0)),
        pl.BlockSpec((groups, LANES), lambda i: (i, 0)),
    )


def end_states(k, v, rate):
    rows, chan = k.shape
    modes = rate.shape[0]
    width = min(chan, 8 * LANES)
    wide, moded, state, _ = block_specs(rows, modes, width)
    return pl.pallas_call(
        ends_kernel,
        grid=(chan // width,),
        in_specs=[wide, wide, moded],
        out_specs=state,
        out_shape=jax.ShapeDtypeStruct((modes, chan // LANES, LANES), jnp.float32),
        scratch_shapes=[
            pltpu.VMEM((rows * width // LANES, LANES), jnp.float32),
            pltpu.VMEM((modes * width // LANES, LANES), jnp.float32),
        ],
        compiler_params=pltpu.CompilerParams(vmem_limit_bytes=VMEM_BYTES),
        cost_estimate=pl.CostEstimate(
            flops=2 * modes * rows * chan, bytes_accessed=4 * rows * chan, transcendentals=modes * chan
        ),
        name="end_states",
    )(k, v, rate)


def gated_conv(q, k, v, rate, residue, skip, enter):
    rows, chan = k.shape
    modes = rate.shape[0]
    width = min(chan, 8 * LANES)
    wide, moded, state, single = block_specs(rows, modes, width)
    spread = pltpu.VMEM((rows * width // LANES, LANES), jnp.float32)
    moded_spread = pltpu.VMEM((modes * width // LANES, LANES), jnp.float32)
    return pl.pallas_call(
        conv_kernel,
        grid=(chan // width,),
        in_specs=[wide, wide, wide, moded, moded, single, state],
        out_specs=pl.BlockSpec((None, rows, width), lambda i: (i, 0, 0)),
        out_shape=jax.ShapeDtypeStruct((chan // width, rows, width), jnp.bfloat16),
        scratch_shapes=[spread, spread, moded_spread, moded_spread],
        compiler_params=pltpu.CompilerParams(vmem_limit_bytes=VMEM_BYTES),
        cost_estimate=pl.CostEstimate(
            flops=4 * modes * rows * chan, bytes_accessed=8 * rows * chan, transcendentals=2 * modes * chan
        ),
        name="gated_conv",
    )(q, k, v, rate, residue, skip, enter)


def shift_ctx(x, by):
    count = lax.axis_size("ctx")
    return lax.ppermute(x, "ctx", [(i, i + by) for i in range(count - by)])


def exchange(x, axis, flip):
    count = lax.axis_size(axis)
    return lax.ppermute(x, axis, [(i, i ^ flip) for i in range(count)])


def tie(*values):
    return lax.optimization_barrier(values)


def entering_states(ends, rate, rows):
    count = lax.axis_size("ctx")
    total = jnp.zeros_like(ends)
    for k in range(1, min(RADIX, count - 1) + 1):
        total = total + jnp.exp(-rate * float(rows * (k - 1))) * shift_ctx(ends, k)
    stride = RADIX
    while stride < count:
        base = total
        for k in range(1, RADIX):
            if stride * k < count:
                total = total + jnp.exp(-rate * float(rows * stride * k)) * shift_ctx(base, stride * k)
        stride *= RADIX
    return total


def box(fn, *args):
    once = (lax.axis_index("ctx") >= 0).astype(jnp.int32)
    shapes = jax.eval_shape(fn, *args)
    empty = jax.tree.map(lambda a: jnp.zeros(a.shape, a.dtype), shapes)

    def run(step, _):
        return fn(*tie(step, *args)[1:])

    return lax.fori_loop(0, once, run, empty)


def product(flags, places, ours, theirs, blocks, accs, widths, out_dtype):
    _, rows, depth = ours[0].shape
    chunk = depth // PLANE
    cols = sum(widths)
    count, parts = len(blocks), len(ours)
    outs = parts * len(widths)
    weights = [array for _, _, pieces in blocks for choices, _ in pieces for array in choices]
    accs = accs or []

    def kernel(flag_ref, place_ref, *refs):
        our_refs, their_refs, refs = refs[:parts], refs[parts : 2 * parts], refs[2 * parts :]
        weight_refs, refs = list(refs[: len(weights)]), refs[len(weights) :]
        acc_refs, out_refs = refs[: len(accs)], refs[len(accs) : len(accs) + outs]
        gated_buf, weight_buf, acc_buf, gated_sems, weight_sems, acc_sem = refs[-6:]

        def target(b, at):
            start = pl.multiple_of(b * depth + place_ref[at // chunk] * chunk, chunk)
            return weight_buf.at[pl.ds(start, chunk), :]

        for b, (flag, pick, pieces) in enumerate(blocks):
            row = 0
            for choices, col in pieces:
                for c in range(len(choices)):
                    ref = weight_refs.pop(0)
                    for at in range(0, ref.shape[0], chunk):
                        source = ref.at[pl.ds(at, chunk), pl.ds(col, cols)]
                        copy = pltpu.make_async_copy(source, target(b, row + at), weight_sems.at[b])
                        if pick is None:
                            copy.start()
                        else:
                            pl.when(flag_ref[pick] == c)(copy.start)
                row += choices[0].shape[0]
            half = flag_ref[flag] & 1
            for r in range(parts):
                for c, refs_of in enumerate((our_refs, their_refs)):
                    target_rows = gated_buf.at[b, pl.ds(r * rows, rows), :]
                    copy = pltpu.make_async_copy(refs_of[r].at[half], target_rows, gated_sems.at[b])
                    pl.when(flag_ref[flag] // 2 == c)(copy.start)
        for r, acc_ref in enumerate(acc_refs):
            pltpu.make_async_copy(acc_ref, acc_buf.at[r], acc_sem).start()
        for b in range(count):
            block = weight_buf.at[pl.ds(b * depth, depth), :]
            pltpu.make_async_copy(block, block, weight_sems.at[b]).wait()
            pltpu.make_async_copy(gated_buf.at[b], gated_buf.at[b], gated_sems.at[b]).wait()
            if accs and not b:
                pltpu.make_async_copy(acc_buf, acc_buf, acc_sem).wait()
            for col in range(0, cols, 2 * LANES):
                here = pl.ds(col, 2 * LANES)
                made = jnp.dot(
                    gated_buf[b], weight_buf[pl.ds(b * depth, depth), here], preferred_element_type=jnp.float32
                )
                part = 0 if col < widths[0] else 1
                inside = pl.ds(col - part * widths[0], 2 * LANES)
                for r in range(parts):
                    total = made[r * rows : (r + 1) * rows]
                    out_ref = out_refs[part * parts + r]
                    if b:
                        total = total + out_ref[:, inside]
                    elif accs:
                        total = total + acc_buf[r, :, here]
                    out_ref[:, inside] = total.astype(out_dtype)

    smem = pl.BlockSpec(memory_space=pltpu.SMEM)
    anywhere = pl.BlockSpec(memory_space=pl.ANY)
    made = pl.pallas_call(
        kernel,
        in_specs=[smem, smem] + [anywhere] * (2 * parts + len(weights) + len(accs)),
        out_specs=[pl.BlockSpec(memory_space=pltpu.VMEM)] * outs,
        out_shape=[jax.ShapeDtypeStruct((rows, width), out_dtype) for width in widths for _ in range(parts)],
        scratch_shapes=[
            pltpu.VMEM((count, parts * rows, depth), jnp.bfloat16),
            pltpu.VMEM((count * depth, cols), jnp.bfloat16),
            pltpu.VMEM((len(accs), *accs[0].shape) if accs else (8, LANES), jnp.float32),
            pltpu.SemaphoreType.DMA((count,)),
            pltpu.SemaphoreType.DMA((count,)),
            pltpu.SemaphoreType.DMA,
        ],
        compiler_params=pltpu.CompilerParams(vmem_limit_bytes=VMEM_BYTES),
        cost_estimate=pl.CostEstimate(
            flops=2 * parts * rows * depth * count * cols,
            bytes_accessed=2 * count * depth * (parts * rows + cols),
            transcendentals=0,
        ),
        name="product",
    )(flags, places, *ours, *theirs, *weights, *accs)
    return [list(made[at : at + parts]) for at in range(0, outs, parts)]


def assemble(places, parts):
    rows = parts[0][0].shape[0]
    widths = [part[0].shape[1] for part in parts]
    cols = sum(widths)
    flat = [piece for part in parts for piece in part]

    def kernel(place_ref, *refs):
        *piece_refs, out_ref, sems = refs
        copies = []
        first = 0
        for part, width in enumerate(widths):
            for r in range(PLANE):
                at = part * PLANE + r
                start = pl.multiple_of(place_ref[r] * cols + first, LANES)
                target = out_ref.at[:, pl.ds(start, width)]
                copies.append(pltpu.make_async_copy(piece_refs[at], target, sems.at[at]))
                copies[-1].start()
            first += width
        for copy in copies:
            copy.wait()

    return pl.pallas_call(
        kernel,
        in_specs=[pl.BlockSpec(memory_space=pltpu.SMEM)] + [pl.BlockSpec(memory_space=pltpu.VMEM)] * len(flat),
        out_specs=pl.BlockSpec(memory_space=pl.ANY),
        out_shape=jax.ShapeDtypeStruct((rows, cols * PLANE), flat[0].dtype),
        scratch_shapes=[pltpu.SemaphoreType.DMA((len(flat),))],
        compiler_params=pltpu.CompilerParams(vmem_limit_bytes=16 << 20),
        name="assemble",
    )(places, *flat)


def split_block(q, k, v, residue, rate, skip, w_out):
    rows, chan = q.shape
    modes = rate.shape[0]
    me = lax.axis_index("ctx")
    core = lax.axis_index("ch")
    spot, plane = me & (PLANE - 1), me // PLANE
    count = lax.axis_size("ctx")
    chunk, feats = w_out.shape
    cols = feats // PLANE
    wide = 2 * cols // 3
    speed = rate.reshape(modes, chan // LANES, LANES)

    def far(x):
        return exchange(x, "ctx", 2 * PLANE)

    def near(x):
        return exchange(x, "ctx", PLANE)

    middle = [i for i in range(count) if PLANE <= i < 3 * PLANE]

    def across(x):
        return lax.ppermute(x, "ctx", [(i, i ^ (3 * PLANE)) for i in middle])

    def outward(x):
        return lax.ppermute(x, "ctx", [(i, i ^ PLANE) for i in middle])

    def group(x, r):
        return lax.dynamic_slice_in_dim(x, (spot ^ r) * cols, cols, axis=1)

    def plane_scan(k, v, rate, speed):
        def fade(span):
            return jnp.exp(-speed * span)

        ends = end_states(k, v, rate)
        other = exchange(ends, "ctx", 1)
        both = jnp.where(x_later, fade(float(rows)) * other + ends, fade(float(rows)) * ends + other)
        before = jnp.where(x_later, other, 0.0)
        other = exchange(both, "ctx", 2)
        before = before + jnp.where(y_later, fade((spot & 1).astype(jnp.float32) * rows) * other, 0.0)
        both = jnp.where(y_later, fade(2.0 * rows) * other + both, fade(2.0 * rows) * both + other)
        return jnp.stack([both, before])

    x_later, y_later = (spot & 1) != 0, (spot & 2) != 0
    w0, w1, w2, w3 = tie(*[group(w_out, r) for r in range(PLANE)])
    f0, n0 = far(w0), near(w0)
    scanned = box(plane_scan, k, v, rate, speed)
    f0, n0, w0, w1, w2, w3, scanned = tie(f0, n0, w0, w1, w2, w3, scanned)

    arrived = [exchange(w, "ctx", r + 1) for r, w in enumerate((w1, w2, w3))]
    both, before = scanned[0], scanned[1]
    decay = jnp.exp(-speed * float(PLANE * rows))
    last = shift_ctx(both, PLANE)
    line = last + decay * shift_ctx(both + decay * last, 2 * PLANE)
    enter = before + jnp.exp(-speed * (spot * rows).astype(jnp.float32)) * line
    f0, w0, enter = tie(f0, w0, enter)
    out0, mid0 = outward(f0), across(w0)
    gated = gated_conv(q, k, v, rate, residue, skip, enter)
    rest = jnp.concatenate(arrived)
    gated, rest, out0, mid0 = tie(gated, rest, out0, mid0)

    fr, nr = far(rest), near(rest)
    ours = [gated] + [exchange(gated, "ctx", r) for r in range(1, PLANE)]
    restA, restB = rest[:, :wide], rest[:, wide:]
    fr, nr, rest, restA, restB, *ours = tie(fr, nr, rest, restA, restB, *ours)

    def source_of(b):
        return jnp.where(b // 2 == core, b & 1, 2 + (b & 1))

    is_middle = jnp.where((plane == 0) | (plane == 3), 0, 1)
    flags = jnp.stack([source_of(plane ^ r) for r in range(4)] + [is_middle]).astype(jnp.int32)
    places = jnp.stack([spot ^ r for r in range(PLANE)]).astype(jnp.int32)

    outA, midA = outward(fr[:, :wide]), across(restA)
    theirs = [exchange(x, "ch", 1) for x in ours]
    blocks = [
        (0, None, [((w0,), 0), ((rest,), 0)]),
        (1, None, [((n0,), 0), ((nr,), 0)]),
        (2, None, [((f0,), 0), ((fr,), 0)]),
    ]
    accA, accB = product(flags, places, ours, theirs, blocks, None, [wide, cols - wide], jnp.float32)
    outA, midA, fr, restB, *accs = tie(outA, midA, fr, restB, *accA, *accB)
    accA, accB = accs[:PLANE], accs[PLANE:]

    outB, midB = outward(fr[:, wide:]), across(restB)

    def finish(first, out1, mid1, accs):
        blocks = [(3, 4, [((out0, mid0), first), ((out1, mid1), 0)])]
        (made,) = product(flags, places, ours, theirs, blocks, accs, [accs[0].shape[1]], jnp.bfloat16)
        return [made[0]] + [exchange(made[r], "ctx", r) for r in range(1, PLANE)]

    return assemble(places, [finish(0, outA, midA, accA), finish(wide, outB, midB, accB)])


def body(q, k, v, residue, rate, skip, w_out):
    rows, chan = q.shape
    modes = rate.shape[0]
    groups = chan // LANES
    count, cores = lax.axis_size("ctx"), lax.axis_size("ch")
    chunk, feats = w_out.shape
    split = (
        count == 4 * PLANE
        and cores == 2
        and chan == 8 * chunk
        and chunk % LANES == 0
        and feats % (6 * PLANE * LANES) == 0
    )
    skip = skip.reshape(groups, LANES)
    if split:
        return split_block(q, k, v, residue, rate, skip, w_out)
    ends = end_states(k, v, rate)
    enter = entering_states(ends, rate.reshape(modes, groups, LANES), rows)
    gated = gated_conv(q, k, v, rate, residue, skip, enter)
    gated = gated.transpose(1, 0, 2).reshape(rows, chan)
    full_gated = lax.all_gather(gated, "ch", axis=1, tiled=True)
    w_full = lax.all_gather(w_out, "ctx", axis=0, tiled=True)
    mixed = jnp.dot(full_gated, w_full, preferred_element_type=jnp.float32)
    return mixed.astype(jnp.bfloat16)


def solution(mesh):
    placed = (
        P("ctx", "ch"),
        P("ctx", "ch"),
        P("ctx", "ch"),
        P(None, "ch"),
        P(None, "ch"),
        P("ch"),
        P("ctx", "ch"),
    )
    return jax.shard_map(
        body, mesh=mesh, in_specs=placed, out_specs=P("ctx", "ch"), check_vma=False
    )
```

```python
import jax
import jax.numpy as jnp
from jax import lax
from jax.experimental import pallas as pl
from jax.experimental.pallas import tpu as pltpu
from jax.sharding import PartitionSpec as P

LANES = 128
RADIX = 4
PLANE = 4
VMEM_BYTES = 60 << 20


def spread_signal(k_ref, v_ref, sig_ref):
    rows, width = k_ref.shape
    groups = width // LANES
    for g in range(groups):
        cols = pl.ds(g * LANES, LANES)
        product = k_ref[:, cols].astype(jnp.float32) * v_ref[:, cols].astype(jnp.float32)
        sig_ref[pl.ds(g, rows, stride=groups), :] = product


def spread_modes(ref, out_ref):
    modes, width = ref.shape
    groups = width // LANES
    for g in range(groups):
        out_ref[pl.ds(g, modes, stride=groups), :] = ref[:, pl.ds(g * LANES, LANES)]


def ends_kernel(k_ref, v_ref, rate_ref, end_ref, speed_ref, sig_ref, mode_ref):
    rows, width = k_ref.shape
    modes, groups, _ = end_ref.shape
    spread_signal(k_ref, v_ref, sig_ref)
    spread_modes(rate_ref, mode_ref)
    decay = [jnp.exp(-mode_ref[pl.ds(m * groups, groups), :]) for m in range(modes)]

    def step(t, state):
        s = sig_ref[pl.ds(pl.multiple_of(t * groups, groups), groups), :]
        return tuple(d * h + s for d, h in zip(decay, state))

    zero = jnp.zeros((groups, LANES), jnp.float32)
    state = lax.fori_loop(0, rows, step, (zero,) * modes, unroll=8)
    for m in range(modes):
        end_ref[m] = state[m]
        speed_ref[m] = mode_ref[pl.ds(m * groups, groups), :]


def conv_kernel(q_ref, k_ref, v_ref, rate_ref, residue_ref, skip_ref, enter_ref, out_ref, sig_ref, conv_ref, mode_ref, weight_ref):
    rows, width = k_ref.shape
    modes, groups, _ = enter_ref.shape
    spread_signal(k_ref, v_ref, sig_ref)
    spread_modes(rate_ref, mode_ref)
    spread_modes(residue_ref, weight_ref)
    rates = [mode_ref[pl.ds(m * groups, groups), :] for m in range(modes)]
    decay = [jnp.exp(-rate) for rate in rates]
    weight = [weight_ref[pl.ds(m * groups, groups), :] * jnp.sqrt(2.0 * rate) for m, rate in enumerate(rates)]
    skip = skip_ref[...]

    def step(t, state):
        at = pl.ds(pl.multiple_of(t * groups, groups), groups)
        s = sig_ref[at, :]
        state = tuple(d * h + s for d, h in zip(decay, state))
        terms = [c * h for c, h in zip(weight, state)] + [skip * s]
        while len(terms) > 1:
            terms = [sum(terms[i : i + 2]) for i in range(0, len(terms), 2)]
        conv_ref[at, :] = terms[0]
        return state

    lax.fori_loop(0, rows, step, tuple(enter_ref[m] for m in range(modes)), unroll=4)
    for g in range(groups):
        cols = pl.ds(g * LANES, LANES)
        conv = conv_ref[pl.ds(g, rows, stride=groups), :]
        out_ref[:, cols] = (q_ref[:, cols].astype(jnp.float32) * conv).astype(out_ref.dtype)


def block_specs(rows, modes, width):
    groups = width // LANES
    return (
        pl.BlockSpec((rows, width), lambda i: (0, i)),
        pl.BlockSpec((modes, width), lambda i: (0, i)),
        pl.BlockSpec((modes, groups, LANES), lambda i: (0, i, 0)),
        pl.BlockSpec((groups, LANES), lambda i: (i, 0)),
    )


def end_states(k, v, rate):
    rows, chan = k.shape
    modes = rate.shape[0]
    width = min(chan, 8 * LANES)
    wide, moded, state, _ = block_specs(rows, modes, width)
    return pl.pallas_call(
        ends_kernel,
        grid=(chan // width,),
        in_specs=[wide, wide, moded],
        out_specs=[state, state],
        out_shape=[jax.ShapeDtypeStruct((modes, chan // LANES, LANES), jnp.float32)] * 2,
        scratch_shapes=[
            pltpu.VMEM((rows * width // LANES, LANES), jnp.float32),
            pltpu.VMEM((modes * width // LANES, LANES), jnp.float32),
        ],
        compiler_params=pltpu.CompilerParams(vmem_limit_bytes=VMEM_BYTES),
        cost_estimate=pl.CostEstimate(
            flops=2 * modes * rows * chan, bytes_accessed=4 * rows * chan, transcendentals=modes * chan
        ),
        name="end_states",
    )(k, v, rate)


def gated_conv(q, k, v, rate, residue, skip, enter):
    rows, chan = k.shape
    modes = rate.shape[0]
    width = min(chan, 8 * LANES)
    wide, moded, state, single = block_specs(rows, modes, width)
    spread = pltpu.VMEM((rows * width // LANES, LANES), jnp.float32)
    moded_spread = pltpu.VMEM((modes * width // LANES, LANES), jnp.float32)
    return pl.pallas_call(
        conv_kernel,
        grid=(chan // width,),
        in_specs=[wide, wide, wide, moded, moded, single, state],
        out_specs=pl.BlockSpec((None, rows, width), lambda i: (i, 0, 0)),
        out_shape=jax.ShapeDtypeStruct((chan // width, rows, width), jnp.bfloat16),
        scratch_shapes=[spread, spread, moded_spread, moded_spread],
        compiler_params=pltpu.CompilerParams(vmem_limit_bytes=VMEM_BYTES),
        cost_estimate=pl.CostEstimate(
            flops=4 * modes * rows * chan, bytes_accessed=8 * rows * chan, transcendentals=2 * modes * chan
        ),
        name="gated_conv",
    )(q, k, v, rate, residue, skip, enter)


def shift_ctx(x, by):
    count = lax.axis_size("ctx")
    return lax.ppermute(x, "ctx", [(i, i + by) for i in range(count - by)])


def exchange(x, axis, flip):
    count = lax.axis_size(axis)
    return lax.ppermute(x, axis, [(i, i ^ flip) for i in range(count)])


def tie(*values):
    return lax.optimization_barrier(values)


def entering_states(ends, rate, rows):
    count = lax.axis_size("ctx")
    total = jnp.zeros_like(ends)
    for k in range(1, min(RADIX, count - 1) + 1):
        total = total + jnp.exp(-rate * float(rows * (k - 1))) * shift_ctx(ends, k)
    stride = RADIX
    while stride < count:
        base = total
        for k in range(1, RADIX):
            if stride * k < count:
                total = total + jnp.exp(-rate * float(rows * stride * k)) * shift_ctx(base, stride * k)
        stride *= RADIX
    return total


def box(fn, *args):
    once = (lax.axis_index("ctx") >= 0).astype(jnp.int32)
    shapes = jax.eval_shape(fn, *args)
    empty = jax.tree.map(lambda a: jnp.zeros(a.shape, a.dtype), shapes)

    def run(step, _):
        return fn(*tie(step, *args)[1:])

    return lax.fori_loop(0, once, run, empty)


def product(flags, places, ours, theirs, blocks, accs, widths, out_dtype):
    _, rows, depth = ours[0].shape
    chunk = depth // PLANE
    cols = sum(widths)
    count, parts = len(blocks), len(ours)
    outs = parts * len(widths)
    weights = [array for _, _, pieces in blocks for choices, _ in pieces for array in choices]
    accs = accs or []

    def kernel(flag_ref, place_ref, *refs):
        our_refs, their_refs, refs = refs[:parts], refs[parts : 2 * parts], refs[2 * parts :]
        weight_refs, refs = list(refs[: len(weights)]), refs[len(weights) :]
        acc_refs, out_refs = refs[: len(accs)], refs[len(accs) : len(accs) + outs]
        gated_buf, weight_buf, acc_buf, gated_sems, weight_sems, acc_sem = refs[-6:]

        def target(b, at):
            start = pl.multiple_of(b * depth + place_ref[at // chunk] * chunk, chunk)
            return weight_buf.at[pl.ds(start, chunk), :]

        for b, (flag, pick, pieces) in enumerate(blocks):
            row = 0
            for choices, col in pieces:
                for c in range(len(choices)):
                    ref = weight_refs.pop(0)
                    for at in range(0, ref.shape[0], chunk):
                        source = ref.at[pl.ds(at, chunk), pl.ds(col, cols)]
                        copy = pltpu.make_async_copy(source, target(b, row + at), weight_sems.at[b])
                        if pick is None:
                            copy.start()
                        else:
                            pl.when(flag_ref[pick] == c)(copy.start)
                row += choices[0].shape[0]
            half = flag_ref[flag] & 1
            for r in range(parts):
                for c, refs_of in enumerate((our_refs, their_refs)):
                    target_rows = gated_buf.at[b, pl.ds(r * rows, rows), :]
                    copy = pltpu.make_async_copy(refs_of[r].at[half], target_rows, gated_sems.at[b])
                    pl.when(flag_ref[flag] // 2 == c)(copy.start)
        for r, acc_ref in enumerate(acc_refs):
            pltpu.make_async_copy(acc_ref, acc_buf.at[r], acc_sem).start()
        for b in range(count):
            block = weight_buf.at[pl.ds(b * depth, depth), :]
            pltpu.make_async_copy(block, block, weight_sems.at[b]).wait()
            pltpu.make_async_copy(gated_buf.at[b], gated_buf.at[b], gated_sems.at[b]).wait()
            if accs and not b:
                pltpu.make_async_copy(acc_buf, acc_buf, acc_sem).wait()
            for col in range(0, cols, 2 * LANES):
                here = pl.ds(col, 2 * LANES)
                made = jnp.dot(
                    gated_buf[b], weight_buf[pl.ds(b * depth, depth), here], preferred_element_type=jnp.float32
                )
                part = 0 if col < widths[0] else 1
                inside = pl.ds(col - part * widths[0], 2 * LANES)
                for r in range(parts):
                    total = made[r * rows : (r + 1) * rows]
                    out_ref = out_refs[part * parts + r]
                    if b or accs:
                        total = total + acc_buf[r, :, here]
                    if b < count - 1:
                        acc_buf[r, :, here] = total
                    else:
                        out_ref[:, inside] = total.astype(out_dtype)

    smem = pl.BlockSpec(memory_space=pltpu.SMEM)
    anywhere = pl.BlockSpec(memory_space=pl.ANY)
    made = pl.pallas_call(
        kernel,
        in_specs=[smem, smem] + [anywhere] * (2 * parts + len(weights) + len(accs)),
        out_specs=[pl.BlockSpec(memory_space=pltpu.VMEM)] * outs,
        out_shape=[jax.ShapeDtypeStruct((rows, width), out_dtype) for width in widths for _ in range(parts)],
        scratch_shapes=[
            pltpu.VMEM((count, parts * rows, depth), jnp.bfloat16),
            pltpu.VMEM((count * depth, cols), jnp.bfloat16),
            pltpu.VMEM((parts, rows, cols), jnp.float32),
            pltpu.SemaphoreType.DMA((count,)),
            pltpu.SemaphoreType.DMA((count,)),
            pltpu.SemaphoreType.DMA,
        ],
        compiler_params=pltpu.CompilerParams(vmem_limit_bytes=VMEM_BYTES),
        cost_estimate=pl.CostEstimate(
            flops=2 * parts * rows * depth * count * cols,
            bytes_accessed=2 * count * depth * (parts * rows + cols),
            transcendentals=0,
        ),
        name="product",
    )(flags, places, *ours, *theirs, *weights, *accs)
    return [list(made[at : at + parts]) for at in range(0, outs, parts)]


def assemble(places, parts):
    rows = parts[0][0].shape[0]
    widths = [part[0].shape[1] for part in parts]
    cols = sum(widths)
    flat = [piece for part in parts for piece in part]

    def kernel(place_ref, *refs):
        *piece_refs, out_ref, sems = refs
        copies = []
        first = 0
        for part, width in enumerate(widths):
            for r in range(PLANE):
                at = part * PLANE + r
                start = pl.multiple_of(place_ref[r] * cols + first, LANES)
                target = out_ref.at[:, pl.ds(start, width)]
                copies.append(pltpu.make_async_copy(piece_refs[at], target, sems.at[at]))
                copies[-1].start()
            first += width
        for copy in copies:
            copy.wait()

    return pl.pallas_call(
        kernel,
        in_specs=[pl.BlockSpec(memory_space=pltpu.SMEM)] + [pl.BlockSpec(memory_space=pltpu.VMEM)] * len(flat),
        out_specs=pl.BlockSpec(memory_space=pl.ANY),
        out_shape=jax.ShapeDtypeStruct((rows, cols * PLANE), flat[0].dtype),
        scratch_shapes=[pltpu.SemaphoreType.DMA((len(flat),))],
        compiler_params=pltpu.CompilerParams(vmem_limit_bytes=16 << 20),
        name="assemble",
    )(places, *flat)


def split_block(q, k, v, residue, rate, skip, w_out):
    rows, chan = q.shape
    me = lax.axis_index("ctx")
    core = lax.axis_index("ch")
    spot, plane = me & (PLANE - 1), me // PLANE
    count = lax.axis_size("ctx")
    chunk, feats = w_out.shape
    cols = feats // PLANE
    wide = 2 * cols // 3

    def far(x):
        return exchange(x, "ctx", 2 * PLANE)

    def near(x):
        return exchange(x, "ctx", PLANE)

    middle = [i for i in range(count) if PLANE <= i < 3 * PLANE]

    def across(x):
        return lax.ppermute(x, "ctx", [(i, i ^ (3 * PLANE)) for i in middle])

    def outward(x):
        return lax.ppermute(x, "ctx", [(i, i ^ PLANE) for i in middle])

    def group(x, r):
        return lax.dynamic_slice_in_dim(x, (spot ^ r) * cols, cols, axis=1)

    def plane_scan(k, v, rate):
        ends, speed = end_states(k, v, rate)
        found = [ends] + [exchange(ends, "ctx", r) for r in range(1, PLANE)]
        total, before = jnp.zeros_like(ends), jnp.zeros_like(ends)
        for r, state in enumerate(found):
            place = spot ^ r
            total = total + jnp.exp(-speed * ((PLANE - 1 - place) * rows).astype(jnp.float32)) * state
            if r:
                gap = jnp.maximum(spot - 1 - place, 0)
                faded = jnp.exp(-speed * (gap * rows).astype(jnp.float32)) * state
                before = before + jnp.where(place < spot, faded, 0.0)
        return jnp.stack([total, before, speed])

    w0, w1, w2, w3 = tie(*[group(w_out, r) for r in range(PLANE)])
    f0, n0 = far(w0), near(w0)
    scanned = box(plane_scan, k, v, rate)
    f0, n0, w0, w1, w2, w3, scanned = tie(f0, n0, w0, w1, w2, w3, scanned)

    arrived = [exchange(w, "ctx", r + 1) for r, w in enumerate((w1, w2, w3))]
    both, before, speed = scanned[0], scanned[1], scanned[2]
    decay = jnp.exp(-speed * float(PLANE * rows))
    last = shift_ctx(both, PLANE)
    line = last + decay * shift_ctx(both + decay * last, 2 * PLANE)
    enter = before + jnp.exp(-speed * (spot * rows).astype(jnp.float32)) * line
    rest = jnp.concatenate(arrived)
    f0, w0, enter, rest = tie(f0, w0, enter, rest)
    out0, mid0 = outward(f0), across(w0)
    gated = gated_conv(q, k, v, rate, residue, skip, enter)
    gated, rest, out0, mid0 = tie(gated, rest, out0, mid0)

    fr, nr = far(rest), near(rest)
    ours = [gated] + [exchange(gated, "ctx", r) for r in range(1, PLANE)]
    restA, restB = rest[:, :wide], rest[:, wide:]
    fr, nr, rest, restA, restB, *ours = tie(fr, nr, rest, restA, restB, *ours)

    def source_of(b):
        return jnp.where(b // 2 == core, b & 1, 2 + (b & 1))

    is_middle = jnp.where((plane == 0) | (plane == 3), 0, 1)
    flags = jnp.stack([source_of(plane ^ r) for r in range(4)] + [is_middle]).astype(jnp.int32)
    places = jnp.stack([spot ^ r for r in range(PLANE)]).astype(jnp.int32)

    outA, midA = outward(fr[:, :wide]), across(restA)
    theirs = [exchange(x, "ch", 1) for x in ours]
    blocks = [
        (0, None, [((w0,), 0), ((rest,), 0)]),
        (1, None, [((n0,), 0), ((nr,), 0)]),
        (2, None, [((f0,), 0), ((fr,), 0)]),
    ]
    (accs,) = product(flags, places, ours, theirs, blocks, None, [wide], jnp.float32)
    outA, midA, fr, restB, *accs = tie(outA, midA, fr, restB, *accs)

    outB, midB = outward(fr[:, wide:]), across(restB)
    last = (3, 4, [((out0, mid0), 0), ((outA, midA), 0)])
    (madeA,) = product(flags, places, ours, theirs, [last], accs, [wide], jnp.bfloat16)
    backA = [madeA[0]] + [exchange(madeA[r], "ctx", r) for r in range(1, PLANE)]
    blocks = [(flag, pick, [(arrays, wide) for arrays, _ in pieces]) for flag, pick, pieces in blocks]
    blocks.append((3, 4, [((out0, mid0), wide), ((outB, midB), 0)]))
    (madeB,) = product(flags, places, ours, theirs, blocks, None, [cols - wide], jnp.bfloat16)
    backB = [madeB[0]] + [exchange(madeB[r], "ctx", r) for r in range(1, PLANE)]
    return assemble(places, [backA, backB])


def body(q, k, v, residue, rate, skip, w_out):
    rows, chan = q.shape
    modes = rate.shape[0]
    groups = chan // LANES
    count, cores = lax.axis_size("ctx"), lax.axis_size("ch")
    chunk, feats = w_out.shape
    split = (
        count == 4 * PLANE
        and cores == 2
        and chan == 8 * chunk
        and chunk % LANES == 0
        and feats % (6 * PLANE * LANES) == 0
    )
    skip = skip.reshape(groups, LANES)
    if split:
        return split_block(q, k, v, residue, rate, skip, w_out)
    ends, _ = end_states(k, v, rate)
    enter = entering_states(ends, rate.reshape(modes, groups, LANES), rows)
    gated = gated_conv(q, k, v, rate, residue, skip, enter)
    gated = gated.transpose(1, 0, 2).reshape(rows, chan)
    full_gated = lax.all_gather(gated, "ch", axis=1, tiled=True)
    w_full = lax.all_gather(w_out, "ctx", axis=0, tiled=True)
    mixed = jnp.dot(full_gated, w_full, preferred_element_type=jnp.float32)
    return mixed.astype(jnp.bfloat16)


def solution(mesh):
    placed = (
        P("ctx", "ch"),
        P("ctx", "ch"),
        P("ctx", "ch"),
        P(None, "ch"),
        P(None, "ch"),
        P("ch"),
        P("ctx", "ch"),
    )
    return jax.shard_map(
        body, mesh=mesh, in_specs=placed, out_specs=P("ctx", "ch"), check_vma=False
    )
```

```python
import jax
import jax.numpy as jnp
from jax import lax
from jax.experimental import pallas as pl
from jax.experimental.pallas import tpu as pltpu
from jax.sharding import PartitionSpec as P

LANES = 128
RADIX = 4
PLANE = 4
VMEM_BYTES = 60 << 20


def spread_signal(k_ref, v_ref, sig_ref):
    rows, width = k_ref.shape
    groups = width // LANES
    for g in range(groups):
        cols = pl.ds(g * LANES, LANES)
        product = k_ref[:, cols].astype(jnp.float32) * v_ref[:, cols].astype(jnp.float32)
        sig_ref[pl.ds(g, rows, stride=groups), :] = product


def spread_modes(ref, out_ref):
    modes, width = ref.shape
    groups = width // LANES
    for g in range(groups):
        out_ref[pl.ds(g, modes, stride=groups), :] = ref[:, pl.ds(g * LANES, LANES)]


def ends_kernel(k_ref, v_ref, rate_ref, end_ref, sig_ref, mode_ref):
    rows, width = k_ref.shape
    modes, groups, _ = end_ref.shape
    spread_signal(k_ref, v_ref, sig_ref)
    spread_modes(rate_ref, mode_ref)
    decay = [jnp.exp(-mode_ref[pl.ds(m * groups, groups), :]) for m in range(modes)]

    def step(t, state):
        s = sig_ref[pl.ds(pl.multiple_of(t * groups, groups), groups), :]
        return tuple(d * h + s for d, h in zip(decay, state))

    zero = jnp.zeros((groups, LANES), jnp.float32)
    state = lax.fori_loop(0, rows, step, (zero,) * modes, unroll=8)
    for m in range(modes):
        end_ref[m] = state[m]


def conv_kernel(q_ref, k_ref, v_ref, rate_ref, residue_ref, skip_ref, enter_ref, out_ref, sig_ref, conv_ref, mode_ref, weight_ref):
    rows, width = k_ref.shape
    modes, groups, _ = enter_ref.shape
    spread_signal(k_ref, v_ref, sig_ref)
    spread_modes(rate_ref, mode_ref)
    spread_modes(residue_ref, weight_ref)
    rates = [mode_ref[pl.ds(m * groups, groups), :] for m in range(modes)]
    decay = [jnp.exp(-rate) for rate in rates]
    weight = [weight_ref[pl.ds(m * groups, groups), :] * jnp.sqrt(2.0 * rate) for m, rate in enumerate(rates)]
    skip = skip_ref[...]

    def step(t, state):
        at = pl.ds(pl.multiple_of(t * groups, groups), groups)
        s = sig_ref[at, :]
        state = tuple(d * h + s for d, h in zip(decay, state))
        terms = [c * h for c, h in zip(weight, state)] + [skip * s]
        while len(terms) > 1:
            terms = [sum(terms[i : i + 2]) for i in range(0, len(terms), 2)]
        conv_ref[at, :] = terms[0]
        return state

    lax.fori_loop(0, rows, step, tuple(enter_ref[m] for m in range(modes)), unroll=4)
    for g in range(groups):
        cols = pl.ds(g * LANES, LANES)
        conv = conv_ref[pl.ds(g, rows, stride=groups), :]
        out_ref[:, cols] = (q_ref[:, cols].astype(jnp.float32) * conv).astype(out_ref.dtype)


def block_specs(rows, modes, width):
    groups = width // LANES
    return (
        pl.BlockSpec((rows, width), lambda i: (0, i)),
        pl.BlockSpec((modes, width), lambda i: (0, i)),
        pl.BlockSpec((modes, groups, LANES), lambda i: (0, i, 0)),
        pl.BlockSpec((groups, LANES), lambda i: (i, 0)),
    )


def end_states(k, v, rate):
    rows, chan = k.shape
    modes = rate.shape[0]
    width = min(chan, 8 * LANES)
    wide, moded, state, _ = block_specs(rows, modes, width)
    return pl.pallas_call(
        ends_kernel,
        grid=(chan // width,),
        in_specs=[wide, wide, moded],
        out_specs=state,
        out_shape=jax.ShapeDtypeStruct((modes, chan // LANES, LANES), jnp.float32),
        scratch_shapes=[
            pltpu.VMEM((rows * width // LANES, LANES), jnp.float32),
            pltpu.VMEM((modes * width // LANES, LANES), jnp.float32),
        ],
        compiler_params=pltpu.CompilerParams(vmem_limit_bytes=VMEM_BYTES),
        cost_estimate=pl.CostEstimate(
            flops=2 * modes * rows * chan, bytes_accessed=4 * rows * chan, transcendentals=modes * chan
        ),
        name="end_states",
    )(k, v, rate)


def gated_conv(q, k, v, rate, residue, skip, enter):
    rows, chan = k.shape
    modes = rate.shape[0]
    width = min(chan, 8 * LANES)
    wide, moded, state, single = block_specs(rows, modes, width)
    spread = pltpu.VMEM((rows * width // LANES, LANES), jnp.float32)
    moded_spread = pltpu.VMEM((modes * width // LANES, LANES), jnp.float32)
    return pl.pallas_call(
        conv_kernel,
        grid=(chan // width,),
        in_specs=[wide, wide, wide, moded, moded, single, state],
        out_specs=pl.BlockSpec((None, rows, width), lambda i: (i, 0, 0)),
        out_shape=jax.ShapeDtypeStruct((chan // width, rows, width), jnp.bfloat16),
        scratch_shapes=[spread, spread, moded_spread, moded_spread],
        compiler_params=pltpu.CompilerParams(vmem_limit_bytes=VMEM_BYTES),
        cost_estimate=pl.CostEstimate(
            flops=4 * modes * rows, bytes_accessed=8 * rows, transcendentals=2 * modes
        ),
        name="gated_conv",
    )(q, k, v, rate, residue, skip, enter)


def shift_ctx(x, by):
    count = lax.axis_size("ctx")
    return lax.ppermute(x, "ctx", [(i, i + by) for i in range(count - by)])


def exchange(x, axis, flip):
    count = lax.axis_size(axis)
    return lax.ppermute(x, axis, [(i, i ^ flip) for i in range(count)])


def tie(*values):
    return lax.optimization_barrier(values)


def entering_states(ends, rate, rows):
    count = lax.axis_size("ctx")
    total = jnp.zeros_like(ends)
    for k in range(1, min(RADIX, count - 1) + 1):
        total = total + jnp.exp(-rate * float(rows * (k - 1))) * shift_ctx(ends, k)
    stride = RADIX
    while stride < count:
        base = total
        for k in range(1, RADIX):
            if stride * k < count:
                total = total + jnp.exp(-rate * float(rows * stride * k)) * shift_ctx(base, stride * k)
        stride *= RADIX
    return total


def box(fn, *args):
    once = (lax.axis_index("ctx") >= 0).astype(jnp.int32)
    shapes = jax.eval_shape(fn, *args)
    empty = jax.tree.map(lambda a: jnp.zeros(a.shape, a.dtype), shapes)

    def run(step, _):
        return fn(*tie(step, *args)[1:])

    return lax.fori_loop(0, once, run, empty)


def product(flags, places, ours, theirs, blocks, accs, widths, out_dtype, vmem_bytes):
    _, rows, depth = ours[0].shape
    chunk = depth // PLANE
    cols = sum(widths)
    count, parts = len(blocks), len(ours)
    outs = parts * len(widths)
    weights = [array for _, _, pieces in blocks for choices, _ in pieces for array in choices]
    accs = accs or []

    def kernel(flag_ref, place_ref, *refs):
        our_refs, their_refs, refs = refs[:parts], refs[parts : 2 * parts], refs[2 * parts :]
        weight_refs, refs = list(refs[: len(weights)]), refs[len(weights) :]
        acc_refs, out_refs = refs[: len(accs)], refs[len(accs) : len(accs) + outs]
        gated_buf, weight_buf, acc_buf, gated_sems, weight_sems, acc_sem = refs[-6:]

        def target(b, at):
            start = pl.multiple_of(b * depth + place_ref[at // chunk] * chunk, chunk)
            return weight_buf.at[pl.ds(start, chunk), :]

        for b, (flag, pick, pieces) in enumerate(blocks):
            row = 0
            for choices, col in pieces:
                for c in range(len(choices)):
                    ref = weight_refs.pop(0)
                    for at in range(0, ref.shape[0], chunk):
                        source = ref.at[pl.ds(at, chunk), pl.ds(col, cols)]
                        copy = pltpu.make_async_copy(source, target(b, row + at), weight_sems.at[b])
                        if pick is None:
                            copy.start()
                        else:
                            pl.when(flag_ref[pick] == c)(copy.start)
                row += choices[0].shape[0]
            half = flag_ref[flag] & 1
            for r in range(parts):
                for c, refs_of in enumerate((our_refs, their_refs)):
                    target_rows = gated_buf.at[b, pl.ds(r * rows, rows), :]
                    copy = pltpu.make_async_copy(refs_of[r].at[half], target_rows, gated_sems.at[b])
                    pl.when(flag_ref[flag] // 2 == c)(copy.start)
        for r, acc_ref in enumerate(acc_refs):
            pltpu.make_async_copy(acc_ref, acc_buf.at[r], acc_sem).start()
        for b in range(count):
            block = weight_buf.at[pl.ds(b * depth, depth), :]
            pltpu.make_async_copy(block, block, weight_sems.at[b]).wait()
            pltpu.make_async_copy(gated_buf.at[b], gated_buf.at[b], gated_sems.at[b]).wait()
            if accs and not b:
                pltpu.make_async_copy(acc_buf, acc_buf, acc_sem).wait()
            for col in range(0, cols, 2 * LANES):
                here = pl.ds(col, 2 * LANES)
                made = jnp.dot(
                    gated_buf[b], weight_buf[pl.ds(b * depth, depth), here], preferred_element_type=jnp.float32
                )
                part = 0 if col < widths[0] else 1
                inside = pl.ds(col - part * widths[0], 2 * LANES)
                for r in range(parts):
                    total = made[r * rows : (r + 1) * rows]
                    out_ref = out_refs[part * parts + r]
                    if b:
                        total = total + out_ref[:, inside]
                    elif accs:
                        total = total + acc_buf[r, :, here]
                    out_ref[:, inside] = total.astype(out_dtype)

    smem = pl.BlockSpec(memory_space=pltpu.SMEM)
    anywhere, hbm = pl.BlockSpec(memory_space=pl.ANY), pl.BlockSpec(memory_space=pltpu.HBM)
    made = pl.pallas_call(
        kernel,
        in_specs=[smem, smem] + [hbm] * (2 * parts) + [anywhere] * len(weights) + [hbm] * len(accs),
        out_specs=[pl.BlockSpec(memory_space=pltpu.VMEM)] * outs,
        out_shape=[jax.ShapeDtypeStruct((rows, width), out_dtype) for width in widths for _ in range(parts)],
        scratch_shapes=[
            pltpu.VMEM((count, parts * rows, depth), jnp.bfloat16),
            pltpu.VMEM((count * depth, cols), jnp.bfloat16),
            pltpu.VMEM((len(accs), *accs[0].shape) if accs else (8, LANES), jnp.float32),
            pltpu.SemaphoreType.DMA((count,)),
            pltpu.SemaphoreType.DMA((count,)),
            pltpu.SemaphoreType.DMA,
        ],
        compiler_params=pltpu.CompilerParams(vmem_limit_bytes=vmem_bytes),
        cost_estimate=pl.CostEstimate(
            flops=2 * parts * rows * depth * count * cols,
            bytes_accessed=2 * count * depth * (parts * rows + cols),
            transcendentals=0,
        ),
        name="product",
    )(flags, places, *ours, *theirs, *weights, *accs)
    return [list(made[at : at + parts]) for at in range(0, outs, parts)]


def assemble(places, parts):
    rows = parts[0][0].shape[0]
    widths = [part[0].shape[1] for part in parts]
    cols = sum(widths)
    flat = [piece for part in parts for piece in part]

    def kernel(place_ref, *refs):
        *piece_refs, out_ref, sems = refs
        copies = []
        first = 0
        for part, width in enumerate(widths):
            for r in range(PLANE):
                at = part * PLANE + r
                start = pl.multiple_of(place_ref[r] * cols + first, LANES)
                target = out_ref.at[:, pl.ds(start, width)]
                copies.append(pltpu.make_async_copy(piece_refs[at], target, sems.at[at]))
                copies[-1].start()
            first += width
        for copy in copies:
            copy.wait()

    return pl.pallas_call(
        kernel,
        in_specs=[pl.BlockSpec(memory_space=pltpu.SMEM)] + [pl.BlockSpec(memory_space=pltpu.VMEM)] * len(flat),
        out_specs=pl.BlockSpec(memory_space=pl.ANY),
        out_shape=jax.ShapeDtypeStruct((rows, cols * PLANE), flat[0].dtype),
        scratch_shapes=[pltpu.SemaphoreType.DMA((len(flat),))],
        compiler_params=pltpu.CompilerParams(vmem_limit_bytes=16 << 20),
        name="assemble",
    )(places, *flat)


def split_block(q, k, v, residue, rate, skip, w_out):
    rows, chan = q.shape
    modes = rate.shape[0]
    me = lax.axis_index("ctx")
    core = lax.axis_index("ch")
    spot, plane = me & (PLANE - 1), me // PLANE
    count = lax.axis_size("ctx")
    chunk, feats = w_out.shape
    cols = feats // PLANE
    wide = 2 * cols // 3
    speed = rate.reshape(modes, chan // LANES, LANES)

    def far(x):
        return exchange(x, "ctx", 2 * PLANE)

    def near(x):
        return exchange(x, "ctx", PLANE)

    middle = [i for i in range(count) if PLANE <= i < 3 * PLANE]

    def across(x):
        return lax.ppermute(x, "ctx", [(i, i ^ (3 * PLANE)) for i in middle])

    def outward(x):
        return lax.ppermute(x, "ctx", [(i, i ^ PLANE) for i in middle])

    def group(x, r):
        return lax.dynamic_slice_in_dim(x, (spot ^ r) * cols, cols, axis=1)

    def plane_scan(k, v, rate, speed):
        def fade(span):
            return jnp.exp(-speed * span)

        ends = end_states(k, v, rate)
        other = exchange(ends, "ctx", 1)
        both = jnp.where(x_later, fade(float(rows)) * other + ends, fade(float(rows)) * ends + other)
        before = jnp.where(x_later, other, 0.0)
        other = exchange(both, "ctx", 2)
        before = before + jnp.where(y_later, fade((spot & 1).astype(jnp.float32) * rows) * other, 0.0)
        both = jnp.where(y_later, fade(2.0 * rows) * other + both, fade(2.0 * rows) * both + other)
        return jnp.stack([both, before])

    x_later, y_later = (spot & 1) != 0, (spot & 2) != 0
    w0, w1, w2, w3 = tie(*[group(w_out, r) for r in range(PLANE)])
    f0 = far(w0)
    arrived = [exchange(w, "ctx", r + 1) for r, w in enumerate((w1, w2, w3))]
    scanned = box(plane_scan, k, v, rate, speed)
    f0, w0, scanned, *arrived = tie(f0, w0, scanned, *arrived)

    both, before = scanned[0], scanned[1]
    decay = jnp.exp(-speed * float(PLANE * rows))
    last = shift_ctx(both, PLANE)
    line = last + decay * shift_ctx(both + decay * last, 2 * PLANE)
    enter = before + jnp.exp(-speed * (spot * rows).astype(jnp.float32)) * line
    f0, w0, enter = tie(f0, w0, enter)
    out0, mid0, n0 = outward(f0), across(w0), near(w0)
    gated = gated_conv(q, k, v, rate, residue, skip, enter)
    rest = jnp.concatenate(arrived)
    gated, rest, out0, mid0, n0 = tie(gated, rest, out0, mid0, n0)

    fr, nr = far(rest), near(rest)
    ours = [gated] + [exchange(gated, "ctx", r) for r in range(1, PLANE)]
    restA, restB = rest[:, :wide], rest[:, wide:]
    ours = list(tie(*ours))
    theirs = [exchange(x, "ch", 1) for x in ours[1:]]
    fr, nr, rest, restA, restB, *held = tie(fr, nr, rest, restA, restB, *ours, *theirs)
    ours, theirs = held[:PLANE], held[PLANE:]

    def source_of(b):
        return jnp.where(b // 2 == core, b & 1, 2 + (b & 1))

    is_middle = jnp.where((plane == 0) | (plane == 3), 0, 1)
    flags = jnp.stack([source_of(plane ^ r) for r in range(4)] + [is_middle]).astype(jnp.int32)
    places = jnp.stack([spot ^ r for r in range(PLANE)]).astype(jnp.int32)

    outA, midA = outward(fr[:, :wide]), across(restA)
    theirs = [exchange(ours[0], "ch", 1)] + theirs
    blocks = [
        (0, None, [((w0,), 0), ((rest,), 0)]),
        (1, None, [((n0,), 0), ((nr,), 0)]),
        (2, None, [((f0,), 0), ((fr,), 0)]),
    ]
    accA, accB = product(flags, places, ours, theirs, blocks, None, [wide, cols - wide], jnp.float32, VMEM_BYTES)
    outA, midA, fr, restB, *accs = tie(outA, midA, fr, restB, *accA, *accB)
    accA, accB = accs[:PLANE], accs[PLANE:]

    outB, midB = outward(fr[:, wide:]), across(restB)

    def finish(first, out1, mid1, accs):
        blocks = [(3, 4, [((out0, mid0), first), ((out1, mid1), 0)])]
        (made,) = product(flags, places, ours, theirs, blocks, accs, [accs[0].shape[1]], jnp.bfloat16, 16 << 20)
        return [made[0]] + [exchange(made[r], "ctx", r) for r in range(1, PLANE)]

    return assemble(places, [finish(0, outA, midA, accA), finish(wide, outB, midB, accB)])


def body(q, k, v, residue, rate, skip, w_out):
    rows, chan = q.shape
    modes = rate.shape[0]
    groups = chan // LANES
    count, cores = lax.axis_size("ctx"), lax.axis_size("ch")
    chunk, feats = w_out.shape
    split = (
        count == 4 * PLANE
        and cores == 2
        and chan == 8 * chunk
        and chunk % LANES == 0
        and feats % (6 * PLANE * LANES) == 0
    )
    skip = skip.reshape(groups, LANES)
    if split:
        return split_block(q, k, v, residue, rate, skip, w_out)
    ends = end_states(k, v, rate)
    enter = entering_states(ends, rate.reshape(modes, groups, LANES), rows)
    gated = gated_conv(q, k, v, rate, residue, skip, enter)
    gated = gated.transpose(1, 0, 2).reshape(rows, chan)
    full_gated = lax.all_gather(gated, "ch", axis=1, tiled=True)
    w_full = lax.all_gather(w_out, "ctx", axis=0, tiled=True)
    mixed = jnp.dot(full_gated, w_full, preferred_element_type=jnp.float32)
    return mixed.astype(jnp.bfloat16)


def solution(mesh):
    placed = (
        P("ctx", "ch"),
        P("ctx", "ch"),
        P("ctx", "ch"),
        P(None, "ch"),
        P(None, "ch"),
        P("ch"),
        P("ctx", "ch"),
    )
    return jax.shard_map(
        body, mesh=mesh, in_specs=placed, out_specs=P("ctx", "ch"), check_vma=False
    )
```

```python
import jax
import jax.numpy as jnp
from jax import lax
from jax.experimental import pallas as pl
from jax.experimental.pallas import tpu as pltpu
from jax.sharding import PartitionSpec as P

LANES = 128
RADIX = 4
PLANE = 4
VMEM_BYTES = 60 << 20


def spread_signal(k_ref, v_ref, sig_ref):
    rows, width = k_ref.shape
    groups = width // LANES
    for g in range(groups):
        cols = pl.ds(g * LANES, LANES)
        product = k_ref[:, cols].astype(jnp.float32) * v_ref[:, cols].astype(jnp.float32)
        sig_ref[pl.ds(g, rows, stride=groups), :] = product


def spread_modes(ref, out_ref):
    modes, width = ref.shape
    groups = width // LANES
    for g in range(groups):
        out_ref[pl.ds(g, modes, stride=groups), :] = ref[:, pl.ds(g * LANES, LANES)]


def ends_kernel(k_ref, v_ref, rate_ref, end_ref, sig_ref, mode_ref):
    rows, width = k_ref.shape
    modes, groups, _ = end_ref.shape
    spread_signal(k_ref, v_ref, sig_ref)
    spread_modes(rate_ref, mode_ref)
    decay = [jnp.exp(-mode_ref[pl.ds(m * groups, groups), :]) for m in range(modes)]

    def step(t, state):
        s = sig_ref[pl.ds(pl.multiple_of(t * groups, groups), groups), :]
        return tuple(d * h + s for d, h in zip(decay, state))

    zero = jnp.zeros((groups, LANES), jnp.float32)
    state = lax.fori_loop(0, rows, step, (zero,) * modes, unroll=8)
    for m in range(modes):
        end_ref[m] = state[m]


def conv_kernel(q_ref, k_ref, v_ref, rate_ref, residue_ref, skip_ref, enter_ref, *refs):
    *plane_refs, out_ref, sig_ref, conv_ref, mode_ref, weight_ref = refs
    rows, width = k_ref.shape
    modes, groups, _ = enter_ref.shape
    spread_signal(k_ref, v_ref, sig_ref)
    spread_modes(rate_ref, mode_ref)
    spread_modes(residue_ref, weight_ref)
    rates = [mode_ref[pl.ds(m * groups, groups), :] for m in range(modes)]
    decay = [jnp.exp(-rate) for rate in rates]
    weight = [weight_ref[pl.ds(m * groups, groups), :] * jnp.sqrt(2.0 * rate) for m, rate in enumerate(rates)]
    skip = skip_ref[...]
    enter = [enter_ref[m] for m in range(modes)]
    if plane_refs:
        last_ref, earlier_ref, spot_ref = plane_refs
        ahead = (spot_ref[0] * rows).astype(jnp.float32)
        for m, rate in enumerate(rates):
            line = last_ref[m] + jnp.exp(-rate * float(PLANE * rows)) * earlier_ref[m]
            enter[m] = enter[m] + jnp.exp(-rate * ahead) * line

    def step(t, state):
        at = pl.ds(pl.multiple_of(t * groups, groups), groups)
        s = sig_ref[at, :]
        state = tuple(d * h + s for d, h in zip(decay, state))
        terms = [c * h for c, h in zip(weight, state)] + [skip * s]
        while len(terms) > 1:
            terms = [sum(terms[i : i + 2]) for i in range(0, len(terms), 2)]
        conv_ref[at, :] = terms[0]
        return state

    lax.fori_loop(0, rows, step, tuple(enter), unroll=4)
    for g in range(groups):
        cols = pl.ds(g * LANES, LANES)
        conv = conv_ref[pl.ds(g, rows, stride=groups), :]
        out_ref[:, cols] = (q_ref[:, cols].astype(jnp.float32) * conv).astype(out_ref.dtype)


def block_specs(rows, modes, width):
    groups = width // LANES
    return (
        pl.BlockSpec((rows, width), lambda i: (0, i)),
        pl.BlockSpec((modes, width), lambda i: (0, i)),
        pl.BlockSpec((modes, groups, LANES), lambda i: (0, i, 0)),
        pl.BlockSpec((groups, LANES), lambda i: (i, 0)),
    )


def end_states(k, v, rate):
    rows, chan = k.shape
    modes = rate.shape[0]
    width = min(chan, 8 * LANES)
    wide, moded, state, _ = block_specs(rows, modes, width)
    return pl.pallas_call(
        ends_kernel,
        grid=(chan // width,),
        in_specs=[wide, wide, moded],
        out_specs=state,
        out_shape=jax.ShapeDtypeStruct((modes, chan // LANES, LANES), jnp.float32),
        scratch_shapes=[
            pltpu.VMEM((rows * width // LANES, LANES), jnp.float32),
            pltpu.VMEM((modes * width // LANES, LANES), jnp.float32),
        ],
        compiler_params=pltpu.CompilerParams(vmem_limit_bytes=VMEM_BYTES),
        cost_estimate=pl.CostEstimate(
            flops=2 * modes * rows * chan, bytes_accessed=4 * rows * chan, transcendentals=modes * chan
        ),
        name="end_states",
    )(k, v, rate)


def gated_conv(q, k, v, rate, residue, skip, enter, planes=None):
    rows, chan = k.shape
    modes = rate.shape[0]
    width = min(chan, 8 * LANES)
    wide, moded, state, single = block_specs(rows, modes, width)
    spread = pltpu.VMEM((rows * width // LANES, LANES), jnp.float32)
    moded_spread = pltpu.VMEM((modes * width // LANES, LANES), jnp.float32)
    extra, extra_specs = [], []
    if planes is not None:
        last, earlier, spot = planes
        extra = [last, earlier, spot.reshape(1).astype(jnp.int32)]
        extra_specs = [state, state, pl.BlockSpec(memory_space=pltpu.SMEM)]
    return pl.pallas_call(
        conv_kernel,
        grid=(chan // width,),
        in_specs=[wide, wide, wide, moded, moded, single, state] + extra_specs,
        out_specs=pl.BlockSpec((None, rows, width), lambda i: (i, 0, 0)),
        out_shape=jax.ShapeDtypeStruct((chan // width, rows, width), jnp.bfloat16),
        scratch_shapes=[spread, spread, moded_spread, moded_spread],
        compiler_params=pltpu.CompilerParams(vmem_limit_bytes=VMEM_BYTES),
        cost_estimate=pl.CostEstimate(
            flops=4 * modes * rows * chan, bytes_accessed=8 * rows * chan, transcendentals=2 * modes * chan
        ),
        name="gated_conv",
    )(q, k, v, rate, residue, skip, enter, *extra)


def shift_ctx(x, by):
    count = lax.axis_size("ctx")
    return lax.ppermute(x, "ctx", [(i, i + by) for i in range(count - by)])


def exchange(x, axis, flip):
    count = lax.axis_size(axis)
    return lax.ppermute(x, axis, [(i, i ^ flip) for i in range(count)])


def tie(*values):
    return lax.optimization_barrier(values)


def entering_states(ends, rate, rows):
    count = lax.axis_size("ctx")
    total = jnp.zeros_like(ends)
    for k in range(1, min(RADIX, count - 1) + 1):
        total = total + jnp.exp(-rate * float(rows * (k - 1))) * shift_ctx(ends, k)
    stride = RADIX
    while stride < count:
        base = total
        for k in range(1, RADIX):
            if stride * k < count:
                total = total + jnp.exp(-rate * float(rows * stride * k)) * shift_ctx(base, stride * k)
        stride *= RADIX
    return total


def box(fn, *args):
    once = (lax.axis_index("ctx") >= 0).astype(jnp.int32)
    shapes = jax.eval_shape(fn, *args)
    empty = pl.pallas_call(
        lambda *refs: None,
        out_specs=[pl.BlockSpec(memory_space=pl.ANY)] * len(shapes),
        out_shape=list(shapes),
        name="blank",
    )()

    def run(step, _):
        return fn(*tie(step, *args)[1:])

    return lax.fori_loop(0, once, run, tuple(empty))


def product(flags, places, ours, theirs, blocks, accs, widths, out_dtype):
    _, rows, depth = ours[0].shape
    chunk = depth // PLANE
    cols = sum(widths)
    count, parts = len(blocks), len(ours)
    outs = parts * len(widths)
    weights = [array for _, _, pieces in blocks for choices, _ in pieces for array in choices]
    accs = accs or []

    def kernel(flag_ref, place_ref, *refs):
        our_refs, their_refs, refs = refs[:parts], refs[parts : 2 * parts], refs[2 * parts :]
        weight_refs, refs = list(refs[: len(weights)]), refs[len(weights) :]
        acc_refs, out_refs = refs[: len(accs)], refs[len(accs) : len(accs) + outs]
        gated_buf, weight_buf, acc_buf, gated_sems, weight_sems, acc_sem = refs[-6:]

        def target(b, at):
            start = pl.multiple_of(b * depth + place_ref[at // chunk] * chunk, chunk)
            return weight_buf.at[pl.ds(start, chunk), :]

        for b, (flag, pick, pieces) in enumerate(blocks):
            row = 0
            for choices, col in pieces:
                for c in range(len(choices)):
                    ref = weight_refs.pop(0)
                    for at in range(0, ref.shape[0], chunk):
                        source = ref.at[pl.ds(at, chunk), pl.ds(col, cols)]
                        copy = pltpu.make_async_copy(source, target(b, row + at), weight_sems.at[b])
                        if pick is None:
                            copy.start()
                        else:
                            pl.when(flag_ref[pick] == c)(copy.start)
                row += choices[0].shape[0]
            half = flag_ref[flag] & 1
            for r in range(parts):
                for c, refs_of in enumerate((our_refs, their_refs)):
                    target_rows = gated_buf.at[b, pl.ds(r * rows, rows), :]
                    copy = pltpu.make_async_copy(refs_of[r].at[half], target_rows, gated_sems.at[b])
                    pl.when(flag_ref[flag] // 2 == c)(copy.start)
        for r, acc_ref in enumerate(acc_refs):
            pltpu.make_async_copy(acc_ref, acc_buf.at[r], acc_sem).start()
        for b in range(count):
            block = weight_buf.at[pl.ds(b * depth, depth), :]
            pltpu.make_async_copy(block, block, weight_sems.at[b]).wait()
            pltpu.make_async_copy(gated_buf.at[b], gated_buf.at[b], gated_sems.at[b]).wait()
            if accs and not b:
                pltpu.make_async_copy(acc_buf, acc_buf, acc_sem).wait()
            for col in range(0, cols, 2 * LANES):
                here = pl.ds(col, 2 * LANES)
                made = jnp.dot(
                    gated_buf[b], weight_buf[pl.ds(b * depth, depth), here], preferred_element_type=jnp.float32
                )
                part = 0 if col < widths[0] else 1
                inside = pl.ds(col - part * widths[0], 2 * LANES)
                for r in range(parts):
                    total = made[r * rows : (r + 1) * rows]
                    out_ref = out_refs[part * parts + r]
                    if b:
                        total = total + out_ref[:, inside]
                    elif accs:
                        total = total + acc_buf[r, :, here]
                    out_ref[:, inside] = total.astype(out_dtype)

    smem = pl.BlockSpec(memory_space=pltpu.SMEM)
    anywhere = pl.BlockSpec(memory_space=pl.ANY)
    made = pl.pallas_call(
        kernel,
        in_specs=[smem, smem] + [anywhere] * (2 * parts + len(weights) + len(accs)),
        out_specs=[pl.BlockSpec(memory_space=pltpu.VMEM)] * outs,
        out_shape=[jax.ShapeDtypeStruct((rows, width), out_dtype) for width in widths for _ in range(parts)],
        scratch_shapes=[
            pltpu.VMEM((count, parts * rows, depth), jnp.bfloat16),
            pltpu.VMEM((count * depth, cols), jnp.bfloat16),
            pltpu.VMEM((len(accs), *accs[0].shape) if accs else (8, LANES), jnp.float32),
            pltpu.SemaphoreType.DMA((count,)),
            pltpu.SemaphoreType.DMA((count,)),
            pltpu.SemaphoreType.DMA,
        ],
        compiler_params=pltpu.CompilerParams(vmem_limit_bytes=VMEM_BYTES),
        cost_estimate=pl.CostEstimate(
            flops=2 * parts * rows * depth * count * cols,
            bytes_accessed=2 * count * depth * (parts * rows + cols),
            transcendentals=0,
        ),
        name="product",
    )(flags, places, *ours, *theirs, *weights, *accs)
    return [list(made[at : at + parts]) for at in range(0, outs, parts)]


def assemble(places, parts):
    rows = parts[0][0].shape[0]
    widths = [part[0].shape[1] for part in parts]
    cols = sum(widths)
    flat = [piece for part in parts for piece in part]

    def kernel(place_ref, *refs):
        *piece_refs, out_ref, sems = refs
        copies = []
        first = 0
        for part, width in enumerate(widths):
            for r in range(PLANE):
                at = part * PLANE + r
                start = pl.multiple_of(place_ref[r] * cols + first, LANES)
                target = out_ref.at[:, pl.ds(start, width)]
                copies.append(pltpu.make_async_copy(piece_refs[at], target, sems.at[at]))
                copies[-1].start()
            first += width
        for copy in copies:
            copy.wait()

    return pl.pallas_call(
        kernel,
        in_specs=[pl.BlockSpec(memory_space=pltpu.SMEM)] + [pl.BlockSpec(memory_space=pltpu.VMEM)] * len(flat),
        out_specs=pl.BlockSpec(memory_space=pl.ANY),
        out_shape=jax.ShapeDtypeStruct((rows, cols * PLANE), flat[0].dtype),
        scratch_shapes=[pltpu.SemaphoreType.DMA((len(flat),))],
        compiler_params=pltpu.CompilerParams(vmem_limit_bytes=16 << 20),
        name="assemble",
    )(places, *flat)


def split_block(q, k, v, residue, rate, skip, w_out):
    rows, chan = q.shape
    modes = rate.shape[0]
    me = lax.axis_index("ctx")
    core = lax.axis_index("ch")
    spot, plane = me & (PLANE - 1), me // PLANE
    count = lax.axis_size("ctx")
    chunk, feats = w_out.shape
    cols = feats // PLANE
    wide = 2 * cols // 3
    speed = rate.reshape(modes, chan // LANES, LANES)

    def far(x):
        return exchange(x, "ctx", 2 * PLANE)

    def near(x):
        return exchange(x, "ctx", PLANE)

    middle = [i for i in range(count) if PLANE <= i < 3 * PLANE]

    def across(x):
        return lax.ppermute(x, "ctx", [(i, i ^ (3 * PLANE)) for i in middle])

    def outward(x):
        return lax.ppermute(x, "ctx", [(i, i ^ PLANE) for i in middle])

    def group(x, r):
        return lax.dynamic_slice_in_dim(x, (spot ^ r) * cols, cols, axis=1)

    def source_of(b):
        return jnp.where(b // 2 == core, b & 1, 2 + (b & 1))

    is_middle = jnp.where((plane == 0) | (plane == 3), 0, 1)
    flags = jnp.stack([source_of(plane ^ r) for r in range(4)] + [is_middle]).astype(jnp.int32)
    places = jnp.stack([spot ^ r for r in range(PLANE)]).astype(jnp.int32)

    def plane_scan(k, v, rate, speed):
        def fade(span):
            return jnp.exp(-speed * span)

        ends = end_states(k, v, rate)
        other = exchange(ends, "ctx", 1)
        both = jnp.where(x_later, fade(float(rows)) * other + ends, fade(float(rows)) * ends + other)
        before = jnp.where(x_later, other, 0.0)
        other = exchange(both, "ctx", 2)
        before = before + jnp.where(y_later, fade((spot & 1).astype(jnp.float32) * rows) * other, 0.0)
        both = jnp.where(y_later, fade(2.0 * rows) * other + both, fade(2.0 * rows) * both + other)
        return both, before

    x_later, y_later = (spot & 1) != 0, (spot & 2) != 0
    w0, w1, w2, w3 = tie(*[group(w_out, r) for r in range(PLANE)])
    f0, n0 = far(w0), near(w0)
    both, before = box(plane_scan, k, v, rate, speed)
    f0, n0, w0, w1, w2, w3, both, before = tie(f0, n0, w0, w1, w2, w3, both, before)

    arrived = [exchange(w, "ctx", r + 1) for r, w in enumerate((w1, w2, w3))]
    decay = jnp.exp(-speed * float(PLANE * rows))
    last = shift_ctx(both, PLANE)
    earlier = shift_ctx(both + decay * last, 2 * PLANE)
    f0, w0, earlier = tie(f0, w0, earlier)
    out0, mid0 = outward(f0), across(w0)
    gated = gated_conv(q, k, v, rate, residue, skip, before, (last, earlier, spot))
    rest = jnp.concatenate(arrived)
    gated, rest, out0, mid0 = tie(gated, rest, out0, mid0)

    fr, nr = far(rest), near(rest)
    ours = [gated] + [exchange(gated, "ctx", r) for r in range(1, PLANE)]
    restA, restB = rest[:, :wide], rest[:, wide:]
    ours = list(tie(*ours))
    theirs = [exchange(x, "ch", 1) for x in ours[1:]]
    fr, nr, rest, restA, restB, flags, places, *held = tie(fr, nr, rest, restA, restB, flags, places, *ours, *theirs)
    ours, theirs = held[:PLANE], held[PLANE:]

    outA, midA = outward(fr[:, :wide]), across(restA)
    theirs = [exchange(ours[0], "ch", 1)] + theirs
    blocks = [
        (0, None, [((w0,), 0), ((rest,), 0)]),
        (1, None, [((n0,), 0), ((nr,), 0)]),
        (2, None, [((f0,), 0), ((fr,), 0)]),
    ]
    accA, accB = product(flags, places, ours, theirs, blocks, None, [wide, cols - wide], jnp.float32)
    frB = fr[:, wide:]
    outA, midA, frB, restB, *accs = tie(outA, midA, frB, restB, *accA, *accB)
    accA, accB = accs[:PLANE], accs[PLANE:]

    outB, midB = outward(frB), across(restB)

    def finish(first, out1, mid1, accs):
        blocks = [(3, 4, [((out0, mid0), first), ((out1, mid1), 0)])]
        (made,) = product(flags, places, ours, theirs, blocks, accs, [accs[0].shape[1]], jnp.bfloat16)
        return [made[0]] + [exchange(made[r], "ctx", r) for r in range(1, PLANE)]

    return assemble(places, [finish(0, outA, midA, accA), finish(wide, outB, midB, accB)])


def body(q, k, v, residue, rate, skip, w_out):
    rows, chan = q.shape
    modes = rate.shape[0]
    groups = chan // LANES
    count, cores = lax.axis_size("ctx"), lax.axis_size("ch")
    chunk, feats = w_out.shape
    split = (
        count == 4 * PLANE
        and cores == 2
        and chan == 8 * chunk
        and chunk % LANES == 0
        and feats % (6 * PLANE * LANES) == 0
    )
    skip = skip.reshape(groups, LANES)
    if split:
        return split_block(q, k, v, residue, rate, skip, w_out)
    ends = end_states(k, v, rate)
    enter = entering_states(ends, rate.reshape(modes, groups, LANES), rows)
    gated = gated_conv(q, k, v, rate, residue, skip, enter)
    gated = gated.transpose(1, 0, 2).reshape(rows, chan)
    full_gated = lax.all_gather(gated, "ch", axis=1, tiled=True)
    w_full = lax.all_gather(w_out, "ctx", axis=0, tiled=True)
    mixed = jnp.dot(full_gated, w_full, preferred_element_type=jnp.float32)
    return mixed.astype(jnp.bfloat16)


def solution(mesh):
    placed = (
        P("ctx", "ch"),
        P("ctx", "ch"),
        P("ctx", "ch"),
        P(None, "ch"),
        P(None, "ch"),
        P("ch"),
        P("ctx", "ch"),
    )
    return jax.shard_map(
        body, mesh=mesh, in_specs=placed, out_specs=P("ctx", "ch"), check_vma=False
    )
```

```python
import jax
import jax.numpy as jnp
from jax import lax
from jax.experimental import pallas as pl
from jax.experimental.pallas import tpu as pltpu
from jax.sharding import PartitionSpec as P

LANES = 128
RADIX = 4
PLANE = 4
VMEM_BYTES = 60 << 20


def spread_signal(k_ref, v_ref, sig_ref):
    rows, width = k_ref.shape
    groups = width // LANES
    for g in range(groups):
        cols = pl.ds(g * LANES, LANES)
        product = k_ref[:, cols].astype(jnp.float32) * v_ref[:, cols].astype(jnp.float32)
        sig_ref[pl.ds(g, rows, stride=groups), :] = product


def spread_modes(ref, out_ref):
    modes, width = ref.shape
    groups = width // LANES
    for g in range(groups):
        out_ref[pl.ds(g, modes, stride=groups), :] = ref[:, pl.ds(g * LANES, LANES)]


def ends_kernel(k_ref, v_ref, rate_ref, end_ref, sig_ref, mode_ref):
    rows, width = k_ref.shape
    modes, groups, _ = end_ref.shape
    spread_signal(k_ref, v_ref, sig_ref)
    spread_modes(rate_ref, mode_ref)
    decay = [jnp.exp(-mode_ref[pl.ds(m * groups, groups), :]) for m in range(modes)]

    def step(t, state):
        s = sig_ref[pl.ds(pl.multiple_of(t * groups, groups), groups), :]
        return tuple(d * h + s for d, h in zip(decay, state))

    zero = jnp.zeros((groups, LANES), jnp.float32)
    state = lax.fori_loop(0, rows, step, (zero,) * modes, unroll=8)
    for m in range(modes):
        end_ref[m] = state[m]


def conv_kernel(q_ref, k_ref, v_ref, rate_ref, residue_ref, skip_ref, enter_ref, *refs):
    *plane_refs, out_ref, sig_ref, conv_ref, mode_ref, weight_ref = refs
    rows, width = k_ref.shape
    modes, groups, _ = enter_ref.shape
    spread_signal(k_ref, v_ref, sig_ref)
    spread_modes(rate_ref, mode_ref)
    spread_modes(residue_ref, weight_ref)
    rates = [mode_ref[pl.ds(m * groups, groups), :] for m in range(modes)]
    decay = [jnp.exp(-rate) for rate in rates]
    weight = [weight_ref[pl.ds(m * groups, groups), :] * jnp.sqrt(2.0 * rate) for m, rate in enumerate(rates)]
    skip = skip_ref[...]
    enter = [enter_ref[m] for m in range(modes)]
    if plane_refs:
        *earlier_refs, spot_ref = plane_refs
        ahead = (spot_ref[0] * rows).astype(jnp.float32)
        for m, rate in enumerate(rates):
            for n, earlier_ref in enumerate(earlier_refs):
                enter[m] = enter[m] + jnp.exp(-rate * (ahead + float(n * PLANE * rows))) * earlier_ref[m]

    def step(t, state):
        at = pl.ds(pl.multiple_of(t * groups, groups), groups)
        s = sig_ref[at, :]
        state = tuple(d * h + s for d, h in zip(decay, state))
        terms = [c * h for c, h in zip(weight, state)] + [skip * s]
        while len(terms) > 1:
            terms = [sum(terms[i : i + 2]) for i in range(0, len(terms), 2)]
        conv_ref[at, :] = terms[0]
        return state

    lax.fori_loop(0, rows, step, tuple(enter), unroll=4)
    for g in range(groups):
        cols = pl.ds(g * LANES, LANES)
        conv = conv_ref[pl.ds(g, rows, stride=groups), :]
        out_ref[:, cols] = (q_ref[:, cols].astype(jnp.float32) * conv).astype(out_ref.dtype)


def block_specs(rows, modes, width):
    groups = width // LANES
    return (
        pl.BlockSpec((rows, width), lambda i: (0, i)),
        pl.BlockSpec((modes, width), lambda i: (0, i)),
        pl.BlockSpec((modes, groups, LANES), lambda i: (0, i, 0)),
        pl.BlockSpec((groups, LANES), lambda i: (i, 0)),
    )


def end_states(k, v, rate):
    rows, chan = k.shape
    modes = rate.shape[0]
    width = min(chan, 8 * LANES)
    wide, moded, state, _ = block_specs(rows, modes, width)
    return pl.pallas_call(
        ends_kernel,
        grid=(chan // width,),
        in_specs=[wide, wide, moded],
        out_specs=state,
        out_shape=jax.ShapeDtypeStruct((modes, chan // LANES, LANES), jnp.float32),
        scratch_shapes=[
            pltpu.VMEM((rows * width // LANES, LANES), jnp.float32),
            pltpu.VMEM((modes * width // LANES, LANES), jnp.float32),
        ],
        compiler_params=pltpu.CompilerParams(vmem_limit_bytes=VMEM_BYTES),
        cost_estimate=pl.CostEstimate(
            flops=2 * modes * rows * chan, bytes_accessed=4 * rows * chan, transcendentals=modes * chan
        ),
        name="end_states",
    )(k, v, rate)


def gated_conv(q, k, v, rate, residue, skip, enter, planes=None):
    rows, chan = k.shape
    modes = rate.shape[0]
    width = min(chan, 8 * LANES)
    wide, moded, state, single = block_specs(rows, modes, width)
    spread = pltpu.VMEM((rows * width // LANES, LANES), jnp.float32)
    moded_spread = pltpu.VMEM((modes * width // LANES, LANES), jnp.float32)
    extra, extra_specs = [], []
    if planes is not None:
        earlier, spot = planes
        extra = [*earlier, spot.reshape(1).astype(jnp.int32)]
        extra_specs = [state] * len(earlier) + [pl.BlockSpec(memory_space=pltpu.SMEM)]
    return pl.pallas_call(
        conv_kernel,
        grid=(chan // width,),
        in_specs=[wide, wide, wide, moded, moded, single, state] + extra_specs,
        out_specs=pl.BlockSpec((None, rows, width), lambda i: (i, 0, 0)),
        out_shape=jax.ShapeDtypeStruct((chan // width, rows, width), jnp.bfloat16),
        scratch_shapes=[spread, spread, moded_spread, moded_spread],
        compiler_params=pltpu.CompilerParams(vmem_limit_bytes=VMEM_BYTES),
        cost_estimate=pl.CostEstimate(
            flops=4 * modes * rows * chan, bytes_accessed=8 * rows * chan, transcendentals=2 * modes * chan
        ),
        name="gated_conv",
    )(q, k, v, rate, residue, skip, enter, *extra)


def shift_ctx(x, by):
    count = lax.axis_size("ctx")
    return lax.ppermute(x, "ctx", [(i, i + by) for i in range(count - by)])


def exchange(x, axis, flip):
    count = lax.axis_size(axis)
    return lax.ppermute(x, axis, [(i, i ^ flip) for i in range(count)])


def tie(*values):
    return lax.optimization_barrier(values)


def entering_states(ends, rate, rows):
    count = lax.axis_size("ctx")
    total = jnp.zeros_like(ends)
    for k in range(1, min(RADIX, count - 1) + 1):
        total = total + jnp.exp(-rate * float(rows * (k - 1))) * shift_ctx(ends, k)
    stride = RADIX
    while stride < count:
        base = total
        for k in range(1, RADIX):
            if stride * k < count:
                total = total + jnp.exp(-rate * float(rows * stride * k)) * shift_ctx(base, stride * k)
        stride *= RADIX
    return total


def box(fn, *args):
    once = (lax.axis_index("ctx") >= 0).astype(jnp.int32)
    shapes = jax.eval_shape(fn, *args)
    empty = pl.pallas_call(
        lambda *refs: None,
        out_specs=[pl.BlockSpec(memory_space=pl.ANY)] * len(shapes),
        out_shape=list(shapes),
        name="blank",
    )()

    def run(step, _):
        return fn(*tie(step, *args)[1:])

    return lax.fori_loop(0, once, run, tuple(empty))


def product(flags, places, ours, theirs, blocks, accs, widths, out_dtype):
    _, rows, depth = ours[0].shape
    chunk = depth // PLANE
    cols = sum(widths)
    count, parts = len(blocks), len(ours)
    outs = parts * len(widths)
    weights = [array for _, _, pieces in blocks for choices, _ in pieces for array in choices]
    accs = accs or []

    def kernel(flag_ref, place_ref, *refs):
        our_refs, their_refs, refs = refs[:parts], refs[parts : 2 * parts], refs[2 * parts :]
        weight_refs, refs = list(refs[: len(weights)]), refs[len(weights) :]
        acc_refs, out_refs = refs[: len(accs)], refs[len(accs) : len(accs) + outs]
        gated_buf, weight_buf, acc_buf, gated_sems, weight_sems, acc_sem = refs[-6:]

        def target(b, at):
            start = pl.multiple_of(b * depth + place_ref[at // chunk] * chunk, chunk)
            return weight_buf.at[pl.ds(start, chunk), :]

        for b, (flag, pick, pieces) in enumerate(blocks):
            row = 0
            for choices, col in pieces:
                for c in range(len(choices)):
                    ref = weight_refs.pop(0)
                    for at in range(0, ref.shape[0], chunk):
                        source = ref.at[pl.ds(at, chunk), pl.ds(col, cols)]
                        copy = pltpu.make_async_copy(source, target(b, row + at), weight_sems.at[b])
                        if pick is None:
                            copy.start()
                        else:
                            pl.when(flag_ref[pick] == c)(copy.start)
                row += choices[0].shape[0]
            half = flag_ref[flag] & 1
            for r in range(parts):
                for c, refs_of in enumerate((our_refs, their_refs)):
                    target_rows = gated_buf.at[b, pl.ds(r * rows, rows), :]
                    copy = pltpu.make_async_copy(refs_of[r].at[half], target_rows, gated_sems.at[b])
                    pl.when(flag_ref[flag] // 2 == c)(copy.start)
        for r, acc_ref in enumerate(acc_refs):
            pltpu.make_async_copy(acc_ref, acc_buf.at[r], acc_sem).start()
        for b in range(count):
            block = weight_buf.at[pl.ds(b * depth, depth), :]
            pltpu.make_async_copy(block, block, weight_sems.at[b]).wait()
            pltpu.make_async_copy(gated_buf.at[b], gated_buf.at[b], gated_sems.at[b]).wait()
            if accs and not b:
                pltpu.make_async_copy(acc_buf, acc_buf, acc_sem).wait()
            for col in range(0, cols, 2 * LANES):
                here = pl.ds(col, 2 * LANES)
                made = jnp.dot(
                    gated_buf[b], weight_buf[pl.ds(b * depth, depth), here], preferred_element_type=jnp.float32
                )
                part = 0 if col < widths[0] else 1
                inside = pl.ds(col - part * widths[0], 2 * LANES)
                for r in range(parts):
                    total = made[r * rows : (r + 1) * rows]
                    out_ref = out_refs[part * parts + r]
                    if b:
                        total = total + out_ref[:, inside]
                    elif accs:
                        total = total + acc_buf[r, :, here]
                    out_ref[:, inside] = total.astype(out_dtype)

    smem = pl.BlockSpec(memory_space=pltpu.SMEM)
    anywhere = pl.BlockSpec(memory_space=pl.ANY)
    made = pl.pallas_call(
        kernel,
        in_specs=[smem, smem] + [anywhere] * (2 * parts + len(weights) + len(accs)),
        out_specs=[pl.BlockSpec(memory_space=pltpu.VMEM)] * outs,
        out_shape=[jax.ShapeDtypeStruct((rows, width), out_dtype) for width in widths for _ in range(parts)],
        scratch_shapes=[
            pltpu.VMEM((count, parts * rows, depth), jnp.bfloat16),
            pltpu.VMEM((count * depth, cols), jnp.bfloat16),
            pltpu.VMEM((len(accs), *accs[0].shape) if accs else (8, LANES), jnp.float32),
            pltpu.SemaphoreType.DMA((count,)),
            pltpu.SemaphoreType.DMA((count,)),
            pltpu.SemaphoreType.DMA,
        ],
        compiler_params=pltpu.CompilerParams(vmem_limit_bytes=VMEM_BYTES),
        cost_estimate=pl.CostEstimate(
            flops=2 * parts * rows * depth * count * cols,
            bytes_accessed=2 * count * depth * (parts * rows + cols),
            transcendentals=0,
        ),
        name="product",
    )(flags, places, *ours, *theirs, *weights, *accs)
    return [list(made[at : at + parts]) for at in range(0, outs, parts)]


def assemble(places, parts):
    rows = parts[0][0].shape[0]
    widths = [part[0].shape[1] for part in parts]
    cols = sum(widths)
    flat = [piece for part in parts for piece in part]

    def kernel(place_ref, *refs):
        *piece_refs, out_ref, sems = refs
        copies = []
        first = 0
        for part, width in enumerate(widths):
            for r in range(PLANE):
                at = part * PLANE + r
                start = pl.multiple_of(place_ref[r] * cols + first, LANES)
                target = out_ref.at[:, pl.ds(start, width)]
                copies.append(pltpu.make_async_copy(piece_refs[at], target, sems.at[at]))
                copies[-1].start()
            first += width
        for copy in copies:
            copy.wait()

    return pl.pallas_call(
        kernel,
        in_specs=[pl.BlockSpec(memory_space=pltpu.SMEM)] + [pl.BlockSpec(memory_space=pltpu.VMEM)] * len(flat),
        out_specs=pl.BlockSpec(memory_space=pl.ANY),
        out_shape=jax.ShapeDtypeStruct((rows, cols * PLANE), flat[0].dtype),
        scratch_shapes=[pltpu.SemaphoreType.DMA((len(flat),))],
        compiler_params=pltpu.CompilerParams(vmem_limit_bytes=16 << 20),
        name="assemble",
    )(places, *flat)


def split_block(q, k, v, residue, rate, skip, w_out):
    rows, chan = q.shape
    modes = rate.shape[0]
    me = lax.axis_index("ctx")
    core = lax.axis_index("ch")
    spot, plane = me & (PLANE - 1), me // PLANE
    count = lax.axis_size("ctx")
    chunk, feats = w_out.shape
    cols = feats // PLANE
    speed = rate.reshape(modes, chan // LANES, LANES)

    def far(x):
        return exchange(x, "ctx", 2 * PLANE)

    def near(x):
        return exchange(x, "ctx", PLANE)

    middle = [i for i in range(count) if PLANE <= i < 3 * PLANE]

    def across(x):
        return lax.ppermute(x, "ctx", [(i, i ^ (3 * PLANE)) for i in middle])

    def outward(x):
        return lax.ppermute(x, "ctx", [(i, i ^ PLANE) for i in middle])

    def group(x, r):
        return lax.dynamic_slice_in_dim(x, (spot ^ r) * cols, cols, axis=1)

    def source_of(b):
        return jnp.where(b // 2 == core, b & 1, 2 + (b & 1))

    is_middle = jnp.where((plane == 0) | (plane == 3), 0, 1)
    flags = jnp.stack([source_of(plane ^ r) for r in range(4)] + [is_middle]).astype(jnp.int32)
    places = jnp.stack([spot ^ r for r in range(PLANE)]).astype(jnp.int32)

    def plane_scan(k, v, rate, speed):
        def fade(span):
            return jnp.exp(-speed * span)

        ends = end_states(k, v, rate)
        other = exchange(ends, "ctx", 1)
        both = jnp.where(x_later, fade(float(rows)) * other + ends, fade(float(rows)) * ends + other)
        before = jnp.where(x_later, other, 0.0)
        other = exchange(both, "ctx", 2)
        before = before + jnp.where(y_later, fade((spot & 1).astype(jnp.float32) * rows) * other, 0.0)
        both = jnp.where(y_later, fade(2.0 * rows) * other + both, fade(2.0 * rows) * both + other)
        return both, before

    x_later, y_later = (spot & 1) != 0, (spot & 2) != 0
    w0, w1, w2, w3 = tie(*[group(w_out, r) for r in range(PLANE)])
    f0, n0 = far(w0), near(w0)
    both, before = box(plane_scan, k, v, rate, speed)
    f0, n0, w0, w1, w2, w3, both, before = tie(f0, n0, w0, w1, w2, w3, both, before)

    arrived = [exchange(w, "ctx", r + 1) for r, w in enumerate((w1, w2, w3))]
    earlier = [shift_ctx(both, PLANE * n) for n in range(1, 4)]
    f0, w0, *earlier = tie(f0, w0, *earlier)
    out0, mid0 = outward(f0), across(w0)
    gated = gated_conv(q, k, v, rate, residue, skip, before, (earlier, spot))
    rest = jnp.concatenate(arrived)
    gated, rest, out0, mid0 = tie(gated, rest, out0, mid0)

    fr, nr = far(rest), near(rest)
    ours = [gated] + [exchange(gated, "ctx", r) for r in range(1, PLANE)]
    ours = list(tie(*ours))
    theirs = [exchange(x, "ch", 1) for x in ours[1:]]
    fr, nr, rest, flags, places, *held = tie(fr, nr, rest, flags, places, *ours, *theirs)
    ours, theirs = held[:PLANE], held[PLANE:]

    out1, mid1 = outward(fr), across(rest)
    theirs = [exchange(ours[0], "ch", 1)] + theirs
    blocks = [
        (0, None, [((w0,), 0), ((rest,), 0)]),
        (1, None, [((n0,), 0), ((nr,), 0)]),
        (2, None, [((f0,), 0), ((fr,), 0)]),
    ]
    (accs,) = product(flags, places, ours, theirs, blocks, None, [cols], jnp.float32)
    out1, mid1, *accs = tie(out1, mid1, *accs)

    blocks = [(3, 4, [((out0, mid0), 0), ((out1, mid1), 0)])]

    def finish(*spots):
        chosen = [ours[r] for r in spots], [theirs[r] for r in spots]
        return product(flags, places, *chosen, blocks, [accs[r] for r in spots], [cols], jnp.bfloat16)[0]

    (made3,) = finish(3)
    back3 = exchange(made3, "ctx", 3)
    back3, made0, made1, made2 = tie(back3, *finish(0, 1, 2))
    return assemble(places, [[made0, exchange(made1, "ctx", 1), exchange(made2, "ctx", 2), back3]])


def body(q, k, v, residue, rate, skip, w_out):
    rows, chan = q.shape
    modes = rate.shape[0]
    groups = chan // LANES
    count, cores = lax.axis_size("ctx"), lax.axis_size("ch")
    chunk, feats = w_out.shape
    split = (
        count == 4 * PLANE
        and cores == 2
        and chan == 8 * chunk
        and chunk % LANES == 0
        and feats % (2 * PLANE * LANES) == 0
    )
    skip = skip.reshape(groups, LANES)
    if split:
        return split_block(q, k, v, residue, rate, skip, w_out)
    ends = end_states(k, v, rate)
    enter = entering_states(ends, rate.reshape(modes, groups, LANES), rows)
    gated = gated_conv(q, k, v, rate, residue, skip, enter)
    gated = gated.transpose(1, 0, 2).reshape(rows, chan)
    full_gated = lax.all_gather(gated, "ch", axis=1, tiled=True)
    w_full = lax.all_gather(w_out, "ctx", axis=0, tiled=True)
    mixed = jnp.dot(full_gated, w_full, preferred_element_type=jnp.float32)
    return mixed.astype(jnp.bfloat16)


def solution(mesh):
    placed = (
        P("ctx", "ch"),
        P("ctx", "ch"),
        P("ctx", "ch"),
        P(None, "ch"),
        P(None, "ch"),
        P("ch"),
        P("ctx", "ch"),
    )
    return jax.shard_map(
        body, mesh=mesh, in_specs=placed, out_specs=P("ctx", "ch"), check_vma=False
    )
```

```python
import jax
import jax.numpy as jnp
from jax import lax
from jax.experimental import pallas as pl
from jax.experimental.pallas import tpu as pltpu
from jax.sharding import PartitionSpec as P

LANES = 128
RADIX = 4
PLANE = 4
VMEM_BYTES = 60 << 20


def spread_signal(k_ref, v_ref, sig_ref):
    rows, width = k_ref.shape
    groups = width // LANES
    for g in range(groups):
        cols = pl.ds(g * LANES, LANES)
        product = k_ref[:, cols].astype(jnp.float32) * v_ref[:, cols].astype(jnp.float32)
        sig_ref[pl.ds(g, rows, stride=groups), :] = product


def spread_modes(ref, out_ref):
    modes, width = ref.shape
    groups = width // LANES
    for g in range(groups):
        out_ref[pl.ds(g, modes, stride=groups), :] = ref[:, pl.ds(g * LANES, LANES)]


def ends_kernel(k_ref, v_ref, rate_ref, end_ref, sig_ref, mode_ref):
    rows, width = k_ref.shape
    modes, groups, _ = end_ref.shape
    spread_signal(k_ref, v_ref, sig_ref)
    spread_modes(rate_ref, mode_ref)
    decay = [jnp.exp(-mode_ref[pl.ds(m * groups, groups), :]) for m in range(modes)]

    def step(t, state):
        s = sig_ref[pl.ds(pl.multiple_of(t * groups, groups), groups), :]
        return tuple(d * h + s for d, h in zip(decay, state))

    zero = jnp.zeros((groups, LANES), jnp.float32)
    state = lax.fori_loop(0, rows, step, (zero,) * modes, unroll=8)
    for m in range(modes):
        end_ref[m] = state[m]


def conv_kernel(q_ref, k_ref, v_ref, rate_ref, residue_ref, skip_ref, enter_ref, *refs):
    *plane_refs, out_ref, sig_ref, conv_ref, mode_ref, weight_ref = refs
    rows, width = k_ref.shape
    modes, groups, _ = enter_ref.shape
    spread_signal(k_ref, v_ref, sig_ref)
    spread_modes(rate_ref, mode_ref)
    spread_modes(residue_ref, weight_ref)
    rates = [mode_ref[pl.ds(m * groups, groups), :] for m in range(modes)]
    decay = [jnp.exp(-rate) for rate in rates]
    weight = [weight_ref[pl.ds(m * groups, groups), :] * jnp.sqrt(2.0 * rate) for m, rate in enumerate(rates)]
    skip = skip_ref[...]
    enter = [enter_ref[m] for m in range(modes)]
    if plane_refs:
        *earlier_refs, spot_ref = plane_refs
        ahead = (spot_ref[0] * rows).astype(jnp.float32)
        for m, rate in enumerate(rates):
            for n, earlier_ref in enumerate(earlier_refs):
                enter[m] = enter[m] + jnp.exp(-rate * (ahead + float(n * PLANE * rows))) * earlier_ref[m]

    def step(t, state):
        at = pl.ds(pl.multiple_of(t * groups, groups), groups)
        s = sig_ref[at, :]
        state = tuple(d * h + s for d, h in zip(decay, state))
        terms = [c * h for c, h in zip(weight, state)] + [skip * s]
        while len(terms) > 1:
            terms = [sum(terms[i : i + 2]) for i in range(0, len(terms), 2)]
        conv_ref[at, :] = terms[0]
        return state

    lax.fori_loop(0, rows, step, tuple(enter), unroll=4)
    for g in range(groups):
        cols = pl.ds(g * LANES, LANES)
        conv = conv_ref[pl.ds(g, rows, stride=groups), :]
        out_ref[:, cols] = (q_ref[:, cols].astype(jnp.float32) * conv).astype(out_ref.dtype)


def block_specs(rows, modes, width):
    groups = width // LANES
    return (
        pl.BlockSpec((rows, width), lambda i: (0, i)),
        pl.BlockSpec((modes, width), lambda i: (0, i)),
        pl.BlockSpec((modes, groups, LANES), lambda i: (0, i, 0)),
        pl.BlockSpec((groups, LANES), lambda i: (i, 0)),
    )


def end_states(k, v, rate):
    rows, chan = k.shape
    modes = rate.shape[0]
    width = min(chan, 8 * LANES)
    wide, moded, state, _ = block_specs(rows, modes, width)
    return pl.pallas_call(
        ends_kernel,
        grid=(chan // width,),
        in_specs=[wide, wide, moded],
        out_specs=state,
        out_shape=jax.ShapeDtypeStruct((modes, chan // LANES, LANES), jnp.float32),
        scratch_shapes=[
            pltpu.VMEM((rows * width // LANES, LANES), jnp.float32),
            pltpu.VMEM((modes * width // LANES, LANES), jnp.float32),
        ],
        compiler_params=pltpu.CompilerParams(vmem_limit_bytes=VMEM_BYTES),
        cost_estimate=pl.CostEstimate(
            flops=2 * modes * rows * chan, bytes_accessed=4 * rows * chan, transcendentals=modes * chan
        ),
        name="end_states",
    )(k, v, rate)


def gated_conv(q, k, v, rate, residue, skip, enter, planes=None):
    rows, chan = k.shape
    modes = rate.shape[0]
    width = min(chan, 8 * LANES)
    wide, moded, state, single = block_specs(rows, modes, width)
    spread = pltpu.VMEM((rows * width // LANES, LANES), jnp.float32)
    moded_spread = pltpu.VMEM((modes * width // LANES, LANES), jnp.float32)
    extra, extra_specs = [], []
    if planes is not None:
        earlier, spot = planes
        extra = [*earlier, spot.reshape(1).astype(jnp.int32)]
        extra_specs = [state] * len(earlier) + [pl.BlockSpec(memory_space=pltpu.SMEM)]
    return pl.pallas_call(
        conv_kernel,
        grid=(chan // width,),
        in_specs=[wide, wide, wide, moded, moded, single, state] + extra_specs,
        out_specs=pl.BlockSpec((None, rows, width), lambda i: (i, 0, 0)),
        out_shape=jax.ShapeDtypeStruct((chan // width, rows, width), jnp.bfloat16),
        scratch_shapes=[spread, spread, moded_spread, moded_spread],
        compiler_params=pltpu.CompilerParams(vmem_limit_bytes=VMEM_BYTES),
        cost_estimate=pl.CostEstimate(
            flops=4 * modes * rows * chan, bytes_accessed=8 * rows * chan, transcendentals=2 * modes * chan
        ),
        name="gated_conv",
    )(q, k, v, rate, residue, skip, enter, *extra)


def shift_ctx(x, by):
    count = lax.axis_size("ctx")
    return lax.ppermute(x, "ctx", [(i, i + by) for i in range(count - by)])


def exchange(x, axis, flip):
    count = lax.axis_size(axis)
    return lax.ppermute(x, axis, [(i, i ^ flip) for i in range(count)])


def tie(*values):
    return lax.optimization_barrier(values)


def entering_states(ends, rate, rows):
    count = lax.axis_size("ctx")
    total = jnp.zeros_like(ends)
    for k in range(1, min(RADIX, count - 1) + 1):
        total = total + jnp.exp(-rate * float(rows * (k - 1))) * shift_ctx(ends, k)
    stride = RADIX
    while stride < count:
        base = total
        for k in range(1, RADIX):
            if stride * k < count:
                total = total + jnp.exp(-rate * float(rows * stride * k)) * shift_ctx(base, stride * k)
        stride *= RADIX
    return total


def box(fn, *args):
    once = (lax.axis_index("ctx") >= 0).astype(jnp.int32)
    shapes = jax.eval_shape(fn, *args)
    empty = pl.pallas_call(
        lambda *refs: None,
        out_specs=[pl.BlockSpec(memory_space=pl.ANY)] * len(shapes),
        out_shape=list(shapes),
        name="blank",
    )()

    def run(step, _):
        return fn(*tie(step, *args)[1:])

    return lax.fori_loop(0, once, run, tuple(empty))


def product(flags, places, ours, theirs, blocks, acc, out_dtype):
    _, _, rows, depth = ours.shape
    chunk = depth // PLANE
    cols = blocks[0][2][0][0][0].shape[1]
    count = len(blocks)
    weights = [array for _, _, pieces in blocks for choices, _ in pieces for array in choices]
    accs = [] if acc is None else [acc]

    def kernel(flag_ref, place_ref, our_ref, their_ref, *refs):
        weight_refs, refs = list(refs[: len(weights)]), refs[len(weights) :]
        acc_refs, out_ref = refs[: len(accs)], refs[len(accs)]
        gated_buf, weight_buf, acc_buf, gated_sems, weight_sems, acc_sem = refs[-6:]

        def target(b, at):
            start = pl.multiple_of(b * depth + place_ref[at // chunk] * chunk, chunk)
            return weight_buf.at[pl.ds(start, chunk), :]

        for b, (flag, pick, pieces) in enumerate(blocks):
            row = 0
            for choices, col in pieces:
                for c in range(len(choices)):
                    ref = weight_refs.pop(0)
                    for at in range(0, ref.shape[0], chunk):
                        source = ref.at[pl.ds(at, chunk), pl.ds(col, cols)]
                        copy = pltpu.make_async_copy(source, target(b, row + at), weight_sems.at[b])
                        if pick is None:
                            copy.start()
                        else:
                            pl.when(flag_ref[pick] == c)(copy.start)
                row += choices[0].shape[0]
            half = flag_ref[flag] & 1
            for c, ref in enumerate((our_ref, their_ref)):
                copy = pltpu.make_async_copy(ref.at[:, half], gated_buf.at[b], gated_sems.at[b])
                pl.when(flag_ref[flag] // 2 == c)(copy.start)
        for acc_ref in acc_refs:
            pltpu.make_async_copy(acc_ref, acc_buf, acc_sem).start()
        for b in range(count):
            block = weight_buf.at[pl.ds(b * depth, depth), :]
            pltpu.make_async_copy(block, block, weight_sems.at[b]).wait()
            pltpu.make_async_copy(gated_buf.at[b], gated_buf.at[b], gated_sems.at[b]).wait()
            if accs and not b:
                pltpu.make_async_copy(acc_buf, acc_buf, acc_sem).wait()
            for col in range(0, cols, 2 * LANES):
                here = pl.ds(col, 2 * LANES)
                made = jnp.dot(
                    gated_buf[b].reshape(PLANE * rows, depth),
                    weight_buf[pl.ds(b * depth, depth), here],
                    preferred_element_type=jnp.float32,
                ).reshape(PLANE, rows, 2 * LANES)
                if b or accs:
                    made = made + acc_buf[:, :, here]
                if b < count - 1:
                    acc_buf[:, :, here] = made
                else:
                    out_ref[:, :, here] = made.astype(out_dtype)

    smem = pl.BlockSpec(memory_space=pltpu.SMEM)
    anywhere = pl.BlockSpec(memory_space=pl.ANY)
    return pl.pallas_call(
        kernel,
        in_specs=[smem, smem] + [anywhere] * (2 + len(weights) + len(accs)),
        out_specs=pl.BlockSpec(memory_space=pltpu.VMEM),
        out_shape=jax.ShapeDtypeStruct((PLANE, rows, cols), out_dtype),
        scratch_shapes=[
            pltpu.VMEM((count, PLANE, rows, depth), jnp.bfloat16),
            pltpu.VMEM((count * depth, cols), jnp.bfloat16),
            pltpu.VMEM((PLANE, rows, cols), jnp.float32),
            pltpu.SemaphoreType.DMA((count,)),
            pltpu.SemaphoreType.DMA((count,)),
            pltpu.SemaphoreType.DMA,
        ],
        compiler_params=pltpu.CompilerParams(vmem_limit_bytes=VMEM_BYTES),
        cost_estimate=pl.CostEstimate(
            flops=2 * PLANE * rows * depth * count * cols,
            bytes_accessed=2 * count * depth * (PLANE * rows + cols),
            transcendentals=0,
        ),
        name="product",
    )(flags, places, ours, theirs, *weights, *accs)


def side_by_side(pieces):
    count, rows, cols = pieces.shape

    def kernel(pieces_ref, out_ref):
        out_ref[...] = pieces_ref[...]

    return pl.pallas_call(
        kernel,
        grid=(count,),
        in_specs=[pl.BlockSpec((None, rows, cols), lambda i: (i, 0, 0))],
        out_specs=pl.BlockSpec((rows, cols), lambda i: (0, i)),
        out_shape=jax.ShapeDtypeStruct((rows, cols * count), pieces.dtype),
        name="side_by_side",
    )(pieces)


def split_block(q, k, v, residue, rate, skip, w_out):
    rows, chan = q.shape
    modes = rate.shape[0]
    me = lax.axis_index("ctx")
    core = lax.axis_index("ch")
    spot, plane = me & (PLANE - 1), me // PLANE
    count = lax.axis_size("ctx")
    chunk, feats = w_out.shape
    cols = feats // PLANE
    speed = rate.reshape(modes, chan // LANES, LANES)

    def far(x):
        return exchange(x, "ctx", 2 * PLANE)

    def near(x):
        return exchange(x, "ctx", PLANE)

    middle = [i for i in range(count) if PLANE <= i < 3 * PLANE]

    def across(x):
        return lax.ppermute(x, "ctx", [(i, i ^ (3 * PLANE)) for i in middle])

    def outward(x):
        return lax.ppermute(x, "ctx", [(i, i ^ PLANE) for i in middle])

    def group(x, r):
        return lax.dynamic_slice_in_dim(x, (spot ^ r) * cols, cols, axis=1)

    def source_of(b):
        return jnp.where(b // 2 == core, b & 1, 2 + (b & 1))

    is_middle = jnp.where((plane == 0) | (plane == 3), 0, 1)
    flags = jnp.stack([source_of(plane ^ r) for r in range(4)] + [is_middle]).astype(jnp.int32)
    places = jnp.stack([spot ^ r for r in range(PLANE)]).astype(jnp.int32)

    def plane_scan(k, v, rate, speed):
        def fade(span):
            return jnp.exp(-speed * span)

        ends = end_states(k, v, rate)
        other = exchange(ends, "ctx", 1)
        both = jnp.where(x_later, fade(float(rows)) * other + ends, fade(float(rows)) * ends + other)
        before = jnp.where(x_later, other, 0.0)
        other = exchange(both, "ctx", 2)
        before = before + jnp.where(y_later, fade((spot & 1).astype(jnp.float32) * rows) * other, 0.0)
        both = jnp.where(y_later, fade(2.0 * rows) * other + both, fade(2.0 * rows) * both + other)
        return both, before

    x_later, y_later = (spot & 1) != 0, (spot & 2) != 0
    w0, w1, w2, w3 = tie(*[group(w_out, r) for r in range(PLANE)])
    f0, n0 = far(w0), near(w0)
    both, before = box(plane_scan, k, v, rate, speed)
    f0, n0, w0, w1, w2, w3, both, before = tie(f0, n0, w0, w1, w2, w3, both, before)

    arrived = [exchange(w, "ctx", r + 1) for r, w in enumerate((w1, w2, w3))]
    decay = jnp.exp(-speed * float(PLANE * rows))
    last = shift_ctx(both, PLANE)
    earlier = shift_ctx(both + decay * last, 2 * PLANE)
    f0, w0, earlier = tie(f0, w0, earlier)
    out0, mid0 = outward(f0), across(w0)
    gated = gated_conv(q, k, v, rate, residue, skip, before, ([last, earlier], spot))
    rest = jnp.concatenate(arrived)
    gated, rest, out0, mid0 = tie(gated, rest, out0, mid0)

    fr, nr = far(rest), near(rest)
    planes = [list(range(first, first + PLANE)) for first in range(0, count, PLANE)]
    ours = lax.all_gather(gated, "ctx", axis_index_groups=planes)
    fr, nr, rest, flags, places, ours = tie(fr, nr, rest, flags, places, ours)

    out1, mid1 = outward(fr), across(rest)
    theirs = exchange(ours, "ch", 1)
    blocks = [
        (0, None, [((w0,), 0), ((rest,), 0)]),
        (1, None, [((n0,), 0), ((nr,), 0)]),
        (2, None, [((f0,), 0), ((fr,), 0)]),
    ]
    accs = product(flags, places, ours, theirs, blocks, None, jnp.float32)
    out1, mid1, accs = tie(out1, mid1, accs)

    blocks = [(3, 4, [((out0, mid0), 0), ((out1, mid1), 0)])]
    made = product(flags, places, ours, theirs, blocks, accs, jnp.bfloat16)
    back = lax.all_to_all(made, "ctx", 0, 0, axis_index_groups=planes)
    return side_by_side(back)


def body(q, k, v, residue, rate, skip, w_out):
    rows, chan = q.shape
    modes = rate.shape[0]
    groups = chan // LANES
    count, cores = lax.axis_size("ctx"), lax.axis_size("ch")
    chunk, feats = w_out.shape
    split = (
        count == 4 * PLANE
        and cores == 2
        and chan == 8 * chunk
        and chunk % LANES == 0
        and feats % (2 * PLANE * LANES) == 0
    )
    skip = skip.reshape(groups, LANES)
    if split:
        return split_block(q, k, v, residue, rate, skip, w_out)
    ends = end_states(k, v, rate)
    enter = entering_states(ends, rate.reshape(modes, groups, LANES), rows)
    gated = gated_conv(q, k, v, rate, residue, skip, enter)
    gated = gated.transpose(1, 0, 2).reshape(rows, chan)
    full_gated = lax.all_gather(gated, "ch", axis=1, tiled=True)
    w_full = lax.all_gather(w_out, "ctx", axis=0, tiled=True)
    mixed = jnp.dot(full_gated, w_full, preferred_element_type=jnp.float32)
    return mixed.astype(jnp.bfloat16)


def solution(mesh):
    placed = (
        P("ctx", "ch"),
        P("ctx", "ch"),
        P("ctx", "ch"),
        P(None, "ch"),
        P(None, "ch"),
        P("ch"),
        P("ctx", "ch"),
    )
    return jax.shard_map(
        body, mesh=mesh, in_specs=placed, out_specs=P("ctx", "ch"), check_vma=False
    )
```

```python
import jax
import jax.numpy as jnp
from jax import lax
from jax.experimental import pallas as pl
from jax.experimental.pallas import tpu as pltpu
from jax.sharding import PartitionSpec as P

LANES = 128
RADIX = 4
PLANE = 4
VMEM_BYTES = 60 << 20


def spread_signal(k_ref, v_ref, sig_ref):
    rows, width = k_ref.shape
    groups = width // LANES
    for g in range(groups):
        cols = pl.ds(g * LANES, LANES)
        product = k_ref[:, cols].astype(jnp.float32) * v_ref[:, cols].astype(jnp.float32)
        sig_ref[pl.ds(g, rows, stride=groups), :] = product


def spread_modes(ref, out_ref):
    modes, width = ref.shape
    groups = width // LANES
    for g in range(groups):
        out_ref[pl.ds(g, modes, stride=groups), :] = ref[:, pl.ds(g * LANES, LANES)]


def ends_kernel(k_ref, v_ref, rate_ref, end_ref, sig_ref, mode_ref):
    rows, width = k_ref.shape
    modes, groups, _ = end_ref.shape
    spread_signal(k_ref, v_ref, sig_ref)
    spread_modes(rate_ref, mode_ref)
    decay = [jnp.exp(-mode_ref[pl.ds(m * groups, groups), :]) for m in range(modes)]

    def step(t, state):
        s = sig_ref[pl.ds(pl.multiple_of(t * groups, groups), groups), :]
        return tuple(d * h + s for d, h in zip(decay, state))

    zero = jnp.zeros((groups, LANES), jnp.float32)
    state = lax.fori_loop(0, rows, step, (zero,) * modes, unroll=8)
    for m in range(modes):
        end_ref[m] = state[m]


def conv_kernel(q_ref, k_ref, v_ref, rate_ref, residue_ref, skip_ref, enter_ref, *refs):
    *plane_refs, out_ref, sig_ref, conv_ref, mode_ref, weight_ref = refs
    rows, width = k_ref.shape
    modes, groups, _ = enter_ref.shape
    spread_signal(k_ref, v_ref, sig_ref)
    spread_modes(rate_ref, mode_ref)
    spread_modes(residue_ref, weight_ref)
    rates = [mode_ref[pl.ds(m * groups, groups), :] for m in range(modes)]
    decay = [jnp.exp(-rate) for rate in rates]
    weight = [weight_ref[pl.ds(m * groups, groups), :] * jnp.sqrt(2.0 * rate) for m, rate in enumerate(rates)]
    skip = skip_ref[...]
    enter = [enter_ref[m] for m in range(modes)]
    if plane_refs:
        *earlier_refs, spot_ref = plane_refs
        ahead = (spot_ref[0] * rows).astype(jnp.float32)
        for m, rate in enumerate(rates):
            for n, earlier_ref in enumerate(earlier_refs):
                enter[m] = enter[m] + jnp.exp(-rate * (ahead + float(n * PLANE * rows))) * earlier_ref[m]

    def step(t, state):
        at = pl.ds(pl.multiple_of(t * groups, groups), groups)
        s = sig_ref[at, :]
        state = tuple(d * h + s for d, h in zip(decay, state))
        terms = [c * h for c, h in zip(weight, state)] + [skip * s]
        while len(terms) > 1:
            terms = [sum(terms[i : i + 2]) for i in range(0, len(terms), 2)]
        conv_ref[at, :] = terms[0]
        return state

    lax.fori_loop(0, rows, step, tuple(enter), unroll=4)
    for g in range(groups):
        cols = pl.ds(g * LANES, LANES)
        conv = conv_ref[pl.ds(g, rows, stride=groups), :]
        out_ref[:, cols] = (q_ref[:, cols].astype(jnp.float32) * conv).astype(out_ref.dtype)


def block_specs(rows, modes, width):
    groups = width // LANES
    return (
        pl.BlockSpec((rows, width), lambda i: (0, i)),
        pl.BlockSpec((modes, width), lambda i: (0, i)),
        pl.BlockSpec((modes, groups, LANES), lambda i: (0, i, 0)),
        pl.BlockSpec((groups, LANES), lambda i: (i, 0)),
    )


def end_states(k, v, rate):
    rows, chan = k.shape
    modes = rate.shape[0]
    width = min(chan, 8 * LANES)
    wide, moded, state, _ = block_specs(rows, modes, width)
    return pl.pallas_call(
        ends_kernel,
        grid=(chan // width,),
        in_specs=[wide, wide, moded],
        out_specs=state,
        out_shape=jax.ShapeDtypeStruct((modes, chan // LANES, LANES), jnp.float32),
        scratch_shapes=[
            pltpu.VMEM((rows * width // LANES, LANES), jnp.float32),
            pltpu.VMEM((modes * width // LANES, LANES), jnp.float32),
        ],
        compiler_params=pltpu.CompilerParams(vmem_limit_bytes=VMEM_BYTES),
        cost_estimate=pl.CostEstimate(
            flops=2 * modes * rows * chan, bytes_accessed=4 * rows * chan, transcendentals=modes * chan
        ),
        name="end_states",
    )(k, v, rate)


def gated_conv(q, k, v, rate, residue, skip, enter, planes=None):
    rows, chan = k.shape
    modes = rate.shape[0]
    width = min(chan, 8 * LANES)
    wide, moded, state, single = block_specs(rows, modes, width)
    spread = pltpu.VMEM((rows * width // LANES, LANES), jnp.float32)
    moded_spread = pltpu.VMEM((modes * width // LANES, LANES), jnp.float32)
    extra, extra_specs = [], []
    if planes is not None:
        earlier, spot = planes
        extra = [*earlier, spot.reshape(1).astype(jnp.int32)]
        extra_specs = [state] * len(earlier) + [pl.BlockSpec(memory_space=pltpu.SMEM)]
    return pl.pallas_call(
        conv_kernel,
        grid=(chan // width,),
        in_specs=[wide, wide, wide, moded, moded, single, state] + extra_specs,
        out_specs=pl.BlockSpec((None, rows, width), lambda i: (i, 0, 0)),
        out_shape=jax.ShapeDtypeStruct((chan // width, rows, width), jnp.bfloat16),
        scratch_shapes=[spread, spread, moded_spread, moded_spread],
        compiler_params=pltpu.CompilerParams(vmem_limit_bytes=VMEM_BYTES),
        cost_estimate=pl.CostEstimate(
            flops=4 * modes * rows * chan, bytes_accessed=8 * rows * chan, transcendentals=2 * modes * chan
        ),
        name="gated_conv",
    )(q, k, v, rate, residue, skip, enter, *extra)


def shift_ctx(x, by):
    count = lax.axis_size("ctx")
    return lax.ppermute(x, "ctx", [(i, i + by) for i in range(count - by)])


def exchange(x, axis, flip):
    count = lax.axis_size(axis)
    return lax.ppermute(x, axis, [(i, i ^ flip) for i in range(count)])


def tie(*values):
    return lax.optimization_barrier(values)


def entering_states(ends, rate, rows):
    count = lax.axis_size("ctx")
    total = jnp.zeros_like(ends)
    for k in range(1, min(RADIX, count - 1) + 1):
        total = total + jnp.exp(-rate * float(rows * (k - 1))) * shift_ctx(ends, k)
    stride = RADIX
    while stride < count:
        base = total
        for k in range(1, RADIX):
            if stride * k < count:
                total = total + jnp.exp(-rate * float(rows * stride * k)) * shift_ctx(base, stride * k)
        stride *= RADIX
    return total


def box(fn, *args):
    once = (lax.axis_index("ctx") >= 0).astype(jnp.int32)
    shapes = jax.eval_shape(fn, *args)
    empty = pl.pallas_call(
        lambda *refs: None,
        out_specs=[pl.BlockSpec(memory_space=pl.ANY)] * len(shapes),
        out_shape=list(shapes),
        name="blank",
    )()

    def run(step, _):
        return fn(*tie(step, *args)[1:])

    return lax.fori_loop(0, once, run, tuple(empty))


def product(flags, places, ours, theirs, blocks, accs, widths, out_dtype):
    _, rows, depth = ours[0].shape
    chunk = depth // PLANE
    cols = sum(widths)
    count, parts = len(blocks), len(ours)
    outs = parts * len(widths)
    weights = [array for _, _, pieces in blocks for choices, _ in pieces for array in choices]
    accs = accs or []

    def kernel(flag_ref, place_ref, *refs):
        our_refs, their_refs, refs = refs[:parts], refs[parts : 2 * parts], refs[2 * parts :]
        weight_refs, refs = list(refs[: len(weights)]), refs[len(weights) :]
        acc_refs, out_refs = refs[: len(accs)], refs[len(accs) : len(accs) + outs]
        gated_buf, weight_buf, acc_buf, gated_sems, weight_sems, acc_sem = refs[-6:]

        def target(b, at):
            start = pl.multiple_of(b * depth + place_ref[at // chunk] * chunk, chunk)
            return weight_buf.at[pl.ds(start, chunk), :]

        for b, (flag, pick, pieces) in enumerate(blocks):
            row = 0
            for choices, col in pieces:
                for c in range(len(choices)):
                    ref = weight_refs.pop(0)
                    for at in range(0, ref.shape[0], chunk):
                        source = ref.at[pl.ds(at, chunk), pl.ds(col, cols)]
                        copy = pltpu.make_async_copy(source, target(b, row + at), weight_sems.at[b])
                        if pick is None:
                            copy.start()
                        else:
                            pl.when(flag_ref[pick] == c)(copy.start)
                row += choices[0].shape[0]
            half = flag_ref[flag] & 1
            for r in range(parts):
                for c, refs_of in enumerate((our_refs, their_refs)):
                    target_rows = gated_buf.at[b, pl.ds(r * rows, rows), :]
                    copy = pltpu.make_async_copy(refs_of[r].at[half], target_rows, gated_sems.at[b])
                    pl.when(flag_ref[flag] // 2 == c)(copy.start)
        for r, acc_ref in enumerate(acc_refs):
            pltpu.make_async_copy(acc_ref, acc_buf.at[r], acc_sem).start()
        for b in range(count):
            block = weight_buf.at[pl.ds(b * depth, depth), :]
            pltpu.make_async_copy(block, block, weight_sems.at[b]).wait()
            pltpu.make_async_copy(gated_buf.at[b], gated_buf.at[b], gated_sems.at[b]).wait()
            if accs and not b:
                pltpu.make_async_copy(acc_buf, acc_buf, acc_sem).wait()
            for col in range(0, cols, 2 * LANES):
                here = pl.ds(col, 2 * LANES)
                made = jnp.dot(
                    gated_buf[b], weight_buf[pl.ds(b * depth, depth), here], preferred_element_type=jnp.float32
                )
                part = 0 if col < widths[0] else 1
                inside = pl.ds(col - part * widths[0], 2 * LANES)
                for r in range(parts):
                    total = made[r * rows : (r + 1) * rows]
                    out_ref = out_refs[part * parts + r]
                    if b:
                        total = total + out_ref[:, inside]
                    elif accs:
                        total = total + acc_buf[r, :, here]
                    out_ref[:, inside] = total.astype(out_dtype)

    smem = pl.BlockSpec(memory_space=pltpu.SMEM)
    anywhere = pl.BlockSpec(memory_space=pl.ANY)
    made = pl.pallas_call(
        kernel,
        in_specs=[smem, smem] + [anywhere] * (2 * parts + len(weights) + len(accs)),
        out_specs=[pl.BlockSpec(memory_space=pltpu.VMEM)] * outs,
        out_shape=[jax.ShapeDtypeStruct((rows, width), out_dtype) for width in widths for _ in range(parts)],
        scratch_shapes=[
            pltpu.VMEM((count, parts * rows, depth), jnp.bfloat16),
            pltpu.VMEM((count * depth, cols), jnp.bfloat16),
            pltpu.VMEM((len(accs), *accs[0].shape) if accs else (8, LANES), jnp.float32),
            pltpu.SemaphoreType.DMA((count,)),
            pltpu.SemaphoreType.DMA((count,)),
            pltpu.SemaphoreType.DMA,
        ],
        compiler_params=pltpu.CompilerParams(vmem_limit_bytes=VMEM_BYTES),
        cost_estimate=pl.CostEstimate(
            flops=2 * parts * rows * depth * count * cols,
            bytes_accessed=2 * count * depth * (parts * rows + cols),
            transcendentals=0,
        ),
        name="product",
    )(flags, places, *ours, *theirs, *weights, *accs)
    return [list(made[at : at + parts]) for at in range(0, outs, parts)]


def assemble(places, parts):
    rows = parts[0][0].shape[0]
    widths = [part[0].shape[1] for part in parts]
    cols = sum(widths)
    flat = [piece for part in parts for piece in part]

    def kernel(place_ref, *refs):
        *piece_refs, out_ref, sems = refs
        copies = []
        first = 0
        for part, width in enumerate(widths):
            for r in range(PLANE):
                at = part * PLANE + r
                start = pl.multiple_of(place_ref[r] * cols + first, LANES)
                target = out_ref.at[:, pl.ds(start, width)]
                copies.append(pltpu.make_async_copy(piece_refs[at], target, sems.at[at]))
                copies[-1].start()
            first += width
        for copy in copies:
            copy.wait()

    return pl.pallas_call(
        kernel,
        in_specs=[pl.BlockSpec(memory_space=pltpu.SMEM)] + [pl.BlockSpec(memory_space=pltpu.VMEM)] * len(flat),
        out_specs=pl.BlockSpec(memory_space=pl.ANY),
        out_shape=jax.ShapeDtypeStruct((rows, cols * PLANE), flat[0].dtype),
        scratch_shapes=[pltpu.SemaphoreType.DMA((len(flat),))],
        compiler_params=pltpu.CompilerParams(vmem_limit_bytes=16 << 20),
        name="assemble",
    )(places, *flat)


def split_block(q, k, v, residue, rate, skip, w_out):
    rows, chan = q.shape
    modes = rate.shape[0]
    me = lax.axis_index("ctx")
    core = lax.axis_index("ch")
    spot, plane = me & (PLANE - 1), me // PLANE
    count = lax.axis_size("ctx")
    chunk, feats = w_out.shape
    cols = feats // PLANE
    speed = rate.reshape(modes, chan // LANES, LANES)

    def far(x):
        return exchange(x, "ctx", 2 * PLANE)

    def near(x):
        return exchange(x, "ctx", PLANE)

    middle = [i for i in range(count) if PLANE <= i < 3 * PLANE]

    def across(x):
        return lax.ppermute(x, "ctx", [(i, i ^ (3 * PLANE)) for i in middle])

    def outward(x):
        return lax.ppermute(x, "ctx", [(i, i ^ PLANE) for i in middle])

    def group(x, r):
        return lax.dynamic_slice_in_dim(x, (spot ^ r) * cols, cols, axis=1)

    def source_of(b):
        return jnp.where(b // 2 == core, b & 1, 2 + (b & 1))

    is_middle = jnp.where((plane == 0) | (plane == 3), 0, 1)
    flags = jnp.stack([source_of(plane ^ r) for r in range(4)] + [is_middle]).astype(jnp.int32)
    places = jnp.stack([spot ^ r for r in range(PLANE)]).astype(jnp.int32)

    def plane_scan(k, v, rate, speed):
        def fade(span):
            return jnp.exp(-speed * span)

        ends = end_states(k, v, rate)
        other = exchange(ends, "ctx", 1)
        both = jnp.where(x_later, fade(float(rows)) * other + ends, fade(float(rows)) * ends + other)
        before = jnp.where(x_later, other, 0.0)
        other = exchange(both, "ctx", 2)
        before = before + jnp.where(y_later, fade((spot & 1).astype(jnp.float32) * rows) * other, 0.0)
        both = jnp.where(y_later, fade(2.0 * rows) * other + both, fade(2.0 * rows) * both + other)
        return both, before

    x_later, y_later = (spot & 1) != 0, (spot & 2) != 0
    w0, w1, w2, w3 = tie(*[group(w_out, r) for r in range(PLANE)])
    f0, n0 = far(w0), near(w0)
    both, before = box(plane_scan, k, v, rate, speed)
    f0, n0, w0, w1, w2, w3, both, before = tie(f0, n0, w0, w1, w2, w3, both, before)

    arrived = [exchange(w, "ctx", r + 1) for r, w in enumerate((w1, w2, w3))]
    decay = jnp.exp(-speed * float(PLANE * rows))
    last = shift_ctx(both, PLANE)
    earlier = shift_ctx(both + decay * last, 2 * PLANE)
    f0, w0, earlier = tie(f0, w0, earlier)
    out0, mid0 = outward(f0), across(w0)
    gated = gated_conv(q, k, v, rate, residue, skip, before, ([last, earlier], spot))
    rest = jnp.concatenate(arrived)
    gated, rest, out0, mid0 = tie(gated, rest, out0, mid0)

    nr, fr = near(rest), far(rest)
    ours = [gated] + [exchange(gated, "ctx", r) for r in range(1, PLANE)]
    theirs_x = exchange(ours[1], "ch", 1)
    fr, nr, rest, flags, places, theirs_x, *ours = tie(fr, nr, rest, flags, places, theirs_x, *ours)

    out1, mid1 = outward(fr), across(rest)
    theirs = [theirs_x if r == 1 else exchange(x, "ch", 1) for r, x in enumerate(ours)]
    blocks = [
        (0, None, [((w0,), 0), ((rest,), 0)]),
        (1, None, [((n0,), 0), ((nr,), 0)]),
        (2, None, [((f0,), 0), ((fr,), 0)]),
    ]
    (accs,) = product(flags, places, ours, theirs, blocks, None, [cols], jnp.float32)
    out1, mid1, *accs = tie(out1, mid1, *accs)

    blocks = [(3, 4, [((out0, mid0), 0), ((out1, mid1), 0)])]

    def finish(*spots):
        chosen = [ours[r] for r in spots], [theirs[r] for r in spots]
        return product(flags, places, *chosen, blocks, [accs[r] for r in spots], [cols], jnp.bfloat16)[0]

    (made3,) = finish(3)
    back3 = exchange(made3, "ctx", 3)
    back3, made0, made1, made2 = tie(back3, *finish(0, 1, 2))
    return assemble(places, [[made0, exchange(made1, "ctx", 1), exchange(made2, "ctx", 2), back3]])


def body(q, k, v, residue, rate, skip, w_out):
    rows, chan = q.shape
    modes = rate.shape[0]
    groups = chan // LANES
    count, cores = lax.axis_size("ctx"), lax.axis_size("ch")
    chunk, feats = w_out.shape
    split = (
        count == 4 * PLANE
        and cores == 2
        and chan == 8 * chunk
        and chunk % LANES == 0
        and feats % (2 * PLANE * LANES) == 0
    )
    skip = skip.reshape(groups, LANES)
    if split:
        return split_block(q, k, v, residue, rate, skip, w_out)
    ends = end_states(k, v, rate)
    enter = entering_states(ends, rate.reshape(modes, groups, LANES), rows)
    gated = gated_conv(q, k, v, rate, residue, skip, enter)
    gated = gated.transpose(1, 0, 2).reshape(rows, chan)
    full_gated = lax.all_gather(gated, "ch", axis=1, tiled=True)
    w_full = lax.all_gather(w_out, "ctx", axis=0, tiled=True)
    mixed = jnp.dot(full_gated, w_full, preferred_element_type=jnp.float32)
    return mixed.astype(jnp.bfloat16)


def solution(mesh):
    placed = (
        P("ctx", "ch"),
        P("ctx", "ch"),
        P("ctx", "ch"),
        P(None, "ch"),
        P(None, "ch"),
        P("ch"),
        P("ctx", "ch"),
    )
    return jax.shard_map(
        body, mesh=mesh, in_specs=placed, out_specs=P("ctx", "ch"), check_vma=False
    )
```

```python
import jax
import jax.numpy as jnp
from jax import lax
from jax.experimental import pallas as pl
from jax.experimental.pallas import tpu as pltpu
from jax.sharding import PartitionSpec as P

LANES = 128
RADIX = 4
PLANE = 4
VMEM_BYTES = 60 << 20


def spread_signal(k_ref, v_ref, sig_ref):
    rows, width = k_ref.shape
    groups = width // LANES
    for g in range(groups):
        cols = pl.ds(g * LANES, LANES)
        product = k_ref[:, cols].astype(jnp.float32) * v_ref[:, cols].astype(jnp.float32)
        sig_ref[pl.ds(g, rows, stride=groups), :] = product


def spread_modes(ref, out_ref):
    modes, width = ref.shape
    groups = width // LANES
    for g in range(groups):
        out_ref[pl.ds(g, modes, stride=groups), :] = ref[:, pl.ds(g * LANES, LANES)]


def ends_kernel(k_ref, v_ref, rate_ref, end_ref, sig_ref, mode_ref):
    rows, width = k_ref.shape
    modes, groups, _ = end_ref.shape
    spread_signal(k_ref, v_ref, sig_ref)
    spread_modes(rate_ref, mode_ref)
    decay = [jnp.exp(-mode_ref[pl.ds(m * groups, groups), :]) for m in range(modes)]

    def step(t, state):
        s = sig_ref[pl.ds(pl.multiple_of(t * groups, groups), groups), :]
        return tuple(d * h + s for d, h in zip(decay, state))

    zero = jnp.zeros((groups, LANES), jnp.float32)
    state = lax.fori_loop(0, rows, step, (zero,) * modes, unroll=8)
    for m in range(modes):
        end_ref[m] = state[m]


def conv_kernel(q_ref, k_ref, v_ref, rate_ref, residue_ref, skip_ref, enter_ref, *refs):
    *plane_refs, out_ref, sig_ref, conv_ref, mode_ref, weight_ref = refs
    rows, width = k_ref.shape
    modes, groups, _ = enter_ref.shape
    spread_signal(k_ref, v_ref, sig_ref)
    spread_modes(rate_ref, mode_ref)
    spread_modes(residue_ref, weight_ref)
    rates = [mode_ref[pl.ds(m * groups, groups), :] for m in range(modes)]
    decay = [jnp.exp(-rate) for rate in rates]
    weight = [weight_ref[pl.ds(m * groups, groups), :] * jnp.sqrt(2.0 * rate) for m, rate in enumerate(rates)]
    skip = skip_ref[...]
    enter = [enter_ref[m] for m in range(modes)]
    if plane_refs:
        *earlier_refs, spot_ref = plane_refs
        ahead = (spot_ref[0] * rows).astype(jnp.float32)
        for m, rate in enumerate(rates):
            for n, earlier_ref in enumerate(earlier_refs):
                enter[m] = enter[m] + jnp.exp(-rate * (ahead + float(n * PLANE * rows))) * earlier_ref[m]

    def step(t, state):
        at = pl.ds(pl.multiple_of(t * groups, groups), groups)
        s = sig_ref[at, :]
        state = tuple(d * h + s for d, h in zip(decay, state))
        terms = [c * h for c, h in zip(weight, state)] + [skip * s]
        while len(terms) > 1:
            terms = [sum(terms[i : i + 2]) for i in range(0, len(terms), 2)]
        conv_ref[at, :] = terms[0]
        return state

    lax.fori_loop(0, rows, step, tuple(enter), unroll=4)
    for g in range(groups):
        cols = pl.ds(g * LANES, LANES)
        conv = conv_ref[pl.ds(g, rows, stride=groups), :]
        out_ref[:, cols] = (q_ref[:, cols].astype(jnp.float32) * conv).astype(out_ref.dtype)


def block_specs(rows, modes, width):
    groups = width // LANES
    return (
        pl.BlockSpec((rows, width), lambda i: (0, i)),
        pl.BlockSpec((modes, width), lambda i: (0, i)),
        pl.BlockSpec((modes, groups, LANES), lambda i: (0, i, 0)),
        pl.BlockSpec((groups, LANES), lambda i: (i, 0)),
    )


def end_states(k, v, rate):
    rows, chan = k.shape
    modes = rate.shape[0]
    width = min(chan, 8 * LANES)
    wide, moded, state, _ = block_specs(rows, modes, width)
    return pl.pallas_call(
        ends_kernel,
        grid=(chan // width,),
        in_specs=[wide, wide, moded],
        out_specs=state,
        out_shape=jax.ShapeDtypeStruct((modes, chan // LANES, LANES), jnp.float32),
        scratch_shapes=[
            pltpu.VMEM((rows * width // LANES, LANES), jnp.float32),
            pltpu.VMEM((modes * width // LANES, LANES), jnp.float32),
        ],
        compiler_params=pltpu.CompilerParams(vmem_limit_bytes=VMEM_BYTES),
        cost_estimate=pl.CostEstimate(
            flops=2 * modes * rows * chan, bytes_accessed=4 * rows * chan, transcendentals=modes * chan
        ),
        name="end_states",
    )(k, v, rate)


def gated_conv(q, k, v, rate, residue, skip, enter, planes=None):
    rows, chan = k.shape
    modes = rate.shape[0]
    width = min(chan, 8 * LANES)
    wide, moded, state, single = block_specs(rows, modes, width)
    spread = pltpu.VMEM((rows * width // LANES, LANES), jnp.float32)
    moded_spread = pltpu.VMEM((modes * width // LANES, LANES), jnp.float32)
    extra, extra_specs = [], []
    if planes is not None:
        earlier, spot = planes
        extra = [*earlier, spot.reshape(1).astype(jnp.int32)]
        extra_specs = [state] * len(earlier) + [pl.BlockSpec(memory_space=pltpu.SMEM)]
    return pl.pallas_call(
        conv_kernel,
        grid=(chan // width,),
        in_specs=[wide, wide, wide, moded, moded, single, state] + extra_specs,
        out_specs=pl.BlockSpec((None, rows, width), lambda i: (i, 0, 0)),
        out_shape=jax.ShapeDtypeStruct((chan // width, rows, width), jnp.bfloat16),
        scratch_shapes=[spread, spread, moded_spread, moded_spread],
        compiler_params=pltpu.CompilerParams(vmem_limit_bytes=VMEM_BYTES),
        cost_estimate=pl.CostEstimate(
            flops=4 * modes * rows * chan, bytes_accessed=8 * rows * chan, transcendentals=2 * modes * chan
        ),
        name="gated_conv",
    )(q, k, v, rate, residue, skip, enter, *extra)


def shift_ctx(x, by):
    count = lax.axis_size("ctx")
    return lax.ppermute(x, "ctx", [(i, i + by) for i in range(count - by)])


def exchange(x, axis, flip):
    count = lax.axis_size(axis)
    return lax.ppermute(x, axis, [(i, i ^ flip) for i in range(count)])


def tie(*values):
    return lax.optimization_barrier(values)


def entering_states(ends, rate, rows):
    count = lax.axis_size("ctx")
    total = jnp.zeros_like(ends)
    for k in range(1, min(RADIX, count - 1) + 1):
        total = total + jnp.exp(-rate * float(rows * (k - 1))) * shift_ctx(ends, k)
    stride = RADIX
    while stride < count:
        base = total
        for k in range(1, RADIX):
            if stride * k < count:
                total = total + jnp.exp(-rate * float(rows * stride * k)) * shift_ctx(base, stride * k)
        stride *= RADIX
    return total


def box(fn, *args):
    once = (lax.axis_index("ctx") >= 0).astype(jnp.int32)
    shapes = jax.eval_shape(fn, *args)
    empty = pl.pallas_call(
        lambda *refs: None,
        out_specs=[pl.BlockSpec(memory_space=pl.ANY)] * len(shapes),
        out_shape=list(shapes),
        name="blank",
    )()

    def run(step, _):
        return fn(*tie(step, *args)[1:])

    return lax.fori_loop(0, once, run, tuple(empty))


def product(flags, places, ours, theirs, blocks, accs, widths, out_dtype, spread=False):
    _, rows, depth = ours[0].shape
    chunk = depth // PLANE
    cols = sum(widths)
    count, parts = len(blocks), len(ours)
    outs = parts * len(widths)
    weights = [array for _, _, pieces in blocks for choices, _ in pieces for array in choices]
    accs = accs or []

    def kernel(flag_ref, place_ref, *refs):
        our_refs, their_refs, refs = refs[:parts], refs[parts : 2 * parts], refs[2 * parts :]
        weight_refs, refs = list(refs[: len(weights)]), refs[len(weights) :]
        acc_refs, out_refs = refs[: len(accs)], list(refs[len(accs) : len(accs) + outs])
        gated_buf, weight_buf, acc_buf, own_buf, gated_sems, weight_sems, acc_sem = refs[-7:]
        spread_ref = out_refs[0]
        if spread:
            out_refs[0] = own_buf

        def target(b, at):
            start = pl.multiple_of(b * depth + place_ref[at // chunk] * chunk, chunk)
            return weight_buf.at[pl.ds(start, chunk), :]

        for b, (flag, pick, pieces) in enumerate(blocks):
            row = 0
            for choices, col in pieces:
                for c in range(len(choices)):
                    ref = weight_refs.pop(0)
                    for at in range(0, ref.shape[0], chunk):
                        source = ref.at[pl.ds(at, chunk), pl.ds(col, cols)]
                        copy = pltpu.make_async_copy(source, target(b, row + at), weight_sems.at[b])
                        if pick is None:
                            copy.start()
                        else:
                            pl.when(flag_ref[pick] == c)(copy.start)
                row += choices[0].shape[0]
            half = flag_ref[flag] & 1
            for r in range(parts):
                for c, refs_of in enumerate((our_refs, their_refs)):
                    target_rows = gated_buf.at[b, pl.ds(r * rows, rows), :]
                    copy = pltpu.make_async_copy(refs_of[r].at[half], target_rows, gated_sems.at[b])
                    pl.when(flag_ref[flag] // 2 == c)(copy.start)
        for r, acc_ref in enumerate(acc_refs):
            pltpu.make_async_copy(acc_ref, acc_buf.at[r], acc_sem).start()
        for b in range(count):
            block = weight_buf.at[pl.ds(b * depth, depth), :]
            pltpu.make_async_copy(block, block, weight_sems.at[b]).wait()
            pltpu.make_async_copy(gated_buf.at[b], gated_buf.at[b], gated_sems.at[b]).wait()
            if accs and not b:
                pltpu.make_async_copy(acc_buf, acc_buf, acc_sem).wait()
            for col in range(0, cols, 2 * LANES):
                here = pl.ds(col, 2 * LANES)
                made = jnp.dot(
                    gated_buf[b], weight_buf[pl.ds(b * depth, depth), here], preferred_element_type=jnp.float32
                )
                part = 0 if col < widths[0] else 1
                inside = pl.ds(col - part * widths[0], 2 * LANES)
                for r in range(parts):
                    total = made[r * rows : (r + 1) * rows]
                    out_ref = out_refs[part * parts + r]
                    if b:
                        total = total + out_ref[:, inside]
                    elif accs:
                        total = total + acc_buf[r, :, here]
                    out_ref[:, inside] = total.astype(out_dtype)

        if spread:
            home = spread_ref.at[:, pl.ds(pl.multiple_of(place_ref[0] * cols, cols), cols)]
            copy = pltpu.make_async_copy(own_buf, home, acc_sem)
            copy.start()
            copy.wait()

    smem = pl.BlockSpec(memory_space=pltpu.SMEM)
    anywhere = pl.BlockSpec(memory_space=pl.ANY)
    out_specs = [pl.BlockSpec(memory_space=pltpu.VMEM)] * outs
    out_shape = [jax.ShapeDtypeStruct((rows, width), out_dtype) for width in widths for _ in range(parts)]
    if spread:
        out_specs[0] = anywhere
        out_shape[0] = jax.ShapeDtypeStruct((rows, PLANE * cols), out_dtype)
    made = pl.pallas_call(
        kernel,
        in_specs=[smem, smem] + [anywhere] * (2 * parts + len(weights) + len(accs)),
        out_specs=out_specs,
        out_shape=out_shape,
        scratch_shapes=[
            pltpu.VMEM((count, parts * rows, depth), jnp.bfloat16),
            pltpu.VMEM((count * depth, cols), jnp.bfloat16),
            pltpu.VMEM((len(accs), *accs[0].shape) if accs else (8, LANES), jnp.float32),
            pltpu.VMEM((rows, cols) if spread else (16, LANES), out_dtype),
            pltpu.SemaphoreType.DMA((count,)),
            pltpu.SemaphoreType.DMA((count,)),
            pltpu.SemaphoreType.DMA,
        ],
        compiler_params=pltpu.CompilerParams(vmem_limit_bytes=VMEM_BYTES),
        cost_estimate=pl.CostEstimate(
            flops=2 * parts * rows * depth * count * cols,
            bytes_accessed=2 * count * depth * (parts * rows + cols),
            transcendentals=0,
        ),
        name="product",
    )(flags, places, *ours, *theirs, *weights, *accs)
    return [list(made[at : at + parts]) for at in range(0, outs, parts)]


def assemble(places, held, pieces):
    rows, cols = pieces[0].shape

    def kernel(place_ref, _, *refs):
        *piece_refs, out_ref, sems = refs
        copies = []
        for n, piece_ref in enumerate(piece_refs):
            target = out_ref.at[:, pl.ds(pl.multiple_of(place_ref[n + 1] * cols, cols), cols)]
            copies.append(pltpu.make_async_copy(piece_ref, target, sems.at[n]))
            copies[-1].start()
        for copy in copies:
            copy.wait()

    anywhere = pl.BlockSpec(memory_space=pl.ANY)
    return pl.pallas_call(
        kernel,
        in_specs=[pl.BlockSpec(memory_space=pltpu.SMEM), anywhere]
        + [pl.BlockSpec(memory_space=pltpu.VMEM)] * len(pieces),
        out_specs=anywhere,
        out_shape=jax.ShapeDtypeStruct(held.shape, held.dtype),
        scratch_shapes=[pltpu.SemaphoreType.DMA((len(pieces),))],
        input_output_aliases={1: 0},
        compiler_params=pltpu.CompilerParams(vmem_limit_bytes=16 << 20),
        name="assemble",
    )(places, held, *pieces)


def split_block(q, k, v, residue, rate, skip, w_out):
    rows, chan = q.shape
    modes = rate.shape[0]
    me = lax.axis_index("ctx")
    core = lax.axis_index("ch")
    spot, plane = me & (PLANE - 1), me // PLANE
    count = lax.axis_size("ctx")
    chunk, feats = w_out.shape
    cols = feats // PLANE
    speed = rate.reshape(modes, chan // LANES, LANES)

    def far(x):
        return exchange(x, "ctx", 2 * PLANE)

    def near(x):
        return exchange(x, "ctx", PLANE)

    middle = [i for i in range(count) if PLANE <= i < 3 * PLANE]

    def across(x):
        return lax.ppermute(x, "ctx", [(i, i ^ (3 * PLANE)) for i in middle])

    def outward(x):
        return lax.ppermute(x, "ctx", [(i, i ^ PLANE) for i in middle])

    def group(x, r):
        return lax.dynamic_slice_in_dim(x, (spot ^ r) * cols, cols, axis=1)

    def source_of(b):
        return jnp.where(b // 2 == core, b & 1, 2 + (b & 1))

    is_middle = jnp.where((plane == 0) | (plane == 3), 0, 1)
    flags = jnp.stack([source_of(plane ^ r) for r in range(4)] + [is_middle]).astype(jnp.int32)
    places = jnp.stack([spot ^ r for r in range(PLANE)]).astype(jnp.int32)

    def plane_scan(k, v, rate, speed):
        def fade(span):
            return jnp.exp(-speed * span)

        ends = end_states(k, v, rate)
        other = exchange(ends, "ctx", 1)
        both = jnp.where(x_later, fade(float(rows)) * other + ends, fade(float(rows)) * ends + other)
        before = jnp.where(x_later, other, 0.0)
        other = exchange(both, "ctx", 2)
        before = before + jnp.where(y_later, fade((spot & 1).astype(jnp.float32) * rows) * other, 0.0)
        both = jnp.where(y_later, fade(2.0 * rows) * other + both, fade(2.0 * rows) * both + other)
        return both, before

    x_later, y_later = (spot & 1) != 0, (spot & 2) != 0
    w0, w1, w2, w3 = tie(*[group(w_out, r) for r in range(PLANE)])
    n0, f0 = near(w0), far(w0)
    both, before = box(plane_scan, k, v, rate, speed)
    n0, f0, w0, w1, w2, w3, both, before = tie(n0, f0, w0, w1, w2, w3, both, before)

    arrived = [exchange(w, "ctx", r + 1) for r, w in enumerate((w1, w2, w3))]
    decay = jnp.exp(-speed * float(PLANE * rows))
    last = shift_ctx(both, PLANE)
    earlier = shift_ctx(both + decay * last, 2 * PLANE)
    f0, w0, earlier = tie(f0, w0, earlier)
    mid0, out0 = across(w0), outward(f0)
    gated = gated_conv(q, k, v, rate, residue, skip, before, ([last, earlier], spot))
    rest = jnp.concatenate(arrived)
    gated, rest, mid0, out0 = tie(gated, rest, mid0, out0)

    nr, fr = near(rest), far(rest)
    ours = [gated] + [exchange(gated, "ctx", r) for r in range(1, PLANE)]
    theirs_x = exchange(ours[1], "ch", 1)
    nr, fr, rest, flags, places, theirs_x, *ours = tie(nr, fr, rest, flags, places, theirs_x, *ours)

    out1, mid1 = outward(fr), across(rest)
    theirs = [theirs_x if r == 1 else exchange(x, "ch", 1) for r, x in enumerate(ours)]
    blocks = [
        (0, None, [((w0,), 0), ((rest,), 0)]),
        (1, None, [((n0,), 0), ((nr,), 0)]),
        (2, None, [((f0,), 0), ((fr,), 0)]),
    ]
    (accs,) = product(flags, places, ours, theirs, blocks, None, [cols], jnp.float32)
    out1, mid1, *accs = tie(out1, mid1, *accs)

    blocks = [(3, 4, [((out0, mid0), 0), ((out1, mid1), 0)])]

    def finish(*spots):
        chosen = [ours[r] for r in spots], [theirs[r] for r in spots]
        return product(flags, places, *chosen, blocks, [accs[r] for r in spots], [cols], jnp.bfloat16, 0 in spots)[0]

    (made3,) = finish(3)
    back3 = exchange(made3, "ctx", 3)
    back3, held, made1, made2 = tie(back3, *finish(0, 1, 2))
    return assemble(places, held, [exchange(made1, "ctx", 1), exchange(made2, "ctx", 2), back3])


def body(q, k, v, residue, rate, skip, w_out):
    rows, chan = q.shape
    modes = rate.shape[0]
    groups = chan // LANES
    count, cores = lax.axis_size("ctx"), lax.axis_size("ch")
    chunk, feats = w_out.shape
    split = (
        count == 4 * PLANE
        and cores == 2
        and chan == 8 * chunk
        and chunk % LANES == 0
        and feats % (2 * PLANE * LANES) == 0
    )
    skip = skip.reshape(groups, LANES)
    if split:
        return split_block(q, k, v, residue, rate, skip, w_out)
    ends = end_states(k, v, rate)
    enter = entering_states(ends, rate.reshape(modes, groups, LANES), rows)
    gated = gated_conv(q, k, v, rate, residue, skip, enter)
    gated = gated.transpose(1, 0, 2).reshape(rows, chan)
    full_gated = lax.all_gather(gated, "ch", axis=1, tiled=True)
    w_full = lax.all_gather(w_out, "ctx", axis=0, tiled=True)
    mixed = jnp.dot(full_gated, w_full, preferred_element_type=jnp.float32)
    return mixed.astype(jnp.bfloat16)


def solution(mesh):
    placed = (
        P("ctx", "ch"),
        P("ctx", "ch"),
        P("ctx", "ch"),
        P(None, "ch"),
        P(None, "ch"),
        P("ch"),
        P("ctx", "ch"),
    )
    return jax.shard_map(
        body, mesh=mesh, in_specs=placed, out_specs=P("ctx", "ch"), check_vma=False
    )
```

```python
import jax
import jax.numpy as jnp
from jax import lax
from jax.experimental import pallas as pl
from jax.experimental.pallas import tpu as pltpu
from jax.sharding import PartitionSpec as P

LANES = 128
RADIX = 4
PLANE = 4
VMEM_BYTES = 60 << 20


def spread_signal(k_ref, v_ref, sig_ref):
    rows, width = k_ref.shape
    groups = width // LANES
    for g in range(groups):
        cols = pl.ds(g * LANES, LANES)
        product = k_ref[:, cols].astype(jnp.float32) * v_ref[:, cols].astype(jnp.float32)
        sig_ref[pl.ds(g, rows, stride=groups), :] = product


def spread_modes(ref, out_ref):
    modes, width = ref.shape
    groups = width // LANES
    for g in range(groups):
        out_ref[pl.ds(g, modes, stride=groups), :] = ref[:, pl.ds(g * LANES, LANES)]


def ends_kernel(k_ref, v_ref, rate_ref, end_ref, sig_ref, mode_ref):
    rows, width = k_ref.shape
    modes, groups, _ = end_ref.shape
    spread_signal(k_ref, v_ref, sig_ref)
    spread_modes(rate_ref, mode_ref)
    decay = [jnp.exp(-mode_ref[pl.ds(m * groups, groups), :]) for m in range(modes)]

    def step(t, state):
        s = sig_ref[pl.ds(pl.multiple_of(t * groups, groups), groups), :]
        return tuple(d * h + s for d, h in zip(decay, state))

    zero = jnp.zeros((groups, LANES), jnp.float32)
    state = lax.fori_loop(0, rows, step, (zero,) * modes, unroll=8)
    for m in range(modes):
        end_ref[m] = state[m]


def conv_kernel(q_ref, k_ref, v_ref, rate_ref, residue_ref, skip_ref, enter_ref, *refs):
    *plane_refs, out_ref, sig_ref, conv_ref, mode_ref, weight_ref = refs
    rows, width = k_ref.shape
    modes, groups, _ = enter_ref.shape
    spread_signal(k_ref, v_ref, sig_ref)
    spread_modes(rate_ref, mode_ref)
    spread_modes(residue_ref, weight_ref)
    rates = [mode_ref[pl.ds(m * groups, groups), :] for m in range(modes)]
    decay = [jnp.exp(-rate) for rate in rates]
    weight = [weight_ref[pl.ds(m * groups, groups), :] * jnp.sqrt(2.0 * rate) for m, rate in enumerate(rates)]
    skip = skip_ref[...]
    enter = [enter_ref[m] for m in range(modes)]
    if plane_refs:
        *earlier_refs, spot_ref = plane_refs
        ahead = (spot_ref[0] * rows).astype(jnp.float32)
        for m, rate in enumerate(rates):
            for n, earlier_ref in enumerate(earlier_refs):
                enter[m] = enter[m] + jnp.exp(-rate * (ahead + float(n * PLANE * rows))) * earlier_ref[m]

    def step(t, state):
        at = pl.ds(pl.multiple_of(t * groups, groups), groups)
        s = sig_ref[at, :]
        state = tuple(d * h + s for d, h in zip(decay, state))
        terms = [c * h for c, h in zip(weight, state)] + [skip * s]
        while len(terms) > 1:
            terms = [sum(terms[i : i + 2]) for i in range(0, len(terms), 2)]
        conv_ref[at, :] = terms[0]
        return state

    lax.fori_loop(0, rows, step, tuple(enter), unroll=4)
    for g in range(groups):
        cols = pl.ds(g * LANES, LANES)
        conv = conv_ref[pl.ds(g, rows, stride=groups), :]
        out_ref[:, cols] = (q_ref[:, cols].astype(jnp.float32) * conv).astype(out_ref.dtype)


def block_specs(rows, modes, width):
    groups = width // LANES
    return (
        pl.BlockSpec((rows, width), lambda i: (0, i)),
        pl.BlockSpec((modes, width), lambda i: (0, i)),
        pl.BlockSpec((modes, groups, LANES), lambda i: (0, i, 0)),
        pl.BlockSpec((groups, LANES), lambda i: (i, 0)),
    )


def end_states(k, v, rate):
    rows, chan = k.shape
    modes = rate.shape[0]
    width = min(chan, 8 * LANES)
    wide, moded, state, _ = block_specs(rows, modes, width)
    return pl.pallas_call(
        ends_kernel,
        grid=(chan // width,),
        in_specs=[wide, wide, moded],
        out_specs=state,
        out_shape=jax.ShapeDtypeStruct((modes, chan // LANES, LANES), jnp.float32),
        scratch_shapes=[
            pltpu.VMEM((rows * width // LANES, LANES), jnp.float32),
            pltpu.VMEM((modes * width // LANES, LANES), jnp.float32),
        ],
        compiler_params=pltpu.CompilerParams(vmem_limit_bytes=VMEM_BYTES),
        cost_estimate=pl.CostEstimate(
            flops=2 * modes * rows * chan, bytes_accessed=4 * rows * chan, transcendentals=modes * chan
        ),
        name="end_states",
    )(k, v, rate)


def gated_conv(q, k, v, rate, residue, skip, enter, planes=None):
    rows, chan = k.shape
    modes = rate.shape[0]
    width = min(chan, 8 * LANES)
    wide, moded, state, single = block_specs(rows, modes, width)
    spread = pltpu.VMEM((rows * width // LANES, LANES), jnp.float32)
    moded_spread = pltpu.VMEM((modes * width // LANES, LANES), jnp.float32)
    extra, extra_specs = [], []
    if planes is not None:
        earlier, spot = planes
        extra = [*earlier, spot.reshape(1).astype(jnp.int32)]
        extra_specs = [state] * len(earlier) + [pl.BlockSpec(memory_space=pltpu.SMEM)]
    return pl.pallas_call(
        conv_kernel,
        grid=(chan // width,),
        in_specs=[wide, wide, wide, moded, moded, single, state] + extra_specs,
        out_specs=pl.BlockSpec((None, rows, width), lambda i: (i, 0, 0)),
        out_shape=jax.ShapeDtypeStruct((chan // width, rows, width), jnp.bfloat16),
        scratch_shapes=[spread, spread, moded_spread, moded_spread],
        compiler_params=pltpu.CompilerParams(vmem_limit_bytes=VMEM_BYTES),
        cost_estimate=pl.CostEstimate(
            flops=4 * modes * rows * chan, bytes_accessed=8 * rows * chan, transcendentals=2 * modes * chan
        ),
        name="gated_conv",
    )(q, k, v, rate, residue, skip, enter, *extra)


def shift_ctx(x, by):
    count = lax.axis_size("ctx")
    return lax.ppermute(x, "ctx", [(i, i + by) for i in range(count - by)])


def exchange(x, axis, flip):
    count = lax.axis_size(axis)
    return lax.ppermute(x, axis, [(i, i ^ flip) for i in range(count)])


def tie(*values):
    return lax.optimization_barrier(values)


def entering_states(ends, rate, rows):
    count = lax.axis_size("ctx")
    total = jnp.zeros_like(ends)
    for k in range(1, min(RADIX, count - 1) + 1):
        total = total + jnp.exp(-rate * float(rows * (k - 1))) * shift_ctx(ends, k)
    stride = RADIX
    while stride < count:
        base = total
        for k in range(1, RADIX):
            if stride * k < count:
                total = total + jnp.exp(-rate * float(rows * stride * k)) * shift_ctx(base, stride * k)
        stride *= RADIX
    return total


def box(fn, *args):
    once = (lax.axis_index("ctx") >= 0).astype(jnp.int32)
    shapes = jax.eval_shape(fn, *args)
    empty = pl.pallas_call(
        lambda *refs: None,
        out_specs=[pl.BlockSpec(memory_space=pl.ANY)] * len(shapes),
        out_shape=list(shapes),
        name="blank",
    )()

    def run(step, _):
        return fn(*tie(step, *args)[1:])

    return lax.fori_loop(0, once, run, tuple(empty))


def product(flags, places, ours, theirs, blocks, accs, first_col, cols, out_dtype):
    _, rows, depth = ours[0].shape
    chunk = depth // PLANE
    count, parts = len(blocks), len(ours)
    weights = [array for _, _, pieces in blocks for choices, _ in pieces for array in choices]
    accs = accs or []

    def kernel(flag_ref, place_ref, *refs):
        our_refs, their_refs, refs = refs[:parts], refs[parts : 2 * parts], refs[2 * parts :]
        weight_refs, refs = list(refs[: len(weights)]), refs[len(weights) :]
        acc_refs, out_refs = refs[: len(accs)], refs[len(accs) : len(accs) + parts]
        gated_buf, weight_buf, acc_buf, gated_sems, weight_sems, acc_sem = refs[-6:]

        def target(b, at):
            start = pl.multiple_of(b * depth + place_ref[at // chunk] * chunk, chunk)
            return weight_buf.at[pl.ds(start, chunk), :]

        for b, (flag, pick, pieces) in enumerate(blocks):
            row = 0
            for choices, col in pieces:
                for c in range(len(choices)):
                    ref = weight_refs.pop(0)
                    for at in range(0, ref.shape[0], chunk):
                        source = ref.at[pl.ds(at, chunk), pl.ds(col, cols)]
                        copy = pltpu.make_async_copy(source, target(b, row + at), weight_sems.at[b])
                        if pick is None:
                            copy.start()
                        else:
                            pl.when(flag_ref[pick] == c)(copy.start)
                row += choices[0].shape[0]
            half = flag_ref[flag] & 1
            for r in range(parts):
                for c, refs_of in enumerate((our_refs, their_refs)):
                    target_rows = gated_buf.at[b, pl.ds(r * rows, rows), :]
                    copy = pltpu.make_async_copy(refs_of[r].at[half], target_rows, gated_sems.at[b])
                    pl.when(flag_ref[flag] // 2 == c)(copy.start)
        for r, acc_ref in enumerate(acc_refs):
            pltpu.make_async_copy(acc_ref.at[:, pl.ds(first_col, cols)], acc_buf.at[r], acc_sem).start()
        for b in range(count):
            block = weight_buf.at[pl.ds(b * depth, depth), :]
            pltpu.make_async_copy(block, block, weight_sems.at[b]).wait()
            pltpu.make_async_copy(gated_buf.at[b], gated_buf.at[b], gated_sems.at[b]).wait()
            if accs and not b:
                pltpu.make_async_copy(acc_buf, acc_buf, acc_sem).wait()
            for col in range(0, cols, 2 * LANES):
                here = pl.ds(col, min(2 * LANES, cols - col))
                made = jnp.dot(
                    gated_buf[b], weight_buf[pl.ds(b * depth, depth), here], preferred_element_type=jnp.float32
                )
                for r in range(parts):
                    total = made[r * rows : (r + 1) * rows]
                    if b:
                        total = total + out_refs[r][:, here]
                    elif accs:
                        total = total + acc_buf[r, :, here]
                    out_refs[r][:, here] = total.astype(out_dtype)

    smem = pl.BlockSpec(memory_space=pltpu.SMEM)
    anywhere = pl.BlockSpec(memory_space=pl.ANY)
    made = pl.pallas_call(
        kernel,
        in_specs=[smem, smem] + [anywhere] * (2 * parts + len(weights) + len(accs)),
        out_specs=[pl.BlockSpec(memory_space=pltpu.VMEM)] * parts,
        out_shape=[jax.ShapeDtypeStruct((rows, cols), out_dtype)] * parts,
        scratch_shapes=[
            pltpu.VMEM((count, parts * rows, depth), jnp.bfloat16),
            pltpu.VMEM((count * depth, cols), jnp.bfloat16),
            pltpu.VMEM((parts, rows, cols) if accs else (8, LANES), jnp.float32),
            pltpu.SemaphoreType.DMA((count,)),
            pltpu.SemaphoreType.DMA((count,)),
            pltpu.SemaphoreType.DMA,
        ],
        compiler_params=pltpu.CompilerParams(vmem_limit_bytes=VMEM_BYTES),
        cost_estimate=pl.CostEstimate(
            flops=2 * parts * rows * depth * count * cols,
            bytes_accessed=2 * count * depth * (parts * rows + cols),
            transcendentals=0,
        ),
        name="product",
    )(flags, places, *ours, *theirs, *weights, *accs)
    return [list(made)]


def assemble(places, parts):
    rows = parts[0][0].shape[0]
    widths = [part[0].shape[1] for part in parts]
    cols = sum(widths)
    flat = [piece for part in parts for piece in part]

    def kernel(place_ref, *refs):
        *piece_refs, out_ref, sems = refs
        copies = []
        first = 0
        for part, width in enumerate(widths):
            for r in range(PLANE):
                at = part * PLANE + r
                start = pl.multiple_of(place_ref[r] * cols + first, LANES)
                target = out_ref.at[:, pl.ds(start, width)]
                copies.append(pltpu.make_async_copy(piece_refs[at], target, sems.at[at]))
                copies[-1].start()
            first += width
        for copy in copies:
            copy.wait()

    return pl.pallas_call(
        kernel,
        in_specs=[pl.BlockSpec(memory_space=pltpu.SMEM)] + [pl.BlockSpec(memory_space=pltpu.VMEM)] * len(flat),
        out_specs=pl.BlockSpec(memory_space=pl.ANY),
        out_shape=jax.ShapeDtypeStruct((rows, cols * PLANE), flat[0].dtype),
        scratch_shapes=[pltpu.SemaphoreType.DMA((len(flat),))],
        compiler_params=pltpu.CompilerParams(vmem_limit_bytes=16 << 20),
        name="assemble",
    )(places, *flat)


def split_block(q, k, v, residue, rate, skip, w_out):
    rows, chan = q.shape
    modes = rate.shape[0]
    me = lax.axis_index("ctx")
    core = lax.axis_index("ch")
    spot, plane = me & (PLANE - 1), me // PLANE
    count = lax.axis_size("ctx")
    chunk, feats = w_out.shape
    cols = feats // PLANE
    speed = rate.reshape(modes, chan // LANES, LANES)

    def far(x):
        return exchange(x, "ctx", 2 * PLANE)

    def near(x):
        return exchange(x, "ctx", PLANE)

    middle = [i for i in range(count) if PLANE <= i < 3 * PLANE]

    def across(x):
        return lax.ppermute(x, "ctx", [(i, i ^ (3 * PLANE)) for i in middle])

    def outward(x):
        return lax.ppermute(x, "ctx", [(i, i ^ PLANE) for i in middle])

    def group(x, r):
        return lax.dynamic_slice_in_dim(x, (spot ^ r) * cols, cols, axis=1)

    def source_of(b):
        return jnp.where(b // 2 == core, b & 1, 2 + (b & 1))

    is_middle = jnp.where((plane == 0) | (plane == 3), 0, 1)
    flags = jnp.stack([source_of(plane ^ r) for r in range(4)] + [is_middle]).astype(jnp.int32)
    places = jnp.stack([spot ^ r for r in range(PLANE)]).astype(jnp.int32)

    def plane_scan(k, v, rate, speed):
        def fade(span):
            return jnp.exp(-speed * span)

        ends = end_states(k, v, rate)
        other = exchange(ends, "ctx", 1)
        both = jnp.where(x_later, fade(float(rows)) * other + ends, fade(float(rows)) * ends + other)
        before = jnp.where(x_later, other, 0.0)
        other = exchange(both, "ctx", 2)
        before = before + jnp.where(y_later, fade((spot & 1).astype(jnp.float32) * rows) * other, 0.0)
        both = jnp.where(y_later, fade(2.0 * rows) * other + both, fade(2.0 * rows) * both + other)
        return both, before

    x_later, y_later = (spot & 1) != 0, (spot & 2) != 0
    w0, w1, w2, w3 = tie(*[group(w_out, r) for r in range(PLANE)])
    f0, n0 = far(w0), near(w0)
    both, before = box(plane_scan, k, v, rate, speed)
    f0, n0, w0, w1, w2, w3, both, before = tie(f0, n0, w0, w1, w2, w3, both, before)

    arrived = [exchange(w, "ctx", r + 1) for r, w in enumerate((w1, w2, w3))]
    decay = jnp.exp(-speed * float(PLANE * rows))
    last = shift_ctx(both, PLANE)
    earlier = shift_ctx(both + decay * last, 2 * PLANE)
    f0, w0, earlier = tie(f0, w0, earlier)
    out0, mid0 = outward(f0), across(w0)
    gated = gated_conv(q, k, v, rate, residue, skip, before, ([last, earlier], spot))
    rest = jnp.concatenate(arrived)
    gated, rest, out0, mid0 = tie(gated, rest, out0, mid0)

    nr, fr = near(rest), far(rest)
    ours = [gated] + [exchange(gated, "ctx", r) for r in range(1, PLANE)]
    theirs_x = exchange(ours[1], "ch", 1)
    half = cols // 2
    restA, restB = rest[:, :half], rest[:, half:]
    fr, nr, rest, restA, restB, flags, places, theirs_x, *ours = tie(
        fr, nr, rest, restA, restB, flags, places, theirs_x, *ours
    )

    outA, midA = outward(fr[:, :half]), across(restA)
    theirs = [theirs_x if r == 1 else exchange(x, "ch", 1) for r, x in enumerate(ours)]
    blocks = [
        (0, None, [((w0,), 0), ((rest,), 0)]),
        (1, None, [((n0,), 0), ((nr,), 0)]),
        (2, None, [((f0,), 0), ((fr,), 0)]),
    ]
    (accs,) = product(flags, places, ours, theirs, blocks, None, 0, cols, jnp.float32)
    frB = fr[:, half:]
    outA, midA, frB, restB, *accs = tie(outA, midA, frB, restB, *accs)

    outB, midB = outward(frB), across(restB)

    def finish(first, out1, mid1):
        blocks = [(3, 4, [((out0, mid0), first), ((out1, mid1), 0)])]
        (made,) = product(flags, places, ours, theirs, blocks, accs, first, half, jnp.bfloat16)
        return [made[0]] + [exchange(made[r], "ctx", r) for r in range(1, PLANE)]

    return assemble(places, [finish(0, outA, midA), finish(half, outB, midB)])


def body(q, k, v, residue, rate, skip, w_out):
    rows, chan = q.shape
    modes = rate.shape[0]
    groups = chan // LANES
    count, cores = lax.axis_size("ctx"), lax.axis_size("ch")
    chunk, feats = w_out.shape
    split = (
        count == 4 * PLANE
        and cores == 2
        and chan == 8 * chunk
        and chunk % LANES == 0
        and feats % (2 * PLANE * LANES) == 0
    )
    skip = skip.reshape(groups, LANES)
    if split:
        return split_block(q, k, v, residue, rate, skip, w_out)
    ends = end_states(k, v, rate)
    enter = entering_states(ends, rate.reshape(modes, groups, LANES), rows)
    gated = gated_conv(q, k, v, rate, residue, skip, enter)
    gated = gated.transpose(1, 0, 2).reshape(rows, chan)
    full_gated = lax.all_gather(gated, "ch", axis=1, tiled=True)
    w_full = lax.all_gather(w_out, "ctx", axis=0, tiled=True)
    mixed = jnp.dot(full_gated, w_full, preferred_element_type=jnp.float32)
    return mixed.astype(jnp.bfloat16)


def solution(mesh):
    placed = (
        P("ctx", "ch"),
        P("ctx", "ch"),
        P("ctx", "ch"),
        P(None, "ch"),
        P(None, "ch"),
        P("ch"),
        P("ctx", "ch"),
    )
    return jax.shard_map(
        body, mesh=mesh, in_specs=placed, out_specs=P("ctx", "ch"), check_vma=False
    )
```

```python
import jax
import jax.numpy as jnp
from jax import lax
from jax.experimental import pallas as pl
from jax.experimental.pallas import tpu as pltpu
from jax.sharding import PartitionSpec as P

LANES = 128
RADIX = 4
PLANE = 4
VMEM_BYTES = 60 << 20


def spread_signal(k_ref, v_ref, sig_ref):
    rows, width = k_ref.shape
    groups = width // LANES
    for g in range(groups):
        cols = pl.ds(g * LANES, LANES)
        product = k_ref[:, cols].astype(jnp.float32) * v_ref[:, cols].astype(jnp.float32)
        sig_ref[pl.ds(g, rows, stride=groups), :] = product


def spread_modes(ref, out_ref):
    modes, width = ref.shape
    groups = width // LANES
    for g in range(groups):
        out_ref[pl.ds(g, modes, stride=groups), :] = ref[:, pl.ds(g * LANES, LANES)]


def ends_kernel(k_ref, v_ref, rate_ref, end_ref, sig_ref, mode_ref):
    rows, width = k_ref.shape
    modes, groups, _ = end_ref.shape
    spread_signal(k_ref, v_ref, sig_ref)
    spread_modes(rate_ref, mode_ref)
    decay = [jnp.exp(-mode_ref[pl.ds(m * groups, groups), :]) for m in range(modes)]

    def step(t, state):
        s = sig_ref[pl.ds(pl.multiple_of(t * groups, groups), groups), :]
        return tuple(d * h + s for d, h in zip(decay, state))

    zero = jnp.zeros((groups, LANES), jnp.float32)
    state = lax.fori_loop(0, rows, step, (zero,) * modes, unroll=8)
    for m in range(modes):
        end_ref[m] = state[m]


def conv_kernel(q_ref, k_ref, v_ref, rate_ref, residue_ref, skip_ref, enter_ref, *refs):
    *plane_refs, out_ref, sig_ref, conv_ref, mode_ref, weight_ref = refs
    rows, width = k_ref.shape
    modes, groups, _ = enter_ref.shape
    spread_signal(k_ref, v_ref, sig_ref)
    spread_modes(rate_ref, mode_ref)
    spread_modes(residue_ref, weight_ref)
    rates = [mode_ref[pl.ds(m * groups, groups), :] for m in range(modes)]
    decay = [jnp.exp(-rate) for rate in rates]
    weight = [weight_ref[pl.ds(m * groups, groups), :] * jnp.sqrt(2.0 * rate) for m, rate in enumerate(rates)]
    skip = skip_ref[...]
    enter = [enter_ref[m] for m in range(modes)]
    if plane_refs:
        *earlier_refs, spot_ref = plane_refs
        ahead = (spot_ref[0] * rows).astype(jnp.float32)
        for m, rate in enumerate(rates):
            for n, earlier_ref in enumerate(earlier_refs):
                enter[m] = enter[m] + jnp.exp(-rate * (ahead + float(n * PLANE * rows))) * earlier_ref[m]

    def step(t, state):
        at = pl.ds(pl.multiple_of(t * groups, groups), groups)
        s = sig_ref[at, :]
        state = tuple(d * h + s for d, h in zip(decay, state))
        terms = [c * h for c, h in zip(weight, state)] + [skip * s]
        while len(terms) > 1:
            terms = [sum(terms[i : i + 2]) for i in range(0, len(terms), 2)]
        conv_ref[at, :] = terms[0]
        return state

    lax.fori_loop(0, rows, step, tuple(enter), unroll=4)
    for g in range(groups):
        cols = pl.ds(g * LANES, LANES)
        conv = conv_ref[pl.ds(g, rows, stride=groups), :]
        out_ref[:, cols] = (q_ref[:, cols].astype(jnp.float32) * conv).astype(out_ref.dtype)


def block_specs(rows, modes, width):
    groups = width // LANES
    return (
        pl.BlockSpec((rows, width), lambda i: (0, i)),
        pl.BlockSpec((modes, width), lambda i: (0, i)),
        pl.BlockSpec((modes, groups, LANES), lambda i: (0, i, 0)),
        pl.BlockSpec((groups, LANES), lambda i: (i, 0)),
    )


def end_states(k, v, rate):
    rows, chan = k.shape
    modes = rate.shape[0]
    width = min(chan, 8 * LANES)
    wide, moded, state, _ = block_specs(rows, modes, width)
    return pl.pallas_call(
        ends_kernel,
        grid=(chan // width,),
        in_specs=[wide, wide, moded],
        out_specs=state,
        out_shape=jax.ShapeDtypeStruct((modes, chan // LANES, LANES), jnp.float32),
        scratch_shapes=[
            pltpu.VMEM((rows * width // LANES, LANES), jnp.float32),
            pltpu.VMEM((modes * width // LANES, LANES), jnp.float32),
        ],
        compiler_params=pltpu.CompilerParams(vmem_limit_bytes=VMEM_BYTES),
        cost_estimate=pl.CostEstimate(
            flops=2 * modes * rows * chan, bytes_accessed=4 * rows * chan, transcendentals=modes * chan
        ),
        name="end_states",
    )(k, v, rate)


def gated_conv(q, k, v, rate, residue, skip, enter, planes=None):
    rows, chan = k.shape
    modes = rate.shape[0]
    width = min(chan, 8 * LANES)
    wide, moded, state, single = block_specs(rows, modes, width)
    spread = pltpu.VMEM((rows * width // LANES, LANES), jnp.float32)
    moded_spread = pltpu.VMEM((modes * width // LANES, LANES), jnp.float32)
    extra, extra_specs = [], []
    if planes is not None:
        earlier, spot = planes
        extra = [*earlier, spot.reshape(1).astype(jnp.int32)]
        extra_specs = [state] * len(earlier) + [pl.BlockSpec(memory_space=pltpu.SMEM)]
    return pl.pallas_call(
        conv_kernel,
        grid=(chan // width,),
        in_specs=[wide, wide, wide, moded, moded, single, state] + extra_specs,
        out_specs=pl.BlockSpec((None, rows, width), lambda i: (i, 0, 0)),
        out_shape=jax.ShapeDtypeStruct((chan // width, rows, width), jnp.bfloat16),
        scratch_shapes=[spread, spread, moded_spread, moded_spread],
        compiler_params=pltpu.CompilerParams(vmem_limit_bytes=VMEM_BYTES),
        cost_estimate=pl.CostEstimate(
            flops=4 * modes * rows * chan, bytes_accessed=8 * rows * chan, transcendentals=2 * modes * chan
        ),
        name="gated_conv",
    )(q, k, v, rate, residue, skip, enter, *extra)


def shift_ctx(x, by):
    count = lax.axis_size("ctx")
    return lax.ppermute(x, "ctx", [(i, i + by) for i in range(count - by)])


def exchange(x, axis, flip):
    count = lax.axis_size(axis)
    return lax.ppermute(x, axis, [(i, i ^ flip) for i in range(count)])


def tie(*values):
    return lax.optimization_barrier(values)


def entering_states(ends, rate, rows):
    count = lax.axis_size("ctx")
    total = jnp.zeros_like(ends)
    for k in range(1, min(RADIX, count - 1) + 1):
        total = total + jnp.exp(-rate * float(rows * (k - 1))) * shift_ctx(ends, k)
    stride = RADIX
    while stride < count:
        base = total
        for k in range(1, RADIX):
            if stride * k < count:
                total = total + jnp.exp(-rate * float(rows * stride * k)) * shift_ctx(base, stride * k)
        stride *= RADIX
    return total


def box(fn, *args):
    once = (lax.axis_index("ctx") >= 0).astype(jnp.int32)
    shapes = jax.eval_shape(fn, *args)
    empty = pl.pallas_call(
        lambda *refs: None,
        out_specs=[pl.BlockSpec(memory_space=pl.ANY)] * len(shapes),
        out_shape=list(shapes),
        name="blank",
    )()

    def run(step, _):
        return fn(*tie(step, *args)[1:])

    return lax.fori_loop(0, once, run, tuple(empty))


def product(flags, places, ours, theirs, blocks, accs, first_col, cols, out_dtype):
    _, rows, depth = ours[0].shape
    chunk = depth // PLANE
    count, parts = len(blocks), len(ours)
    weights = [array for _, _, pieces in blocks for choices, _ in pieces for array in choices]
    accs = accs or []

    def kernel(flag_ref, place_ref, *refs):
        our_refs, their_refs, refs = refs[:parts], refs[parts : 2 * parts], refs[2 * parts :]
        weight_refs, refs = list(refs[: len(weights)]), refs[len(weights) :]
        acc_refs, out_refs = refs[: len(accs)], refs[len(accs) : len(accs) + parts]
        gated_buf, weight_buf, acc_buf, gated_sems, weight_sems, acc_sem = refs[-6:]

        def target(b, at):
            start = pl.multiple_of(b * depth + place_ref[at // chunk] * chunk, chunk)
            return weight_buf.at[pl.ds(start, chunk), :]

        for b, (flag, pick, pieces) in enumerate(blocks):
            row = 0
            for choices, col in pieces:
                for c in range(len(choices)):
                    ref = weight_refs.pop(0)
                    for at in range(0, ref.shape[0], chunk):
                        source = ref.at[pl.ds(at, chunk), pl.ds(col, cols)]
                        copy = pltpu.make_async_copy(source, target(b, row + at), weight_sems.at[b])
                        if pick is None:
                            copy.start()
                        else:
                            pl.when(flag_ref[pick] == c)(copy.start)
                row += choices[0].shape[0]
            half = flag_ref[flag] & 1
            for r in range(parts):
                for c, refs_of in enumerate((our_refs, their_refs)):
                    target_rows = gated_buf.at[b, pl.ds(r * rows, rows), :]
                    copy = pltpu.make_async_copy(refs_of[r].at[half], target_rows, gated_sems.at[b])
                    pl.when(flag_ref[flag] // 2 == c)(copy.start)
        for r, acc_ref in enumerate(acc_refs):
            pltpu.make_async_copy(acc_ref.at[:, pl.ds(first_col, cols)], acc_buf.at[r], acc_sem).start()
        for b in range(count):
            block = weight_buf.at[pl.ds(b * depth, depth), :]
            pltpu.make_async_copy(block, block, weight_sems.at[b]).wait()
            pltpu.make_async_copy(gated_buf.at[b], gated_buf.at[b], gated_sems.at[b]).wait()
            if accs and not b:
                pltpu.make_async_copy(acc_buf, acc_buf, acc_sem).wait()
            for col in range(0, cols, 2 * LANES):
                here = pl.ds(col, min(2 * LANES, cols - col))
                made = jnp.dot(
                    gated_buf[b], weight_buf[pl.ds(b * depth, depth), here], preferred_element_type=jnp.float32
                )
                for r in range(parts):
                    total = made[r * rows : (r + 1) * rows]
                    if b:
                        total = total + out_refs[r][:, here]
                    elif accs:
                        total = total + acc_buf[r, :, here]
                    out_refs[r][:, here] = total.astype(out_dtype)

    smem = pl.BlockSpec(memory_space=pltpu.SMEM)
    anywhere = pl.BlockSpec(memory_space=pl.ANY)
    made = pl.pallas_call(
        kernel,
        in_specs=[smem, smem] + [anywhere] * (2 * parts + len(weights) + len(accs)),
        out_specs=[pl.BlockSpec(memory_space=pltpu.VMEM)] * parts,
        out_shape=[jax.ShapeDtypeStruct((rows, cols), out_dtype)] * parts,
        scratch_shapes=[
            pltpu.VMEM((count, parts * rows, depth), jnp.bfloat16),
            pltpu.VMEM((count * depth, cols), jnp.bfloat16),
            pltpu.VMEM((parts, rows, cols) if accs else (8, LANES), jnp.float32),
            pltpu.SemaphoreType.DMA((count,)),
            pltpu.SemaphoreType.DMA((count,)),
            pltpu.SemaphoreType.DMA,
        ],
        compiler_params=pltpu.CompilerParams(vmem_limit_bytes=VMEM_BYTES),
        cost_estimate=pl.CostEstimate(
            flops=2 * parts * rows * depth * count * cols,
            bytes_accessed=2 * count * depth * (parts * rows + cols),
            transcendentals=0,
        ),
        name="product",
    )(flags, places, *ours, *theirs, *weights, *accs)
    return [list(made)]


def assemble(places, parts):
    rows = parts[0][0].shape[0]
    widths = [part[0].shape[1] for part in parts]
    cols = sum(widths)
    flat = [piece for part in parts for piece in part]

    def kernel(place_ref, *refs):
        *piece_refs, out_ref, sems = refs
        copies = []
        first = 0
        for part, width in enumerate(widths):
            for r in range(PLANE):
                at = part * PLANE + r
                start = pl.multiple_of(place_ref[r] * cols + first, LANES)
                target = out_ref.at[:, pl.ds(start, width)]
                copies.append(pltpu.make_async_copy(piece_refs[at], target, sems.at[at]))
                copies[-1].start()
            first += width
        for copy in copies:
            copy.wait()

    return pl.pallas_call(
        kernel,
        in_specs=[pl.BlockSpec(memory_space=pltpu.SMEM)] + [pl.BlockSpec(memory_space=pltpu.VMEM)] * len(flat),
        out_specs=pl.BlockSpec(memory_space=pl.ANY),
        out_shape=jax.ShapeDtypeStruct((rows, cols * PLANE), flat[0].dtype),
        scratch_shapes=[pltpu.SemaphoreType.DMA((len(flat),))],
        compiler_params=pltpu.CompilerParams(vmem_limit_bytes=16 << 20),
        name="assemble",
    )(places, *flat)


def split_block(q, k, v, residue, rate, skip, w_out):
    rows, chan = q.shape
    modes = rate.shape[0]
    me = lax.axis_index("ctx")
    core = lax.axis_index("ch")
    spot, plane = me & (PLANE - 1), me // PLANE
    count = lax.axis_size("ctx")
    chunk, feats = w_out.shape
    cols = feats // PLANE
    speed = rate.reshape(modes, chan // LANES, LANES)

    def far(x):
        return exchange(x, "ctx", 2 * PLANE)

    def near(x):
        return exchange(x, "ctx", PLANE)

    middle = [i for i in range(count) if PLANE <= i < 3 * PLANE]

    def across(x):
        return lax.ppermute(x, "ctx", [(i, i ^ (3 * PLANE)) for i in middle])

    def outward(x):
        return lax.ppermute(x, "ctx", [(i, i ^ PLANE) for i in middle])

    def group(x, r):
        return lax.dynamic_slice_in_dim(x, (spot ^ r) * cols, cols, axis=1)

    def source_of(b):
        return jnp.where(b // 2 == core, b & 1, 2 + (b & 1))

    is_middle = jnp.where((plane == 0) | (plane == 3), 0, 1)
    flags = jnp.stack([source_of(plane ^ r) for r in range(4)] + [is_middle]).astype(jnp.int32)
    places = jnp.stack([spot ^ r for r in range(PLANE)]).astype(jnp.int32)

    def plane_scan(k, v, rate, speed):
        def fade(span):
            return jnp.exp(-speed * span)

        ends = end_states(k, v, rate)
        other = exchange(ends, "ctx", 1)
        both = jnp.where(x_later, fade(float(rows)) * other + ends, fade(float(rows)) * ends + other)
        before = jnp.where(x_later, other, 0.0)
        other = exchange(both, "ctx", 2)
        before = before + jnp.where(y_later, fade((spot & 1).astype(jnp.float32) * rows) * other, 0.0)
        both = jnp.where(y_later, fade(2.0 * rows) * other + both, fade(2.0 * rows) * both + other)
        return both, before

    x_later, y_later = (spot & 1) != 0, (spot & 2) != 0
    w0, w1, w2, w3 = tie(*[group(w_out, r) for r in range(PLANE)])
    f0, n0 = far(w0), near(w0)
    both, before = box(plane_scan, k, v, rate, speed)
    n0, f0, w0, w1, w2, w3, both, before = tie(n0, f0, w0, w1, w2, w3, both, before)

    arrived = [exchange(w, "ctx", r + 1) for r, w in enumerate((w1, w2, w3))]
    decay = jnp.exp(-speed * float(PLANE * rows))
    last = shift_ctx(both, PLANE)
    earlier = shift_ctx(both + decay * last, 2 * PLANE)
    f0, w0, earlier = tie(f0, w0, earlier)
    out0, mid0 = outward(f0), across(w0)
    gated = gated_conv(q, k, v, rate, residue, skip, before, ([last, earlier], spot))
    rest = jnp.concatenate(arrived)
    gated, rest, mid0, out0 = tie(gated, rest, mid0, out0)

    nr, fr = near(rest), far(rest)
    ours = [gated] + [exchange(gated, "ctx", r) for r in range(1, PLANE)]
    theirs_x = exchange(ours[1], "ch", 1)
    wide = 2 * cols // 3
    restA, restB = rest[:, :wide], rest[:, wide:]
    fr, nr, rest, restA, restB, flags, places, theirs_x, *ours = tie(
        fr, nr, rest, restA, restB, flags, places, theirs_x, *ours
    )

    outA, midA = outward(fr[:, :wide]), across(restA)
    theirs = [theirs_x if r == 1 else exchange(x, "ch", 1) for r, x in enumerate(ours)]
    blocks = [
        (0, None, [((w0,), 0), ((rest,), 0)]),
        (1, None, [((n0,), 0), ((nr,), 0)]),
        (2, None, [((f0,), 0), ((fr,), 0)]),
    ]
    late, theirs[0] = tie(fr, theirs[0])
    frB = late[:, wide:]
    (accs,) = product(flags, places, ours, theirs, blocks, None, 0, cols, jnp.float32)
    outA, midA, frB, restB, *accs = tie(outA, midA, frB, restB, *accs)

    outB, midB = outward(frB), across(restB)

    def finish(first, width, out1, mid1):
        blocks = [(3, 4, [((out0, mid0), first), ((out1, mid1), 0)])]
        (made,) = product(flags, places, ours, theirs, blocks, accs, first, width, jnp.bfloat16)
        return [made[0]] + [exchange(made[r], "ctx", r) for r in range(1, PLANE)]

    return assemble(places, [finish(0, wide, outA, midA), finish(wide, cols - wide, outB, midB)])


def body(q, k, v, residue, rate, skip, w_out):
    rows, chan = q.shape
    modes = rate.shape[0]
    groups = chan // LANES
    count, cores = lax.axis_size("ctx"), lax.axis_size("ch")
    chunk, feats = w_out.shape
    split = (
        count == 4 * PLANE
        and cores == 2
        and chan == 8 * chunk
        and chunk % LANES == 0
        and feats % (6 * PLANE * LANES) == 0
    )
    skip = skip.reshape(groups, LANES)
    if split:
        return split_block(q, k, v, residue, rate, skip, w_out)
    ends = end_states(k, v, rate)
    enter = entering_states(ends, rate.reshape(modes, groups, LANES), rows)
    gated = gated_conv(q, k, v, rate, residue, skip, enter)
    gated = gated.transpose(1, 0, 2).reshape(rows, chan)
    full_gated = lax.all_gather(gated, "ch", axis=1, tiled=True)
    w_full = lax.all_gather(w_out, "ctx", axis=0, tiled=True)
    mixed = jnp.dot(full_gated, w_full, preferred_element_type=jnp.float32)
    return mixed.astype(jnp.bfloat16)


def solution(mesh):
    placed = (
        P("ctx", "ch"),
        P("ctx", "ch"),
        P("ctx", "ch"),
        P(None, "ch"),
        P(None, "ch"),
        P("ch"),
        P("ctx", "ch"),
    )
    return jax.shard_map(
        body, mesh=mesh, in_specs=placed, out_specs=P("ctx", "ch"), check_vma=False
    )
```

```python
import jax
import jax.numpy as jnp
from jax import lax
from jax.experimental import pallas as pl
from jax.experimental.pallas import tpu as pltpu
from jax.sharding import PartitionSpec as P

LANES = 128
RADIX = 4
PLANE = 4
VMEM_BYTES = 60 << 20


def spread_signal(k_ref, v_ref, sig_ref):
    rows, width = k_ref.shape
    groups = width // LANES
    for g in range(groups):
        cols = pl.ds(g * LANES, LANES)
        product = k_ref[:, cols].astype(jnp.float32) * v_ref[:, cols].astype(jnp.float32)
        sig_ref[pl.ds(g, rows, stride=groups), :] = product


def spread_modes(ref, out_ref):
    modes, width = ref.shape
    groups = width // LANES
    for g in range(groups):
        out_ref[pl.ds(g, modes, stride=groups), :] = ref[:, pl.ds(g * LANES, LANES)]


def ends_kernel(k_ref, v_ref, rate_ref, end_ref, sig_ref, mode_ref):
    rows, width = k_ref.shape
    modes, groups, _ = end_ref.shape
    spread_signal(k_ref, v_ref, sig_ref)
    spread_modes(rate_ref, mode_ref)
    decay = [jnp.exp(-mode_ref[pl.ds(m * groups, groups), :]) for m in range(modes)]

    def step(t, state):
        s = sig_ref[pl.ds(pl.multiple_of(t * groups, groups), groups), :]
        return tuple(d * h + s for d, h in zip(decay, state))

    zero = jnp.zeros((groups, LANES), jnp.float32)
    state = lax.fori_loop(0, rows, step, (zero,) * modes, unroll=8)
    for m in range(modes):
        end_ref[m] = state[m]


def conv_kernel(q_ref, k_ref, v_ref, rate_ref, residue_ref, skip_ref, enter_ref, *refs):
    *plane_refs, out_ref, sig_ref, conv_ref, mode_ref, weight_ref = refs
    rows, width = k_ref.shape
    modes, groups, _ = enter_ref.shape
    spread_signal(k_ref, v_ref, sig_ref)
    spread_modes(rate_ref, mode_ref)
    spread_modes(residue_ref, weight_ref)
    rates = [mode_ref[pl.ds(m * groups, groups), :] for m in range(modes)]
    decay = [jnp.exp(-rate) for rate in rates]
    weight = [weight_ref[pl.ds(m * groups, groups), :] * jnp.sqrt(2.0 * rate) for m, rate in enumerate(rates)]
    skip = skip_ref[...]
    enter = [enter_ref[m] for m in range(modes)]
    if plane_refs:
        *earlier_refs, spot_ref = plane_refs
        ahead = (spot_ref[0] * rows).astype(jnp.float32)
        for m, rate in enumerate(rates):
            for n, earlier_ref in enumerate(earlier_refs):
                enter[m] = enter[m] + jnp.exp(-rate * (ahead + float(n * PLANE * rows))) * earlier_ref[m]

    def step(t, state):
        at = pl.ds(pl.multiple_of(t * groups, groups), groups)
        s = sig_ref[at, :]
        state = tuple(d * h + s for d, h in zip(decay, state))
        terms = [c * h for c, h in zip(weight, state)] + [skip * s]
        while len(terms) > 1:
            terms = [sum(terms[i : i + 2]) for i in range(0, len(terms), 2)]
        conv_ref[at, :] = terms[0]
        return state

    lax.fori_loop(0, rows, step, tuple(enter), unroll=4)
    for g in range(groups):
        cols = pl.ds(g * LANES, LANES)
        conv = conv_ref[pl.ds(g, rows, stride=groups), :]
        out_ref[:, cols] = (q_ref[:, cols].astype(jnp.float32) * conv).astype(out_ref.dtype)


def block_specs(rows, modes, width):
    groups = width // LANES
    return (
        pl.BlockSpec((rows, width), lambda i: (0, i)),
        pl.BlockSpec((modes, width), lambda i: (0, i)),
        pl.BlockSpec((modes, groups, LANES), lambda i: (0, i, 0)),
        pl.BlockSpec((groups, LANES), lambda i: (i, 0)),
    )


def end_states(k, v, rate):
    rows, chan = k.shape
    modes = rate.shape[0]
    width = min(chan, 8 * LANES)
    wide, moded, state, _ = block_specs(rows, modes, width)
    return pl.pallas_call(
        ends_kernel,
        grid=(chan // width,),
        in_specs=[wide, wide, moded],
        out_specs=state,
        out_shape=jax.ShapeDtypeStruct((modes, chan // LANES, LANES), jnp.float32),
        scratch_shapes=[
            pltpu.VMEM((rows * width // LANES, LANES), jnp.float32),
            pltpu.VMEM((modes * width // LANES, LANES), jnp.float32),
        ],
        compiler_params=pltpu.CompilerParams(vmem_limit_bytes=VMEM_BYTES),
        cost_estimate=pl.CostEstimate(
            flops=2 * modes * rows * chan, bytes_accessed=4 * rows * chan, transcendentals=modes * chan
        ),
        name="end_states",
    )(k, v, rate)


def gated_conv(q, k, v, rate, residue, skip, enter, planes=None):
    rows, chan = k.shape
    modes = rate.shape[0]
    width = min(chan, 8 * LANES)
    wide, moded, state, single = block_specs(rows, modes, width)
    spread = pltpu.VMEM((rows * width // LANES, LANES), jnp.float32)
    moded_spread = pltpu.VMEM((modes * width // LANES, LANES), jnp.float32)
    extra, extra_specs = [], []
    if planes is not None:
        earlier, spot = planes
        extra = [*earlier, spot.reshape(1).astype(jnp.int32)]
        extra_specs = [state] * len(earlier) + [pl.BlockSpec(memory_space=pltpu.SMEM)]
    return pl.pallas_call(
        conv_kernel,
        grid=(chan // width,),
        in_specs=[wide, wide, wide, moded, moded, single, state] + extra_specs,
        out_specs=pl.BlockSpec((None, rows, width), lambda i: (i, 0, 0)),
        out_shape=jax.ShapeDtypeStruct((chan // width, rows, width), jnp.bfloat16),
        scratch_shapes=[spread, spread, moded_spread, moded_spread],
        compiler_params=pltpu.CompilerParams(vmem_limit_bytes=VMEM_BYTES),
        cost_estimate=pl.CostEstimate(
            flops=4 * modes * rows * chan, bytes_accessed=8 * rows * chan, transcendentals=2 * modes * chan
        ),
        name="gated_conv",
    )(q, k, v, rate, residue, skip, enter, *extra)


def shift_ctx(x, by):
    count = lax.axis_size("ctx")
    return lax.ppermute(x, "ctx", [(i, i + by) for i in range(count - by)])


def exchange(x, axis, flip):
    count = lax.axis_size(axis)
    return lax.ppermute(x, axis, [(i, i ^ flip) for i in range(count)])


def tie(*values):
    return lax.optimization_barrier(values)


def entering_states(ends, rate, rows):
    count = lax.axis_size("ctx")
    total = jnp.zeros_like(ends)
    for k in range(1, min(RADIX, count - 1) + 1):
        total = total + jnp.exp(-rate * float(rows * (k - 1))) * shift_ctx(ends, k)
    stride = RADIX
    while stride < count:
        base = total
        for k in range(1, RADIX):
            if stride * k < count:
                total = total + jnp.exp(-rate * float(rows * stride * k)) * shift_ctx(base, stride * k)
        stride *= RADIX
    return total


def box(fn, *args):
    once = (lax.axis_index("ctx") >= 0).astype(jnp.int32)
    shapes = jax.eval_shape(fn, *args)
    empty = pl.pallas_call(
        lambda *refs: None,
        out_specs=[pl.BlockSpec(memory_space=pl.ANY)] * len(shapes),
        out_shape=list(shapes),
        name="blank",
    )()

    def run(step, _):
        return fn(*tie(step, *args)[1:])

    return lax.fori_loop(0, once, run, tuple(empty))


def product(flags, places, ours, theirs, blocks, accs, first_col, cols, out_dtype):
    _, rows, depth = ours[0].shape
    chunk = depth // PLANE
    count, parts = len(blocks), len(ours)
    weights = [array for _, _, pieces in blocks for choices, _ in pieces for array in choices]
    accs = accs or []

    def kernel(flag_ref, place_ref, *refs):
        our_refs, their_refs, refs = refs[:parts], refs[parts : 2 * parts], refs[2 * parts :]
        weight_refs, refs = list(refs[: len(weights)]), refs[len(weights) :]
        acc_refs, out_refs = refs[: len(accs)], refs[len(accs) : len(accs) + parts]
        gated_buf, weight_buf, acc_buf, gated_sems, weight_sems, acc_sem = refs[-6:]

        def target(b, at):
            start = pl.multiple_of(b * depth + place_ref[at // chunk] * chunk, chunk)
            return weight_buf.at[pl.ds(start, chunk), :]

        for b, (flag, pick, pieces) in enumerate(blocks):
            row = 0
            for choices, col in pieces:
                for c in range(len(choices)):
                    ref = weight_refs.pop(0)
                    for at in range(0, ref.shape[0], chunk):
                        source = ref.at[pl.ds(at, chunk), pl.ds(col, cols)]
                        copy = pltpu.make_async_copy(source, target(b, row + at), weight_sems.at[b])
                        if pick is None:
                            copy.start()
                        else:
                            pl.when(flag_ref[pick] == c)(copy.start)
                row += choices[0].shape[0]
            half = flag_ref[flag] & 1
            for r in range(parts):
                for c, refs_of in enumerate((our_refs, their_refs)):
                    target_rows = gated_buf.at[b, pl.ds(r * rows, rows), :]
                    copy = pltpu.make_async_copy(refs_of[r].at[half], target_rows, gated_sems.at[b])
                    pl.when(flag_ref[flag] // 2 == c)(copy.start)
        for r, acc_ref in enumerate(acc_refs):
            pltpu.make_async_copy(acc_ref.at[:, pl.ds(first_col, cols)], acc_buf.at[r], acc_sem).start()
        for b in range(count):
            block = weight_buf.at[pl.ds(b * depth, depth), :]
            pltpu.make_async_copy(block, block, weight_sems.at[b]).wait()
            pltpu.make_async_copy(gated_buf.at[b], gated_buf.at[b], gated_sems.at[b]).wait()
            if accs and not b:
                pltpu.make_async_copy(acc_buf, acc_buf, acc_sem).wait()
            for col in range(0, cols, 2 * LANES):
                here = pl.ds(col, min(2 * LANES, cols - col))
                made = jnp.dot(
                    gated_buf[b], weight_buf[pl.ds(b * depth, depth), here], preferred_element_type=jnp.float32
                )
                for r in range(parts):
                    total = made[r * rows : (r + 1) * rows]
                    if b:
                        total = total + out_refs[r][:, here]
                    elif accs:
                        total = total + acc_buf[r, :, here]
                    out_refs[r][:, here] = total.astype(out_dtype)

    smem = pl.BlockSpec(memory_space=pltpu.SMEM)
    anywhere = pl.BlockSpec(memory_space=pl.ANY)
    made = pl.pallas_call(
        kernel,
        in_specs=[smem, smem] + [anywhere] * (2 * parts + len(weights) + len(accs)),
        out_specs=[pl.BlockSpec(memory_space=pltpu.VMEM)] * parts,
        out_shape=[jax.ShapeDtypeStruct((rows, cols), out_dtype)] * parts,
        scratch_shapes=[
            pltpu.VMEM((count, parts * rows, depth), jnp.bfloat16),
            pltpu.VMEM((count * depth, cols), jnp.bfloat16),
            pltpu.VMEM((parts, rows, cols) if accs else (8, LANES), jnp.float32),
            pltpu.SemaphoreType.DMA((count,)),
            pltpu.SemaphoreType.DMA((count,)),
            pltpu.SemaphoreType.DMA,
        ],
        compiler_params=pltpu.CompilerParams(vmem_limit_bytes=VMEM_BYTES),
        cost_estimate=pl.CostEstimate(
            flops=2 * parts * rows * depth * count * cols,
            bytes_accessed=2 * count * depth * (parts * rows + cols),
            transcendentals=0,
        ),
        name="product",
    )(flags, places, *ours, *theirs, *weights, *accs)
    return [list(made)]


def assemble(places, parts):
    rows = parts[0][0].shape[0]
    widths = [part[0].shape[1] for part in parts]
    cols = sum(widths)
    flat = [piece for part in parts for piece in part]

    def kernel(place_ref, *refs):
        *piece_refs, out_ref, sems = refs
        copies = []
        first = 0
        for part, width in enumerate(widths):
            for r in range(PLANE):
                at = part * PLANE + r
                start = pl.multiple_of(place_ref[r] * cols + first, LANES)
                target = out_ref.at[:, pl.ds(start, width)]
                copies.append(pltpu.make_async_copy(piece_refs[at], target, sems.at[at]))
                copies[-1].start()
            first += width
        for copy in copies:
            copy.wait()

    return pl.pallas_call(
        kernel,
        in_specs=[pl.BlockSpec(memory_space=pltpu.SMEM)] + [pl.BlockSpec(memory_space=pltpu.VMEM)] * len(flat),
        out_specs=pl.BlockSpec(memory_space=pl.ANY),
        out_shape=jax.ShapeDtypeStruct((rows, cols * PLANE), flat[0].dtype),
        scratch_shapes=[pltpu.SemaphoreType.DMA((len(flat),))],
        compiler_params=pltpu.CompilerParams(vmem_limit_bytes=16 << 20),
        name="assemble",
    )(places, *flat)


def split_block(q, k, v, residue, rate, skip, w_out):
    rows, chan = q.shape
    modes = rate.shape[0]
    me = lax.axis_index("ctx")
    core = lax.axis_index("ch")
    spot, plane = me & (PLANE - 1), me // PLANE
    count = lax.axis_size("ctx")
    chunk, feats = w_out.shape
    cols = feats // PLANE
    speed = rate.reshape(modes, chan // LANES, LANES)

    def far(x):
        return exchange(x, "ctx", 2 * PLANE)

    def near(x):
        return exchange(x, "ctx", PLANE)

    middle = [i for i in range(count) if PLANE <= i < 3 * PLANE]

    def across(x):
        return lax.ppermute(x, "ctx", [(i, i ^ (3 * PLANE)) for i in middle])

    def outward(x):
        return lax.ppermute(x, "ctx", [(i, i ^ PLANE) for i in middle])

    def group(x, r):
        return lax.dynamic_slice_in_dim(x, (spot ^ r) * cols, cols, axis=1)

    def source_of(b):
        return jnp.where(b // 2 == core, b & 1, 2 + (b & 1))

    is_middle = jnp.where((plane == 0) | (plane == 3), 0, 1)
    flags = jnp.stack([source_of(plane ^ r) for r in range(4)] + [is_middle]).astype(jnp.int32)
    places = jnp.stack([spot ^ r for r in range(PLANE)]).astype(jnp.int32)

    def plane_scan(k, v, rate, speed):
        def fade(span):
            return jnp.exp(-speed * span)

        ends = end_states(k, v, rate)
        other = exchange(ends, "ctx", 1)
        both = jnp.where(x_later, fade(float(rows)) * other + ends, fade(float(rows)) * ends + other)
        before = jnp.where(x_later, other, 0.0)
        other = exchange(both, "ctx", 2)
        before = before + jnp.where(y_later, fade((spot & 1).astype(jnp.float32) * rows) * other, 0.0)
        both = jnp.where(y_later, fade(2.0 * rows) * other + both, fade(2.0 * rows) * both + other)
        return both, before

    x_later, y_later = (spot & 1) != 0, (spot & 2) != 0
    w0, w1, w2, w3 = tie(*[group(w_out, r) for r in range(PLANE)])
    f0, n0 = far(w0), near(w0)
    both, before = box(plane_scan, k, v, rate, speed)
    n0, f0, w0, w1, w2, w3, both, before = tie(n0, f0, w0, w1, w2, w3, both, before)

    arrived = [exchange(w, "ctx", r + 1) for r, w in enumerate((w1, w2, w3))]
    decay = jnp.exp(-speed * float(PLANE * rows))
    last = shift_ctx(both, PLANE)
    earlier = shift_ctx(both + decay * last, 2 * PLANE)
    f0, w0, earlier = tie(f0, w0, earlier)
    out0, mid0 = outward(f0), across(w0)
    gated = gated_conv(q, k, v, rate, residue, skip, before, ([last, earlier], spot))
    rest = jnp.concatenate(arrived)

    nr, fr = near(rest), far(rest)
    ours = [gated] + [exchange(gated, "ctx", r) for r in range(1, PLANE)]
    wide = 2 * cols // 3
    restA, restB = rest[:, :wide], rest[:, wide:]
    fr, nr, rest, restA, restB, mid0, out0, flags, places, *ours = tie(
        fr, nr, rest, restA, restB, mid0, out0, flags, places, *ours
    )

    outA, midA = outward(fr[:, :wide]), across(restA)
    theirs = [exchange(x, "ch", 1) for x in ours]
    blocks = [
        (0, None, [((w0,), 0), ((rest,), 0)]),
        (1, None, [((n0,), 0), ((nr,), 0)]),
        (2, None, [((f0,), 0), ((fr,), 0)]),
    ]
    late, theirs[0] = tie(fr, theirs[0])
    frB = late[:, wide:]
    (accs,) = product(flags, places, ours, theirs, blocks, None, 0, cols, jnp.float32)
    outA, midA, frB, restB, *accs = tie(outA, midA, frB, restB, *accs)

    outB, midB = outward(frB), across(restB)

    def finish(first, width, out1, mid1):
        blocks = [(3, 4, [((out0, mid0), first), ((out1, mid1), 0)])]
        (made,) = product(flags, places, ours, theirs, blocks, accs, first, width, jnp.bfloat16)
        return [made[0]] + [exchange(made[r], "ctx", r) for r in range(1, PLANE)]

    return assemble(places, [finish(0, wide, outA, midA), finish(wide, cols - wide, outB, midB)])


def body(q, k, v, residue, rate, skip, w_out):
    rows, chan = q.shape
    modes = rate.shape[0]
    groups = chan // LANES
    count, cores = lax.axis_size("ctx"), lax.axis_size("ch")
    chunk, feats = w_out.shape
    split = (
        count == 4 * PLANE
        and cores == 2
        and chan == 8 * chunk
        and chunk % LANES == 0
        and feats % (6 * PLANE * LANES) == 0
    )
    skip = skip.reshape(groups, LANES)
    if split:
        return split_block(q, k, v, residue, rate, skip, w_out)
    ends = end_states(k, v, rate)
    enter = entering_states(ends, rate.reshape(modes, groups, LANES), rows)
    gated = gated_conv(q, k, v, rate, residue, skip, enter)
    gated = gated.transpose(1, 0, 2).reshape(rows, chan)
    full_gated = lax.all_gather(gated, "ch", axis=1, tiled=True)
    w_full = lax.all_gather(w_out, "ctx", axis=0, tiled=True)
    mixed = jnp.dot(full_gated, w_full, preferred_element_type=jnp.float32)
    return mixed.astype(jnp.bfloat16)


def solution(mesh):
    placed = (
        P("ctx", "ch"),
        P("ctx", "ch"),
        P("ctx", "ch"),
        P(None, "ch"),
        P(None, "ch"),
        P("ch"),
        P("ctx", "ch"),
    )
    return jax.shard_map(
        body, mesh=mesh, in_specs=placed, out_specs=P("ctx", "ch"), check_vma=False
    )
```

```python
import jax
import jax.numpy as jnp
from jax import lax
from jax.experimental import pallas as pl
from jax.experimental.pallas import tpu as pltpu
from jax.sharding import PartitionSpec as P

LANES = 128
RADIX = 4
PLANE = 4
VMEM_BYTES = 60 << 20


def spread_signal(k_ref, v_ref, sig_ref):
    rows, width = k_ref.shape
    groups = width // LANES
    for g in range(groups):
        cols = pl.ds(g * LANES, LANES)
        product = k_ref[:, cols].astype(jnp.float32) * v_ref[:, cols].astype(jnp.float32)
        sig_ref[pl.ds(g, rows, stride=groups), :] = product


def spread_modes(ref, out_ref):
    modes, width = ref.shape
    groups = width // LANES
    for g in range(groups):
        out_ref[pl.ds(g, modes, stride=groups), :] = ref[:, pl.ds(g * LANES, LANES)]


def ends_kernel(k_ref, v_ref, rate_ref, end_ref, sig_ref, mode_ref):
    rows, width = k_ref.shape
    modes, groups, _ = end_ref.shape
    spread_signal(k_ref, v_ref, sig_ref)
    spread_modes(rate_ref, mode_ref)
    decay = [jnp.exp(-mode_ref[pl.ds(m * groups, groups), :]) for m in range(modes)]

    def step(t, state):
        s = sig_ref[pl.ds(pl.multiple_of(t * groups, groups), groups), :]
        return tuple(d * h + s for d, h in zip(decay, state))

    zero = jnp.zeros((groups, LANES), jnp.float32)
    state = lax.fori_loop(0, rows, step, (zero,) * modes, unroll=8)
    for m in range(modes):
        end_ref[m] = state[m]


def conv_kernel(q_ref, k_ref, v_ref, rate_ref, residue_ref, skip_ref, enter_ref, *refs):
    *plane_refs, out_ref, sig_ref, conv_ref, mode_ref, weight_ref = refs
    rows, width = k_ref.shape
    modes, groups, _ = enter_ref.shape
    spread_signal(k_ref, v_ref, sig_ref)
    spread_modes(rate_ref, mode_ref)
    spread_modes(residue_ref, weight_ref)
    rates = [mode_ref[pl.ds(m * groups, groups), :] for m in range(modes)]
    decay = [jnp.exp(-rate) for rate in rates]
    weight = [weight_ref[pl.ds(m * groups, groups), :] * jnp.sqrt(2.0 * rate) for m, rate in enumerate(rates)]
    skip = skip_ref[...]
    enter = [enter_ref[m] for m in range(modes)]
    if plane_refs:
        *earlier_refs, spot_ref = plane_refs
        ahead = (spot_ref[0] * rows).astype(jnp.float32)
        for m, rate in enumerate(rates):
            for n, earlier_ref in enumerate(earlier_refs):
                enter[m] = enter[m] + jnp.exp(-rate * (ahead + float(n * PLANE * rows))) * earlier_ref[m]

    def step(t, state):
        at = pl.ds(pl.multiple_of(t * groups, groups), groups)
        s = sig_ref[at, :]
        state = tuple(d * h + s for d, h in zip(decay, state))
        terms = [c * h for c, h in zip(weight, state)] + [skip * s]
        while len(terms) > 1:
            terms = [sum(terms[i : i + 2]) for i in range(0, len(terms), 2)]
        conv_ref[at, :] = terms[0]
        return state

    lax.fori_loop(0, rows, step, tuple(enter), unroll=4)
    for g in range(groups):
        cols = pl.ds(g * LANES, LANES)
        conv = conv_ref[pl.ds(g, rows, stride=groups), :]
        out_ref[:, cols] = (q_ref[:, cols].astype(jnp.float32) * conv).astype(out_ref.dtype)


def block_specs(rows, modes, width):
    groups = width // LANES
    return (
        pl.BlockSpec((rows, width), lambda i: (0, i)),
        pl.BlockSpec((modes, width), lambda i: (0, i)),
        pl.BlockSpec((modes, groups, LANES), lambda i: (0, i, 0)),
        pl.BlockSpec((groups, LANES), lambda i: (i, 0)),
    )


def end_states(k, v, rate):
    rows, chan = k.shape
    modes = rate.shape[0]
    width = min(chan, 8 * LANES)
    wide, moded, state, _ = block_specs(rows, modes, width)
    return pl.pallas_call(
        ends_kernel,
        grid=(chan // width,),
        in_specs=[wide, wide, moded],
        out_specs=state,
        out_shape=jax.ShapeDtypeStruct((modes, chan // LANES, LANES), jnp.float32),
        scratch_shapes=[
            pltpu.VMEM((rows * width // LANES, LANES), jnp.float32),
            pltpu.VMEM((modes * width // LANES, LANES), jnp.float32),
        ],
        compiler_params=pltpu.CompilerParams(vmem_limit_bytes=VMEM_BYTES),
        cost_estimate=pl.CostEstimate(
            flops=2 * modes * rows * chan, bytes_accessed=4 * rows * chan, transcendentals=modes * chan
        ),
        name="end_states",
    )(k, v, rate)


def gated_conv(q, k, v, rate, residue, skip, enter, planes=None):
    rows, chan = k.shape
    modes = rate.shape[0]
    width = min(chan, 8 * LANES)
    wide, moded, state, single = block_specs(rows, modes, width)
    spread = pltpu.VMEM((rows * width // LANES, LANES), jnp.float32)
    moded_spread = pltpu.VMEM((modes * width // LANES, LANES), jnp.float32)
    extra, extra_specs = [], []
    if planes is not None:
        earlier, spot = planes
        extra = [*earlier, spot.reshape(1).astype(jnp.int32)]
        extra_specs = [state] * len(earlier) + [pl.BlockSpec(memory_space=pltpu.SMEM)]
    return pl.pallas_call(
        conv_kernel,
        grid=(chan // width,),
        in_specs=[wide, wide, wide, moded, moded, single, state] + extra_specs,
        out_specs=pl.BlockSpec((None, rows, width), lambda i: (i, 0, 0)),
        out_shape=jax.ShapeDtypeStruct((chan // width, rows, width), jnp.bfloat16),
        scratch_shapes=[spread, spread, moded_spread, moded_spread],
        compiler_params=pltpu.CompilerParams(vmem_limit_bytes=VMEM_BYTES),
        cost_estimate=pl.CostEstimate(
            flops=4 * modes * rows * chan, bytes_accessed=8 * rows * chan, transcendentals=2 * modes * chan
        ),
        name="gated_conv",
    )(q, k, v, rate, residue, skip, enter, *extra)


def shift_ctx(x, by):
    count = lax.axis_size("ctx")
    return lax.ppermute(x, "ctx", [(i, i + by) for i in range(count - by)])


def exchange(x, axis, flip):
    count = lax.axis_size(axis)
    return lax.ppermute(x, axis, [(i, i ^ flip) for i in range(count)])


def tie(*values):
    return lax.optimization_barrier(values)


def entering_states(ends, rate, rows):
    count = lax.axis_size("ctx")
    total = jnp.zeros_like(ends)
    for k in range(1, min(RADIX, count - 1) + 1):
        total = total + jnp.exp(-rate * float(rows * (k - 1))) * shift_ctx(ends, k)
    stride = RADIX
    while stride < count:
        base = total
        for k in range(1, RADIX):
            if stride * k < count:
                total = total + jnp.exp(-rate * float(rows * stride * k)) * shift_ctx(base, stride * k)
        stride *= RADIX
    return total


def box(fn, *args):
    once = (lax.axis_index("ctx") >= 0).astype(jnp.int32)
    shapes = jax.eval_shape(fn, *args)
    empty = pl.pallas_call(
        lambda *refs: None,
        out_specs=[pl.BlockSpec(memory_space=pl.ANY)] * len(shapes),
        out_shape=list(shapes),
        name="blank",
    )()

    def run(step, _):
        return fn(*tie(step, *args)[1:])

    return lax.fori_loop(0, once, run, tuple(empty))


def product(flags, places, ours, theirs, blocks, accs, first_col, cols, out_dtype):
    _, rows, depth = ours[0].shape
    chunk = depth // PLANE
    count, parts = len(blocks), len(ours)
    weights = [array for _, _, pieces in blocks for choices, _ in pieces for array in choices]
    accs = accs or []

    def kernel(flag_ref, place_ref, *refs):
        our_refs, their_refs, refs = refs[:parts], refs[parts : 2 * parts], refs[2 * parts :]
        weight_refs, refs = list(refs[: len(weights)]), refs[len(weights) :]
        acc_refs, out_refs = refs[: len(accs)], refs[len(accs) : len(accs) + parts]
        gated_buf, weight_buf, acc_buf, gated_sems, weight_sems, acc_sem = refs[-6:]

        def target(b, at):
            start = pl.multiple_of(b * depth + place_ref[at // chunk] * chunk, chunk)
            return weight_buf.at[pl.ds(start, chunk), :]

        for b, (flag, pick, pieces) in enumerate(blocks):
            row = 0
            for choices, col in pieces:
                for c in range(len(choices)):
                    ref = weight_refs.pop(0)
                    for at in range(0, ref.shape[0], chunk):
                        source = ref.at[pl.ds(at, chunk), pl.ds(col, cols)]
                        copy = pltpu.make_async_copy(source, target(b, row + at), weight_sems.at[b])
                        if pick is None:
                            copy.start()
                        else:
                            pl.when(flag_ref[pick] == c)(copy.start)
                row += choices[0].shape[0]
            half = flag_ref[flag] & 1
            for r in range(parts):
                for c, refs_of in enumerate((our_refs, their_refs)):
                    target_rows = gated_buf.at[b, pl.ds(r * rows, rows), :]
                    copy = pltpu.make_async_copy(refs_of[r].at[half], target_rows, gated_sems.at[b])
                    pl.when(flag_ref[flag] // 2 == c)(copy.start)
        for r, acc_ref in enumerate(acc_refs):
            pltpu.make_async_copy(acc_ref.at[:, pl.ds(first_col, cols)], acc_buf.at[r], acc_sem).start()
        for b in range(count):
            block = weight_buf.at[pl.ds(b * depth, depth), :]
            pltpu.make_async_copy(block, block, weight_sems.at[b]).wait()
            pltpu.make_async_copy(gated_buf.at[b], gated_buf.at[b], gated_sems.at[b]).wait()
            if accs and not b:
                pltpu.make_async_copy(acc_buf, acc_buf, acc_sem).wait()
            for col in range(0, cols, 2 * LANES):
                here = pl.ds(col, min(2 * LANES, cols - col))
                made = jnp.dot(
                    gated_buf[b], weight_buf[pl.ds(b * depth, depth), here], preferred_element_type=jnp.float32
                )
                for r in range(parts):
                    total = made[r * rows : (r + 1) * rows]
                    if b:
                        total = total + out_refs[r][:, here]
                    elif accs:
                        total = total + acc_buf[r, :, here]
                    out_refs[r][:, here] = total.astype(out_dtype)

    smem = pl.BlockSpec(memory_space=pltpu.SMEM)
    anywhere = pl.BlockSpec(memory_space=pl.ANY)
    made = pl.pallas_call(
        kernel,
        in_specs=[smem, smem] + [anywhere] * (2 * parts + len(weights) + len(accs)),
        out_specs=[pl.BlockSpec(memory_space=pltpu.VMEM)] * parts,
        out_shape=[jax.ShapeDtypeStruct((rows, cols), out_dtype)] * parts,
        scratch_shapes=[
            pltpu.VMEM((count, parts * rows, depth), jnp.bfloat16),
            pltpu.VMEM((count * depth, cols), jnp.bfloat16),
            pltpu.VMEM((parts, rows, cols) if accs else (8, LANES), jnp.float32),
            pltpu.SemaphoreType.DMA((count,)),
            pltpu.SemaphoreType.DMA((count,)),
            pltpu.SemaphoreType.DMA,
        ],
        compiler_params=pltpu.CompilerParams(vmem_limit_bytes=VMEM_BYTES),
        cost_estimate=pl.CostEstimate(
            flops=2 * parts * rows * depth * count * cols,
            bytes_accessed=2 * count * depth * (parts * rows + cols),
            transcendentals=0,
        ),
        name="product",
    )(flags, places, *ours, *theirs, *weights, *accs)
    return [list(made)]


def assemble(places, parts):
    rows = parts[0][0].shape[0]
    widths = [part[0].shape[1] for part in parts]
    cols = sum(widths)
    flat = [piece for part in parts for piece in part]

    def kernel(place_ref, *refs):
        *piece_refs, out_ref, sems = refs
        copies = []
        first = 0
        for part, width in enumerate(widths):
            for r in range(PLANE):
                at = part * PLANE + r
                start = pl.multiple_of(place_ref[r] * cols + first, LANES)
                target = out_ref.at[:, pl.ds(start, width)]
                copies.append(pltpu.make_async_copy(piece_refs[at], target, sems.at[at]))
                copies[-1].start()
            first += width
        for copy in copies:
            copy.wait()

    return pl.pallas_call(
        kernel,
        in_specs=[pl.BlockSpec(memory_space=pltpu.SMEM)] + [pl.BlockSpec(memory_space=pltpu.VMEM)] * len(flat),
        out_specs=pl.BlockSpec(memory_space=pl.ANY),
        out_shape=jax.ShapeDtypeStruct((rows, cols * PLANE), flat[0].dtype),
        scratch_shapes=[pltpu.SemaphoreType.DMA((len(flat),))],
        compiler_params=pltpu.CompilerParams(vmem_limit_bytes=16 << 20),
        name="assemble",
    )(places, *flat)


def split_block(q, k, v, residue, rate, skip, w_out):
    rows, chan = q.shape
    modes = rate.shape[0]
    me = lax.axis_index("ctx")
    core = lax.axis_index("ch")
    spot, plane = me & (PLANE - 1), me // PLANE
    count = lax.axis_size("ctx")
    chunk, feats = w_out.shape
    cols = feats // PLANE
    speed = rate.reshape(modes, chan // LANES, LANES)

    def far(x):
        return exchange(x, "ctx", 2 * PLANE)

    def near(x):
        return exchange(x, "ctx", PLANE)

    middle = [i for i in range(count) if PLANE <= i < 3 * PLANE]

    def across(x):
        return lax.ppermute(x, "ctx", [(i, i ^ (3 * PLANE)) for i in middle])

    def outward(x):
        return lax.ppermute(x, "ctx", [(i, i ^ PLANE) for i in middle])

    def group(x, r):
        return lax.dynamic_slice_in_dim(x, (spot ^ r) * cols, cols, axis=1)

    def source_of(b):
        return jnp.where(b // 2 == core, b & 1, 2 + (b & 1))

    is_middle = jnp.where((plane == 0) | (plane == 3), 0, 1)
    flags = jnp.stack([source_of(plane ^ r) for r in range(4)] + [is_middle]).astype(jnp.int32)
    places = jnp.stack([spot ^ r for r in range(PLANE)]).astype(jnp.int32)

    def plane_scan(k, v, rate, speed):
        def fade(span):
            return jnp.exp(-speed * span)

        ends = end_states(k, v, rate)
        other = exchange(ends, "ctx", 1)
        both = jnp.where(x_later, fade(float(rows)) * other + ends, fade(float(rows)) * ends + other)
        before = jnp.where(x_later, other, 0.0)
        other = exchange(both, "ctx", 2)
        before = before + jnp.where(y_later, fade((spot & 1).astype(jnp.float32) * rows) * other, 0.0)
        both = jnp.where(y_later, fade(2.0 * rows) * other + both, fade(2.0 * rows) * both + other)
        return both, before

    x_later, y_later = (spot & 1) != 0, (spot & 2) != 0
    w0, w1, w2, w3 = tie(*[group(w_out, r) for r in range(PLANE)])
    f0, n0 = far(w0), near(w0)
    both, before = box(plane_scan, k, v, rate, speed)
    n0, f0, w0, w1, w2, w3, both, before = tie(n0, f0, w0, w1, w2, w3, both, before)

    arrived = [exchange(w, "ctx", r + 1) for r, w in enumerate((w1, w2, w3))]
    decay = jnp.exp(-speed * float(PLANE * rows))
    last = shift_ctx(both, PLANE)
    earlier = shift_ctx(both + decay * last, 2 * PLANE)
    f0, w0, earlier = tie(f0, w0, earlier)
    out0, mid0 = outward(f0), across(w0)
    gated = gated_conv(q, k, v, rate, residue, skip, before, ([last, earlier], spot))
    rest = jnp.concatenate(arrived)
    gated, rest, out0, mid0 = tie(gated, rest, out0, mid0)

    nr, fr = near(rest), far(rest)
    ours = [gated] + [exchange(gated, "ctx", r) for r in range(1, PLANE)]
    theirs_x = exchange(ours[1], "ch", 1)
    wide = 2 * cols // 3
    restA, restB = rest[:, :wide], rest[:, wide:]
    fr, nr, rest, restA, restB, flags, places, theirs_x, *ours = tie(
        fr, nr, rest, restA, restB, flags, places, theirs_x, *ours
    )

    outA, midA = outward(fr[:, :wide]), across(restA)
    theirs = [theirs_x if r == 1 else exchange(x, "ch", 1) for r, x in enumerate(ours)]
    blocks = [
        (0, None, [((w0,), 0), ((rest,), 0)]),
        (1, None, [((n0,), 0), ((nr,), 0)]),
        (2, None, [((f0,), 0), ((fr,), 0)]),
    ]
    late, theirs[0] = tie(fr, theirs[0])
    frB = late[:, wide:]
    (accs,) = product(flags, places, ours, theirs, blocks, None, 0, cols, jnp.float32)
    outA, midA, frB, restB, *accs = tie(outA, midA, frB, restB, *accs)

    outB, midB = outward(frB), across(restB)

    def finish(first, width, out1, mid1):
        blocks = [(3, 4, [((out0, mid0), first), ((out1, mid1), 0)])]
        (made,) = product(flags, places, ours, theirs, blocks, accs, first, width, jnp.bfloat16)
        return [made[0]] + [exchange(made[r], "ctx", r) for r in range(1, PLANE)]

    return assemble(places, [finish(0, wide, outA, midA), finish(wide, cols - wide, outB, midB)])


def body(q, k, v, residue, rate, skip, w_out):
    rows, chan = q.shape
    modes = rate.shape[0]
    groups = chan // LANES
    count, cores = lax.axis_size("ctx"), lax.axis_size("ch")
    chunk, feats = w_out.shape
    split = (
        count == 4 * PLANE
        and cores == 2
        and chan == 8 * chunk
        and chunk % LANES == 0
        and feats % (6 * PLANE * LANES) == 0
    )
    skip = skip.reshape(groups, LANES)
    if split:
        return split_block(q, k, v, residue, rate, skip, w_out)
    ends = end_states(k, v, rate)
    enter = entering_states(ends, rate.reshape(modes, groups, LANES), rows)
    gated = gated_conv(q, k, v, rate, residue, skip, enter)
    gated = gated.transpose(1, 0, 2).reshape(rows, chan)
    full_gated = lax.all_gather(gated, "ch", axis=1, tiled=True)
    w_full = lax.all_gather(w_out, "ctx", axis=0, tiled=True)
    mixed = jnp.dot(full_gated, w_full, preferred_element_type=jnp.float32)
    return mixed.astype(jnp.bfloat16)


def solution(mesh):
    placed = (
        P("ctx", "ch"),
        P("ctx", "ch"),
        P("ctx", "ch"),
        P(None, "ch"),
        P(None, "ch"),
        P("ch"),
        P("ctx", "ch"),
    )
    return jax.shard_map(
        body, mesh=mesh, in_specs=placed, out_specs=P("ctx", "ch"), check_vma=False
    )
```

```python
import jax
import jax.numpy as jnp
from jax import lax
from jax.experimental import pallas as pl
from jax.experimental.pallas import tpu as pltpu
from jax.sharding import PartitionSpec as P

LANES = 128
RADIX = 4
PLANE = 4
VMEM_BYTES = 60 << 20


def spread_signal(k_ref, v_ref, sig_ref):
    rows, width = k_ref.shape
    groups = width // LANES
    for g in range(groups):
        cols = pl.ds(g * LANES, LANES)
        product = k_ref[:, cols].astype(jnp.float32) * v_ref[:, cols].astype(jnp.float32)
        sig_ref[pl.ds(g, rows, stride=groups), :] = product


def spread_modes(ref, out_ref):
    modes, width = ref.shape
    groups = width // LANES
    for g in range(groups):
        out_ref[pl.ds(g, modes, stride=groups), :] = ref[:, pl.ds(g * LANES, LANES)]


def ends_kernel(k_ref, v_ref, rate_ref, end_ref, sig_ref, mode_ref):
    rows, width = k_ref.shape
    modes, groups, _ = end_ref.shape
    spread_signal(k_ref, v_ref, sig_ref)
    spread_modes(rate_ref, mode_ref)
    decay = [jnp.exp(-mode_ref[pl.ds(m * groups, groups), :]) for m in range(modes)]

    def step(t, state):
        s = sig_ref[pl.ds(pl.multiple_of(t * groups, groups), groups), :]
        return tuple(d * h + s for d, h in zip(decay, state))

    zero = jnp.zeros((groups, LANES), jnp.float32)
    state = lax.fori_loop(0, rows, step, (zero,) * modes, unroll=16)
    for m in range(modes):
        end_ref[m] = state[m]


def conv_kernel(q_ref, k_ref, v_ref, rate_ref, residue_ref, skip_ref, enter_ref, *refs):
    *plane_refs, out_ref, sig_ref, conv_ref, mode_ref, weight_ref = refs
    rows, width = k_ref.shape
    modes, groups, _ = enter_ref.shape
    spread_signal(k_ref, v_ref, sig_ref)
    spread_modes(rate_ref, mode_ref)
    spread_modes(residue_ref, weight_ref)
    rates = [mode_ref[pl.ds(m * groups, groups), :] for m in range(modes)]
    decay = [jnp.exp(-rate) for rate in rates]
    weight = [weight_ref[pl.ds(m * groups, groups), :] * jnp.sqrt(2.0 * rate) for m, rate in enumerate(rates)]
    skip = skip_ref[...]
    enter = [enter_ref[m] for m in range(modes)]
    if plane_refs:
        *earlier_refs, spot_ref = plane_refs
        ahead = (spot_ref[0] * rows).astype(jnp.float32)
        for m, rate in enumerate(rates):
            for n, earlier_ref in enumerate(earlier_refs):
                enter[m] = enter[m] + jnp.exp(-rate * (ahead + float(n * PLANE * rows))) * earlier_ref[m]

    def step(t, state):
        at = pl.ds(pl.multiple_of(t * groups, groups), groups)
        s = sig_ref[at, :]
        state = tuple(d * h + s for d, h in zip(decay, state))
        terms = [c * h for c, h in zip(weight, state)] + [skip * s]
        while len(terms) > 1:
            terms = [sum(terms[i : i + 2]) for i in range(0, len(terms), 2)]
        conv_ref[at, :] = terms[0]
        return state

    lax.fori_loop(0, rows, step, tuple(enter), unroll=8)
    for g in range(groups):
        cols = pl.ds(g * LANES, LANES)
        conv = conv_ref[pl.ds(g, rows, stride=groups), :]
        out_ref[:, cols] = (q_ref[:, cols].astype(jnp.float32) * conv).astype(out_ref.dtype)


def block_specs(rows, modes, width):
    groups = width // LANES
    return (
        pl.BlockSpec((rows, width), lambda i: (0, i)),
        pl.BlockSpec((modes, width), lambda i: (0, i)),
        pl.BlockSpec((modes, groups, LANES), lambda i: (0, i, 0)),
        pl.BlockSpec((groups, LANES), lambda i: (i, 0)),
    )


def end_states(k, v, rate):
    rows, chan = k.shape
    modes = rate.shape[0]
    width = min(chan, 8 * LANES)
    wide, moded, state, _ = block_specs(rows, modes, width)
    return pl.pallas_call(
        ends_kernel,
        grid=(chan // width,),
        in_specs=[wide, wide, moded],
        out_specs=state,
        out_shape=jax.ShapeDtypeStruct((modes, chan // LANES, LANES), jnp.float32),
        scratch_shapes=[
            pltpu.VMEM((rows * width // LANES, LANES), jnp.float32),
            pltpu.VMEM((modes * width // LANES, LANES), jnp.float32),
        ],
        compiler_params=pltpu.CompilerParams(vmem_limit_bytes=VMEM_BYTES),
        cost_estimate=pl.CostEstimate(
            flops=2 * modes * rows * chan, bytes_accessed=4 * rows * chan, transcendentals=modes * chan
        ),
        name="end_states",
    )(k, v, rate)


def gated_conv(q, k, v, rate, residue, skip, enter, planes=None):
    rows, chan = k.shape
    modes = rate.shape[0]
    width = min(chan, 8 * LANES)
    wide, moded, state, single = block_specs(rows, modes, width)
    spread = pltpu.VMEM((rows * width // LANES, LANES), jnp.float32)
    moded_spread = pltpu.VMEM((modes * width // LANES, LANES), jnp.float32)
    extra, extra_specs = [], []
    if planes is not None:
        earlier, spot = planes
        extra = [*earlier, spot.reshape(1).astype(jnp.int32)]
        extra_specs = [state] * len(earlier) + [pl.BlockSpec(memory_space=pltpu.SMEM)]
    return pl.pallas_call(
        conv_kernel,
        grid=(chan // width,),
        in_specs=[wide, wide, wide, moded, moded, single, state] + extra_specs,
        out_specs=pl.BlockSpec((None, rows, width), lambda i: (i, 0, 0)),
        out_shape=jax.ShapeDtypeStruct((chan // width, rows, width), jnp.bfloat16),
        scratch_shapes=[spread, spread, moded_spread, moded_spread],
        compiler_params=pltpu.CompilerParams(vmem_limit_bytes=VMEM_BYTES),
        cost_estimate=pl.CostEstimate(
            flops=4 * modes * rows * chan, bytes_accessed=8 * rows * chan, transcendentals=2 * modes * chan
        ),
        name="gated_conv",
    )(q, k, v, rate, residue, skip, enter, *extra)


def shift_ctx(x, by):
    count = lax.axis_size("ctx")
    return lax.ppermute(x, "ctx", [(i, i + by) for i in range(count - by)])


def exchange(x, axis, flip):
    count = lax.axis_size(axis)
    return lax.ppermute(x, axis, [(i, i ^ flip) for i in range(count)])


def tie(*values):
    return lax.optimization_barrier(values)


def entering_states(ends, rate, rows):
    count = lax.axis_size("ctx")
    total = jnp.zeros_like(ends)
    for k in range(1, min(RADIX, count - 1) + 1):
        total = total + jnp.exp(-rate * float(rows * (k - 1))) * shift_ctx(ends, k)
    stride = RADIX
    while stride < count:
        base = total
        for k in range(1, RADIX):
            if stride * k < count:
                total = total + jnp.exp(-rate * float(rows * stride * k)) * shift_ctx(base, stride * k)
        stride *= RADIX
    return total


def box(fn, *args):
    once = (lax.axis_index("ctx") >= 0).astype(jnp.int32)
    shapes = jax.eval_shape(fn, *args)
    empty = pl.pallas_call(
        lambda *refs: None,
        out_specs=[pl.BlockSpec(memory_space=pl.ANY)] * len(shapes),
        out_shape=list(shapes),
        name="blank",
    )()

    def run(step, _):
        return fn(*tie(step, *args)[1:])

    return lax.fori_loop(0, once, run, tuple(empty))


def product(flags, places, ours, theirs, blocks, accs, first_col, cols, out_dtype):
    _, rows, depth = ours[0].shape
    chunk = depth // PLANE
    count, parts = len(blocks), len(ours)
    weights = [array for _, _, pieces in blocks for choices, _ in pieces for array in choices]
    accs = accs or []

    def kernel(flag_ref, place_ref, *refs):
        our_refs, their_refs, refs = refs[:parts], refs[parts : 2 * parts], refs[2 * parts :]
        weight_refs, refs = list(refs[: len(weights)]), refs[len(weights) :]
        acc_refs, out_refs = refs[: len(accs)], refs[len(accs) : len(accs) + parts]
        gated_buf, weight_buf, acc_buf, gated_sems, weight_sems, acc_sem = refs[-6:]

        def target(b, at):
            start = pl.multiple_of(b * depth + place_ref[at // chunk] * chunk, chunk)
            return weight_buf.at[pl.ds(start, chunk), :]

        for b, (flag, pick, pieces) in enumerate(blocks):
            row = 0
            for choices, col in pieces:
                for c in range(len(choices)):
                    ref = weight_refs.pop(0)
                    for at in range(0, ref.shape[0], chunk):
                        source = ref.at[pl.ds(at, chunk), pl.ds(col, cols)]
                        copy = pltpu.make_async_copy(source, target(b, row + at), weight_sems.at[b])
                        if pick is None:
                            copy.start()
                        else:
                            pl.when(flag_ref[pick] == c)(copy.start)
                row += choices[0].shape[0]
            half = flag_ref[flag] & 1
            for r in range(parts):
                for c, refs_of in enumerate((our_refs, their_refs)):
                    target_rows = gated_buf.at[b, pl.ds(r * rows, rows), :]
                    copy = pltpu.make_async_copy(refs_of[r].at[half], target_rows, gated_sems.at[b])
                    pl.when(flag_ref[flag] // 2 == c)(copy.start)
        for r, acc_ref in enumerate(acc_refs):
            pltpu.make_async_copy(acc_ref.at[:, pl.ds(first_col, cols)], acc_buf.at[r], acc_sem).start()
        for b in range(count):
            block = weight_buf.at[pl.ds(b * depth, depth), :]
            pltpu.make_async_copy(block, block, weight_sems.at[b]).wait()
            pltpu.make_async_copy(gated_buf.at[b], gated_buf.at[b], gated_sems.at[b]).wait()
            for col in range(0, cols, 2 * LANES):
                here = pl.ds(col, min(2 * LANES, cols - col))
                made = jnp.dot(
                    gated_buf[b], weight_buf[pl.ds(b * depth, depth), here], preferred_element_type=jnp.float32
                )
                if accs and not b and not col:
                    pltpu.make_async_copy(acc_buf, acc_buf, acc_sem).wait()
                for r in range(parts):
                    total = made[r * rows : (r + 1) * rows]
                    if b:
                        total = total + out_refs[r][:, here]
                    elif accs:
                        total = total + acc_buf[r, :, here]
                    out_refs[r][:, here] = total.astype(out_dtype)

    smem = pl.BlockSpec(memory_space=pltpu.SMEM)
    anywhere = pl.BlockSpec(memory_space=pl.ANY)
    made = pl.pallas_call(
        kernel,
        in_specs=[smem, smem] + [anywhere] * (2 * parts + len(weights) + len(accs)),
        out_specs=[pl.BlockSpec(memory_space=pltpu.VMEM)] * parts,
        out_shape=[jax.ShapeDtypeStruct((rows, cols), out_dtype)] * parts,
        scratch_shapes=[
            pltpu.VMEM((count, parts * rows, depth), jnp.bfloat16),
            pltpu.VMEM((count * depth, cols), jnp.bfloat16),
            pltpu.VMEM((parts, rows, cols) if accs else (8, LANES), jnp.float32),
            pltpu.SemaphoreType.DMA((count,)),
            pltpu.SemaphoreType.DMA((count,)),
            pltpu.SemaphoreType.DMA,
        ],
        compiler_params=pltpu.CompilerParams(vmem_limit_bytes=VMEM_BYTES),
        cost_estimate=pl.CostEstimate(
            flops=2 * parts * rows * depth * count * cols,
            bytes_accessed=2 * count * depth * (parts * rows + cols),
            transcendentals=0,
        ),
        name="product",
    )(flags, places, *ours, *theirs, *weights, *accs)
    return [list(made)]


def assemble(places, parts):
    rows = parts[0][0].shape[0]
    widths = [part[0].shape[1] for part in parts]
    cols = sum(widths)
    flat = [piece for part in parts for piece in part]

    def kernel(place_ref, *refs):
        *piece_refs, out_ref, sems = refs
        copies = []
        first = 0
        for part, width in enumerate(widths):
            for r in range(PLANE):
                at = part * PLANE + r
                start = pl.multiple_of(place_ref[r] * cols + first, LANES)
                target = out_ref.at[:, pl.ds(start, width)]
                copies.append(pltpu.make_async_copy(piece_refs[at], target, sems.at[at]))
                copies[-1].start()
            first += width
        for copy in copies:
            copy.wait()

    return pl.pallas_call(
        kernel,
        in_specs=[pl.BlockSpec(memory_space=pltpu.SMEM)] + [pl.BlockSpec(memory_space=pltpu.VMEM)] * len(flat),
        out_specs=pl.BlockSpec(memory_space=pl.ANY),
        out_shape=jax.ShapeDtypeStruct((rows, cols * PLANE), flat[0].dtype),
        scratch_shapes=[pltpu.SemaphoreType.DMA((len(flat),))],
        compiler_params=pltpu.CompilerParams(vmem_limit_bytes=16 << 20),
        name="assemble",
    )(places, *flat)


def split_block(q, k, v, residue, rate, skip, w_out):
    rows, chan = q.shape
    modes = rate.shape[0]
    me = lax.axis_index("ctx")
    core = lax.axis_index("ch")
    spot, plane = me & (PLANE - 1), me // PLANE
    count = lax.axis_size("ctx")
    chunk, feats = w_out.shape
    cols = feats // PLANE
    speed = rate.reshape(modes, chan // LANES, LANES)

    def far(x):
        return exchange(x, "ctx", 2 * PLANE)

    def near(x):
        return exchange(x, "ctx", PLANE)

    middle = [i for i in range(count) if PLANE <= i < 3 * PLANE]

    def across(x):
        return lax.ppermute(x, "ctx", [(i, i ^ (3 * PLANE)) for i in middle])

    def outward(x):
        return lax.ppermute(x, "ctx", [(i, i ^ PLANE) for i in middle])

    def group(x, r):
        return lax.dynamic_slice_in_dim(x, (spot ^ r) * cols, cols, axis=1)

    def source_of(b):
        return jnp.where(b // 2 == core, b & 1, 2 + (b & 1))

    is_middle = jnp.where((plane == 0) | (plane == 3), 0, 1)
    flags = jnp.stack([source_of(plane ^ r) for r in range(4)] + [is_middle]).astype(jnp.int32)
    places = jnp.stack([spot ^ r for r in range(PLANE)]).astype(jnp.int32)

    def plane_scan(k, v, rate, speed):
        def fade(span):
            return jnp.exp(-speed * span)

        ends = end_states(k, v, rate)
        other = exchange(ends, "ctx", 1)
        both = jnp.where(x_later, fade(float(rows)) * other + ends, fade(float(rows)) * ends + other)
        before = jnp.where(x_later, other, 0.0)
        other = exchange(both, "ctx", 2)
        before = before + jnp.where(y_later, fade((spot & 1).astype(jnp.float32) * rows) * other, 0.0)
        both = jnp.where(y_later, fade(2.0 * rows) * other + both, fade(2.0 * rows) * both + other)
        return both, before

    x_later, y_later = (spot & 1) != 0, (spot & 2) != 0
    w0, w1, w2, w3 = tie(*[group(w_out, r) for r in range(PLANE)])
    f0, n0 = far(w0), near(w0)
    both, before = box(plane_scan, k, v, rate, speed)
    n0, f0, w0, w1, w2, w3, both, before = tie(n0, f0, w0, w1, w2, w3, both, before)

    arrived = [exchange(w, "ctx", r + 1) for r, w in enumerate((w1, w2, w3))]
    decay = jnp.exp(-speed * float(PLANE * rows))
    last = shift_ctx(both, PLANE)
    earlier = shift_ctx(both + decay * last, 2 * PLANE)
    f0, w0, earlier = tie(f0, w0, earlier)
    out0, mid0 = outward(f0), across(w0)
    gated = gated_conv(q, k, v, rate, residue, skip, before, ([last, earlier], spot))
    rest = jnp.concatenate(arrived)
    gated, rest, out0, mid0 = tie(gated, rest, out0, mid0)

    nr, fr = near(rest), far(rest)
    ours = [gated] + [exchange(gated, "ctx", r) for r in range(1, PLANE)]
    theirs_x = exchange(ours[1], "ch", 1)
    wide = 2 * cols // 3
    restA, restB = rest[:, :wide], rest[:, wide:]
    fr, nr, rest, restA, restB, flags, places, theirs_x, *ours = tie(
        fr, nr, rest, restA, restB, flags, places, theirs_x, *ours
    )

    outA, midA = outward(fr[:, :wide]), across(restA)
    theirs = [theirs_x if r == 1 else exchange(x, "ch", 1) for r, x in enumerate(ours)]
    blocks = [
        (0, None, [((w0,), 0), ((rest,), 0)]),
        (1, None, [((n0,), 0), ((nr,), 0)]),
        (2, None, [((f0,), 0), ((fr,), 0)]),
    ]
    late, theirs[0] = tie(fr, theirs[0])
    frB = late[:, wide:]
    (accs,) = product(flags, places, ours, theirs, blocks, None, 0, cols, jnp.float32)
    outA, midA, frB, restB, *accs = tie(outA, midA, frB, restB, *accs)

    outB, midB = outward(frB), across(restB)

    def finish(first, width, out1, mid1):
        blocks = [(3, 4, [((out0, mid0), first), ((out1, mid1), 0)])]
        (made,) = product(flags, places, ours, theirs, blocks, accs, first, width, jnp.bfloat16)
        return [made[0]] + [exchange(made[r], "ctx", r) for r in range(1, PLANE)]

    return assemble(places, [finish(0, wide, outA, midA), finish(wide, cols - wide, outB, midB)])


def body(q, k, v, residue, rate, skip, w_out):
    rows, chan = q.shape
    modes = rate.shape[0]
    groups = chan // LANES
    count, cores = lax.axis_size("ctx"), lax.axis_size("ch")
    chunk, feats = w_out.shape
    split = (
        count == 4 * PLANE
        and cores == 2
        and chan == 8 * chunk
        and chunk % LANES == 0
        and feats % (6 * PLANE * LANES) == 0
    )
    skip = skip.reshape(groups, LANES)
    if split:
        return split_block(q, k, v, residue, rate, skip, w_out)
    ends = end_states(k, v, rate)
    enter = entering_states(ends, rate.reshape(modes, groups, LANES), rows)
    gated = gated_conv(q, k, v, rate, residue, skip, enter)
    gated = gated.transpose(1, 0, 2).reshape(rows, chan)
    full_gated = lax.all_gather(gated, "ch", axis=1, tiled=True)
    w_full = lax.all_gather(w_out, "ctx", axis=0, tiled=True)
    mixed = jnp.dot(full_gated, w_full, preferred_element_type=jnp.float32)
    return mixed.astype(jnp.bfloat16)


def solution(mesh):
    placed = (
        P("ctx", "ch"),
        P("ctx", "ch"),
        P("ctx", "ch"),
        P(None, "ch"),
        P(None, "ch"),
        P("ch"),
        P("ctx", "ch"),
    )
    return jax.shard_map(
        body, mesh=mesh, in_specs=placed, out_specs=P("ctx", "ch"), check_vma=False
    )
```

```python
import jax
import jax.numpy as jnp
from jax import lax
from jax.experimental import pallas as pl
from jax.experimental.pallas import tpu as pltpu
from jax.sharding import PartitionSpec as P

LANES = 128
RADIX = 4
PLANE = 4
VMEM_BYTES = 60 << 20


def spread_signal(k_ref, v_ref, sig_ref):
    rows, width = k_ref.shape
    groups = width // LANES
    for g in range(groups):
        cols = pl.ds(g * LANES, LANES)
        product = k_ref[:, cols].astype(jnp.float32) * v_ref[:, cols].astype(jnp.float32)
        sig_ref[pl.ds(g, rows, stride=groups), :] = product


def spread_modes(ref, out_ref):
    modes, width = ref.shape
    groups = width // LANES
    for g in range(groups):
        out_ref[pl.ds(g, modes, stride=groups), :] = ref[:, pl.ds(g * LANES, LANES)]


def ends_kernel(k_ref, v_ref, rate_ref, end_ref, sig_ref, mode_ref):
    rows, width = k_ref.shape
    modes, groups, _ = end_ref.shape
    spread_signal(k_ref, v_ref, sig_ref)
    spread_modes(rate_ref, mode_ref)
    decay = [jnp.exp(-mode_ref[pl.ds(m * groups, groups), :]) for m in range(modes)]

    def step(t, state):
        s = sig_ref[pl.ds(pl.multiple_of(t * groups, groups), groups), :]
        return tuple(d * h + s for d, h in zip(decay, state))

    zero = jnp.zeros((groups, LANES), jnp.float32)
    state = lax.fori_loop(0, rows, step, (zero,) * modes, unroll=16)
    for m in range(modes):
        end_ref[m] = state[m]


def conv_kernel(q_ref, k_ref, v_ref, rate_ref, residue_ref, skip_ref, enter_ref, *refs):
    *plane_refs, out_ref, sig_ref, conv_ref, mode_ref, weight_ref = refs
    rows, width = k_ref.shape
    modes, groups, _ = enter_ref.shape
    spread_signal(k_ref, v_ref, sig_ref)
    spread_modes(rate_ref, mode_ref)
    spread_modes(residue_ref, weight_ref)
    rates = [mode_ref[pl.ds(m * groups, groups), :] for m in range(modes)]
    decay = [jnp.exp(-rate) for rate in rates]
    weight = [weight_ref[pl.ds(m * groups, groups), :] * jnp.sqrt(2.0 * rate) for m, rate in enumerate(rates)]
    skip = skip_ref[...]
    enter = [enter_ref[m] for m in range(modes)]
    if plane_refs:
        *earlier_refs, spot_ref = plane_refs
        ahead = (spot_ref[0] * rows).astype(jnp.float32)
        for m, rate in enumerate(rates):
            for n, earlier_ref in enumerate(earlier_refs):
                enter[m] = enter[m] + jnp.exp(-rate * (ahead + float(n * PLANE * rows))) * earlier_ref[m]

    def step(t, state):
        at = pl.ds(pl.multiple_of(t * groups, groups), groups)
        s = sig_ref[at, :]
        state = tuple(d * h + s for d, h in zip(decay, state))
        terms = [c * h for c, h in zip(weight, state)] + [skip * s]
        while len(terms) > 1:
            terms = [sum(terms[i : i + 2]) for i in range(0, len(terms), 2)]
        conv_ref[at, :] = terms[0]
        return state

    lax.fori_loop(0, rows, step, tuple(enter), unroll=8)
    for g in range(groups):
        cols = pl.ds(g * LANES, LANES)
        conv = conv_ref[pl.ds(g, rows, stride=groups), :]
        out_ref[:, cols] = (q_ref[:, cols].astype(jnp.float32) * conv).astype(out_ref.dtype)


def block_specs(rows, modes, width):
    groups = width // LANES
    return (
        pl.BlockSpec((rows, width), lambda i: (0, i)),
        pl.BlockSpec((modes, width), lambda i: (0, i)),
        pl.BlockSpec((modes, groups, LANES), lambda i: (0, i, 0)),
        pl.BlockSpec((groups, LANES), lambda i: (i, 0)),
    )


def end_states(k, v, rate):
    rows, chan = k.shape
    modes = rate.shape[0]
    width = min(chan, 8 * LANES)
    wide, moded, state, _ = block_specs(rows, modes, width)
    return pl.pallas_call(
        ends_kernel,
        grid=(chan // width,),
        in_specs=[wide, wide, moded],
        out_specs=state,
        out_shape=jax.ShapeDtypeStruct((modes, chan // LANES, LANES), jnp.float32),
        scratch_shapes=[
            pltpu.VMEM((rows * width // LANES, LANES), jnp.float32),
            pltpu.VMEM((modes * width // LANES, LANES), jnp.float32),
        ],
        compiler_params=pltpu.CompilerParams(vmem_limit_bytes=VMEM_BYTES),
        cost_estimate=pl.CostEstimate(
            flops=2 * modes * rows * chan, bytes_accessed=4 * rows * chan, transcendentals=modes * chan
        ),
        name="end_states",
    )(k, v, rate)


def gated_conv(q, k, v, rate, residue, skip, enter, planes=None):
    rows, chan = k.shape
    modes = rate.shape[0]
    width = min(chan, 8 * LANES)
    wide, moded, state, single = block_specs(rows, modes, width)
    spread = pltpu.VMEM((rows * width // LANES, LANES), jnp.float32)
    moded_spread = pltpu.VMEM((modes * width // LANES, LANES), jnp.float32)
    extra, extra_specs = [], []
    if planes is not None:
        earlier, spot = planes
        extra = [*earlier, spot.reshape(1).astype(jnp.int32)]
        extra_specs = [state] * len(earlier) + [pl.BlockSpec(memory_space=pltpu.SMEM)]
    return pl.pallas_call(
        conv_kernel,
        grid=(chan // width,),
        in_specs=[wide, wide, wide, moded, moded, single, state] + extra_specs,
        out_specs=pl.BlockSpec((None, rows, width), lambda i: (i, 0, 0)),
        out_shape=jax.ShapeDtypeStruct((chan // width, rows, width), jnp.bfloat16),
        scratch_shapes=[spread, spread, moded_spread, moded_spread],
        compiler_params=pltpu.CompilerParams(vmem_limit_bytes=VMEM_BYTES),
        cost_estimate=pl.CostEstimate(
            flops=4 * modes * rows * chan, bytes_accessed=8 * rows * chan, transcendentals=2 * modes * chan
        ),
        name="gated_conv",
    )(q, k, v, rate, residue, skip, enter, *extra)


def shift_ctx(x, by):
    count = lax.axis_size("ctx")
    return lax.ppermute(x, "ctx", [(i, i + by) for i in range(count - by)])


def exchange(x, axis, flip):
    count = lax.axis_size(axis)
    return lax.ppermute(x, axis, [(i, i ^ flip) for i in range(count)])


def tie(*values):
    return lax.optimization_barrier(values)


def entering_states(ends, rate, rows):
    count = lax.axis_size("ctx")
    total = jnp.zeros_like(ends)
    for k in range(1, min(RADIX, count - 1) + 1):
        total = total + jnp.exp(-rate * float(rows * (k - 1))) * shift_ctx(ends, k)
    stride = RADIX
    while stride < count:
        base = total
        for k in range(1, RADIX):
            if stride * k < count:
                total = total + jnp.exp(-rate * float(rows * stride * k)) * shift_ctx(base, stride * k)
        stride *= RADIX
    return total


def box(fn, *args):
    once = (lax.axis_index("ctx") >= 0).astype(jnp.int32)
    shapes = jax.eval_shape(fn, *args)
    empty = pl.pallas_call(
        lambda *refs: None,
        out_specs=[pl.BlockSpec(memory_space=pl.ANY)] * len(shapes),
        out_shape=list(shapes),
        name="blank",
    )()

    def run(step, _):
        return fn(*tie(step, *args)[1:])

    return lax.fori_loop(0, once, run, tuple(empty))


def product(flags, places, ours, theirs, blocks, accs, first_col, cols, out_dtype):
    _, rows, depth = ours[0].shape
    chunk = depth // PLANE
    count, parts = len(blocks), len(ours)
    weights = [array for _, _, pieces in blocks for choices, _ in pieces for array in choices]
    accs = accs or []

    def kernel(flag_ref, place_ref, *refs):
        our_refs, their_refs, refs = refs[:parts], refs[parts : 2 * parts], refs[2 * parts :]
        weight_refs, refs = list(refs[: len(weights)]), refs[len(weights) :]
        acc_refs, out_refs = refs[: len(accs)], refs[len(accs) : len(accs) + parts]
        gated_buf, weight_buf, acc_buf, gated_sems, weight_sems, acc_sem = refs[-6:]

        def target(b, at):
            start = pl.multiple_of(b * depth + place_ref[at // chunk] * chunk, chunk)
            return weight_buf.at[pl.ds(start, chunk), :]

        for b, (flag, pick, pieces) in enumerate(blocks):
            row = 0
            for choices, col in pieces:
                for c in range(len(choices)):
                    ref = weight_refs.pop(0)
                    for at in range(0, ref.shape[0], chunk):
                        source = ref.at[pl.ds(at, chunk), pl.ds(col, cols)]
                        copy = pltpu.make_async_copy(source, target(b, row + at), weight_sems.at[b])
                        if pick is None:
                            copy.start()
                        else:
                            pl.when(flag_ref[pick] == c)(copy.start)
                row += choices[0].shape[0]
            half = flag_ref[flag] & 1
            for r in range(parts):
                for c, refs_of in enumerate((our_refs, their_refs)):
                    target_rows = gated_buf.at[b, pl.ds(r * rows, rows), :]
                    copy = pltpu.make_async_copy(refs_of[r].at[half], target_rows, gated_sems.at[b])
                    pl.when(flag_ref[flag] // 2 == c)(copy.start)
        for r, acc_ref in enumerate(acc_refs):
            pltpu.make_async_copy(acc_ref.at[:, pl.ds(first_col, cols)], acc_buf.at[r], acc_sem).start()
        for b in range(count):
            block = weight_buf.at[pl.ds(b * depth, depth), :]
            pltpu.make_async_copy(block, block, weight_sems.at[b]).wait()
            pltpu.make_async_copy(gated_buf.at[b], gated_buf.at[b], gated_sems.at[b]).wait()
            if accs and not b:
                pltpu.make_async_copy(acc_buf, acc_buf, acc_sem).wait()
            for col in range(0, cols, 2 * LANES):
                here = pl.ds(col, min(2 * LANES, cols - col))
                made = jnp.dot(
                    gated_buf[b], weight_buf[pl.ds(b * depth, depth), here], preferred_element_type=jnp.float32
                )
                for r in range(parts):
                    total = made[r * rows : (r + 1) * rows]
                    if b:
                        total = total + out_refs[r][:, here]
                    elif accs:
                        total = total + acc_buf[r, :, here]
                    out_refs[r][:, here] = total.astype(out_dtype)

    smem = pl.BlockSpec(memory_space=pltpu.SMEM)
    anywhere = pl.BlockSpec(memory_space=pl.ANY)
    made = pl.pallas_call(
        kernel,
        in_specs=[smem, smem] + [anywhere] * (2 * parts + len(weights) + len(accs)),
        out_specs=[pl.BlockSpec(memory_space=pltpu.VMEM)] * parts,
        out_shape=[jax.ShapeDtypeStruct((rows, cols), out_dtype)] * parts,
        scratch_shapes=[
            pltpu.VMEM((count, parts * rows, depth), jnp.bfloat16),
            pltpu.VMEM((count * depth, cols), jnp.bfloat16),
            pltpu.VMEM((parts, rows, cols) if accs else (8, LANES), jnp.float32),
            pltpu.SemaphoreType.DMA((count,)),
            pltpu.SemaphoreType.DMA((count,)),
            pltpu.SemaphoreType.DMA,
        ],
        compiler_params=pltpu.CompilerParams(vmem_limit_bytes=VMEM_BYTES),
        cost_estimate=pl.CostEstimate(
            flops=2 * parts * rows * depth * count * cols,
            bytes_accessed=2 * count * depth * (parts * rows + cols),
            transcendentals=0,
        ),
        name="product",
    )(flags, places, *ours, *theirs, *weights, *accs)
    return [list(made)]


def assemble(places, parts):
    rows = parts[0][0].shape[0]
    widths = [part[0].shape[1] for part in parts]
    cols = sum(widths)
    flat = [piece for part in parts for piece in part]

    def kernel(place_ref, *refs):
        *piece_refs, out_ref, sems = refs
        copies = []
        first = 0
        for part, width in enumerate(widths):
            for r in range(PLANE):
                at = part * PLANE + r
                start = pl.multiple_of(place_ref[r] * cols + first, LANES)
                target = out_ref.at[:, pl.ds(start, width)]
                copies.append(pltpu.make_async_copy(piece_refs[at], target, sems.at[at]))
                copies[-1].start()
            first += width
        for copy in copies:
            copy.wait()

    return pl.pallas_call(
        kernel,
        in_specs=[pl.BlockSpec(memory_space=pltpu.SMEM)] + [pl.BlockSpec(memory_space=pltpu.VMEM)] * len(flat),
        out_specs=pl.BlockSpec(memory_space=pl.ANY),
        out_shape=jax.ShapeDtypeStruct((rows, cols * PLANE), flat[0].dtype),
        scratch_shapes=[pltpu.SemaphoreType.DMA((len(flat),))],
        compiler_params=pltpu.CompilerParams(vmem_limit_bytes=16 << 20),
        name="assemble",
    )(places, *flat)


def split_block(q, k, v, residue, rate, skip, w_out):
    rows, chan = q.shape
    modes = rate.shape[0]
    me = lax.axis_index("ctx")
    core = lax.axis_index("ch")
    spot, plane = me & (PLANE - 1), me // PLANE
    count = lax.axis_size("ctx")
    chunk, feats = w_out.shape
    cols = feats // PLANE
    speed = rate.reshape(modes, chan // LANES, LANES)

    def far(x):
        return exchange(x, "ctx", 2 * PLANE)

    def near(x):
        return exchange(x, "ctx", PLANE)

    middle = [i for i in range(count) if PLANE <= i < 3 * PLANE]

    def across(x):
        return lax.ppermute(x, "ctx", [(i, i ^ (3 * PLANE)) for i in middle])

    def outward(x):
        return lax.ppermute(x, "ctx", [(i, i ^ PLANE) for i in middle])

    def group(x, r):
        return lax.dynamic_slice_in_dim(x, (spot ^ r) * cols, cols, axis=1)

    def source_of(b):
        return jnp.where(b // 2 == core, b & 1, 2 + (b & 1))

    is_middle = jnp.where((plane == 0) | (plane == 3), 0, 1)
    flags = jnp.stack([source_of(plane ^ r) for r in range(4)] + [is_middle]).astype(jnp.int32)
    places = jnp.stack([spot ^ r for r in range(PLANE)]).astype(jnp.int32)

    def plane_scan(k, v, rate, speed):
        def fade(span):
            return jnp.exp(-speed * span)

        ends = end_states(k, v, rate)
        other = exchange(ends, "ctx", 1)
        both = jnp.where(x_later, fade(float(rows)) * other + ends, fade(float(rows)) * ends + other)
        before = jnp.where(x_later, other, 0.0)
        other = exchange(both, "ctx", 2)
        before = before + jnp.where(y_later, fade((spot & 1).astype(jnp.float32) * rows) * other, 0.0)
        both = jnp.where(y_later, fade(2.0 * rows) * other + both, fade(2.0 * rows) * both + other)
        return both, before

    x_later, y_later = (spot & 1) != 0, (spot & 2) != 0
    w0, w1, w2, w3 = tie(*[group(w_out, r) for r in range(PLANE)])
    f0, n0 = far(w0), near(w0)
    both, before = box(plane_scan, k, v, rate, speed)
    n0, f0, w0, w1, w2, w3, both, before = tie(n0, f0, w0, w1, w2, w3, both, before)

    arrived = [exchange(w, "ctx", r + 1) for r, w in enumerate((w1, w2, w3))]
    decay = jnp.exp(-speed * float(PLANE * rows))
    last = shift_ctx(both, PLANE)
    earlier = shift_ctx(both + decay * last, 2 * PLANE)
    f0, w0, earlier = tie(f0, w0, earlier)
    out0, mid0 = outward(f0), across(w0)
    gated = gated_conv(q, k, v, rate, residue, skip, before, ([last, earlier], spot))
    rest = jnp.concatenate(arrived)
    gated, rest, out0, mid0 = tie(gated, rest, out0, mid0)

    nr, fr = near(rest), far(rest)
    ours = [gated] + [exchange(gated, "ctx", r) for r in range(1, PLANE)]
    theirs_x = exchange(ours[1], "ch", 1)
    wide = 2 * cols // 3
    restA, restB = rest[:, :wide], rest[:, wide:]
    fr, nr, rest, restA, restB, flags, places, theirs_x, *ours = tie(
        fr, nr, rest, restA, restB, flags, places, theirs_x, *ours
    )

    outA, midA = outward(fr[:, :wide]), across(restA)
    theirs = [theirs_x if r == 1 else exchange(x, "ch", 1) for r, x in enumerate(ours)]
    blocks = [
        (0, None, [((w0,), 0), ((rest,), 0)]),
        (1, None, [((n0,), 0), ((nr,), 0)]),
        (2, None, [((f0,), 0), ((fr,), 0)]),
    ]
    late, theirs[0] = tie(fr, theirs[0])
    frB = late[:, wide:]
    (accs,) = product(flags, places, ours, theirs, blocks, None, 0, cols, jnp.float32)
    outA, midA, frB, restB, *accs = tie(outA, midA, frB, restB, *accs)

    outB, midB = outward(frB), across(restB)

    def finish(first, width, out1, mid1):
        blocks = [(3, 4, [((out0, mid0), first), ((out1, mid1), 0)])]
        (made,) = product(flags, places, ours, theirs, blocks, accs, first, width, jnp.bfloat16)
        return [made[0]] + [exchange(made[r], "ctx", r) for r in range(1, PLANE)]

    return assemble(places, [finish(0, wide, outA, midA), finish(wide, cols - wide, outB, midB)])


def body(q, k, v, residue, rate, skip, w_out):
    rows, chan = q.shape
    modes = rate.shape[0]
    groups = chan // LANES
    count, cores = lax.axis_size("ctx"), lax.axis_size("ch")
    chunk, feats = w_out.shape
    split = (
        count == 4 * PLANE
        and cores == 2
        and chan == 8 * chunk
        and chunk % LANES == 0
        and feats % (6 * PLANE * LANES) == 0
    )
    skip = skip.reshape(groups, LANES)
    if split:
        return split_block(q, k, v, residue, rate, skip, w_out)
    ends = end_states(k, v, rate)
    enter = entering_states(ends, rate.reshape(modes, groups, LANES), rows)
    gated = gated_conv(q, k, v, rate, residue, skip, enter)
    gated = gated.transpose(1, 0, 2).reshape(rows, chan)
    full_gated = lax.all_gather(gated, "ch", axis=1, tiled=True)
    w_full = lax.all_gather(w_out, "ctx", axis=0, tiled=True)
    mixed = jnp.dot(full_gated, w_full, preferred_element_type=jnp.float32)
    return mixed.astype(jnp.bfloat16)


def solution(mesh):
    placed = (
        P("ctx", "ch"),
        P("ctx", "ch"),
        P("ctx", "ch"),
        P(None, "ch"),
        P(None, "ch"),
        P("ch"),
        P("ctx", "ch"),
    )
    return jax.shard_map(
        body, mesh=mesh, in_specs=placed, out_specs=P("ctx", "ch"), check_vma=False
    )
```
